32 devices in a mesh: ctx: 8 (over z, y), wa: 4 (over x, core).
Axes of the slice: x: 2, y: 2, z: 4, core: 2. Of those that a mesh axis runs over, the one named last changes fastest.
Arguments:
- tokens: bfloat16 [4, 2048, 896], P('wa', 'ctx'), may hold values from -6 to 6
- neighbours: bfloat16 [4, 32, 2, 128, 896], P('wa', 'ctx'), may hold values from -6 to 6
- cotangent: bfloat16 [4, 2048, 896], P('wa', 'ctx'), may hold values from -6 to 6
- selfnorm: bfloat16 [896], P('wa'), may hold values from 0.099609375 to 1.8984375
- selfquery: bfloat16 [896, 1024], P('wa'), may hold values from -0.1875 to 0.1875
- selfkey: bfloat16 [896, 1024], P('wa'), may hold values from -0.1875 to 0.1875
- selfvalue: bfloat16 [896, 1024], P('wa'), may hold values from -0.1875 to 0.1875
- selfout: bfloat16 [1024, 896], P('wa'), may hold values from -1.5 to 1.5
- biastable: bfloat16 [32, 16], P('wa'), may hold values from -4 to 4
- crossnorm: bfloat16 [896], P('wa'), may hold values from 0.099609375 to 1.8984375
- crossquery: bfloat16 [896, 1024], P('wa'), may hold values from -0.1875 to 0.1875
- crosskey: bfloat16 [896, 1024], P('wa'), may hold values from -0.1875 to 0.1875
- crossvalue: bfloat16 [896, 1024], P('wa'), may hold values from -0.1875 to 0.1875
- crossout: bfloat16 [1024, 896], P('wa'), may hold values from -1.5 to 1.5
- feednorm: bfloat16 [896], P('wa'), may hold values from 0.099609375 to 1.8984375
- feedin: bfloat16 [896, 3584], P('wa'), may hold values from -0.1875 to 0.1875
- feedbias: bfloat16 [3584], P('wa'), may hold values from -3 to 3
- feedout: bfloat16 [3584, 896], P('wa'), may hold values from -0.09375 to 0.09375
- outbias: bfloat16 [896], P('wa'), may hold values from -3 to 3
Outputs:
- result: bfloat16 [4, 2048, 896], P('wa', 'ctx')
- grad_tokens: bfloat16 [4, 2048, 896], P('wa', 'ctx')
- grad_neighbours: bfloat16 [4, 32, 2, 128, 896], P('wa', 'ctx')
- grad_selfnorm: float32 [896], P('wa')
- grad_selfquery: float32 [896, 1024], P('wa')
- grad_selfkey: float32 [896, 1024], P('wa')
- grad_selfvalue: float32 [896, 1024], P('wa')
- grad_selfout: float32 [1024, 896], P('wa')
- grad_biastable: float32 [32, 16], P('wa')
- grad_crossnorm: float32 [896], P('wa')
- grad_crossquery: float32 [896, 1024], P('wa')
- grad_crosskey: float32 [896, 1024], P('wa')
- grad_crossvalue: float32 [896, 1024], P('wa')
- grad_crossout: float32 [1024, 896], P('wa')
- grad_feednorm: float32 [896], P('wa')
- grad_feedin: float32 [896, 3584], P('wa')
- grad_feedbias: float32 [3584], P('wa')
- grad_feedout: float32 [3584, 896], P('wa')
- grad_outbias: float32 [896], P('wa')
The draws below stay inside these ranges and needn't reach their ends.
All inputs are finite; a program needn't handle non-finite values.
Results may differ from the reference program's by a relative error of at most 0.03.
Values may be sent and summed in bfloat16 or wider, within the bound.
A program may use at most 320 MiB of HBM per device.

```python
import math
import jax
import jax.numpy as jnp
from jax import lax

D = 896
H = 16
HD = 64
FF = 3584
AW = 1024
NB = 32
MAXD = 128
BLOCK = 256
SPAN = 64
NEIGH = 2
RLEN = 128
SEQ = 2048
SEQS = 4
NCH = 32


def shard_levels(stream_key, extent, split, least, largest):
    level, own = 1.0, jax.random.fold_in(stream_key, 6)
    for position, parts in split:
        steps = jnp.exp(jax.random.uniform(jax.random.fold_in(own, position), (parts,), jnp.float32, least / len(split), largest / len(split)))
        level = level * jnp.repeat(steps, extent[position] // parts).reshape([-1 if axis == position else 1 for axis in range(len(extent))])
    return level


def noise(stream_key, extent, scale, reach, shards=(), held_as=jnp.bfloat16):
    factor_of = shard_levels(stream_key, extent, shards, -0.22, 0.18) if shards else 1.0
    result = jax.random.normal(stream_key, extent, jnp.float32) * scale * factor_of
    return jnp.minimum(jnp.maximum(result, -reach), reach).astype(held_as)


def setup_inputs(seed: int = 0) -> dict:
    key_of = jax.random.split(jax.random.key(seed), 20)
    return {
        "tokens": noise(key_of[0], (SEQS, SEQ, D), 1.0, 6.0, ((0, 4), (1, 8))),
        "neighbours": noise(key_of[1], (SEQS, NCH, NEIGH, RLEN, D), 1.0, 6.0, ((0, 4), (1, 8))),
        "cotangent": noise(key_of[2], (SEQS, SEQ, D), 1.0, 6.0, ((0, 4), (1, 8))),
        "selfnorm": jnp.clip(1.0 + 0.18 * jax.random.normal(key_of[3], (D,), jnp.float32), 0.099609375, 1.8984375).astype(jnp.bfloat16),
        "selfquery": noise(key_of[4], (D, AW), D ** -0.5, 0.1875, ((0, 4),)),
        "selfkey": noise(key_of[5], (D, AW), D ** -0.5, 0.1875, ((0, 4),)),
        "selfvalue": noise(key_of[6], (D, AW), D ** -0.5, 0.1875, ((0, 4),)),
        "selfout": noise(key_of[7], (AW, D), (max(AW // 64, 2)) ** -0.5, 1.5, ((0, 4),)),
        "biastable": noise(key_of[8], (NB, H), 1.0, 4.0, ((0, 4),)),
        "crossnorm": jnp.clip(1.0 + 0.18 * jax.random.normal(key_of[9], (D,), jnp.float32), 0.099609375, 1.8984375).astype(jnp.bfloat16),
        "crossquery": noise(key_of[10], (D, AW), D ** -0.5, 0.1875, ((0, 4),)),
        "crosskey": noise(key_of[11], (D, AW), D ** -0.5, 0.1875, ((0, 4),)),
        "crossvalue": noise(key_of[12], (D, AW), D ** -0.5, 0.1875, ((0, 4),)),
        "crossout": noise(key_of[13], (AW, D), (max(AW // 64, 2)) ** -0.5, 1.5, ((0, 4),)),
        "feednorm": jnp.clip(1.0 + 0.18 * jax.random.normal(key_of[14], (D,), jnp.float32), 0.099609375, 1.8984375).astype(jnp.bfloat16),
        "feedin": noise(key_of[15], (D, FF), D ** -0.5, 0.1875, ((0, 4),)),
        "feedbias": noise(key_of[16], (FF,), 0.5, 3.0, ((0, 4),)),
        "feedout": noise(key_of[17], (FF, D), FF ** -0.5, 0.09375, ((0, 4),)),
        "outbias": noise(key_of[18], (D,), 0.5, 3.0, ((0, 4),)),
    }


@jax.custom_vjp
def low(v):
    return lax.optimization_barrier(v.astype(jnp.bfloat16)).astype(jnp.float32)

@jax.custom_vjp
def low_back(v):
    return v

def low_keep(v):
    return (low(v), None)

def low_pass(kept, grad):
    return (grad,)

def back_keep(v):
    return (v, None)

def back_low(kept, grad):
    return (low(grad),)
low.defvjp(low_keep, low_pass)
low_back.defvjp(back_keep, back_low)
epsilon = 1e-06
negative = -1e+30
strongest_precision = lax.Precision.HIGHEST

def bucket_edges():
    half_count = NB // 2
    exact_part = half_count // 2
    edge_list = []
    for level_index in range(exact_part + 1, half_count):
        hits = [distance_now for distance_now in range(exact_part, MAXD + 1) if exact_part + int(math.log(distance_now / exact_part) / math.log(MAXD / exact_part) * (half_count - exact_part)) >= level_index]
        edge_list.append(min(hits + [MAXD]))
    return (half_count, exact_part, edge_list)

def bucket_of(offset_value):
    half_count, exact_part, edge_list = bucket_edges()
    magnitude = jnp.abs(offset_value)
    far_part = exact_part + sum([(magnitude >= edge_value).astype(magnitude.dtype) for edge_value in edge_list], jnp.zeros_like(magnitude))
    return jnp.where(offset_value > 0, half_count, 0) + jnp.where(magnitude < exact_part, magnitude, far_part)

def root_norm(values, gain_vector):
    return values * lax.rsqrt(lax.optimization_barrier(jnp.mean(values * values, axis=-1, keepdims=True)) + epsilon) * gain_vector

def matmul(left_side, right_side):
    return jnp.dot(left_side, right_side, precision=strongest_precision)

def gelu_tanh(values):
    return jax.nn.gelu(values, approximate=True)

def self_attention(query, key_rows, value_rows, bias_table):
    block_rows = min(512, SEQ)
    scale_factor = HD ** (-0.5)
    key_heads = key_rows.reshape(SEQ, H, HD)
    value_heads = value_rows.reshape(SEQ, H, HD)
    key_place = jnp.arange(SEQ)

    def one_block(block_items):
        query_block, first_row = block_items
        query_place = first_row + jnp.arange(block_rows)
        raw_scores = low_back(jnp.einsum('qhd,khd->hqk', query_block, key_heads, precision=strongest_precision))
        offsets = key_place[None, :] - query_place[:, None]
        bias_rows = jnp.transpose(bias_table[bucket_of(offsets)], (2, 0, 1))
        allowed = key_place[None, :] // BLOCK <= query_place[:, None] // BLOCK
        scores = jnp.where(allowed[None], raw_scores * scale_factor + bias_rows, negative)
        weights_now = low(jax.nn.softmax(scores, axis=-1))
        return jnp.einsum('hqk,khd->qhd', weights_now, value_heads, precision=strongest_precision).reshape(block_rows, H * HD)
    blocks = query.reshape(SEQ // block_rows, block_rows, H, HD)
    firsts = jnp.arange(SEQ // block_rows) * block_rows
    return lax.map(jax.checkpoint(one_block), (blocks, firsts)).reshape(SEQ, H * HD)

def layer(inputs, neighbour_rows, params):
    selfnorm, selfquery, selfkey, selfvalue, selfout, biastable, crossnorm, crossquery, crosskey, crossvalue, crossout, feednorm, feedin, feedbias, feedout, outbias = params
    scale_factor = HD ** (-0.5)
    attn_width = H * HD
    normed = low(root_norm(inputs, selfnorm))
    query = low(low_back(matmul(normed, selfquery)))
    key_rows = low(low_back(matmul(normed, selfkey)))
    value_rows = low(low_back(matmul(normed, selfvalue)))
    attended = low(low_back(self_attention(query, key_rows, value_rows, biastable)))
    hidden = inputs + low_back(matmul(attended, selfout))
    cross_in = low(root_norm(hidden, crossnorm))
    query_cross = low(low_back(matmul(cross_in, crossquery)))
    flat_rows = neighbour_rows.reshape(NCH * NEIGH * RLEN, D)
    keys_cross = low(low_back(matmul(flat_rows, crosskey))).reshape(NCH, NEIGH * RLEN, H, HD)
    values_cross = low(low_back(matmul(flat_rows, crossvalue))).reshape(NCH, NEIGH * RLEN, H, HD)
    shifted = jnp.concatenate([query_cross[SPAN - 1:], jnp.zeros((SPAN - 1, attn_width), jnp.float32)], 0).reshape(NCH, SPAN, H, HD)
    raw_scores = low_back(jnp.einsum('gqhd,gkhd->ghqk', shifted, keys_cross, precision=strongest_precision))
    weights_now = low(jax.nn.softmax(raw_scores * scale_factor, axis=-1))
    mixed_rows = jnp.einsum('ghqk,gkhd->gqhd', weights_now, values_cross, precision=strongest_precision).reshape(SEQ, attn_width)
    crossed = low(low_back(jnp.concatenate([jnp.zeros((SPAN - 1, attn_width), jnp.float32), mixed_rows[:SEQ - SPAN + 1]], 0)))
    hidden_two = hidden + low_back(matmul(crossed, crossout))
    feed_rows = low(root_norm(hidden_two, feednorm))
    pre_act = low_back(matmul(feed_rows, feedin)) + feedbias
    activated = low(gelu_tanh(pre_act))
    return hidden_two + low_back(matmul(activated, feedout)) + outbias

def reference(tokens, neighbours, cotangent, selfnorm, selfquery, selfkey, selfvalue, selfout, biastable, crossnorm, crossquery, crosskey, crossvalue, crossout, feednorm, feedin, feedbias, feedout, outbias):
    params = tuple((weight.astype(jnp.float32) for weight in (selfnorm, selfquery, selfkey, selfvalue, selfout, biastable, crossnorm, crossquery, crosskey, crossvalue, crossout, feednorm, feedin, feedbias, feedout, outbias)))

    def per_sequence(totals, seq_items):
        seq_tokens, seq_neighbours, seq_cotangent = seq_items
        output, pullback = jax.vjp(layer, seq_tokens.astype(jnp.float32), seq_neighbours.astype(jnp.float32), params)
        grad_inputs, grad_rows, grad_params = pullback(seq_cotangent.astype(jnp.float32))
        totals = jax.tree.map(jnp.add, totals, grad_params)
        return (totals, (output.astype(jnp.bfloat16), grad_inputs.astype(jnp.bfloat16), grad_rows.astype(jnp.bfloat16)))
    zero_params = jax.tree.map(jnp.zeros_like, params)
    totals, outputs = lax.scan(per_sequence, zero_params, (tokens, neighbours, cotangent))
    return (outputs[0], outputs[1], outputs[2], totals[0], totals[1], totals[2], totals[3], totals[4], totals[5], totals[6], totals[7], totals[8], totals[9], totals[10], totals[11], totals[12], totals[13], totals[14], totals[15])
```

```python
import functools
import math

import jax
import jax.numpy as jnp
from jax import lax
from jax.experimental import pallas as pl
from jax.experimental.pallas import tpu as pltpu
from jax.sharding import PartitionSpec as P

H = 16
HD = 64
NB = 32
MAXD = 128
BLOCK = 256
SPAN = 64
MESH = pl.DeviceIdType.MESH
WIDE = 128
LINE = 1024
BF = jnp.bfloat16
F32 = jnp.float32


epsilon = 1e-06
negative = -1e30
strongest_precision = lax.Precision.HIGHEST


def passed_along(value, axis, by):
    peers = lax.axis_size(axis)
    pairs = [(i, i + by) for i in range(peers) if 0 <= i + by < peers]
    return lax.ppermute(value, axis, pairs)


def from_behind(block, axis, distance):
    devices = range(lax.axis_size(axis))
    route = [((i - distance) % len(devices), i) for i in devices]
    return lax.ppermute(block, axis, route)


def bucket_edges():
    half_count = NB // 2
    exact_part = half_count // 2
    edge_list = []
    for level_index in range(exact_part + 1, half_count):
        hits = [
            distance_now
            for distance_now in range(exact_part, MAXD + 1)
            if exact_part
            + int(
                math.log(distance_now / exact_part)
                / math.log(MAXD / exact_part)
                * (half_count - exact_part)
            )
            >= level_index
        ]
        edge_list.append(min(hits + [MAXD]))
    return (half_count, exact_part, edge_list)


def bucket_of(offset_value):
    half_count, exact_part, edge_list = bucket_edges()
    magnitude = jnp.abs(offset_value)
    far_part = exact_part + sum(
        [(magnitude >= edge_value).astype(magnitude.dtype) for edge_value in edge_list],
        jnp.zeros_like(magnitude),
    )
    return jnp.where(offset_value > 0, half_count, 0) + jnp.where(
        magnitude < exact_part, magnitude, far_part
    )


def root_norm(values, gain_vector):
    return (
        values
        * lax.rsqrt(jnp.mean(values * values, axis=-1, keepdims=True) + epsilon)
        * gain_vector
    )


def gelu_tanh(values):
    return jax.nn.gelu(values, approximate=True)


def forward_product(values, weight):
    return jnp.dot(values, weight, preferred_element_type=jnp.float32)


def outer_product(left_side, right_side):
    return lax.dot_general(
        left_side, right_side, (((0,), (0,)), ((), ())), preferred_element_type=jnp.float32
    )


def back_product(grad_low, weight):
    return lax.dot_general(
        grad_low, weight, (((1,), (1,)), ((), ())), preferred_element_type=jnp.float32
    )


def make_bias(bucket_bias_rows, row_count):
    query_place = jnp.arange(row_count)[:, None]
    key_place = jnp.arange(row_count)[None, :]
    levels = jnp.arange(NB)
    current_bucket_selector = (
        bucket_of(key_place - query_place)[None] == levels[:, None, None]
    ).astype(jnp.float32)
    previous_bucket_selector = (
        bucket_of(key_place - row_count - query_place)[None] == levels[:, None, None]
    ).astype(jnp.float32)
    onehot_far = (bucket_of(jnp.array(-MAXD, jnp.int32)) == levels).astype(jnp.float32)
    current_block_bias = jnp.einsum(
        "smz,sj->jmz", current_bucket_selector, bucket_bias_rows, precision=strongest_precision
    )
    previous_block_bias = jnp.einsum(
        "smz,sj->jmz", previous_bucket_selector, bucket_bias_rows, precision=strongest_precision
    )
    bias_far = jnp.dot(onehot_far, bucket_bias_rows, precision=strongest_precision)
    mask_same = key_place // BLOCK <= query_place // BLOCK
    return (
        (current_block_bias, previous_block_bias, bias_far, mask_same),
        (current_bucket_selector, previous_bucket_selector, onehot_far),
    )


def pair_scores(query_heads, key_heads, relation, bias_set, scale_factor):
    current_block_bias, previous_block_bias, bias_far, mask_same = bias_set
    raw_scores = jnp.einsum(
        "qhd,khd->hqk", query_heads, key_heads, preferred_element_type=jnp.float32
    )
    bias_rows = jnp.where(
        relation == 0,
        current_block_bias,
        jnp.where(relation == 1, previous_block_bias, bias_far[:, None, None]),
    )
    allowed = jnp.logical_or(relation > 0, mask_same)
    return jnp.where(allowed[None], raw_scores * scale_factor + bias_rows, negative)


def pair_core(
    query_heads,
    dout_heads,
    log_total,
    row_delta,
    key_heads,
    value_heads,
    relation,
    bias_set,
    scale_factor,
):
    scores = pair_scores(query_heads, key_heads, relation, bias_set, scale_factor)
    weights_now = jnp.exp(scores - log_total[:, :, None])
    grad_weights = jnp.einsum(
        "qhd,khd->hqk", dout_heads, value_heads, preferred_element_type=jnp.float32
    )
    dscores = weights_now * (grad_weights - row_delta[:, :, None])
    return (weights_now, dscores, (dscores * scale_factor).astype(jnp.bfloat16))


def add_tables(relative_bias_tables, dscores, relation):
    same_sum, prev_sum, far_sum = relative_bias_tables
    return (
        same_sum + jnp.where(relation == 0, dscores, 0.0),
        prev_sum + jnp.where(relation == 1, dscores, 0.0),
        far_sum + jnp.where(relation >= 2, jnp.sum(dscores, axis=(1, 2)), 0.0),
    )


def forward_fold(query_heads, position, row_count, bias_set, scale_factor, running, pieces):
    keys_all, values_all = pieces

    def one_shard(folded, shard_step):
        key_heads = lax.dynamic_slice_in_dim(
            keys_all, shard_step * row_count, row_count, 0
        ).reshape(row_count, H, HD)
        value_heads = lax.dynamic_slice_in_dim(
            values_all, shard_step * row_count, row_count, 0
        ).reshape(row_count, H, HD)
        relation = position - shard_step

        def one_compute(current):
            running_max, running_sum, running_acc = current
            scores = pair_scores(query_heads, key_heads, relation, bias_set, scale_factor)
            new_max = jnp.maximum(running_max, jnp.max(scores, axis=-1))
            factor = jnp.exp(running_max - new_max)
            weights_now = jnp.exp(scores - new_max[:, :, None])
            new_sum = running_sum * factor + jnp.sum(weights_now, axis=-1)
            update = jnp.einsum(
                "hqk,khd->qhd",
                weights_now.astype(jnp.bfloat16),
                value_heads,
                preferred_element_type=jnp.float32,
            )
            scaled = running_acc.reshape(row_count, H, HD) * factor.T[:, :, None]
            return (new_max, new_sum, (scaled + update).reshape(row_count, H * HD))

        return (lax.cond(relation >= 0, one_compute, lambda unchanged: unchanged, folded), None)

    running, unused = lax.scan(one_shard, running, jnp.arange(keys_all.shape[0] // row_count))
    return running


def nt_dot(left, right):
    return lax.dot_general(left, right, (((1,), (1,)), ((), ())), preferred_element_type=F32)


def nn_dot(left, right):
    return jnp.dot(left, right, preferred_element_type=F32)


def greet(axis, count):
    me = lax.axis_index(axis)
    barrier = pltpu.get_barrier_semaphore()
    for d in range(1, count):
        pl.semaphore_signal(
            barrier, inc=1, device_id={axis: lax.rem(me + d, count)}, device_id_type=MESH
        )
    pl.semaphore_wait(barrier, count - 1)
    return me


def lanes_of(index):
    return pl.ds(pl.multiple_of(index * WIDE, WIDE), WIDE)


def rows_of(index, rows):
    return pl.ds(pl.multiple_of(index * rows, rows), rows)


def to_ctx(src, dst, send_sem, recv_sem, target):
    return pltpu.make_async_remote_copy(
        src_ref=src,
        dst_ref=dst,
        send_sem=send_sem,
        recv_sem=recv_sem,
        device_id={"ctx": target},
        device_id_type=MESH,
    )


def head_mask(h, rows):
    lane = lax.broadcasted_iota(jnp.int32, (rows, WIDE), 1)
    return (lane < HD) if h == 0 else (lane >= HD)


def bias_tiles(bias_ref, me, tiles):
    for h in range(2):
        line = bias_ref[pl.ds(2 * me + h, 1), :]
        rolled = pltpu.roll(
            jnp.broadcast_to(line, (BLOCK, LINE)), 0, 1, stride=1, stride_axis=0
        )
        tiles[h, 0] = rolled[:, :BLOCK]
        tiles[h, 1] = rolled[:, BLOCK : 2 * BLOCK]


def spread(n, me, pairs, send, recv):
    for d in range(1, n):
        peer = lax.rem(me + d, n)
        for t, (src, dst) in enumerate(pairs):
            to_ctx(
                src.at[:, lanes_of(peer)],
                dst.at[rows_of(me, BLOCK)],
                send.at[t, d],
                recv.at[t, d],
                peer,
            ).start()
    for src, dst in pairs:
        dst[rows_of(me, BLOCK), :] = src[:, lanes_of(me)]


def attn_forward_kernel(
    n, q_ref, k_ref, v_ref, bias_ref, o_ref, qh_out, kh_out, vh_out, ot_out, lse_out,
    qh, kh, vh, vt, oh, land, tiles, acc, stat, send, recv, osend, orecv,
):
    me = greet("ctx", n)
    pairs = ((q_ref, qh), (k_ref, kh), (v_ref, vh))
    spread(n, me, pairs, send, recv)
    bias_tiles(bias_ref, me, tiles)

    def arrive(i):
        @pl.when(i != me)
        def _():
            d = lax.rem(me - i + n, n)
            for t, (src, dst) in enumerate(pairs):
                to_ctx(
                    src.at[:, lanes_of(i)], dst.at[rows_of(i, BLOCK)], send.at[t, d], recv.at[t, d], i
                ).wait_recv()

    def query_block(i, unused):
        arrive(i)
        rows = rows_of(i, BLOCK)
        vt[:, rows] = vh[rows, :].astype(F32).T.astype(BF)
        q_now = qh[rows, :] * BF(HD**-0.5)
        masked = [jnp.where(head_mask(h, BLOCK), q_now, BF(0)) for h in range(2)]

        def fold(j, which, first):
            keys = kh[rows_of(j, BLOCK), :]
            for h in range(2):
                scores = nt_dot(keys, masked[h])
                if which is None:
                    scores = scores + bias_ref[pl.ds(2 * me + h, 1), WIDE : WIDE + BLOCK]
                else:
                    scores = scores + tiles[h, which]
                top = jnp.max(scores, axis=0, keepdims=True)
                if not first:
                    old = stat[h : h + 1, :]
                    top = jnp.maximum(old, top)
                weights = jnp.exp(scores - top)
                total = jnp.sum(weights, axis=0, keepdims=True)
                vals = vt[h * HD : (h + 1) * HD, rows_of(j, BLOCK)]
                mixed = nn_dot(vals, weights.astype(BF))
                if not first:
                    factor = jnp.exp(old - top)
                    total = total + stat[2 + h : 3 + h, :] * factor
                    mixed = mixed + acc[h * HD : (h + 1) * HD, :] * factor
                stat[h : h + 1, :] = top
                stat[2 + h : 3 + h, :] = total
                acc[h * HD : (h + 1) * HD, :] = mixed

        fold(i, 0, True)

        @pl.when(i >= 1)
        def _():
            fold(i - 1, 1, False)

        def far(j, unused):
            fold(j, None, False)
            return unused

        lax.fori_loop(0, i - 1, far, 0)
        for h in range(2):
            total = stat[2 + h : 3 + h, :]
            part = acc[h * HD : (h + 1) * HD, :] / total
            acc[h * HD : (h + 1) * HD, :] = part
            lse_out[h : h + 1, rows] = stat[h : h + 1, :] + jnp.log(total)
        done = acc[...]
        ot_out[:, rows] = done
        oh[rows, :] = done.T.astype(BF)

        @pl.when(i != me)
        def _():
            d = lax.rem(i - me + n, n)
            to_ctx(oh.at[rows], land.at[:, lanes_of(me)], osend.at[d], orecv.at[d], i).start()

        @pl.when(i == me)
        def _():
            land[:, lanes_of(me)] = oh[rows, :]

        return unused

    lax.fori_loop(0, n, query_block, 0)
    qh_out[...] = qh[...]
    kh_out[...] = kh[...]
    vh_out[...] = vh[...]
    for d in range(1, n):
        peer = lax.rem(me + d, n)
        for t, (src, dst) in enumerate(pairs):
            to_ctx(
                src.at[:, lanes_of(peer)], dst.at[rows_of(me, BLOCK)], send.at[t, d], recv.at[t, d], peer
            ).wait_send()
        back = to_ctx(
            oh.at[rows_of(peer, BLOCK)], land.at[:, lanes_of(me)], osend.at[d], orecv.at[d], peer
        )
        back.wait_send()
        back.wait_recv()
    o_ref[...] = land[...]


def vmem(count):
    return [pl.BlockSpec(memory_space=pltpu.VMEM)] * count


def attn_forward(n, query, key, value, bias_lines):
    rows, seq = query.shape[0], n * query.shape[0]
    heads = jax.ShapeDtypeStruct((seq, WIDE), BF)
    return pl.pallas_call(
        functools.partial(attn_forward_kernel, n),
        out_shape=(
            jax.ShapeDtypeStruct(query.shape, BF),
            heads,
            heads,
            heads,
            jax.ShapeDtypeStruct((WIDE, seq), F32),
            jax.ShapeDtypeStruct((8, seq), F32),
        ),
        in_specs=vmem(4),
        out_specs=tuple(vmem(6)),
        scratch_shapes=[
            pltpu.VMEM((seq, WIDE), BF),
            pltpu.VMEM((seq, WIDE), BF),
            pltpu.VMEM((seq, WIDE), BF),
            pltpu.VMEM((WIDE, seq), BF),
            pltpu.VMEM((seq, WIDE), BF),
            pltpu.VMEM(query.shape, BF),
            pltpu.VMEM((2, 2, BLOCK, BLOCK), F32),
            pltpu.VMEM((WIDE, BLOCK), F32),
            pltpu.VMEM((8, BLOCK), F32),
            pltpu.SemaphoreType.DMA((3, n)),
            pltpu.SemaphoreType.DMA((3, n)),
            pltpu.SemaphoreType.DMA((n,)),
            pltpu.SemaphoreType.DMA((n,)),
        ],
        compiler_params=pltpu.CompilerParams(
            collective_id=1, has_side_effects=True, vmem_limit_bytes=40 << 20
        ),
        name="attn_forward",
    )(query, key, value, bias_lines)


def attn_backward_kernel(
    n, do_ref, qh, kh, vh, ot_ref, lse_ref, bias_ref, dq_ref, dk_ref, dv_ref, line_ref,
    doh, kt, stage, land, dk_acc, dv_acc, dqt, tiles, dtiles, far_sum, send, recv, gsend, grecv,
):
    me = greet("ctx", n)
    pairs = ((do_ref, doh),)
    spread(n, me, pairs, send, recv)
    bias_tiles(bias_ref, me, tiles)
    for j in range(n):
        part = slice(j * BLOCK, (j + 1) * BLOCK)
        kt[:, part] = (kh[part, :].astype(F32) * HD**-0.5).T.astype(BF)
    dk_acc[...] = jnp.zeros_like(dk_acc)
    dv_acc[...] = jnp.zeros_like(dv_acc)
    dtiles[...] = jnp.zeros_like(dtiles)
    far_sum[...] = jnp.zeros_like(far_sum)

    def query_block(step, unused):
        i = n - 1 - step

        @pl.when(i != me)
        def _():
            d = lax.rem(me - i + n, n)
            to_ctx(
                do_ref.at[:, lanes_of(i)], doh.at[rows_of(i, BLOCK)], send.at[0, d], recv.at[0, d], i
            ).wait_recv()

        rows = rows_of(i, BLOCK)
        q_now = qh[rows, :] * BF(HD**-0.5)
        do_now = doh[rows, :]
        q_masked = [jnp.where(head_mask(h, BLOCK), q_now, BF(0)) for h in range(2)]
        do_masked = [jnp.where(head_mask(h, BLOCK), do_now, BF(0)) for h in range(2)]
        products = do_now.astype(F32).T * ot_ref[:, rows]
        delta = [
            jnp.sum(products[h * HD : (h + 1) * HD], axis=0, keepdims=True) for h in range(2)
        ]
        lse = [lse_ref[h : h + 1, rows] for h in range(2)]
        dqt[...] = jnp.zeros_like(dqt)

        def fold(j, which):
            there = rows_of(j, BLOCK)
            keys, vals = kh[there, :], vh[there, :]
            dk_part, dv_part = None, None
            for h in range(2):
                scores = nt_dot(keys, q_masked[h])
                if which is None:
                    bias = bias_ref[pl.ds(2 * me + h, 1), WIDE : WIDE + BLOCK]
                    weights = jnp.exp(scores - (lse[h] - bias))
                else:
                    weights = jnp.exp(scores + tiles[h, which] - lse[h])
                dweights = nt_dot(vals, do_masked[h])
                dscores = weights * (dweights - delta[h])
                if which is None:
                    far_sum[h : h + 1, :] += jnp.sum(dscores, axis=0, keepdims=True)
                else:
                    dtiles[h, which] += dscores
                low = dscores.astype(BF)
                dv_now = nn_dot(weights.astype(BF), do_masked[h])
                dk_now = nn_dot(low, q_masked[h])
                dv_part = dv_now if dv_part is None else dv_part + dv_now
                dk_part = dk_now if dk_part is None else dk_part + dk_now
                half = slice(h * HD, (h + 1) * HD)
                dqt[half, :] += nn_dot(kt[half, there], low)
            dk_acc[there, :] += dk_part
            dv_acc[there, :] += dv_part

        fold(i, 0)

        @pl.when(i >= 1)
        def _():
            fold(i - 1, 1)

        def far(j, unused):
            fold(j, None)
            return unused

        lax.fori_loop(0, i - 1, far, 0)
        stage[0, rows, :] = dqt[...].T.astype(BF)
        stage[1, rows, :] = dk_acc[rows, :].astype(BF)
        stage[2, rows, :] = dv_acc[rows, :].astype(BF)

        @pl.when(i != me)
        def _():
            d = lax.rem(i - me + n, n)
            for t in range(3):
                to_ctx(
                    stage.at[t, rows], land.at[t, :, lanes_of(me)], gsend.at[t, d], grecv.at[t, d], i
                ).start()

        @pl.when(i == me)
        def _():
            for t in range(3):
                land[t, :, lanes_of(me)] = stage[t, rows, :]

        return unused

    lax.fori_loop(0, n, query_block, 0)
    for h in range(2):
        line = jnp.concatenate(
            [dtiles[h, 0], dtiles[h, 1], jnp.zeros((BLOCK, LINE - 2 * BLOCK), F32)], axis=1
        )
        row = lax.broadcasted_iota(jnp.int32, (BLOCK, LINE), 0)
        for bit in range(8):
            moved = pltpu.roll(line, LINE - (1 << bit), 1)
            line = jnp.where((row >> bit) & 1 == 1, moved, line)
        line_ref[h : h + 1, :] = jnp.sum(line, axis=0, keepdims=True)
    line_ref[2:4, :BLOCK] = far_sum[0:2, :]
    line_ref[2:4, BLOCK:] = jnp.zeros((2, LINE - BLOCK), F32)
    line_ref[4:8, :] = jnp.zeros((4, LINE), F32)
    for d in range(1, n):
        peer = lax.rem(me + d, n)
        to_ctx(
            do_ref.at[:, lanes_of(peer)], doh.at[rows_of(me, BLOCK)], send.at[0, d], recv.at[0, d], peer
        ).wait_send()
        for t in range(3):
            back = to_ctx(
                stage.at[t, rows_of(peer, BLOCK)], land.at[t, :, lanes_of(me)], gsend.at[t, d], grecv.at[t, d], peer
            )
            back.wait_send()
            back.wait_recv()
    dq_ref[...] = land[0]
    dk_ref[...] = land[1]
    dv_ref[...] = land[2]


def attn_backward(n, dout, qh, kh, vh, ot, lse, bias_lines):
    rows, seq = dout.shape[0], n * dout.shape[0]
    grads = jax.ShapeDtypeStruct(dout.shape, BF)
    return pl.pallas_call(
        functools.partial(attn_backward_kernel, n),
        out_shape=(grads, grads, grads, jax.ShapeDtypeStruct((8, LINE), F32)),
        in_specs=vmem(7),
        out_specs=tuple(vmem(4)),
        scratch_shapes=[
            pltpu.VMEM((seq, WIDE), BF),
            pltpu.VMEM((WIDE, seq), BF),
            pltpu.VMEM((3, seq, WIDE), BF),
            pltpu.VMEM((3, *dout.shape), BF),
            pltpu.VMEM((seq, WIDE), F32),
            pltpu.VMEM((seq, WIDE), F32),
            pltpu.VMEM((WIDE, BLOCK), F32),
            pltpu.VMEM((2, 2, BLOCK, BLOCK), F32),
            pltpu.VMEM((2, 2, BLOCK, BLOCK), F32),
            pltpu.VMEM((8, BLOCK), F32),
            pltpu.SemaphoreType.DMA((1, n)),
            pltpu.SemaphoreType.DMA((1, n)),
            pltpu.SemaphoreType.DMA((3, n)),
            pltpu.SemaphoreType.DMA((3, n)),
        ],
        compiler_params=pltpu.CompilerParams(
            collective_id=2, has_side_effects=True, vmem_limit_bytes=40 << 20
        ),
        name="attn_backward",
    )(dout, qh, kh, vh, ot, lse, bias_lines)


def line_selector():
    place = jnp.arange(LINE)
    offset = jnp.where(place < LINE // 2, -place, LINE - place)
    return (bucket_of(offset)[None, :] == jnp.arange(NB)[:, None]).astype(jnp.float32)


def ring_forward(query_low, key_low, value_low, bucket_table):
    row_count, attn_width = query_low.shape
    position = lax.axis_index("ctx")
    scale_factor = HD ** (-0.5)
    bias_set, onehots = make_bias(bucket_table.astype(jnp.float32), row_count)
    query_heads = query_low.reshape(row_count, H, HD)
    start_state = (
        jnp.full((H, row_count), negative, jnp.float32),
        jnp.zeros((H, row_count), jnp.float32),
        jnp.zeros((row_count, attn_width), jnp.float32),
    )
    running_max, running_sum, running_acc = forward_fold(
        query_heads,
        position,
        row_count,
        bias_set,
        scale_factor,
        start_state,
        (
            lax.all_gather(key_low, "ctx", axis=0, tiled=True),
            lax.all_gather(value_low, "ctx", axis=0, tiled=True),
        ),
    )
    attended = (running_acc.reshape(row_count, H, HD) / running_sum.T[:, :, None]).reshape(
        row_count, attn_width
    )
    log_total = running_max + jnp.log(running_sum)
    state = (query_heads, key_low, value_low, attended, log_total, bias_set, onehots)
    return attended.astype(jnp.bfloat16), state


def ring_backward(state, dout_low):
    query_heads, key_low, value_low, attended, log_total, bias_set, onehots = state
    row_count, attn_width = dout_low.shape
    cycle_size = lax.axis_size("ctx")
    position = lax.axis_index("ctx")
    scale_factor = HD ** (-0.5)
    dout_heads = dout_low.reshape(row_count, H, HD)
    row_delta = jnp.sum(
        (dout_low.astype(jnp.float32) * attended).reshape(row_count, H, HD), axis=-1
    ).T
    zero_rows = jnp.zeros((row_count, attn_width), jnp.float32)
    zero_tables = (
        jnp.zeros((H, row_count, row_count), jnp.float32),
        jnp.zeros((H, row_count, row_count), jnp.float32),
        jnp.zeros((H,), jnp.float32),
    )

    def visit(folded, key_now, value_now, relation):

        def visit_compute(current):
            dquery_acc, dkey_acc, dvalue_acc, relative_bias_tables = current
            key_heads = key_now.reshape(row_count, H, HD)
            weights_now, dscores, ds_low = pair_core(
                query_heads,
                dout_heads,
                log_total,
                row_delta,
                key_heads,
                value_now.reshape(row_count, H, HD),
                relation,
                bias_set,
                scale_factor,
            )
            dquery = jnp.einsum(
                "hqk,khd->qhd", ds_low, key_heads, preferred_element_type=jnp.float32
            ).reshape(row_count, attn_width)
            dkey = jnp.einsum(
                "hqk,qhd->khd", ds_low, query_heads, preferred_element_type=jnp.float32
            ).reshape(row_count, attn_width)
            dvalue = jnp.einsum(
                "hqk,qhd->khd",
                weights_now.astype(jnp.bfloat16),
                dout_heads,
                preferred_element_type=jnp.float32,
            ).reshape(row_count, attn_width)
            return (
                dquery_acc + dquery,
                dkey_acc + dkey,
                dvalue_acc + dvalue,
                add_tables(relative_bias_tables, dscores, relation),
            )

        return lax.cond(relation >= 0, visit_compute, lambda unchanged: unchanged, folded)

    first_state = visit(
        (zero_rows, zero_rows, zero_rows, zero_tables), key_low, value_low, jnp.array(0, jnp.int32)
    )

    def cycle_step(carried, cycle_index):
        key_now, value_now, (dquery_acc, dkey_acc, dvalue_acc, relative_bias_tables) = carried
        key_next, value_next = passed_along((key_now, value_now), "ctx", 1)
        dkey_next, dvalue_next = (
            from_behind(dkey_acc.astype(jnp.bfloat16), "ctx", 1).astype(dkey_acc.dtype),
            from_behind(dvalue_acc.astype(jnp.bfloat16), "ctx", 1).astype(dvalue_acc.dtype),
        )
        relation = jnp.where(position >= cycle_index, cycle_index, -1)
        updated = visit(
            (dquery_acc, dkey_next, dvalue_next, relative_bias_tables),
            key_next,
            value_next,
            relation,
        )
        return ((key_next, value_next, updated), None)

    (
        unused_key,
        unused_value,
        (dquery_total, dkey_part, dvalue_part, relative_bias_tables),
    ), unused = lax.scan(cycle_step, (key_low, value_low, first_state), jnp.arange(1, cycle_size))
    dkey_total, dvalue_total = (
        from_behind(dkey_part.astype(jnp.bfloat16), "ctx", 1).astype(dkey_part.dtype),
        from_behind(dvalue_part.astype(jnp.bfloat16), "ctx", 1).astype(dvalue_part.dtype),
    )
    dquery_low = dquery_total.astype(jnp.bfloat16)
    dkey_low = dkey_total.astype(jnp.bfloat16)
    dvalue_low = dvalue_total.astype(jnp.bfloat16)
    current_bucket_selector, previous_bucket_selector, onehot_far = onehots
    grad_biastable = (
        jnp.einsum(
            "afw,mfw->am",
            current_bucket_selector,
            relative_bias_tables[0],
            precision=strongest_precision,
        )
        + jnp.einsum(
            "afw,mfw->am",
            previous_bucket_selector,
            relative_bias_tables[1],
            precision=strongest_precision,
        )
        + onehot_far[:, None] * relative_bias_tables[2][None, :]
    )
    return dquery_low, dkey_low, dvalue_low, grad_biastable


def heads_forward(query_low, key_low, value_low, bucket_table):
    lines = jnp.dot(
        bucket_table.astype(jnp.float32).T, line_selector(), precision=strongest_precision
    )
    peers = lax.axis_size("ctx")
    attended_low, *saved = attn_forward(peers, query_low, key_low, value_low, lines)
    return attended_low, (*saved, lines)


def heads_backward(state, dout_low):
    peers = lax.axis_size("ctx")
    dquery_low, dkey_low, dvalue_low, sums = attn_backward(peers, dout_low, *state)
    selector = line_selector()
    table = jnp.dot(selector, sums[:2].T, precision=strongest_precision)
    far = jnp.sum(sums[2:4], axis=1)
    table = table + selector[:, WIDE : WIDE + 1] * far[None, :]
    whole = jnp.zeros((NB, H), jnp.float32)
    whole = lax.dynamic_update_slice(whole, table, (0, 2 * lax.axis_index("ctx")))
    return dquery_low, dkey_low, dvalue_low, whole


def per_device(
    tokens,
    neighbours,
    cotangent,
    selfnorm,
    selfquery,
    selfkey,
    selfvalue,
    selfout,
    biastable,
    crossnorm,
    crossquery,
    crosskey,
    crossvalue,
    crossout,
    feednorm,
    feedin,
    feedbias,
    feedout,
    outbias,
):
    gathered = (
        lax.all_gather(selfnorm, "wa", axis=0, tiled=True),
        lax.all_gather(selfquery, "wa", axis=0, tiled=True),
        lax.all_gather(selfkey, "wa", axis=0, tiled=True),
        lax.all_gather(selfvalue, "wa", axis=0, tiled=True),
        lax.all_gather(selfout, "wa", axis=0, tiled=True),
        lax.all_gather(biastable, "wa", axis=0, tiled=True),
        lax.all_gather(crossnorm, "wa", axis=0, tiled=True),
        lax.all_gather(crossquery, "wa", axis=0, tiled=True),
        lax.all_gather(crosskey, "wa", axis=0, tiled=True),
        lax.all_gather(crossvalue, "wa", axis=0, tiled=True),
        lax.all_gather(crossout, "wa", axis=0, tiled=True),
        lax.all_gather(feednorm, "wa", axis=0, tiled=True),
        lax.all_gather(feedin, "wa", axis=0, tiled=True),
        lax.all_gather(feedbias, "wa", axis=0, tiled=True),
        lax.all_gather(feedout, "wa", axis=0, tiled=True),
        lax.all_gather(outbias, "wa", axis=0, tiled=True),
    )
    (
        gain_self,
        proj_query,
        proj_key,
        proj_value,
        proj_out,
        bucket_table,
        gain_cross,
        cross_query,
        cross_key,
        cross_value,
        cross_out,
        gain_feed,
        feed_in,
        feed_bias,
        feed_out,
        out_bias,
    ) = gathered
    row_count = tokens.shape[1]
    model_width = tokens.shape[2]
    attn_width = proj_query.shape[1]
    split_heads = lax.axis_size("ctx") * 2 == H and row_count == BLOCK
    self_forward = heads_forward if split_heads else ring_forward
    self_backward = heads_backward if split_heads else ring_backward
    position = lax.axis_index("ctx")
    scale_factor = HD ** (-0.5)
    inputs = tokens[0].astype(jnp.float32)
    normed_self, back_self = jax.vjp(root_norm, inputs, gain_self.astype(jnp.float32))
    normed_low = normed_self.astype(jnp.bfloat16)
    query_low = forward_product(normed_low, proj_query).astype(jnp.bfloat16)
    key_low = forward_product(normed_low, proj_key).astype(jnp.bfloat16)
    value_low = forward_product(normed_low, proj_value).astype(jnp.bfloat16)
    attended_low, attention_state = self_forward(query_low, key_low, value_low, bucket_table)
    hidden = inputs + forward_product(attended_low, proj_out)
    normed_cross, back_cross = jax.vjp(root_norm, hidden, gain_cross.astype(jnp.float32))
    cross_in = normed_cross.astype(jnp.bfloat16)
    query_cross = forward_product(cross_in, cross_query).astype(jnp.bfloat16)
    spans = neighbours.shape[1]
    neighbour_rows = neighbours.shape[2] * neighbours.shape[3]
    flat_neigh = neighbours[0].reshape(spans * neighbour_rows, model_width)
    keys_cross = (
        forward_product(flat_neigh, cross_key)
        .astype(jnp.bfloat16)
        .reshape(spans, neighbour_rows, attn_width)
    )
    values_cross = (
        forward_product(flat_neigh, cross_value)
        .astype(jnp.bfloat16)
        .reshape(spans, neighbour_rows, attn_width)
    )
    prev_key, prev_value = passed_along((keys_cross[spans - 1], values_cross[spans - 1]), "ctx", 1)
    group_keys = jnp.concatenate([prev_key[None], keys_cross], 0).reshape(
        spans + 1, neighbour_rows, H, HD
    )
    group_values = jnp.concatenate([prev_value[None], values_cross], 0).reshape(
        spans + 1, neighbour_rows, H, HD
    )
    padded = jnp.concatenate(
        [
            jnp.zeros((1, attn_width), jnp.bfloat16),
            query_cross,
            jnp.zeros((SPAN - 1, attn_width), jnp.bfloat16),
        ],
        0,
    ).reshape(spans + 1, SPAN, H, HD)
    cross_scores = (
        jnp.einsum("gqhd,gkhd->ghqk", padded, group_keys, preferred_element_type=jnp.float32)
        * scale_factor
    )
    cross_weights = jax.nn.softmax(cross_scores, axis=-1)
    cross_low = cross_weights.astype(jnp.bfloat16)
    mixed_rows = jnp.einsum(
        "ghqk,gkhd->gqhd", cross_low, group_values, preferred_element_type=jnp.float32
    ).reshape((spans + 1) * SPAN, attn_width)[1 : row_count + 1]
    keep_mask = jnp.logical_or(position > 0, jnp.arange(row_count) >= SPAN - 1).astype(jnp.float32)[
        :, None
    ]
    mixed_low = (mixed_rows * keep_mask).astype(jnp.bfloat16)
    hidden_two = hidden + forward_product(mixed_low, cross_out)
    normed_feed, back_feed = jax.vjp(root_norm, hidden_two, gain_feed.astype(jnp.float32))
    feed_low = normed_feed.astype(jnp.bfloat16)
    pre_act = forward_product(feed_low, feed_in) + feed_bias.astype(jnp.float32)
    activated, back_gelu = jax.vjp(gelu_tanh, pre_act)
    act_low = activated.astype(jnp.bfloat16)
    result = hidden_two + forward_product(act_low, feed_out) + out_bias.astype(jnp.float32)
    upstream_low = cotangent[0]
    upstream = upstream_low.astype(jnp.float32)
    grad_outbias = jnp.sum(upstream, axis=0)
    grad_feedout = outer_product(act_low, upstream_low)
    (grad_pre,) = back_gelu(back_product(upstream_low, feed_out))
    grad_feedbias = jnp.sum(grad_pre, axis=0)
    pre_low = grad_pre.astype(jnp.bfloat16)
    grad_feedin = outer_product(feed_low, pre_low)
    grad_two_part, grad_feednorm = back_feed(back_product(pre_low, feed_in))
    grad_two = upstream + grad_two_part
    two_low = grad_two.astype(jnp.bfloat16)
    grad_crossout = outer_product(mixed_low, two_low)
    grad_mixed = (back_product(two_low, cross_out) * keep_mask).astype(jnp.bfloat16)
    mixed_pad = jnp.concatenate(
        [
            jnp.zeros((1, attn_width), jnp.bfloat16),
            grad_mixed,
            jnp.zeros((SPAN - 1, attn_width), jnp.bfloat16),
        ],
        0,
    ).reshape(spans + 1, SPAN, H, HD)
    grad_cross_weights = jnp.einsum(
        "gqhd,gkhd->ghqk", mixed_pad, group_values, preferred_element_type=jnp.float32
    )
    cross_dscores = cross_weights * (
        grad_cross_weights - jnp.sum(cross_weights * grad_cross_weights, axis=-1, keepdims=True)
    )
    cross_ds_low = (cross_dscores * scale_factor).astype(jnp.bfloat16)
    grad_query_cross = (
        jnp.einsum("ghqk,gkhd->gqhd", cross_ds_low, group_keys, preferred_element_type=jnp.float32)
        .reshape((spans + 1) * SPAN, attn_width)[1 : row_count + 1]
        .astype(jnp.bfloat16)
    )
    grad_group_keys = jnp.einsum(
        "ghqk,gqhd->gkhd", cross_ds_low, padded, preferred_element_type=jnp.float32
    ).reshape(spans + 1, neighbour_rows, attn_width)
    grad_group_values = jnp.einsum(
        "ghqk,gqhd->gkhd", cross_low, mixed_pad, preferred_element_type=jnp.float32
    ).reshape(spans + 1, neighbour_rows, attn_width)
    back_key, back_value = (
        passed_along(grad_group_keys[0].astype(jnp.bfloat16), "ctx", -1).astype(jnp.float32),
        passed_along(grad_group_values[0].astype(jnp.bfloat16), "ctx", -1).astype(jnp.float32),
    )
    key_grads_low = (
        jnp.concatenate([grad_group_keys[1:spans], (grad_group_keys[spans] + back_key)[None]], 0)
        .astype(jnp.bfloat16)
        .reshape(spans * neighbour_rows, attn_width)
    )
    value_grads_low = (
        jnp.concatenate(
            [grad_group_values[1:spans], (grad_group_values[spans] + back_value)[None]], 0
        )
        .astype(jnp.bfloat16)
        .reshape(spans * neighbour_rows, attn_width)
    )
    grad_crosskey = outer_product(flat_neigh, key_grads_low)
    grad_crossvalue = outer_product(flat_neigh, value_grads_low)
    grad_neigh = (
        (back_product(key_grads_low, cross_key) + back_product(value_grads_low, cross_value))
        .astype(jnp.bfloat16)
        .reshape(neighbours.shape)
    )
    grad_crossquery = outer_product(cross_in, grad_query_cross)
    grad_hidden_part, grad_crossnorm = back_cross(back_product(grad_query_cross, cross_query))
    grad_hidden = grad_two + grad_hidden_part
    hidden_low = grad_hidden.astype(jnp.bfloat16)
    grad_selfout = outer_product(attended_low, hidden_low)
    dout_low = back_product(hidden_low, proj_out).astype(jnp.bfloat16)
    dquery_low, dkey_low, dvalue_low, grad_biastable = self_backward(
        attention_state, dout_low
    )
    grad_selfquery = outer_product(normed_low, dquery_low)
    grad_selfkey = outer_product(normed_low, dkey_low)
    grad_selfvalue = outer_product(normed_low, dvalue_low)
    grad_normed = (
        back_product(dquery_low, proj_query)
        + back_product(dkey_low, proj_key)
        + back_product(dvalue_low, proj_value)
    )
    grad_input_part, grad_selfnorm = back_self(grad_normed)
    grad_inputs = (grad_hidden + grad_input_part).astype(jnp.bfloat16)
    shares = (
        lax.psum_scatter(
            grad_selfnorm.astype(jnp.bfloat16), "wa", scatter_dimension=0, tiled=True
        ).astype(jnp.float32),
        lax.psum_scatter(
            grad_selfquery.astype(jnp.bfloat16), "wa", scatter_dimension=0, tiled=True
        ).astype(jnp.float32),
        lax.psum_scatter(
            grad_selfkey.astype(jnp.bfloat16), "wa", scatter_dimension=0, tiled=True
        ).astype(jnp.float32),
        lax.psum_scatter(
            grad_selfvalue.astype(jnp.bfloat16), "wa", scatter_dimension=0, tiled=True
        ).astype(jnp.float32),
        lax.psum_scatter(
            grad_selfout.astype(jnp.bfloat16), "wa", scatter_dimension=0, tiled=True
        ).astype(jnp.float32),
        lax.psum_scatter(
            grad_biastable.astype(jnp.bfloat16), "wa", scatter_dimension=0, tiled=True
        ).astype(jnp.float32),
        lax.psum_scatter(
            grad_crossnorm.astype(jnp.bfloat16), "wa", scatter_dimension=0, tiled=True
        ).astype(jnp.float32),
        lax.psum_scatter(
            grad_crossquery.astype(jnp.bfloat16), "wa", scatter_dimension=0, tiled=True
        ).astype(jnp.float32),
        lax.psum_scatter(
            grad_crosskey.astype(jnp.bfloat16), "wa", scatter_dimension=0, tiled=True
        ).astype(jnp.float32),
        lax.psum_scatter(
            grad_crossvalue.astype(jnp.bfloat16), "wa", scatter_dimension=0, tiled=True
        ).astype(jnp.float32),
        lax.psum_scatter(
            grad_crossout.astype(jnp.bfloat16), "wa", scatter_dimension=0, tiled=True
        ).astype(jnp.float32),
        lax.psum_scatter(
            grad_feednorm.astype(jnp.bfloat16), "wa", scatter_dimension=0, tiled=True
        ).astype(jnp.float32),
        lax.psum_scatter(
            grad_feedin.astype(jnp.bfloat16), "wa", scatter_dimension=0, tiled=True
        ).astype(jnp.float32),
        lax.psum_scatter(
            grad_feedbias.astype(jnp.bfloat16), "wa", scatter_dimension=0, tiled=True
        ).astype(jnp.float32),
        lax.psum_scatter(
            grad_feedout.astype(jnp.bfloat16), "wa", scatter_dimension=0, tiled=True
        ).astype(jnp.float32),
        lax.psum_scatter(
            grad_outbias.astype(jnp.bfloat16), "wa", scatter_dimension=0, tiled=True
        ).astype(jnp.float32),
    )
    totals = lax.psum(
        (
            shares[0],
            shares[1],
            shares[2],
            shares[3],
            shares[4],
            shares[5],
            shares[6],
            shares[7],
            shares[8],
            shares[9],
            shares[10],
            shares[11],
            shares[12],
            shares[13],
            shares[14],
            shares[15],
        ),
        "ctx",
    )
    return (
        result.astype(jnp.bfloat16)[None],
        grad_inputs[None],
        grad_neigh,
        totals[0],
        totals[1],
        totals[2],
        totals[3],
        totals[4],
        totals[5],
        totals[6],
        totals[7],
        totals[8],
        totals[9],
        totals[10],
        totals[11],
        totals[12],
        totals[13],
        totals[14],
        totals[15],
    )


def solution(mesh):
    return jax.shard_map(
        per_device,
        mesh=mesh,
        in_specs=(
            P("wa", "ctx", None),
            P("wa", "ctx", None, None, None),
            P("wa", "ctx", None),
            P("wa"),
            P("wa", None),
            P("wa", None),
            P("wa", None),
            P("wa", None),
            P("wa", None),
            P("wa"),
            P("wa", None),
            P("wa", None),
            P("wa", None),
            P("wa", None),
            P("wa"),
            P("wa", None),
            P("wa"),
            P("wa", None),
            P("wa"),
        ),
        out_specs=(
            P("wa", "ctx", None),
            P("wa", "ctx", None),
            P("wa", "ctx", None, None, None),
            P("wa"),
            P("wa", None),
            P("wa", None),
            P("wa", None),
            P("wa", None),
            P("wa", None),
            P("wa"),
            P("wa", None),
            P("wa", None),
            P("wa", None),
            P("wa", None),
            P("wa"),
            P("wa", None),
            P("wa"),
            P("wa", None),
            P("wa"),
        ),
        check_vma=False,
    )
```

```python
import functools
import math

import jax
import jax.numpy as jnp
from jax import lax
from jax.experimental import pallas as pl
from jax.experimental.pallas import tpu as pltpu
from jax.sharding import PartitionSpec as P

H = 16
HD = 64
NB = 32
MAXD = 128
BLOCK = 256
SPAN = 64
MESH = pl.DeviceIdType.MESH
WIDE = 128
LINE = 1024
BF = jnp.bfloat16
F32 = jnp.float32


epsilon = 1e-06
negative = -1e30
strongest_precision = lax.Precision.HIGHEST


def passed_along(value, axis, by):
    peers = lax.axis_size(axis)
    pairs = [(i, i + by) for i in range(peers) if 0 <= i + by < peers]
    return lax.ppermute(value, axis, pairs)


def from_behind(block, axis, distance):
    devices = range(lax.axis_size(axis))
    route = [((i - distance) % len(devices), i) for i in devices]
    return lax.ppermute(block, axis, route)


def bucket_edges():
    half_count = NB // 2
    exact_part = half_count // 2
    edge_list = []
    for level_index in range(exact_part + 1, half_count):
        hits = [
            distance_now
            for distance_now in range(exact_part, MAXD + 1)
            if exact_part
            + int(
                math.log(distance_now / exact_part)
                / math.log(MAXD / exact_part)
                * (half_count - exact_part)
            )
            >= level_index
        ]
        edge_list.append(min(hits + [MAXD]))
    return (half_count, exact_part, edge_list)


def bucket_of(offset_value):
    half_count, exact_part, edge_list = bucket_edges()
    magnitude = jnp.abs(offset_value)
    far_part = exact_part + sum(
        [(magnitude >= edge_value).astype(magnitude.dtype) for edge_value in edge_list],
        jnp.zeros_like(magnitude),
    )
    return jnp.where(offset_value > 0, half_count, 0) + jnp.where(
        magnitude < exact_part, magnitude, far_part
    )


def root_norm(values, gain_vector):
    return (
        values
        * lax.rsqrt(jnp.mean(values * values, axis=-1, keepdims=True) + epsilon)
        * gain_vector
    )


def gelu_tanh(values):
    return jax.nn.gelu(values, approximate=True)


def forward_product(values, weight):
    return jnp.dot(values, weight, preferred_element_type=jnp.float32)


def outer_product(left_side, right_side):
    return lax.dot_general(
        left_side, right_side, (((0,), (0,)), ((), ())), preferred_element_type=jnp.float32
    )


def back_product(grad_low, weight):
    return lax.dot_general(
        grad_low, weight, (((1,), (1,)), ((), ())), preferred_element_type=jnp.float32
    )


def make_bias(bucket_bias_rows, row_count):
    query_place = jnp.arange(row_count)[:, None]
    key_place = jnp.arange(row_count)[None, :]
    levels = jnp.arange(NB)
    current_bucket_selector = (
        bucket_of(key_place - query_place)[None] == levels[:, None, None]
    ).astype(jnp.float32)
    previous_bucket_selector = (
        bucket_of(key_place - row_count - query_place)[None] == levels[:, None, None]
    ).astype(jnp.float32)
    onehot_far = (bucket_of(jnp.array(-MAXD, jnp.int32)) == levels).astype(jnp.float32)
    current_block_bias = jnp.einsum(
        "smz,sj->jmz", current_bucket_selector, bucket_bias_rows, precision=strongest_precision
    )
    previous_block_bias = jnp.einsum(
        "smz,sj->jmz", previous_bucket_selector, bucket_bias_rows, precision=strongest_precision
    )
    bias_far = jnp.dot(onehot_far, bucket_bias_rows, precision=strongest_precision)
    mask_same = key_place // BLOCK <= query_place // BLOCK
    return (
        (current_block_bias, previous_block_bias, bias_far, mask_same),
        (current_bucket_selector, previous_bucket_selector, onehot_far),
    )


def pair_scores(query_heads, key_heads, relation, bias_set, scale_factor):
    current_block_bias, previous_block_bias, bias_far, mask_same = bias_set
    raw_scores = jnp.einsum(
        "qhd,khd->hqk", query_heads, key_heads, preferred_element_type=jnp.float32
    )
    bias_rows = jnp.where(
        relation == 0,
        current_block_bias,
        jnp.where(relation == 1, previous_block_bias, bias_far[:, None, None]),
    )
    allowed = jnp.logical_or(relation > 0, mask_same)
    return jnp.where(allowed[None], raw_scores * scale_factor + bias_rows, negative)


def pair_core(
    query_heads,
    dout_heads,
    log_total,
    row_delta,
    key_heads,
    value_heads,
    relation,
    bias_set,
    scale_factor,
):
    scores = pair_scores(query_heads, key_heads, relation, bias_set, scale_factor)
    weights_now = jnp.exp(scores - log_total[:, :, None])
    grad_weights = jnp.einsum(
        "qhd,khd->hqk", dout_heads, value_heads, preferred_element_type=jnp.float32
    )
    dscores = weights_now * (grad_weights - row_delta[:, :, None])
    return (weights_now, dscores, (dscores * scale_factor).astype(jnp.bfloat16))


def add_tables(relative_bias_tables, dscores, relation):
    same_sum, prev_sum, far_sum = relative_bias_tables
    return (
        same_sum + jnp.where(relation == 0, dscores, 0.0),
        prev_sum + jnp.where(relation == 1, dscores, 0.0),
        far_sum + jnp.where(relation >= 2, jnp.sum(dscores, axis=(1, 2)), 0.0),
    )


def forward_fold(query_heads, position, row_count, bias_set, scale_factor, running, pieces):
    keys_all, values_all = pieces

    def one_shard(folded, shard_step):
        key_heads = lax.dynamic_slice_in_dim(
            keys_all, shard_step * row_count, row_count, 0
        ).reshape(row_count, H, HD)
        value_heads = lax.dynamic_slice_in_dim(
            values_all, shard_step * row_count, row_count, 0
        ).reshape(row_count, H, HD)
        relation = position - shard_step

        def one_compute(current):
            running_max, running_sum, running_acc = current
            scores = pair_scores(query_heads, key_heads, relation, bias_set, scale_factor)
            new_max = jnp.maximum(running_max, jnp.max(scores, axis=-1))
            factor = jnp.exp(running_max - new_max)
            weights_now = jnp.exp(scores - new_max[:, :, None])
            new_sum = running_sum * factor + jnp.sum(weights_now, axis=-1)
            update = jnp.einsum(
                "hqk,khd->qhd",
                weights_now.astype(jnp.bfloat16),
                value_heads,
                preferred_element_type=jnp.float32,
            )
            scaled = running_acc.reshape(row_count, H, HD) * factor.T[:, :, None]
            return (new_max, new_sum, (scaled + update).reshape(row_count, H * HD))

        return (lax.cond(relation >= 0, one_compute, lambda unchanged: unchanged, folded), None)

    running, unused = lax.scan(one_shard, running, jnp.arange(keys_all.shape[0] // row_count))
    return running


def nt_dot(left, right):
    return lax.dot_general(left, right, (((1,), (1,)), ((), ())), preferred_element_type=F32)


def nn_dot(left, right):
    return jnp.dot(left, right, preferred_element_type=F32)


def greet(axis, count):
    me = lax.axis_index(axis)
    barrier = pltpu.get_barrier_semaphore()
    for d in range(1, count):
        pl.semaphore_signal(
            barrier, inc=1, device_id={axis: lax.rem(me + d, count)}, device_id_type=MESH
        )
    pl.semaphore_wait(barrier, count - 1)
    return me


def lanes_of(index):
    return pl.ds(pl.multiple_of(index * WIDE, WIDE), WIDE)


def rows_of(index, rows):
    return pl.ds(pl.multiple_of(index * rows, rows), rows)


def to_ctx(src, dst, send_sem, recv_sem, target):
    return pltpu.make_async_remote_copy(
        src_ref=src,
        dst_ref=dst,
        send_sem=send_sem,
        recv_sem=recv_sem,
        device_id={"ctx": target},
        device_id_type=MESH,
    )


def head_mask(h, rows):
    lane = lax.broadcasted_iota(jnp.int32, (rows, WIDE), 1)
    return (lane < HD) if h == 0 else (lane >= HD)


def bias_tiles(bias_ref, me, tiles):
    for h in range(2):
        line = bias_ref[pl.ds(2 * me + h, 1), :]
        rolled = pltpu.roll(
            jnp.broadcast_to(line, (BLOCK, LINE)), 0, 1, stride=1, stride_axis=0
        )
        tiles[h, 0] = rolled[:, :BLOCK]
        tiles[h, 1] = rolled[:, BLOCK : 2 * BLOCK]


def spread(n, me, pairs, send, recv):
    for d in range(1, n):
        peer = lax.rem(me + d, n)
        for t, (src, dst) in enumerate(pairs):
            to_ctx(
                src.at[:, lanes_of(peer)],
                dst.at[rows_of(me, BLOCK)],
                send.at[t, d],
                recv.at[t, d],
                peer,
            ).start()
    for src, dst in pairs:
        dst[rows_of(me, BLOCK), :] = src[:, lanes_of(me)]


def attn_forward_kernel(
    n, q_ref, k_ref, v_ref, bias_ref, o_ref, qh_out, kh_out, vh_out, ot_out, lse_out,
    qh, kh, vh, vt, oh, land, tiles, acc, stat, send, recv, osend, orecv,
):
    me = greet("ctx", n)
    pairs = ((q_ref, qh), (k_ref, kh), (v_ref, vh))
    spread(n, me, pairs, send, recv)
    bias_tiles(bias_ref, me, tiles)

    def arrive(i):
        @pl.when(i != me)
        def _():
            d = lax.rem(me - i + n, n)
            for t, (src, dst) in enumerate(pairs):
                to_ctx(
                    src.at[:, lanes_of(i)], dst.at[rows_of(i, BLOCK)], send.at[t, d], recv.at[t, d], i
                ).wait_recv()

    def query_block(i, unused):
        arrive(i)
        rows = rows_of(i, BLOCK)
        vt[:, rows] = vh[rows, :].astype(F32).T.astype(BF)
        q_now = qh[rows, :] * BF(HD**-0.5)
        masked = [jnp.where(head_mask(h, BLOCK), q_now, BF(0)) for h in range(2)]

        def fold(j, which, first):
            keys = kh[rows_of(j, BLOCK), :]
            for h in range(2):
                scores = nt_dot(keys, masked[h])
                if which is None:
                    scores = scores + bias_ref[pl.ds(2 * me + h, 1), WIDE : WIDE + BLOCK]
                else:
                    scores = scores + tiles[h, which]
                top = jnp.max(scores, axis=0, keepdims=True)
                if not first:
                    old = stat[h : h + 1, :]
                    top = jnp.maximum(old, top)
                weights = jnp.exp(scores - top)
                total = jnp.sum(weights, axis=0, keepdims=True)
                vals = vt[h * HD : (h + 1) * HD, rows_of(j, BLOCK)]
                mixed = nn_dot(vals, weights.astype(BF))
                if not first:
                    factor = jnp.exp(old - top)
                    total = total + stat[2 + h : 3 + h, :] * factor
                    mixed = mixed + acc[h * HD : (h + 1) * HD, :] * factor
                stat[h : h + 1, :] = top
                stat[2 + h : 3 + h, :] = total
                acc[h * HD : (h + 1) * HD, :] = mixed

        fold(i, 0, True)

        @pl.when(i >= 1)
        def _():
            fold(i - 1, 1, False)

        def far(j, unused):
            fold(j, None, False)
            return unused

        lax.fori_loop(0, i - 1, far, 0)
        for h in range(2):
            total = stat[2 + h : 3 + h, :]
            part = acc[h * HD : (h + 1) * HD, :] / total
            acc[h * HD : (h + 1) * HD, :] = part
            lse_out[h : h + 1, rows] = stat[h : h + 1, :] + jnp.log(total)
        done = acc[...]
        ot_out[:, rows] = done
        oh[rows, :] = done.T.astype(BF)

        @pl.when(i != me)
        def _():
            d = lax.rem(i - me + n, n)
            to_ctx(oh.at[rows], land.at[:, lanes_of(me)], osend.at[d], orecv.at[d], i).start()

        @pl.when(i == me)
        def _():
            land[:, lanes_of(me)] = oh[rows, :]

        return unused

    lax.fori_loop(0, n, query_block, 0)
    qh_out[...] = qh[...]
    kh_out[...] = kh[...]
    vh_out[...] = vh[...]
    for d in range(1, n):
        peer = lax.rem(me + d, n)
        for t, (src, dst) in enumerate(pairs):
            to_ctx(
                src.at[:, lanes_of(peer)], dst.at[rows_of(me, BLOCK)], send.at[t, d], recv.at[t, d], peer
            ).wait_send()
        back = to_ctx(
            oh.at[rows_of(peer, BLOCK)], land.at[:, lanes_of(me)], osend.at[d], orecv.at[d], peer
        )
        back.wait_send()
        back.wait_recv()
    o_ref[...] = land[...]


def vmem(count):
    return [pl.BlockSpec(memory_space=pltpu.VMEM)] * count


def attn_forward(n, query, key, value, bias_lines):
    rows, seq = query.shape[0], n * query.shape[0]
    heads = jax.ShapeDtypeStruct((seq, WIDE), BF)
    return pl.pallas_call(
        functools.partial(attn_forward_kernel, n),
        out_shape=(
            jax.ShapeDtypeStruct(query.shape, BF),
            heads,
            heads,
            heads,
            jax.ShapeDtypeStruct((WIDE, seq), F32),
            jax.ShapeDtypeStruct((8, seq), F32),
        ),
        in_specs=vmem(4),
        out_specs=tuple(vmem(6)),
        scratch_shapes=[
            pltpu.VMEM((seq, WIDE), BF),
            pltpu.VMEM((seq, WIDE), BF),
            pltpu.VMEM((seq, WIDE), BF),
            pltpu.VMEM((WIDE, seq), BF),
            pltpu.VMEM((seq, WIDE), BF),
            pltpu.VMEM(query.shape, BF),
            pltpu.VMEM((2, 2, BLOCK, BLOCK), F32),
            pltpu.VMEM((WIDE, BLOCK), F32),
            pltpu.VMEM((8, BLOCK), F32),
            pltpu.SemaphoreType.DMA((3, n)),
            pltpu.SemaphoreType.DMA((3, n)),
            pltpu.SemaphoreType.DMA((n,)),
            pltpu.SemaphoreType.DMA((n,)),
        ],
        compiler_params=pltpu.CompilerParams(
            collective_id=1, has_side_effects=True, vmem_limit_bytes=40 << 20
        ),
        name="attn_forward",
    )(query, key, value, bias_lines)


def attn_backward_kernel(
    n, do_ref, qh, kh, vh, ot_ref, lse_ref, bias_ref, dq_ref, dk_ref, dv_ref, line_ref,
    doh, kt, stage, land, dk_acc, dv_acc, dqt, tiles, dtiles, far_sum, send, recv, gsend, grecv,
):
    me = greet("ctx", n)
    pairs = ((do_ref, doh),)
    spread(n, me, pairs, send, recv)
    bias_tiles(bias_ref, me, tiles)
    for j in range(n):
        part = slice(j * BLOCK, (j + 1) * BLOCK)
        kt[:, part] = (kh[part, :].astype(F32) * HD**-0.5).T.astype(BF)
    dk_acc[...] = jnp.zeros_like(dk_acc)
    dv_acc[...] = jnp.zeros_like(dv_acc)
    dtiles[...] = jnp.zeros_like(dtiles)
    far_sum[...] = jnp.zeros_like(far_sum)

    def query_block(step, unused):
        i = n - 1 - step

        @pl.when(i != me)
        def _():
            d = lax.rem(me - i + n, n)
            to_ctx(
                do_ref.at[:, lanes_of(i)], doh.at[rows_of(i, BLOCK)], send.at[0, d], recv.at[0, d], i
            ).wait_recv()

        rows = rows_of(i, BLOCK)
        q_now = qh[rows, :] * BF(HD**-0.5)
        do_now = doh[rows, :]
        q_masked = [jnp.where(head_mask(h, BLOCK), q_now, BF(0)) for h in range(2)]
        do_masked = [jnp.where(head_mask(h, BLOCK), do_now, BF(0)) for h in range(2)]
        products = do_now.astype(F32).T * ot_ref[:, rows]
        delta = [
            jnp.sum(products[h * HD : (h + 1) * HD], axis=0, keepdims=True) for h in range(2)
        ]
        lse = [lse_ref[h : h + 1, rows] for h in range(2)]
        dqt[...] = jnp.zeros_like(dqt)

        def fold(j, which):
            there = rows_of(j, BLOCK)
            keys, vals = kh[there, :], vh[there, :]
            dk_part, dv_part = None, None
            for h in range(2):
                scores = nt_dot(keys, q_masked[h])
                if which is None:
                    bias = bias_ref[pl.ds(2 * me + h, 1), WIDE : WIDE + BLOCK]
                    weights = jnp.exp(scores - (lse[h] - bias))
                else:
                    weights = jnp.exp(scores + tiles[h, which] - lse[h])
                dweights = nt_dot(vals, do_masked[h])
                dscores = weights * (dweights - delta[h])
                if which is None:
                    far_sum[h : h + 1, :] += jnp.sum(dscores, axis=0, keepdims=True)
                else:
                    dtiles[h, which] += dscores
                low = dscores.astype(BF)
                dv_now = nn_dot(weights.astype(BF), do_masked[h])
                dk_now = nn_dot(low, q_masked[h])
                dv_part = dv_now if dv_part is None else dv_part + dv_now
                dk_part = dk_now if dk_part is None else dk_part + dk_now
                half = slice(h * HD, (h + 1) * HD)
                dqt[half, :] += nn_dot(kt[half, there], low)
            dk_acc[there, :] += dk_part
            dv_acc[there, :] += dv_part

        fold(i, 0)

        @pl.when(i >= 1)
        def _():
            fold(i - 1, 1)

        def far(j, unused):
            fold(j, None)
            return unused

        lax.fori_loop(0, i - 1, far, 0)
        stage[0, rows, :] = dqt[...].T.astype(BF)
        stage[1, rows, :] = dk_acc[rows, :].astype(BF)
        stage[2, rows, :] = dv_acc[rows, :].astype(BF)

        @pl.when(i != me)
        def _():
            d = lax.rem(i - me + n, n)
            for t in range(3):
                to_ctx(
                    stage.at[t, rows], land.at[t, :, lanes_of(me)], gsend.at[t, d], grecv.at[t, d], i
                ).start()

        @pl.when(i == me)
        def _():
            for t in range(3):
                land[t, :, lanes_of(me)] = stage[t, rows, :]

        return unused

    lax.fori_loop(0, n, query_block, 0)
    for h in range(2):
        line = jnp.concatenate(
            [dtiles[h, 0], dtiles[h, 1], jnp.zeros((BLOCK, LINE - 2 * BLOCK), F32)], axis=1
        )
        row = lax.broadcasted_iota(jnp.int32, (BLOCK, LINE), 0)
        for bit in range(8):
            moved = pltpu.roll(line, LINE - (1 << bit), 1)
            line = jnp.where((row >> bit) & 1 == 1, moved, line)
        line_ref[h : h + 1, :] = jnp.sum(line, axis=0, keepdims=True)
    line_ref[2:4, :BLOCK] = far_sum[0:2, :]
    line_ref[2:4, BLOCK:] = jnp.zeros((2, LINE - BLOCK), F32)
    line_ref[4:8, :] = jnp.zeros((4, LINE), F32)
    for d in range(1, n):
        peer = lax.rem(me + d, n)
        to_ctx(
            do_ref.at[:, lanes_of(peer)], doh.at[rows_of(me, BLOCK)], send.at[0, d], recv.at[0, d], peer
        ).wait_send()
        for t in range(3):
            back = to_ctx(
                stage.at[t, rows_of(peer, BLOCK)], land.at[t, :, lanes_of(me)], gsend.at[t, d], grecv.at[t, d], peer
            )
            back.wait_send()
            back.wait_recv()
    dq_ref[...] = land[0]
    dk_ref[...] = land[1]
    dv_ref[...] = land[2]


def attn_backward(n, dout, qh, kh, vh, ot, lse, bias_lines):
    rows, seq = dout.shape[0], n * dout.shape[0]
    grads = jax.ShapeDtypeStruct(dout.shape, BF)
    return pl.pallas_call(
        functools.partial(attn_backward_kernel, n),
        out_shape=(grads, grads, grads, jax.ShapeDtypeStruct((8, LINE), F32)),
        in_specs=vmem(7),
        out_specs=tuple(vmem(4)),
        scratch_shapes=[
            pltpu.VMEM((seq, WIDE), BF),
            pltpu.VMEM((WIDE, seq), BF),
            pltpu.VMEM((3, seq, WIDE), BF),
            pltpu.VMEM((3, *dout.shape), BF),
            pltpu.VMEM((seq, WIDE), F32),
            pltpu.VMEM((seq, WIDE), F32),
            pltpu.VMEM((WIDE, BLOCK), F32),
            pltpu.VMEM((2, 2, BLOCK, BLOCK), F32),
            pltpu.VMEM((2, 2, BLOCK, BLOCK), F32),
            pltpu.VMEM((8, BLOCK), F32),
            pltpu.SemaphoreType.DMA((1, n)),
            pltpu.SemaphoreType.DMA((1, n)),
            pltpu.SemaphoreType.DMA((3, n)),
            pltpu.SemaphoreType.DMA((3, n)),
        ],
        compiler_params=pltpu.CompilerParams(
            collective_id=2, has_side_effects=True, vmem_limit_bytes=40 << 20
        ),
        name="attn_backward",
    )(dout, qh, kh, vh, ot, lse, bias_lines)


def line_selector():
    place = jnp.arange(LINE)
    offset = jnp.where(place < LINE // 2, -place, LINE - place)
    return (bucket_of(offset)[None, :] == jnp.arange(NB)[:, None]).astype(jnp.float32)


def ring_forward(query_low, key_low, value_low, bucket_table):
    row_count, attn_width = query_low.shape
    position = lax.axis_index("ctx")
    scale_factor = HD ** (-0.5)
    bias_set, onehots = make_bias(bucket_table.astype(jnp.float32), row_count)
    query_heads = query_low.reshape(row_count, H, HD)
    start_state = (
        jnp.full((H, row_count), negative, jnp.float32),
        jnp.zeros((H, row_count), jnp.float32),
        jnp.zeros((row_count, attn_width), jnp.float32),
    )
    running_max, running_sum, running_acc = forward_fold(
        query_heads,
        position,
        row_count,
        bias_set,
        scale_factor,
        start_state,
        (
            lax.all_gather(key_low, "ctx", axis=0, tiled=True),
            lax.all_gather(value_low, "ctx", axis=0, tiled=True),
        ),
    )
    attended = (running_acc.reshape(row_count, H, HD) / running_sum.T[:, :, None]).reshape(
        row_count, attn_width
    )
    log_total = running_max + jnp.log(running_sum)
    state = (query_heads, key_low, value_low, attended, log_total, bias_set, onehots)
    return attended.astype(jnp.bfloat16), state


def ring_backward(state, dout_low):
    query_heads, key_low, value_low, attended, log_total, bias_set, onehots = state
    row_count, attn_width = dout_low.shape
    cycle_size = lax.axis_size("ctx")
    position = lax.axis_index("ctx")
    scale_factor = HD ** (-0.5)
    dout_heads = dout_low.reshape(row_count, H, HD)
    row_delta = jnp.sum(
        (dout_low.astype(jnp.float32) * attended).reshape(row_count, H, HD), axis=-1
    ).T
    zero_rows = jnp.zeros((row_count, attn_width), jnp.float32)
    zero_tables = (
        jnp.zeros((H, row_count, row_count), jnp.float32),
        jnp.zeros((H, row_count, row_count), jnp.float32),
        jnp.zeros((H,), jnp.float32),
    )

    def visit(folded, key_now, value_now, relation):

        def visit_compute(current):
            dquery_acc, dkey_acc, dvalue_acc, relative_bias_tables = current
            key_heads = key_now.reshape(row_count, H, HD)
            weights_now, dscores, ds_low = pair_core(
                query_heads,
                dout_heads,
                log_total,
                row_delta,
                key_heads,
                value_now.reshape(row_count, H, HD),
                relation,
                bias_set,
                scale_factor,
            )
            dquery = jnp.einsum(
                "hqk,khd->qhd", ds_low, key_heads, preferred_element_type=jnp.float32
            ).reshape(row_count, attn_width)
            dkey = jnp.einsum(
                "hqk,qhd->khd", ds_low, query_heads, preferred_element_type=jnp.float32
            ).reshape(row_count, attn_width)
            dvalue = jnp.einsum(
                "hqk,qhd->khd",
                weights_now.astype(jnp.bfloat16),
                dout_heads,
                preferred_element_type=jnp.float32,
            ).reshape(row_count, attn_width)
            return (
                dquery_acc + dquery,
                dkey_acc + dkey,
                dvalue_acc + dvalue,
                add_tables(relative_bias_tables, dscores, relation),
            )

        return lax.cond(relation >= 0, visit_compute, lambda unchanged: unchanged, folded)

    first_state = visit(
        (zero_rows, zero_rows, zero_rows, zero_tables), key_low, value_low, jnp.array(0, jnp.int32)
    )

    def cycle_step(carried, cycle_index):
        key_now, value_now, (dquery_acc, dkey_acc, dvalue_acc, relative_bias_tables) = carried
        key_next, value_next = passed_along((key_now, value_now), "ctx", 1)
        dkey_next, dvalue_next = (
            from_behind(dkey_acc.astype(jnp.bfloat16), "ctx", 1).astype(dkey_acc.dtype),
            from_behind(dvalue_acc.astype(jnp.bfloat16), "ctx", 1).astype(dvalue_acc.dtype),
        )
        relation = jnp.where(position >= cycle_index, cycle_index, -1)
        updated = visit(
            (dquery_acc, dkey_next, dvalue_next, relative_bias_tables),
            key_next,
            value_next,
            relation,
        )
        return ((key_next, value_next, updated), None)

    (
        unused_key,
        unused_value,
        (dquery_total, dkey_part, dvalue_part, relative_bias_tables),
    ), unused = lax.scan(cycle_step, (key_low, value_low, first_state), jnp.arange(1, cycle_size))
    dkey_total, dvalue_total = (
        from_behind(dkey_part.astype(jnp.bfloat16), "ctx", 1).astype(dkey_part.dtype),
        from_behind(dvalue_part.astype(jnp.bfloat16), "ctx", 1).astype(dvalue_part.dtype),
    )
    dquery_low = dquery_total.astype(jnp.bfloat16)
    dkey_low = dkey_total.astype(jnp.bfloat16)
    dvalue_low = dvalue_total.astype(jnp.bfloat16)
    current_bucket_selector, previous_bucket_selector, onehot_far = onehots
    grad_biastable = (
        jnp.einsum(
            "afw,mfw->am",
            current_bucket_selector,
            relative_bias_tables[0],
            precision=strongest_precision,
        )
        + jnp.einsum(
            "afw,mfw->am",
            previous_bucket_selector,
            relative_bias_tables[1],
            precision=strongest_precision,
        )
        + onehot_far[:, None] * relative_bias_tables[2][None, :]
    )
    return dquery_low, dkey_low, dvalue_low, grad_biastable


def heads_forward(query_low, key_low, value_low, bucket_table):
    lines = jnp.dot(
        bucket_table.astype(jnp.float32).T, line_selector(), precision=strongest_precision
    )
    peers = lax.axis_size("ctx")
    attended_low, *saved = attn_forward(peers, query_low, key_low, value_low, lines)
    return attended_low, (*saved, lines)


def heads_backward(state, dout_low):
    peers = lax.axis_size("ctx")
    dquery_low, dkey_low, dvalue_low, sums = attn_backward(peers, dout_low, *state)
    selector = line_selector()
    table = jnp.dot(selector, sums[:2].T, precision=strongest_precision)
    far = jnp.sum(sums[2:4], axis=1)
    table = table + selector[:, WIDE : WIDE + 1] * far[None, :]
    whole = jnp.zeros((NB, H), jnp.float32)
    whole = lax.dynamic_update_slice(whole, table, (0, 2 * lax.axis_index("ctx")))
    return dquery_low, dkey_low, dvalue_low, whole


RING = 8
HOPS = RING - 1


def ring_place(n):
    me = lax.axis_index("ctx")
    half = n // 2

    def at(place):
        return jnp.where(place < half, 2 * place, 2 * (n - 1 - place) + 1)

    place = jnp.where(lax.rem(me, 2) == 0, me // 2, n - 1 - me // 2)
    return place, at(lax.rem(place + 1, n)), at(lax.rem(place + n - 1, n))


def other_wa(me, bit):
    flipped = lax.rem(me // bit, 2)
    return me + bit - 2 * bit * flipped


def remote(src, dst, send_sem, recv_sem, **device):
    return pltpu.make_async_remote_copy(
        src_ref=src,
        dst_ref=dst,
        send_sem=send_sem,
        recv_sem=recv_sem,
        device_id=device,
        device_id_type=MESH,
    )


TALL, FLAT = (224, 1024), (256, 896)
UNITS = ("cq", "ck", "cv", "co", "q", "k", "v", "so")
LANES = (
    (1, ("fin",), 0),
    (-1, ("fout",), 0),
    (1, ("cA",), 9),
    (-1, ("cB", "co"), 9),
    (1, ("sA",), 15),
    (-1, ("sB", "so"), 15),
)
MEMBERS = {"cA": ("cq", "ck"), "cB": ("cv",), "sA": ("q", "k"), "sB": ("v",)}
BUFFERS = {
    "fin": (112, 896),
    "fout": (112, 896),
    "cA": (448, 128),
    "cB": (224, 128),
    "co": (32, 896),
    "sA": (448, 128),
    "sB": (224, 128),
    "so": (32, 896),
}
NAMES = tuple(BUFFERS)


def reduce_kernel(*refs):
    parts = dict(zip(UNITS, refs[:8], strict=True))
    fin_ref, fout_ref = refs[8:10]
    full = dict(zip(NAMES, refs[10:18], strict=True))
    rest = refs[18:]
    share = dict(zip(NAMES, rest[:8], strict=True))
    hold = dict(zip(NAMES, rest[8:16], strict=True))
    rest = rest[16:]
    tall_own, tall_in, tall_out, tall_x, flat_own, flat_in, flat_out, flat_x = rest[:8]
    (own_sem, core_send, core_recv, x_send, x_recv, a_send, a_recv, ring_send, ring_recv, f_sem) = rest[8:]

    wa = lax.axis_index("wa")
    place, after, before = ring_place(RING)
    mate, across = other_wa(wa, 1), other_wa(wa, 2)
    core, half = lax.rem(wa, 2), wa // 2
    barrier = pltpu.get_barrier_semaphore()
    neighbours = [{"wa": mate}, {"wa": across}, {"wa": other_wa(across, 1)}, {"ctx": after}, {"ctx": before}]
    for who in neighbours:
        pl.semaphore_signal(barrier, inc=1, device_id=who, device_id_type=MESH)
    pl.semaphore_wait(barrier, len(neighbours))

    load_out = pltpu.make_async_copy(fout_ref, share["fout"], f_sem.at[0])
    load_out.start()
    own_fin = pltpu.make_async_copy(
        fin_ref.at[pl.ds(2 * wa, 2)], share["fin"].at[pl.ds(2 * wa, 2)], f_sem.at[1]
    )
    own_fin.start()
    fin_copies = []
    for d, peer in enumerate((across, other_wa(across, 1), mate)):
        copy = remote(
            fin_ref.at[pl.ds(2 * peer, 2)],
            share["fin"].at[pl.ds(2 * wa, 2)],
            a_send.at[d],
            a_recv.at[d],
            wa=peer,
        )
        copy.start()
        fin_copies.append(copy)

    own_copies, core_copies, x_copies = {}, {}, {}
    place_of = {}
    counts = {TALL: 0, FLAT: 0}
    for u, name in enumerate(UNITS):
        shape = FLAT if name in ("co", "so") else TALL
        slot = counts[shape]
        counts[shape] += 1
        own, inn = (tall_own, tall_in) if shape == TALL else (flat_own, flat_in)
        place_of[name] = (shape, slot)
        rows = shape[0]
        for x in range(2):
            mine = pl.ds(pl.multiple_of((2 * x + core) * rows, 16), rows)
            theirs = pl.ds(pl.multiple_of((2 * x + 1 - core) * rows, 16), rows)
            copy = pltpu.make_async_copy(parts[name].at[mine], own.at[slot, x], own_sem.at[u, x])
            copy.start()
            own_copies[name, x] = copy
            copy = remote(
                parts[name].at[theirs], inn.at[slot, x], core_send.at[u, x], core_recv.at[u, x], wa=mate
            )
            copy.start()
            core_copies[name, x] = copy

    def send_across(name):
        u = UNITS.index(name)
        shape, slot = place_of[name]
        own, inn, out, land = (
            (tall_own, tall_in, tall_out, tall_x) if shape == TALL else (flat_own, flat_in, flat_out, flat_x)
        )
        for x in range(2):
            own_copies[name, x].wait()
            core_copies[name, x].wait_recv()
        out[slot] = (own[slot, 1 - half].astype(F32) + inn[slot, 1 - half].astype(F32)).astype(BF)
        copy = remote(out.at[slot], land.at[slot], x_send.at[u], x_recv.at[u], wa=across)
        copy.start()
        x_copies[name] = copy

    def gather_share(name):
        shape, slot = place_of[name]
        own, inn, land = (tall_own, tall_in, tall_x) if shape == TALL else (flat_own, flat_in, flat_x)
        x_copies[name].wait_recv()
        total = (
            own[slot, half].astype(F32) + inn[slot, half].astype(F32) + land[slot].astype(F32)
        ).astype(BF)
        if shape == FLAT:
            for c in range(RING):
                share[name][c] = total[c * 32 : (c + 1) * 32, :]
        else:
            [(target, at)] = [(b, m.index(name)) for b, m in MEMBERS.items() if name in m]
            for c in range(RING):
                share[target][c, at * 224 : (at + 1) * 224, :] = total[:, c * 128 : (c + 1) * 128]

    copies = {}

    def ring_step(lane, step):
        way, buffers, unused = LANES[lane]
        here = place if way == 1 else lax.rem(RING - place, RING)
        target = after if way == 1 else before
        for name in buffers:
            b = NAMES.index(name)

            def chunk(offset):
                return lax.rem(here + offset + 2 * RING, RING)

            if step < HOPS:
                now = chunk(-step)
                if step > 0:
                    copies[name, step - 1].wait_recv()
                    share[name][now] = (
                        share[name][now].astype(F32) + hold[name][step - 1].astype(F32)
                    ).astype(BF)
                src, dst = share[name].at[now], hold[name].at[step]
            elif step == HOPS:
                now = chunk(1)
                copies[name, step - 1].wait_recv()
                full[name][now] = (
                    share[name][now].astype(F32) + hold[name][step - 1].astype(F32)
                ).astype(BF)
                src = dst = full[name].at[now]
            else:
                copies[name, step - 1].wait_recv()
                now = chunk(1 - (step - HOPS))
                if step == 2 * HOPS:
                    continue
                src = dst = full[name].at[now]
            copy = remote(src, dst, ring_send.at[b, step], ring_recv.at[b, step], ctx=target)
            copy.start()
            copies[name, step] = copy

    load_out.wait()
    ring_step(1, 0)
    for name in UNITS[:4]:
        send_across(name)
    own_fin.wait()
    for copy in fin_copies:
        copy.wait_recv()
    ring_step(0, 0)
    for name in UNITS[4:]:
        send_across(name)
    last = max(start for _, _, start in LANES) + 2 * HOPS
    for tick in range(1, last + 1):
        for lane, (_, buffers, start) in enumerate(LANES):
            step = tick - start
            if step == 0:
                for name in buffers:
                    for member in MEMBERS.get(name, (name,)):
                        gather_share(member)
            if 0 <= step <= 2 * HOPS:
                ring_step(lane, step)
    for copy in fin_copies:
        copy.wait_send()
    for name in UNITS:
        for x in range(2):
            core_copies[name, x].wait_send()
        x_copies[name].wait_send()
    for copy in copies.values():
        copy.wait_send()


def reduce_grads(parts, fin, fout):
    any_spec = pl.BlockSpec(memory_space=pl.ANY)
    dma = pltpu.SemaphoreType.DMA
    return pl.pallas_call(
        reduce_kernel,
        out_shape=tuple(jax.ShapeDtypeStruct((RING, *BUFFERS[b]), BF) for b in NAMES),
        in_specs=[any_spec] * 10,
        out_specs=tuple(vmem(len(NAMES))),
        scratch_shapes=[
            *(pltpu.VMEM((RING, *BUFFERS[b]), BF) for b in NAMES),
            *(pltpu.VMEM((HOPS, *BUFFERS[b]), BF) for b in NAMES),
            pltpu.VMEM((6, 2, *TALL), BF),
            pltpu.VMEM((6, 2, *TALL), BF),
            pltpu.VMEM((6, *TALL), BF),
            pltpu.VMEM((6, *TALL), BF),
            pltpu.VMEM((2, 2, *FLAT), BF),
            pltpu.VMEM((2, 2, *FLAT), BF),
            pltpu.VMEM((2, *FLAT), BF),
            pltpu.VMEM((2, *FLAT), BF),
            dma((8, 2)),
            dma((8, 2)),
            dma((8, 2)),
            dma((8,)),
            dma((8,)),
            dma((3,)),
            dma((3,)),
            dma((8, 2 * HOPS)),
            dma((8, 2 * HOPS)),
            dma((2,)),
        ],
        compiler_params=pltpu.CompilerParams(
            collective_id=3, has_side_effects=True, vmem_limit_bytes=60 << 20
        ),
        name="reduce_grads",
    )(*parts, *(part.reshape(RING, *BUFFERS["fin"]) for part in (fin, fout)))


def unfold(full):
    def tall(name, at):
        piece = full[name][:, at * 224 : (at + 1) * 224, :].astype(F32)
        return jnp.transpose(piece, (1, 0, 2)).reshape(TALL)

    out = {m: tall(b, at) for b, members in MEMBERS.items() for at, m in enumerate(members)}
    for name in ("co", "so"):
        out[name] = full[name].reshape(FLAT).astype(F32)
    out["fout"] = full["fout"].reshape(896, 896).astype(F32)
    out["fin"] = jnp.transpose(full["fin"].reshape(4, 224, 896).astype(F32), (1, 0, 2)).reshape(224, 3584)
    return out


GELU = (2.0 / math.pi) ** 0.5


def ffn_kernel(
    f_ref, cot_ref, win_ref, wout_ref, bias_ref, res_ref, df_ref, dwin_ref, dwout_ref, dbias_ref,
    f_all, g_all, dul_all, own, kept, out_mate, out_cross, in_mate, in_cross, x_out, x_in,
    f_send, f_recv, p_send, p_recv,
):
    me = lax.axis_index("wa")
    mate, across = other_wa(me, 1), other_wa(me, 2)
    both = other_wa(across, 1)
    barrier = pltpu.get_barrier_semaphore()
    for peer in (mate, across):
        pl.semaphore_signal(barrier, inc=1, device_id={"wa": peer}, device_id_type=MESH)
    pl.semaphore_wait(barrier, 2)
    to_across = remote(f_ref, f_all.at[me], f_send.at[1], f_recv.at[1], wa=across)
    to_across.start()
    to_mate = remote(f_ref, f_all.at[me], f_send.at[0], f_recv.at[0], wa=mate)
    to_mate.start()
    forward = remote(f_all.at[across], f_all.at[across], f_send.at[2], f_recv.at[2], wa=mate)
    f_all[me] = f_ref[...]
    order = (me, mate, across, both)
    dbias_ref[...] = jnp.zeros_like(dbias_ref)
    for k, s in enumerate(order):
        if k == 1:
            to_mate.wait_recv()
        if k == 2:
            to_across.wait_recv()
            forward.start()
        if k == 3:
            forward.wait_recv()
        u = nn_dot(f_all[s], win_ref[...]) + bias_ref[...]
        square = u * u
        t = jnp.tanh(GELU * (u + 0.044715 * (square * u)))
        g_all[s] = (0.5 * u * (1.0 + t)).astype(BF)
        slope = 0.5 * (1.0 + t) + 0.5 * u * (1.0 - t * t) * (GELU * (1.0 + 3 * 0.044715 * square))
        du = nt_dot(cot_ref[s], wout_ref[...]) * slope
        dbias_ref[...] += jnp.sum(du.reshape(32, 8, du.shape[1]), axis=0)
        dul_all[s] = du.astype(BF)

    def scatter(which, product):
        out_cross[which] = product(both).astype(BF)
        cross = remote(
            out_cross.at[which], in_cross.at[which], p_send.at[which, 0], p_recv.at[which, 0], wa=mate
        )
        cross.start()
        kept[...] = product(across)
        cross.wait_recv()
        x_out[which] = (kept[...] + in_cross[which].astype(F32)).astype(BF)
        over = remote(
            x_out.at[which], x_in.at[which], p_send.at[which, 1], p_recv.at[which, 1], wa=across
        )
        over.start()
        out_mate[which] = product(mate).astype(BF)
        near = remote(
            out_mate.at[which], in_mate.at[which], p_send.at[which, 2], p_recv.at[which, 2], wa=mate
        )
        near.start()
        own[which] = product(me)
        return cross, over, near

    def finish(which, copies, out_ref):
        cross, over, near = copies
        near.wait_recv()
        over.wait_recv()
        out_ref[...] = own[which] + in_mate[which].astype(F32) + x_in[which].astype(F32)
        for copy in copies:
            copy.wait_send()

    df_copies = scatter(0, lambda s: nt_dot(dul_all[s], win_ref[...]))
    res_copies = scatter(1, lambda s: nn_dot(g_all[s], wout_ref[...]))
    width = f_ref.shape[1]

    def outer(left_all, right, out_ref):
        for c in range(width // WIDE):
            lanes = slice(c * WIDE, (c + 1) * WIDE)
            total = None
            for s in range(4):
                left = left_all[s, :, lanes].astype(F32).T.astype(BF)
                now = nn_dot(left, right[s])
                total = now if total is None else total + now
            out_ref[lanes, :] = total.astype(BF)

    outer(f_all, dul_all, dwin_ref)
    outer(g_all, cot_ref, dwout_ref)
    finish(0, df_copies, df_ref)
    finish(1, res_copies, res_ref)
    for copy in (to_mate, to_across, forward):
        copy.wait_send()


def ffn(f_low, cot_all, win, wout, bias):
    rows, width = f_low.shape
    hidden = win.shape[1]
    dma = pltpu.SemaphoreType.DMA
    block = (rows, width)
    return pl.pallas_call(
        ffn_kernel,
        out_shape=(
            jax.ShapeDtypeStruct(block, F32),
            jax.ShapeDtypeStruct(block, F32),
            jax.ShapeDtypeStruct(win.shape, BF),
            jax.ShapeDtypeStruct(wout.shape, BF),
            jax.ShapeDtypeStruct((8, hidden), F32),
        ),
        in_specs=vmem(5),
        out_specs=tuple(vmem(5)),
        scratch_shapes=[
            pltpu.VMEM((4, *block), BF),
            pltpu.VMEM((4, rows, hidden), BF),
            pltpu.VMEM((4, rows, hidden), BF),
            pltpu.VMEM((2, *block), F32),
            pltpu.VMEM(block, F32),
            *[pltpu.VMEM((2, *block), BF)] * 6,
            dma((3,)),
            dma((3,)),
            dma((2, 3)),
            dma((2, 3)),
        ],
        compiler_params=pltpu.CompilerParams(
            collective_id=4, has_side_effects=True, vmem_limit_bytes=56 << 20
        ),
        name="feed_forward",
    )(f_low, cot_all, win, wout, bias)


def padded_rows(pad, values):
    rows = values.shape[0]
    pad[...] = jnp.zeros_like(pad)
    pad[1 : rows + 1, :] = values.astype(F32)


def both_heads(pad, g):
    here = pad[g * SPAN : (g + 1) * SPAN, :]
    left = head_mask(0, SPAN)
    return jnp.concatenate([jnp.where(left, here, 0.0), jnp.where(left, 0.0, here)], 0).astype(BF)


def join_heads(stacked):
    return jnp.where(head_mask(0, SPAN), stacked[:SPAN], stacked[SPAN:])


def cross_forward_kernel(groups, keep_ref, q_ref, k_ref, v_ref, x_ref, q_pad, x_pad):
    padded_rows(q_pad, q_ref[...])
    for g in range(groups):
        rows = slice(g * 256, (g + 1) * 256)
        query = both_heads(q_pad, g) * BF(HD**-0.5)
        scores = nt_dot(query, k_ref[rows, :])
        weights = jnp.exp(scores - jnp.max(scores, axis=1, keepdims=True))
        weights = weights / jnp.sum(weights, axis=1, keepdims=True)
        mixed = join_heads(nn_dot(weights.astype(BF), v_ref[rows, :]))
        if g == 0:
            mixed = mixed * keep_ref[0:1, :]
        x_pad[g * SPAN : (g + 1) * SPAN, :] = mixed
    x_ref[...] = x_pad[1 : x_ref.shape[0] + 1, :].astype(BF)


def pair_specs(*rows):
    return [pl.BlockSpec((r, WIDE), lambda p: (0, p)) for r in rows]


def cross_forward(keep, query, keys, values):
    rows, width = query.shape
    many = keys.shape[0]
    groups = many // 256
    return pl.pallas_call(
        functools.partial(cross_forward_kernel, groups),
        grid=(width // WIDE,),
        out_shape=jax.ShapeDtypeStruct(query.shape, BF),
        in_specs=[pl.BlockSpec((8, WIDE), lambda p: (0, 0)), *pair_specs(rows, many, many)],
        out_specs=pair_specs(rows)[0],
        scratch_shapes=[pltpu.VMEM((groups * SPAN, WIDE), F32)] * 2,
        compiler_params=pltpu.CompilerParams(vmem_limit_bytes=16 << 20),
        name="cross_forward",
    )(keep, query, keys, values)


def cross_backward_kernel(
    groups, keep_ref, q_ref, dx_ref, k_ref, v_ref, dq_ref, dk_ref, dv_ref, q_pad, dx_pad, dq_pad
):
    padded_rows(q_pad, q_ref[...])
    padded_rows(dx_pad, dx_ref[...])
    dx_pad[:SPAN, :] = dx_pad[:SPAN, :] * keep_ref[0:1, :]
    for g in range(groups):
        rows = slice(g * 256, (g + 1) * 256)
        query = both_heads(q_pad, g) * BF(HD**-0.5)
        dmixed = both_heads(dx_pad, g)
        keys, values = k_ref[rows, :], v_ref[rows, :]
        scores = nt_dot(keys, query)
        weights = jnp.exp(scores - jnp.max(scores, axis=0, keepdims=True))
        weights = weights / jnp.sum(weights, axis=0, keepdims=True)
        dweights = nt_dot(values, dmixed)
        dscores = weights * (dweights - jnp.sum(weights * dweights, axis=0, keepdims=True))
        dk_ref[rows, :] = nn_dot(dscores.astype(BF), query).astype(BF)
        dv_ref[rows, :] = nn_dot(weights.astype(BF), dmixed).astype(BF)
        back = (dscores * HD**-0.5).T.astype(BF)
        dq_pad[g * SPAN : (g + 1) * SPAN, :] = join_heads(nn_dot(back, keys))
    dq_ref[...] = dq_pad[1 : dq_ref.shape[0] + 1, :].astype(BF)


def cross_backward(keep, query, dmixed, keys, values):
    rows, width = query.shape
    many = keys.shape[0]
    groups = many // 256
    return pl.pallas_call(
        functools.partial(cross_backward_kernel, groups),
        grid=(width // WIDE,),
        out_shape=(
            jax.ShapeDtypeStruct(query.shape, BF),
            jax.ShapeDtypeStruct(keys.shape, BF),
            jax.ShapeDtypeStruct(keys.shape, BF),
        ),
        in_specs=[
            pl.BlockSpec((8, WIDE), lambda p: (0, 0)),
            *pair_specs(rows, rows, many, many),
        ],
        out_specs=tuple(pair_specs(rows, many, many)),
        scratch_shapes=[pltpu.VMEM((groups * SPAN, WIDE), F32)] * 3,
        compiler_params=pltpu.CompilerParams(vmem_limit_bytes=16 << 20),
        name="cross_backward",
    )(keep, query, dmixed, keys, values)


NAMES_OF_WEIGHTS = (
    "selfnorm", "selfquery", "selfkey", "selfvalue", "selfout", "biastable", "crossnorm", "crossquery",
    "crosskey", "crossvalue", "crossout", "feednorm", "feedin", "feedbias", "feedout", "outbias",
)
UNIT_WEIGHTS = (
    "crossquery", "crosskey", "crossvalue", "crossout", "selfquery", "selfkey", "selfvalue", "selfout",
)


def whole_over_wa(shard):
    return lax.all_gather(shard, "wa", axis=0, tiled=True)


def reduce_plain(parts, fin, fout):
    shares = [
        lax.psum_scatter(part, "wa", scatter_dimension=0, tiled=True).astype(F32) for part in parts
    ]
    own_rows = lax.all_to_all(fin, "wa", 0, 1, tiled=True).astype(F32)
    totals = lax.psum((*shares, own_rows, fout.astype(F32)), "ctx")
    return dict(zip((*UNITS, "fin", "fout"), totals, strict=True))


def per_device(tokens, neighbours, cotangent, *shards):
    given = dict(zip(NAMES_OF_WEIGHTS, shards, strict=True))
    peers = lax.axis_size("ctx")
    position = lax.axis_index("ctx")
    row_count, model_width = tokens.shape[1:]
    split_heads = peers * 2 == H and row_count == BLOCK
    self_forward = heads_forward if split_heads else ring_forward
    self_backward = heads_backward if split_heads else ring_backward

    small_names = ("selfnorm", "crossnorm", "feednorm", "outbias", "biastable")
    small = jnp.concatenate([given[name].reshape(-1) for name in small_names])
    small = lax.all_gather(small, "wa", axis=0)
    small_of, start = {}, 0
    for name in small_names:
        size = given[name].size
        small_of[name] = small[:, start : start + size].reshape(-1).astype(F32)
        start += size
    bucket_table = small_of["biastable"].reshape(NB, H)
    full = {name: whole_over_wa(given[name]) for name in UNIT_WEIGHTS}
    upstream_low = cotangent[0]
    upstream = upstream_low.astype(F32)
    upstream_all = lax.all_gather(upstream_low, "wa", axis=0)
    feed_in = lax.all_to_all(given["feedin"], "wa", 1, 0, tiled=True)

    inputs = tokens[0].astype(F32)
    normed_self, back_self = jax.vjp(root_norm, inputs, small_of["selfnorm"])
    normed_low = normed_self.astype(BF)
    query_low = forward_product(normed_low, full["selfquery"]).astype(BF)
    key_low = forward_product(normed_low, full["selfkey"]).astype(BF)
    value_low = forward_product(normed_low, full["selfvalue"]).astype(BF)
    attended_low, attention_state = self_forward(query_low, key_low, value_low, bucket_table)
    hidden = inputs + forward_product(attended_low, full["selfout"])

    spans = neighbours.shape[1]
    span_rows = neighbours.shape[2] * neighbours.shape[3]
    own_rows = neighbours[0].reshape(spans * span_rows, model_width)
    before = passed_along(own_rows[-span_rows:], "ctx", 1)
    near_rows = jnp.concatenate([before, own_rows], 0)
    keys_cross = forward_product(near_rows, full["crosskey"]).astype(BF)
    values_cross = forward_product(near_rows, full["crossvalue"]).astype(BF)
    normed_cross, back_cross = jax.vjp(root_norm, hidden, small_of["crossnorm"])
    cross_in = normed_cross.astype(BF)
    query_cross = forward_product(cross_in, full["crossquery"]).astype(BF)
    keep = jnp.full((8, WIDE), jnp.where(position > 0, 1.0, 0.0), F32)
    mixed_low = cross_forward(keep, query_cross, keys_cross, values_cross)
    hidden_two = hidden + forward_product(mixed_low, full["crossout"])

    normed_feed, back_feed = jax.vjp(root_norm, hidden_two, small_of["feednorm"])
    feed_low = normed_feed.astype(BF)
    bias_row = given["feedbias"].astype(F32)[None]
    fed, grad_feed, fin, fout, bias_sums = ffn(
        feed_low, upstream_all, feed_in, given["feedout"], bias_row
    )
    result = (hidden_two + fed + small_of["outbias"]).astype(BF)
    grad_two_part, grad_feednorm = back_feed(grad_feed)
    grad_two = upstream + grad_two_part
    two_low = grad_two.astype(BF)

    grad_mixed = back_product(two_low, full["crossout"]).astype(BF)
    grad_query_cross, dkeys, dvalues = cross_backward(
        keep, query_cross, grad_mixed, keys_cross, values_cross
    )
    edge = span_rows * spans

    def owned(grads):
        back = passed_along(grads[:span_rows], "ctx", -1).astype(F32)
        last = (grads[edge:].astype(F32) + back).astype(BF)
        return jnp.concatenate([grads[span_rows:edge], last], 0)

    key_grads, value_grads = owned(dkeys), owned(dvalues)
    grad_neigh = (
        (back_product(key_grads, full["crosskey"]) + back_product(value_grads, full["crossvalue"]))
        .astype(BF)
        .reshape(neighbours.shape)
    )
    grad_hidden_part, grad_crossnorm = back_cross(
        back_product(grad_query_cross, full["crossquery"])
    )
    grad_hidden = grad_two + grad_hidden_part
    hidden_low = grad_hidden.astype(BF)
    dout_low = back_product(hidden_low, full["selfout"]).astype(BF)
    dquery_low, dkey_low, dvalue_low, grad_biastable = self_backward(attention_state, dout_low)
    grad_normed = (
        back_product(dquery_low, full["selfquery"])
        + back_product(dkey_low, full["selfkey"])
        + back_product(dvalue_low, full["selfvalue"])
    )
    grad_input_part, grad_selfnorm = back_self(grad_normed)
    grad_inputs = (grad_hidden + grad_input_part).astype(BF)

    pairs = {
        "cq": (cross_in, grad_query_cross),
        "ck": (own_rows, key_grads),
        "cv": (own_rows, value_grads),
        "co": (mixed_low, two_low),
        "q": (normed_low, dquery_low),
        "k": (normed_low, dkey_low),
        "v": (normed_low, dvalue_low),
        "so": (attended_low, hidden_low),
    }
    parts = [outer_product(*pairs[name]).astype(BF) for name in UNITS]
    if peers == RING:
        grads = unfold(dict(zip(NAMES, reduce_grads(parts, fin, fout), strict=True)))
    else:
        grads = reduce_plain(parts, fin, fout)

    wa, owners = lax.axis_index("wa"), lax.axis_size("wa")
    bias_grad = jnp.sum(bias_sums, axis=0)
    placed = lax.dynamic_update_slice(
        jnp.zeros((owners, bias_grad.size), F32), bias_grad[None], (wa, 0)
    )
    sums = [grad_selfnorm, grad_crossnorm, grad_feednorm, jnp.sum(upstream, axis=0), grad_biastable]
    packed = jnp.concatenate([*(v.reshape(owners, -1) for v in sums), placed], axis=1)
    packed = lax.psum(packed, ("ctx", "wa"))
    mine = lax.dynamic_index_in_dim(packed, wa, 0, keepdims=False)
    cuts, start = [], 0
    for v in (*sums, placed):
        cuts.append(mine[start : start + v.size // owners])
        start += v.size // owners
    own_selfnorm, own_crossnorm, own_feednorm, own_outbias, own_table, own_feedbias = cuts
    return (
        result[None],
        grad_inputs[None],
        grad_neigh,
        own_selfnorm,
        grads["q"],
        grads["k"],
        grads["v"],
        grads["so"],
        own_table.reshape(-1, H),
        own_crossnorm,
        grads["cq"],
        grads["ck"],
        grads["cv"],
        grads["co"],
        own_feednorm,
        grads["fin"],
        own_feedbias,
        grads["fout"],
        own_outbias,
    )


def solution(mesh):
    return jax.shard_map(
        per_device,
        mesh=mesh,
        in_specs=(
            P("wa", "ctx", None),
            P("wa", "ctx", None, None, None),
            P("wa", "ctx", None),
            P("wa"),
            P("wa", None),
            P("wa", None),
            P("wa", None),
            P("wa", None),
            P("wa", None),
            P("wa"),
            P("wa", None),
            P("wa", None),
            P("wa", None),
            P("wa", None),
            P("wa"),
            P("wa", None),
            P("wa"),
            P("wa", None),
            P("wa"),
        ),
        out_specs=(
            P("wa", "ctx", None),
            P("wa", "ctx", None),
            P("wa", "ctx", None, None, None),
            P("wa"),
            P("wa", None),
            P("wa", None),
            P("wa", None),
            P("wa", None),
            P("wa", None),
            P("wa"),
            P("wa", None),
            P("wa", None),
            P("wa", None),
            P("wa", None),
            P("wa"),
            P("wa", None),
            P("wa"),
            P("wa", None),
            P("wa"),
        ),
        check_vma=False,
    )
```

```python
import functools
import math

import jax
import jax.numpy as jnp
from jax import lax
from jax.experimental import pallas as pl
from jax.experimental.pallas import tpu as pltpu
from jax.sharding import PartitionSpec as P

H = 16
HD = 64
NB = 32
MAXD = 128
BLOCK = 256
SPAN = 64
MESH = pl.DeviceIdType.MESH
WIDE = 128
LINE = 1024
BF = jnp.bfloat16
F32 = jnp.float32


epsilon = 1e-06
negative = -1e30
strongest_precision = lax.Precision.HIGHEST


def passed_along(value, axis, by):
    peers = lax.axis_size(axis)
    pairs = [(i, i + by) for i in range(peers) if 0 <= i + by < peers]
    return lax.ppermute(value, axis, pairs)


def from_behind(block, axis, distance):
    devices = range(lax.axis_size(axis))
    route = [((i - distance) % len(devices), i) for i in devices]
    return lax.ppermute(block, axis, route)


def bucket_edges():
    half_count = NB // 2
    exact_part = half_count // 2
    edge_list = []
    for level_index in range(exact_part + 1, half_count):
        hits = [
            distance_now
            for distance_now in range(exact_part, MAXD + 1)
            if exact_part
            + int(
                math.log(distance_now / exact_part)
                / math.log(MAXD / exact_part)
                * (half_count - exact_part)
            )
            >= level_index
        ]
        edge_list.append(min(hits + [MAXD]))
    return (half_count, exact_part, edge_list)


def bucket_of(offset_value):
    half_count, exact_part, edge_list = bucket_edges()
    magnitude = jnp.abs(offset_value)
    far_part = exact_part + sum(
        [(magnitude >= edge_value).astype(magnitude.dtype) for edge_value in edge_list],
        jnp.zeros_like(magnitude),
    )
    return jnp.where(offset_value > 0, half_count, 0) + jnp.where(
        magnitude < exact_part, magnitude, far_part
    )


def root_norm(values, gain_vector):
    return (
        values
        * lax.rsqrt(jnp.mean(values * values, axis=-1, keepdims=True) + epsilon)
        * gain_vector
    )


def gelu_tanh(values):
    return jax.nn.gelu(values, approximate=True)


def forward_product(values, weight):
    return jnp.dot(values, weight, preferred_element_type=jnp.float32)


def outer_product(left_side, right_side):
    return lax.dot_general(
        left_side, right_side, (((0,), (0,)), ((), ())), preferred_element_type=jnp.float32
    )


def back_product(grad_low, weight):
    return lax.dot_general(
        grad_low, weight, (((1,), (1,)), ((), ())), preferred_element_type=jnp.float32
    )


def make_bias(bucket_bias_rows, row_count):
    query_place = jnp.arange(row_count)[:, None]
    key_place = jnp.arange(row_count)[None, :]
    levels = jnp.arange(NB)
    current_bucket_selector = (
        bucket_of(key_place - query_place)[None] == levels[:, None, None]
    ).astype(jnp.float32)
    previous_bucket_selector = (
        bucket_of(key_place - row_count - query_place)[None] == levels[:, None, None]
    ).astype(jnp.float32)
    onehot_far = (bucket_of(jnp.array(-MAXD, jnp.int32)) == levels).astype(jnp.float32)
    current_block_bias = jnp.einsum(
        "smz,sj->jmz", current_bucket_selector, bucket_bias_rows, precision=strongest_precision
    )
    previous_block_bias = jnp.einsum(
        "smz,sj->jmz", previous_bucket_selector, bucket_bias_rows, precision=strongest_precision
    )
    bias_far = jnp.dot(onehot_far, bucket_bias_rows, precision=strongest_precision)
    mask_same = key_place // BLOCK <= query_place // BLOCK
    return (
        (current_block_bias, previous_block_bias, bias_far, mask_same),
        (current_bucket_selector, previous_bucket_selector, onehot_far),
    )


def pair_scores(query_heads, key_heads, relation, bias_set, scale_factor):
    current_block_bias, previous_block_bias, bias_far, mask_same = bias_set
    raw_scores = jnp.einsum(
        "qhd,khd->hqk", query_heads, key_heads, preferred_element_type=jnp.float32
    )
    bias_rows = jnp.where(
        relation == 0,
        current_block_bias,
        jnp.where(relation == 1, previous_block_bias, bias_far[:, None, None]),
    )
    allowed = jnp.logical_or(relation > 0, mask_same)
    return jnp.where(allowed[None], raw_scores * scale_factor + bias_rows, negative)


def pair_core(
    query_heads,
    dout_heads,
    log_total,
    row_delta,
    key_heads,
    value_heads,
    relation,
    bias_set,
    scale_factor,
):
    scores = pair_scores(query_heads, key_heads, relation, bias_set, scale_factor)
    weights_now = jnp.exp(scores - log_total[:, :, None])
    grad_weights = jnp.einsum(
        "qhd,khd->hqk", dout_heads, value_heads, preferred_element_type=jnp.float32
    )
    dscores = weights_now * (grad_weights - row_delta[:, :, None])
    return (weights_now, dscores, (dscores * scale_factor).astype(jnp.bfloat16))


def add_tables(relative_bias_tables, dscores, relation):
    same_sum, prev_sum, far_sum = relative_bias_tables
    return (
        same_sum + jnp.where(relation == 0, dscores, 0.0),
        prev_sum + jnp.where(relation == 1, dscores, 0.0),
        far_sum + jnp.where(relation >= 2, jnp.sum(dscores, axis=(1, 2)), 0.0),
    )


def forward_fold(query_heads, position, row_count, bias_set, scale_factor, running, pieces):
    keys_all, values_all = pieces

    def one_shard(folded, shard_step):
        key_heads = lax.dynamic_slice_in_dim(
            keys_all, shard_step * row_count, row_count, 0
        ).reshape(row_count, H, HD)
        value_heads = lax.dynamic_slice_in_dim(
            values_all, shard_step * row_count, row_count, 0
        ).reshape(row_count, H, HD)
        relation = position - shard_step

        def one_compute(current):
            running_max, running_sum, running_acc = current
            scores = pair_scores(query_heads, key_heads, relation, bias_set, scale_factor)
            new_max = jnp.maximum(running_max, jnp.max(scores, axis=-1))
            factor = jnp.exp(running_max - new_max)
            weights_now = jnp.exp(scores - new_max[:, :, None])
            new_sum = running_sum * factor + jnp.sum(weights_now, axis=-1)
            update = jnp.einsum(
                "hqk,khd->qhd",
                weights_now.astype(jnp.bfloat16),
                value_heads,
                preferred_element_type=jnp.float32,
            )
            scaled = running_acc.reshape(row_count, H, HD) * factor.T[:, :, None]
            return (new_max, new_sum, (scaled + update).reshape(row_count, H * HD))

        return (lax.cond(relation >= 0, one_compute, lambda unchanged: unchanged, folded), None)

    running, unused = lax.scan(one_shard, running, jnp.arange(keys_all.shape[0] // row_count))
    return running


def nt_dot(left, right):
    return lax.dot_general(left, right, (((1,), (1,)), ((), ())), preferred_element_type=F32)


def nn_dot(left, right):
    return jnp.dot(left, right, preferred_element_type=F32)


def meet(neighbours):
    barrier = pltpu.get_barrier_semaphore()
    for who in neighbours:
        pl.semaphore_signal(barrier, inc=1, device_id=who, device_id_type=MESH)
    pl.semaphore_wait(barrier, len(neighbours))


def ctx_peers(n):
    me = lax.axis_index("ctx")
    return [{"ctx": lax.rem(me + d, n)} for d in range(1, n)]


def other_wa(me, bit):
    flipped = lax.rem(me // bit, 2)
    return me + bit - 2 * bit * flipped


def remote(src, dst, send_sem, recv_sem, **device):
    return pltpu.make_async_remote_copy(
        src_ref=src,
        dst_ref=dst,
        send_sem=send_sem,
        recv_sem=recv_sem,
        device_id=device,
        device_id_type=MESH,
    )


RING = 8
HOPS = RING - 1


def ring_place(n):
    me = lax.axis_index("ctx")
    half = n // 2

    def at(place):
        return jnp.where(place < half, 2 * place, 2 * (n - 1 - place) + 1)

    place = jnp.where(lax.rem(me, 2) == 0, me // 2, n - 1 - me // 2)
    return place, at(lax.rem(place + 1, n)), at(lax.rem(place + n - 1, n))


class Ring:
    def __init__(self, lanes, send, recv, share=None, hold=None, full=None):
        self.lanes, self.share, self.hold, self.full = lanes, share, hold, full
        self.sems = send, recv
        self.place, self.after, self.before = ring_place(RING)

    def copy(self, lane, src, dst, step):
        send, recv = self.sems
        way = self.lanes[lane][1]
        return remote(
            src, dst, send.at[lane, step], recv.at[lane, step], ctx=self.after if way == 1 else self.before
        )

    def chunk(self, lane, offset):
        here = self.place if self.lanes[lane][1] == 1 else RING - self.place
        return lax.rem(here + offset + 2 * RING, RING)

    def scatter(self, step, which):
        for lane in which:
            b, _, rows = self.lanes[lane]
            share = self.share.at[b, self.chunk(lane, -step), rows]

            @pl.when(step > 0)
            def _():
                there = self.hold.at[b, jnp.maximum(step - 1, 0), rows]
                self.copy(lane, share, there, jnp.maximum(step - 1, 0)).wait_recv()
                share[...] = (share[...].astype(F32) + there[...].astype(F32)).astype(BF)

            @pl.when(step < HOPS)
            def _():
                there = jnp.minimum(step, HOPS - 1)
                self.copy(lane, share, self.hold.at[b, there, rows], there).start()

    def gather(self, step, which):
        for lane in which:
            b, _, rows = self.lanes[lane]
            full = self.full[b].at[self.chunk(lane, 1 - step), rows]

            @pl.when(step > 0)
            def _():
                self.copy(lane, full, full, jnp.maximum(step - 1, 0)).wait_recv()

            @pl.when(step < HOPS)
            def _():
                self.copy(lane, full, full, jnp.minimum(step, HOPS - 1)).start()

    def finish(self, part):
        def one(step, unused):
            for lane in range(len(self.lanes)):
                self.copy(lane, part(lane), part(lane), step).wait_send()
            return unused

        lax.fori_loop(0, HOPS, one, 0)


TALL, FLAT = (224, 1024), (256, 896)
EARLY = ("cq", "ck", "cv", "co", "so")
LATE = ("q", "k", "v")
FEED = (8, 112, 896)
FEED_LANES = (
    (0, 1, slice(0, 64)),
    (1, -1, slice(0, 64)),
    (0, 1, slice(64, 112)),
    (1, -1, slice(64, 112)),
)
FEED_TURNS = ((0, 1), (2, 3))


class Folding:
    def __init__(self, names, parts, scratch):
        self.names = names
        self.parts = parts
        tall, flat, sems = scratch
        self.sets = {TALL: tall, FLAT: flat}
        self.own_sem, self.core_send, self.core_recv, self.x_send, self.x_recv = sems
        self.wa = lax.axis_index("wa")
        self.mate, self.across = other_wa(self.wa, 1), other_wa(self.wa, 2)
        self.core, self.half = lax.rem(self.wa, 2), self.wa // 2
        self.slots, count = {}, {TALL: 0, FLAT: 0}
        for name in names:
            shape = self.shape_of(name)
            self.slots[name] = (count[shape], self.sets[shape])
            count[shape] += 1
        self.own_copies, self.core_copies, self.x_copies = {}, {}, {}

    @staticmethod
    def shape_of(name):
        return FLAT if name in ("co", "so") else TALL

    @classmethod
    def scratch(cls, names):
        shapes = []
        for shape in (TALL, FLAT):
            many = sum(cls.shape_of(name) == shape for name in names)
            if many:
                shapes += [pltpu.VMEM((many, 2, *shape), BF)] * 2 + [pltpu.VMEM((many, *shape), BF)] * 2
        dma = pltpu.SemaphoreType.DMA
        many = len(names)
        return shapes + [dma((many, 2))] * 3 + [dma((many,))] * 2

    def start(self):
        for u, name in enumerate(self.names):
            slot, (own, inn, _, _) = self.slots[name]
            rows = self.shape_of(name)[0]
            for x in range(2):
                mine = pl.ds(pl.multiple_of((2 * x + self.core) * rows, 16), rows)
                theirs = pl.ds(pl.multiple_of((2 * x + 1 - self.core) * rows, 16), rows)
                copy = remote(
                    self.parts[name].at[theirs],
                    inn.at[slot, x],
                    self.core_send.at[u, x],
                    self.core_recv.at[u, x],
                    wa=self.mate,
                )
                copy.start()
                self.core_copies[name, x] = copy
                copy = pltpu.make_async_copy(
                    self.parts[name].at[mine], own.at[slot, x], self.own_sem.at[u, x]
                )
                copy.start()
                self.own_copies[name, x] = copy
            slot, (_, _, out, land) = self.slots[name]
            self.x_copies[name] = remote(
                out.at[slot], land.at[slot], self.x_send.at[u], self.x_recv.at[u], wa=self.across
            )

    def send(self, name):
        slot, (own, inn, out, _) = self.slots[name]
        for x in range(2):
            self.own_copies[name, x].wait()
            self.core_copies[name, x].wait_recv()
        away = 1 - self.half
        out[slot] = (own[slot, away].astype(F32) + inn[slot, away].astype(F32)).astype(BF)
        self.x_copies[name].start()

    def total(self, name):
        slot, (own, inn, _, land) = self.slots[name]
        self.x_copies[name].wait_recv()
        here = self.half
        return (
            own[slot, here].astype(F32) + inn[slot, here].astype(F32) + land[slot].astype(F32)
        ).astype(BF)

    def finish(self):
        for name in self.names:
            for x in range(2):
                self.core_copies[name, x].wait_send()
            self.x_copies[name].wait_send()


def lasting(microseconds):
    return pl.CostEstimate(
        flops=0, bytes_accessed=int(microseconds * 3.0e6), transcendentals=0
    )


def lanes_of(index):
    return pl.ds(pl.multiple_of(index * WIDE, WIDE), WIDE)


def rows_of(index, rows):
    return pl.ds(pl.multiple_of(index * rows, rows), rows)


def to_ctx(src, dst, send_sem, recv_sem, target):
    return pltpu.make_async_remote_copy(
        src_ref=src,
        dst_ref=dst,
        send_sem=send_sem,
        recv_sem=recv_sem,
        device_id={"ctx": target},
        device_id_type=MESH,
    )


def head_mask(h, rows):
    lane = lax.broadcasted_iota(jnp.int32, (rows, WIDE), 1)
    return (lane < HD) if h == 0 else (lane >= HD)


def bias_tiles(bias_ref, me, tiles):
    for h in range(2):
        line = bias_ref[pl.ds(2 * me + h, 1), :]
        rolled = pltpu.roll(
            jnp.broadcast_to(line, (BLOCK, LINE)), 0, 1, stride=1, stride_axis=0
        )
        tiles[h, 0] = rolled[:, :BLOCK]
        tiles[h, 1] = rolled[:, BLOCK : 2 * BLOCK]
        tiles[h, 2] = jnp.broadcast_to(line[:, WIDE : WIDE + BLOCK], (BLOCK, BLOCK))


def spread(n, me, pairs, send, recv, t):
    src, dst = pairs[t]
    for d in range(1, n):
        peer = lax.rem(me + d, n)
        to_ctx(
            src.at[:, lanes_of(peer)], dst.at[rows_of(me, BLOCK)], send.at[t, d], recv.at[t, d], peer
        ).start()
    dst[rows_of(me, BLOCK), :] = src[:, lanes_of(me)]


GATHERED = ("q", "k", "v", "so", "ck", "cv", "cq", "co")
GAINS = ("selfnorm", "crossnorm", "feednorm", "outbias")


class Gathering:
    def __init__(self, names, shards, whole, own_sem, send, recv):
        self.names, self.shards, self.whole = names, shards, whole
        self.sems = own_sem, send, recv
        self.wa = lax.axis_index("wa")
        self.mate, self.across = other_wa(self.wa, 1), other_wa(self.wa, 2)
        self.copies = {}

    def start(self):
        own_sem, send, recv = self.sems
        for u, name in enumerate(self.names):
            rows = self.shards[name].shape[0]
            shard, whole = self.shards[name], self.whole[name]
            mine = whole.at[pl.ds(pl.multiple_of(self.wa * rows, 16), rows)]
            theirs = whole.at[pl.ds(pl.multiple_of(self.across * rows, 16), rows)]
            over = remote(shard, mine, send.at[u, 0], recv.at[u, 0], wa=self.across)
            near = remote(shard, mine, send.at[u, 1], recv.at[u, 1], wa=self.mate)
            near.start()
            own = pltpu.make_async_copy(shard, mine, own_sem.at[u])
            own.start()
            pass_on = remote(theirs, theirs, send.at[u, 2], recv.at[u, 2], wa=self.mate)
            self.copies[name] = (over, near, pass_on, own)

    def cross(self, *names):
        for name in names:
            self.copies[name][0].start()

    def forward(self, *names):
        for name in names:
            over, _, pass_on, _ = self.copies[name]
            over.wait_recv()
            pass_on.start()

    def arrive(self, name):
        _, near, pass_on, own = self.copies[name]
        near.wait_recv()
        pass_on.wait_recv()
        own.wait()

    def finish(self):
        for copies in self.copies.values():
            for copy in copies[:3]:
                copy.wait_send()


def attn_forward_kernel(n, tokens_ref, small_ref, *refs):
    shards = dict(zip(GATHERED, refs[:8], strict=True))
    wholes = dict(zip(GATHERED, refs[8:16], strict=True))
    o_ref, low_ref, qh_out, kh_out, vh_out, ot_out, lse_out, small_out = refs[16:24]
    (
        held_q, held_k, held_v, proj, small_in, small_mid, qh, kh, vh, vt, oh, land, tiles, acc, stat,
        send, recv, osend, orecv, small_sem, own_sem, out_sem, gather_send, gather_recv,
    ) = refs[24:]
    held = {"q": held_q, "k": held_k, "v": held_v}
    gathering = Gathering(GATHERED, shards, wholes | held, own_sem, gather_send, gather_recv)
    meet([*ctx_peers(n), {"wa": gathering.mate}, {"wa": gathering.across}])
    me = lax.axis_index("ctx")
    near = remote(small_ref, small_in.at[0], small_sem.at[0], small_sem.at[1], wa=gathering.mate)
    near.start()
    gathering.start()
    gathering.cross("q")
    over = remote(small_mid, small_in.at[1], small_sem.at[2], small_sem.at[3], wa=gathering.across)
    near.wait_recv()
    small_mid[...] = (small_ref[...].astype(F32) + small_in[0].astype(F32)).astype(BF)
    over.start()
    over.wait_recv()
    small_out[...] = small_mid[...].astype(F32) + small_in[1].astype(F32)
    bias_ref = small_out
    values = tokens_ref[...].astype(F32)
    width = values.shape[1]
    norm = lax.rsqrt(jnp.mean(values * values, axis=1, keepdims=True) + epsilon)
    low_ref[...] = (values * norm * small_out[H : H + 1, :width]).astype(BF)
    bias_tiles(bias_ref, me, tiles)
    pairs = tuple((proj.at[t], dst) for t, dst in enumerate((qh, kh, vh)))
    saving = []
    for t, name in enumerate(("q", "k", "v")):
        gathering.forward(name)
        gathering.cross(*(("k",), ("v",), ("so", "ck"))[t])
        gathering.arrive(name)
        proj[t] = nn_dot(low_ref[...], held[name][...]).astype(BF)
        spread(n, me, pairs, send, recv, t)
        copy = pltpu.make_async_copy(held[name], wholes[name], out_sem.at[t])
        copy.start()
        saving.append(copy)

    def arrive(i):
        @pl.when(i != me)
        def _():
            d = lax.rem(me - i + n, n)
            for t, (src, dst) in enumerate(pairs):
                to_ctx(
                    src.at[:, lanes_of(i)], dst.at[rows_of(i, BLOCK)], send.at[t, d], recv.at[t, d], i
                ).wait_recv()

    def query_block(i, unused):
        @pl.when(i == 5)
        def _():
            gathering.forward("so", "ck")
            gathering.cross("cv", "cq")

        @pl.when(i == 7)
        def _():
            gathering.forward("cv", "cq")
            gathering.cross("co")

        arrive(i)
        rows = rows_of(i, BLOCK)
        vt[:, rows] = vh[rows, :].astype(F32).T.astype(BF)
        q_now = qh[rows, :] * BF(HD**-0.5)
        masked = [jnp.where(head_mask(h, BLOCK), q_now, BF(0)) for h in range(2)]

        def fold(j, which, first):
            keys = kh[rows_of(j, BLOCK), :]
            for h in range(2):
                scores = nt_dot(keys, masked[h])
                if which is None:
                    scores = scores + bias_ref[pl.ds(2 * me + h, 1), WIDE : WIDE + BLOCK]
                else:
                    scores = scores + tiles[h, which]
                top = jnp.max(scores, axis=0, keepdims=True)
                if not first:
                    old = stat[h : h + 1, :]
                    top = jnp.maximum(old, top)
                weights = jnp.exp(scores - top)
                total = jnp.sum(weights, axis=0, keepdims=True)
                vals = vt[h * HD : (h + 1) * HD, rows_of(j, BLOCK)]
                mixed = nn_dot(vals, weights.astype(BF))
                if not first:
                    factor = jnp.exp(old - top)
                    total = total + stat[2 + h : 3 + h, :] * factor
                    mixed = mixed + acc[h * HD : (h + 1) * HD, :] * factor
                stat[h : h + 1, :] = top
                stat[2 + h : 3 + h, :] = total
                acc[h * HD : (h + 1) * HD, :] = mixed

        fold(i, 0, True)

        @pl.when(i >= 1)
        def _():
            fold(i - 1, 1, False)

        def far(j, unused):
            fold(j, None, False)
            return unused

        lax.fori_loop(0, i - 1, far, 0)
        for h in range(2):
            total = stat[2 + h : 3 + h, :]
            part = acc[h * HD : (h + 1) * HD, :] / total
            acc[h * HD : (h + 1) * HD, :] = part
            lse_out[h : h + 1, rows] = stat[h : h + 1, :] + jnp.log(total)
        done = acc[...]
        ot_out[:, rows] = done
        oh[rows, :] = done.T.astype(BF)

        @pl.when(i != me)
        def _():
            d = lax.rem(i - me + n, n)
            to_ctx(oh.at[rows], land.at[:, lanes_of(me)], osend.at[d], orecv.at[d], i).start()

        @pl.when(i == me)
        def _():
            land[:, lanes_of(me)] = oh[rows, :]

        return unused

    lax.fori_loop(0, n, query_block, 0)
    qh_out[...] = qh[...]
    kh_out[...] = kh[...]
    vh_out[...] = vh[...]
    gathering.forward("co")
    for d in range(1, n):
        peer = lax.rem(me + d, n)
        for t, (src, dst) in enumerate(pairs):
            to_ctx(
                src.at[:, lanes_of(peer)], dst.at[rows_of(me, BLOCK)], send.at[t, d], recv.at[t, d], peer
            ).wait_send()
        back = to_ctx(
            oh.at[rows_of(peer, BLOCK)], land.at[:, lanes_of(me)], osend.at[d], orecv.at[d], peer
        )
        back.wait_send()
        back.wait_recv()
    o_ref[...] = land[...]
    for name in GATHERED[3:]:
        gathering.arrive(name)
    gathering.finish()
    near.wait_send()
    over.wait_send()
    for copy in saving:
        copy.wait()


def vmem(count):
    return [pl.BlockSpec(memory_space=pltpu.VMEM)] * count


def attn_forward(n, tokens, small, shards):
    rows, seq = tokens.shape[0], n * tokens.shape[0]
    owners = lax.axis_size("wa")
    heads = jax.ShapeDtypeStruct((seq, WIDE), BF)
    wholes = [jax.ShapeDtypeStruct((owners * s.shape[0], s.shape[1]), BF) for s in shards]
    width = wholes[0].shape[1]
    dma = pltpu.SemaphoreType.DMA
    return pl.pallas_call(
        functools.partial(attn_forward_kernel, n),
        out_shape=(
            *wholes,
            jax.ShapeDtypeStruct((rows, width), BF),
            jax.ShapeDtypeStruct(tokens.shape, BF),
            heads,
            heads,
            heads,
            jax.ShapeDtypeStruct((WIDE, seq), F32),
            jax.ShapeDtypeStruct((8, seq), F32),
            jax.ShapeDtypeStruct(small.shape, F32),
        ),
        in_specs=vmem(2) + [pl.BlockSpec(memory_space=pl.ANY)] * 8,
        out_specs=tuple([pl.BlockSpec(memory_space=pl.ANY)] * 8 + vmem(8)),
        scratch_shapes=[
            *(pltpu.VMEM(w.shape, BF) for w in wholes[:3]),
            pltpu.VMEM((3, rows, width), BF),
            pltpu.VMEM((2, *small.shape), BF),
            pltpu.VMEM(small.shape, BF),
            pltpu.VMEM((seq, WIDE), BF),
            pltpu.VMEM((seq, WIDE), BF),
            pltpu.VMEM((seq, WIDE), BF),
            pltpu.VMEM((WIDE, seq), BF),
            pltpu.VMEM((seq, WIDE), BF),
            pltpu.VMEM((rows, width), BF),
            pltpu.VMEM((2, 3, BLOCK, BLOCK), F32),
            pltpu.VMEM((WIDE, BLOCK), F32),
            pltpu.VMEM((8, BLOCK), F32),
            dma((3, n)),
            dma((3, n)),
            dma((n,)),
            dma((n,)),
            dma((4,)),
            dma((8,)),
            dma((3,)),
            dma((8, 3)),
            dma((8, 3)),
        ],
        compiler_params=pltpu.CompilerParams(
            collective_id=1, has_side_effects=True, vmem_limit_bytes=44 << 20
        ),
        cost_estimate=lasting(85),
        name="attn_forward",
    )(tokens, small, *shards)


def attn_backward_kernel(
    n, do_ref, qh, kh, vh, ot_ref, lse_ref, bias_ref, *rest
):
    parts = dict(zip(EARLY, rest[:5], strict=True))
    feed_part = rest[5]
    dq_ref, dk_ref, dv_ref, line_ref, tall_pair, tall_one, flat_out = rest[6:13]
    feed_full = rest[13:15]
    (
        doh, kt, stage, land, dk_acc, dv_acc, dqt, q_masked, do_masked, rowstat, tiles, dtiles,
        send, recv, gsend, grecv, ring_send, ring_recv,
    ) = rest[15:33]
    extra = rest[33:]
    fold_wa = Folding(EARLY, parts, (extra[0:4], extra[4:8], extra[8:13]))
    ring = Ring(FEED_LANES, ring_send, ring_recv, full=feed_full)
    for lane in range(2):
        feed_full[lane][ring.chunk(lane, 1)] = feed_part[lane]
    meet([*ctx_peers(n), {"wa": fold_wa.mate}, {"wa": fold_wa.across}])
    me = lax.axis_index("ctx")
    pairs = ((do_ref, doh),)
    spread(n, me, pairs, send, recv, 0)
    fold_wa.start()
    bias_tiles(bias_ref, me, tiles)
    for j in range(n):
        part = slice(j * BLOCK, (j + 1) * BLOCK)
        kt[:, part] = (kh[part, :].astype(F32) * HD**-0.5).T.astype(BF)
    dk_acc[...] = jnp.zeros_like(dk_acc)
    dv_acc[...] = jnp.zeros_like(dv_acc)
    dtiles[...] = jnp.zeros_like(dtiles)
    for name in EARLY[:2]:
        fold_wa.send(name)

    def pair(t, now):
        i, j = now
        rows, there = rows_of(i, BLOCK), rows_of(j, BLOCK)

        @pl.when(t == n)
        def _():
            for name in EARLY[2:]:
                fold_wa.send(name)

        for turn, lanes in enumerate(FEED_TURNS):

            @pl.when((lax.rem(t, 4) == 2 * turn) & (t <= 4 * HOPS + 2))
            def _():
                ring.gather(t // 4, lanes)

        @pl.when(j == i)
        def _():
            @pl.when(i != me)
            def _():
                d = lax.rem(me - i + n, n)
                to_ctx(
                    do_ref.at[:, lanes_of(i)], doh.at[rows], send.at[0, d], recv.at[0, d], i
                ).wait_recv()

            q_now = qh[rows, :] * BF(HD**-0.5)
            do_now = doh[rows, :]
            products = do_now.astype(F32).T * ot_ref[:, rows]
            for h in range(2):
                mask = head_mask(h, BLOCK)
                q_masked[h] = jnp.where(mask, q_now, BF(0))
                do_masked[h] = jnp.where(mask, do_now, BF(0))
                rowstat[h : h + 1, :] = lse_ref[h : h + 1, rows]
                rowstat[2 + h : 3 + h, :] = jnp.sum(
                    products[h * HD : (h + 1) * HD], axis=0, keepdims=True
                )
            dqt[...] = jnp.zeros_like(dqt)

        which = jnp.minimum(i - j, 2)
        keys, vals = kh[there, :], vh[there, :]
        dk_part, dv_part = None, None
        for h in range(2):
            scores = nt_dot(keys, q_masked[h])
            weights = jnp.exp(scores + tiles[h, which] - rowstat[h : h + 1, :])
            dweights = nt_dot(vals, do_masked[h])
            dscores = weights * (dweights - rowstat[2 + h : 3 + h, :])
            dtiles[h, which] += dscores
            low = dscores.astype(BF)
            dv_now = nn_dot(weights.astype(BF), do_masked[h])
            dk_now = nn_dot(low, q_masked[h])
            dv_part = dv_now if dv_part is None else dv_part + dv_now
            dk_part = dk_now if dk_part is None else dk_part + dk_now
            half = slice(h * HD, (h + 1) * HD)
            dqt[half, :] += nn_dot(kt[half, there], low)
        dk_acc[there, :] += dk_part
        dv_acc[there, :] += dv_part
        last = j == 0

        @pl.when(last)
        def _():
            stage[0, rows, :] = dqt[...].T.astype(BF)
            stage[1, rows, :] = dk_acc[rows, :].astype(BF)
            stage[2, rows, :] = dv_acc[rows, :].astype(BF)

            @pl.when(i != me)
            def _():
                d = lax.rem(i - me + n, n)
                for t in range(3):
                    to_ctx(
                        stage.at[t, rows],
                        land.at[t, :, lanes_of(me)],
                        gsend.at[t, d],
                        grecv.at[t, d],
                        i,
                    ).start()

            @pl.when(i == me)
            def _():
                for t in range(3):
                    land[t, :, lanes_of(me)] = stage[t, rows, :]

        return jnp.where(last, i - 1, i), jnp.where(last, i - 1, j - 1)

    lax.fori_loop(0, n * (n + 1) // 2, pair, (jnp.int32(n - 1), jnp.int32(n - 1)))
    ring.finish(lambda lane: feed_full[FEED_LANES[lane][0]].at[0, FEED_LANES[lane][2]])
    tall_pair[:224, :] = fold_wa.total("cq")
    tall_pair[224:, :] = fold_wa.total("ck")
    tall_one[...] = fold_wa.total("cv")
    for at, name in ((0, "co"), (32, "so")):
        flat_out[:, at : at + 32, :] = fold_wa.total(name).reshape(8, 32, 896)
    fold_wa.finish()
    for h in range(2):
        line = jnp.concatenate(
            [dtiles[h, 0], dtiles[h, 1], jnp.zeros((BLOCK, LINE - 2 * BLOCK), F32)], axis=1
        )
        row = lax.broadcasted_iota(jnp.int32, (BLOCK, LINE), 0)
        for bit in range(8):
            moved = pltpu.roll(line, LINE - (1 << bit), 1)
            line = jnp.where((row >> bit) & 1 == 1, moved, line)
        line_ref[h : h + 1, :] = jnp.sum(line, axis=0, keepdims=True)
        line_ref[2 + h : 3 + h, :BLOCK] = jnp.sum(dtiles[h, 2], axis=0, keepdims=True)
    line_ref[2:4, BLOCK:] = jnp.zeros((2, LINE - BLOCK), F32)
    line_ref[4:8, :] = jnp.zeros((4, LINE), F32)
    for d in range(1, n):
        peer = lax.rem(me + d, n)
        to_ctx(
            do_ref.at[:, lanes_of(peer)], doh.at[rows_of(me, BLOCK)], send.at[0, d], recv.at[0, d], peer
        ).wait_send()
        for t in range(3):
            back = to_ctx(
                stage.at[t, rows_of(peer, BLOCK)], land.at[t, :, lanes_of(me)], gsend.at[t, d], grecv.at[t, d], peer
            )
            back.wait_send()
            back.wait_recv()
    dq_ref[...] = land[0]
    dk_ref[...] = land[1]
    dv_ref[...] = land[2]


def attn_backward(n, dout, qh, kh, vh, ot, lse, bias_lines, parts, feed_part):
    rows, seq = dout.shape[0], n * dout.shape[0]
    grads = jax.ShapeDtypeStruct(dout.shape, BF)
    feed = jax.ShapeDtypeStruct(FEED, BF)
    return pl.pallas_call(
        functools.partial(attn_backward_kernel, n),
        out_shape=(
            grads,
            grads,
            grads,
            jax.ShapeDtypeStruct((8, LINE), F32),
            jax.ShapeDtypeStruct((448, 1024), BF),
            jax.ShapeDtypeStruct((224, 1024), BF),
            jax.ShapeDtypeStruct((8, 64, 896), BF),
            feed,
            feed,
        ),
        in_specs=vmem(7) + [pl.BlockSpec(memory_space=pl.ANY)] * 5 + vmem(1),
        out_specs=tuple(vmem(9)),
        scratch_shapes=[
            pltpu.VMEM((seq, WIDE), BF),
            pltpu.VMEM((WIDE, seq), BF),
            pltpu.VMEM((3, seq, WIDE), BF),
            pltpu.VMEM((3, *dout.shape), BF),
            pltpu.VMEM((seq, WIDE), F32),
            pltpu.VMEM((seq, WIDE), F32),
            pltpu.VMEM((WIDE, BLOCK), F32),
            pltpu.VMEM((2, BLOCK, WIDE), BF),
            pltpu.VMEM((2, BLOCK, WIDE), BF),
            pltpu.VMEM((8, BLOCK), F32),
            pltpu.VMEM((2, 3, BLOCK, BLOCK), F32),
            pltpu.VMEM((2, 3, BLOCK, BLOCK), F32),
            pltpu.SemaphoreType.DMA((1, n)),
            pltpu.SemaphoreType.DMA((1, n)),
            pltpu.SemaphoreType.DMA((3, n)),
            pltpu.SemaphoreType.DMA((3, n)),
            pltpu.SemaphoreType.DMA((len(FEED_LANES), HOPS)),
            pltpu.SemaphoreType.DMA((len(FEED_LANES), HOPS)),
            *Folding.scratch(EARLY),
        ],
        compiler_params=pltpu.CompilerParams(
            collective_id=2, has_side_effects=True, vmem_limit_bytes=58 << 20
        ),
        cost_estimate=lasting(100),
        name="attn_backward",
    )(dout, qh, kh, vh, ot, lse, bias_lines, *parts, feed_part)


LANES = (
    (1, ("cA",), 0),
    (-1, ("cB", "out"), 0),
    (1, ("sA",), 5),
    (-1, ("sB", "small"), 5),
)
BUFFERS = {
    "cA": (448, 1024),
    "cB": (224, 1024),
    "out": (8, 64, 896),
    "sA": (448, 1024),
    "sB": (224, 1024),
    "small": (8, 8, 128),
}
NAMES = tuple(BUFFERS)


def kind_of(name):
    return F32 if name == "small" else BF


def chunk_shape(name):
    shape = BUFFERS[name]
    return (shape[0], WIDE) if len(shape) == 2 else shape[1:]


def chunk_of(ref, name, c):
    return ref.at[:, lanes_of(c)] if len(BUFFERS[name]) == 2 else ref.at[c]


def reduce_kernel(*refs):
    ca_ref, cb_ref, out_ref, small_ref = refs[:4]
    parts = dict(zip(LATE, refs[4:7], strict=True))
    fin_ref, fin_out = refs[7], refs[14]
    full = dict(zip(NAMES, refs[8:14], strict=True))
    share = dict(zip(NAMES, refs[15:21], strict=True))
    hold = dict(zip(NAMES, refs[21:27], strict=True))
    small_in, small_mid, small_sem = refs[27:30]
    ring_send, ring_recv, fin_send, fin_recv = refs[30:34]
    extra = refs[34:]
    fold_wa = Folding(LATE, parts, (extra[0:4], None, extra[4:9]))
    place, after, before = ring_place(RING)
    wa, both = fold_wa.wa, other_wa(fold_wa.across, 1)
    meet(
        [{"wa": peer} for peer in (fold_wa.mate, fold_wa.across, both)]
        + [{"ctx": after}, {"ctx": before}]
    )
    own_fin = pltpu.make_async_copy(fin_ref.at[wa], fin_out.at[wa], fin_send.at[3])
    own_fin.start()
    fin_copies = [
        remote(fin_ref.at[peer], fin_out.at[wa], fin_send.at[d], fin_recv.at[d], wa=peer)
        for d, peer in enumerate((fold_wa.across, both, fold_wa.mate))
    ]
    fold_wa.start()
    near = remote(small_ref, small_in.at[0], small_sem.at[0], small_sem.at[1], wa=fold_wa.mate)
    near.start()
    over = remote(small_mid, small_in.at[1], small_sem.at[2], small_sem.at[3], wa=fold_wa.across)
    share["cA"][...] = ca_ref[...]
    share["cB"][...] = cb_ref[...]
    share["out"][...] = out_ref[...]
    copies = {}

    def ring_step(lane, step):
        way, buffers, unused = LANES[lane]
        here = place if way == 1 else lax.rem(RING - place, RING)
        target = after if way == 1 else before

        def number(offset):
            return lax.rem(here + offset + 2 * RING, RING)

        for name in buffers:
            b = NAMES.index(name)
            if step > 0:
                copies[name, step - 1].wait_recv()
            if step == 2 * HOPS:
                continue
            if step <= HOPS:
                now = number(-step) if step < HOPS else number(1)
                mine = chunk_of(share[name], name, now)
                if step > 0:
                    total = mine[...].astype(F32) + hold[name][step - 1].astype(F32)
                    if step == HOPS:
                        mine = chunk_of(full[name], name, now)
                    mine[...] = total.astype(kind_of(name))
                src, dst = (mine, hold[name].at[step]) if step < HOPS else (mine, mine)
            else:
                src = dst = chunk_of(full[name], name, number(1 - (step - HOPS)))
            copy = remote(src, dst, ring_send.at[b, step], ring_recv.at[b, step], ctx=target)
            copy.start()
            copies[name, step] = copy

    ring_step(0, 0)
    ring_step(1, 0)
    for name in LATE:
        fold_wa.send(name)
    near.wait_recv()
    small_mid[...] = small_ref[...] + small_in[0]
    over.start()
    last = max(start for _, _, start in LANES) + 2 * HOPS
    for tick in range(1, last + 1):
        if tick == 8:
            for copy in fin_copies:
                copy.start()
        for lane, (_, buffers, start) in enumerate(LANES):
            step = tick - start
            if step == 0 and buffers[0] == "sA":
                share["sA"][:224, :] = fold_wa.total("q")
                share["sA"][224:, :] = fold_wa.total("k")
            if step == 0 and buffers[0] == "sB":
                share["sB"][...] = fold_wa.total("v")
                over.wait_recv()
                share["small"][...] = (small_mid[...] + small_in[1]).reshape(8, 8, 128)
            if 0 <= step <= 2 * HOPS:
                ring_step(lane, step)
    fold_wa.finish()
    near.wait_send()
    over.wait_send()
    for copy in copies.values():
        copy.wait_send()
    own_fin.wait()
    for copy in fin_copies:
        copy.wait()


def reduce_grads(pair, one, flat, small, parts, fin):
    dma = pltpu.SemaphoreType.DMA
    return pl.pallas_call(
        reduce_kernel,
        out_shape=(
            *(jax.ShapeDtypeStruct(BUFFERS[b], kind_of(b)) for b in NAMES),
            jax.ShapeDtypeStruct((4, 224, 896), BF),
        ),
        in_specs=vmem(4) + [pl.BlockSpec(memory_space=pl.ANY)] * 4,
        out_specs=(*vmem(len(NAMES)), pl.BlockSpec(memory_space=pl.ANY)),
        scratch_shapes=[
            *(pltpu.VMEM(BUFFERS[b], kind_of(b)) for b in NAMES),
            *(pltpu.VMEM((HOPS, *chunk_shape(b)), kind_of(b)) for b in NAMES),
            pltpu.VMEM((2, 64, 128), F32),
            pltpu.VMEM((64, 128), F32),
            dma((4,)),
            dma((len(NAMES), 2 * HOPS)),
            dma((len(NAMES), 2 * HOPS)),
            dma((4,)),
            dma((3,)),
            *Folding.scratch(LATE),
        ],
        compiler_params=pltpu.CompilerParams(
            collective_id=3, has_side_effects=True, vmem_limit_bytes=56 << 20
        ),
        cost_estimate=lasting(90),
        name="reduce_grads",
    )(pair, one, flat, small, *parts, fin.reshape(4, 224, 896))


def unfold(full):
    wide = {name: value.astype(F32) for name, value in full.items()}
    return {
        "cq": wide["cA"][:224],
        "ck": wide["cA"][224:],
        "cv": wide["cB"],
        "co": wide["out"][:, :32].reshape(FLAT),
        "so": wide["out"][:, 32:].reshape(FLAT),
        "q": wide["sA"][:224],
        "k": wide["sA"][224:],
        "v": wide["sB"],
    }


GELU = (2.0 / math.pi) ** 0.5


def ffn_kernel(
    f_ref, cot_ref, win_ref, wout_ref, bias_ref, res_ref, df_ref, dwin_ref, dwout_ref, dbias_ref,
    f_all, g_all, dul_all, own, kept, out_mate, out_cross, in_mate, in_cross, x_out, x_in,
    f_send, f_recv, p_send, p_recv,
):
    me = lax.axis_index("wa")
    mate, across = other_wa(me, 1), other_wa(me, 2)
    both = other_wa(across, 1)
    barrier = pltpu.get_barrier_semaphore()
    for peer in (mate, across):
        pl.semaphore_signal(barrier, inc=1, device_id={"wa": peer}, device_id_type=MESH)
    pl.semaphore_wait(barrier, 2)
    to_across = remote(f_ref, f_all.at[me], f_send.at[1], f_recv.at[1], wa=across)
    to_across.start()
    to_mate = remote(f_ref, f_all.at[me], f_send.at[0], f_recv.at[0], wa=mate)
    to_mate.start()
    forward = remote(f_all.at[across], f_all.at[across], f_send.at[2], f_recv.at[2], wa=mate)
    f_all[me] = f_ref[...]
    order = (me, mate, across, both)
    dbias_ref[...] = jnp.zeros_like(dbias_ref)
    for k, s in enumerate(order):
        if k == 1:
            to_mate.wait_recv()
        if k == 2:
            to_across.wait_recv()
            forward.start()
        if k == 3:
            forward.wait_recv()
        u = nn_dot(f_all[s], win_ref[...]) + bias_ref[...]
        square = u * u
        t = jnp.tanh(GELU * (u + 0.044715 * (square * u)))
        g_all[s] = (0.5 * u * (1.0 + t)).astype(BF)
        slope = 0.5 * (1.0 + t) + 0.5 * u * (1.0 - t * t) * (GELU * (1.0 + 3 * 0.044715 * square))
        du = nt_dot(cot_ref[s], wout_ref[...]) * slope
        dbias_ref[...] += jnp.sum(du.reshape(32, 8, du.shape[1]), axis=0)
        dul_all[s] = du.astype(BF)

    def scatter(which, product):
        out_cross[which] = product(both).astype(BF)
        cross = remote(
            out_cross.at[which], in_cross.at[which], p_send.at[which, 0], p_recv.at[which, 0], wa=mate
        )
        cross.start()
        kept[...] = product(across)
        cross.wait_recv()
        x_out[which] = (kept[...] + in_cross[which].astype(F32)).astype(BF)
        over = remote(
            x_out.at[which], x_in.at[which], p_send.at[which, 1], p_recv.at[which, 1], wa=across
        )
        over.start()
        out_mate[which] = product(mate).astype(BF)
        near = remote(
            out_mate.at[which], in_mate.at[which], p_send.at[which, 2], p_recv.at[which, 2], wa=mate
        )
        near.start()
        own[which] = product(me)
        return cross, over, near

    def finish(which, copies, out_ref):
        cross, over, near = copies
        near.wait_recv()
        over.wait_recv()
        out_ref[...] = own[which] + in_mate[which].astype(F32) + x_in[which].astype(F32)
        for copy in copies:
            copy.wait_send()

    df_copies = scatter(0, lambda s: nt_dot(dul_all[s], win_ref[...]))
    res_copies = scatter(1, lambda s: nn_dot(g_all[s], wout_ref[...]))
    width = f_ref.shape[1]

    def outer(left_all, right, out_ref):
        for c in range(width // WIDE):
            lanes = slice(c * WIDE, (c + 1) * WIDE)
            total = None
            for s in range(4):
                left = left_all[s, :, lanes].astype(F32).T.astype(BF)
                now = nn_dot(left, right[s])
                total = now if total is None else total + now
            out_ref[lanes, :] = total.astype(BF)

    outer(f_all, dul_all, dwin_ref)
    outer(g_all, cot_ref, dwout_ref)
    finish(0, df_copies, df_ref)
    finish(1, res_copies, res_ref)
    for copy in (to_mate, to_across, forward):
        copy.wait_send()


def ffn(f_low, cot_all, win, wout, bias):
    rows, width = f_low.shape
    hidden = win.shape[1]
    dma = pltpu.SemaphoreType.DMA
    block = (rows, width)
    return pl.pallas_call(
        ffn_kernel,
        out_shape=(
            jax.ShapeDtypeStruct(block, F32),
            jax.ShapeDtypeStruct(block, F32),
            jax.ShapeDtypeStruct(win.shape, BF),
            jax.ShapeDtypeStruct(wout.shape, BF),
            jax.ShapeDtypeStruct((8, hidden), F32),
        ),
        in_specs=vmem(5),
        out_specs=tuple(vmem(5)),
        scratch_shapes=[
            pltpu.VMEM((4, *block), BF),
            pltpu.VMEM((4, rows, hidden), BF),
            pltpu.VMEM((4, rows, hidden), BF),
            pltpu.VMEM((2, *block), F32),
            pltpu.VMEM(block, F32),
            *[pltpu.VMEM((2, *block), BF)] * 6,
            dma((3,)),
            dma((3,)),
            dma((2, 3)),
            dma((2, 3)),
        ],
        compiler_params=pltpu.CompilerParams(
            collective_id=4, has_side_effects=True, vmem_limit_bytes=56 << 20
        ),
        cost_estimate=lasting(44),
        name="feed_forward",
    )(f_low, cot_all, win, wout, bias)


def padded_rows(pad, values):
    rows = values.shape[0]
    pad[...] = jnp.zeros_like(pad)
    pad[1 : rows + 1, :] = values.astype(F32)


def both_heads(pad, g):
    here = pad[g * SPAN : (g + 1) * SPAN, :]
    left = head_mask(0, SPAN)
    return jnp.concatenate([jnp.where(left, here, 0.0), jnp.where(left, 0.0, here)], 0).astype(BF)


def join_heads(stacked):
    return jnp.where(head_mask(0, SPAN), stacked[:SPAN], stacked[SPAN:])


def cross_forward_kernel(groups, keep_ref, q_ref, k_ref, v_ref, x_ref, q_pad, x_pad):
    padded_rows(q_pad, q_ref[...])
    for g in range(groups):
        rows = slice(g * 256, (g + 1) * 256)
        query = both_heads(q_pad, g) * BF(HD**-0.5)
        scores = nt_dot(query, k_ref[rows, :])
        weights = jnp.exp(scores - jnp.max(scores, axis=1, keepdims=True))
        weights = weights / jnp.sum(weights, axis=1, keepdims=True)
        mixed = join_heads(nn_dot(weights.astype(BF), v_ref[rows, :]))
        if g == 0:
            mixed = mixed * keep_ref[0:1, :]
        x_pad[g * SPAN : (g + 1) * SPAN, :] = mixed
    x_ref[...] = x_pad[1 : x_ref.shape[0] + 1, :].astype(BF)


def pair_specs(*rows):
    return [pl.BlockSpec((r, WIDE), lambda p: (0, p)) for r in rows]


def cross_forward(keep, query, keys, values):
    rows, width = query.shape
    many = keys.shape[0]
    groups = many // 256
    return pl.pallas_call(
        functools.partial(cross_forward_kernel, groups),
        grid=(width // WIDE,),
        out_shape=jax.ShapeDtypeStruct(query.shape, BF),
        in_specs=[pl.BlockSpec((8, WIDE), lambda p: (0, 0)), *pair_specs(rows, many, many)],
        out_specs=pair_specs(rows)[0],
        scratch_shapes=[pltpu.VMEM((groups * SPAN, WIDE), F32)] * 2,
        compiler_params=pltpu.CompilerParams(vmem_limit_bytes=16 << 20),
        cost_estimate=lasting(9),
        name="cross_forward",
    )(keep, query, keys, values)


def cross_backward_kernel(
    groups, keep_ref, q_ref, dx_ref, k_ref, v_ref, dq_ref, dk_ref, dv_ref, q_pad, dx_pad, dq_pad
):
    padded_rows(q_pad, q_ref[...])
    padded_rows(dx_pad, dx_ref[...])
    dx_pad[:SPAN, :] = dx_pad[:SPAN, :] * keep_ref[0:1, :]
    for g in range(groups):
        rows = slice(g * 256, (g + 1) * 256)
        query = both_heads(q_pad, g) * BF(HD**-0.5)
        dmixed = both_heads(dx_pad, g)
        keys, values = k_ref[rows, :], v_ref[rows, :]
        scores = nt_dot(keys, query)
        weights = jnp.exp(scores - jnp.max(scores, axis=0, keepdims=True))
        weights = weights / jnp.sum(weights, axis=0, keepdims=True)
        dweights = nt_dot(values, dmixed)
        dscores = weights * (dweights - jnp.sum(weights * dweights, axis=0, keepdims=True))
        dk_ref[rows, :] = nn_dot(dscores.astype(BF), query).astype(BF)
        dv_ref[rows, :] = nn_dot(weights.astype(BF), dmixed).astype(BF)
        back = (dscores * HD**-0.5).T.astype(BF)
        dq_pad[g * SPAN : (g + 1) * SPAN, :] = join_heads(nn_dot(back, keys))
    dq_ref[...] = dq_pad[1 : dq_ref.shape[0] + 1, :].astype(BF)


def cross_backward(keep, query, dmixed, keys, values):
    rows, width = query.shape
    many = keys.shape[0]
    groups = many // 256
    return pl.pallas_call(
        functools.partial(cross_backward_kernel, groups),
        grid=(width // WIDE,),
        out_shape=(
            jax.ShapeDtypeStruct(query.shape, BF),
            jax.ShapeDtypeStruct(keys.shape, BF),
            jax.ShapeDtypeStruct(keys.shape, BF),
        ),
        in_specs=[
            pl.BlockSpec((8, WIDE), lambda p: (0, 0)),
            *pair_specs(rows, rows, many, many),
        ],
        out_specs=tuple(pair_specs(rows, many, many)),
        scratch_shapes=[pltpu.VMEM((groups * SPAN, WIDE), F32)] * 3,
        compiler_params=pltpu.CompilerParams(vmem_limit_bytes=16 << 20),
        cost_estimate=lasting(17),
        name="cross_backward",
    )(keep, query, dmixed, keys, values)


def line_selector():
    place = jnp.arange(LINE)
    offset = jnp.where(place < LINE // 2, -place, LINE - place)
    return (bucket_of(offset)[None, :] == jnp.arange(NB)[:, None]).astype(jnp.float32)


def ring_forward(query_low, key_low, value_low, bucket_table):
    row_count, attn_width = query_low.shape
    position = lax.axis_index("ctx")
    scale_factor = HD ** (-0.5)
    bias_set, onehots = make_bias(bucket_table.astype(jnp.float32), row_count)
    query_heads = query_low.reshape(row_count, H, HD)
    start_state = (
        jnp.full((H, row_count), negative, jnp.float32),
        jnp.zeros((H, row_count), jnp.float32),
        jnp.zeros((row_count, attn_width), jnp.float32),
    )
    running_max, running_sum, running_acc = forward_fold(
        query_heads,
        position,
        row_count,
        bias_set,
        scale_factor,
        start_state,
        (
            lax.all_gather(key_low, "ctx", axis=0, tiled=True),
            lax.all_gather(value_low, "ctx", axis=0, tiled=True),
        ),
    )
    attended = (running_acc.reshape(row_count, H, HD) / running_sum.T[:, :, None]).reshape(
        row_count, attn_width
    )
    log_total = running_max + jnp.log(running_sum)
    state = (query_heads, key_low, value_low, attended, log_total, bias_set, onehots)
    return attended.astype(jnp.bfloat16), state


def ring_backward(state, dout_low):
    query_heads, key_low, value_low, attended, log_total, bias_set, onehots = state
    row_count, attn_width = dout_low.shape
    cycle_size = lax.axis_size("ctx")
    position = lax.axis_index("ctx")
    scale_factor = HD ** (-0.5)
    dout_heads = dout_low.reshape(row_count, H, HD)
    row_delta = jnp.sum(
        (dout_low.astype(jnp.float32) * attended).reshape(row_count, H, HD), axis=-1
    ).T
    zero_rows = jnp.zeros((row_count, attn_width), jnp.float32)
    zero_tables = (
        jnp.zeros((H, row_count, row_count), jnp.float32),
        jnp.zeros((H, row_count, row_count), jnp.float32),
        jnp.zeros((H,), jnp.float32),
    )

    def visit(folded, key_now, value_now, relation):

        def visit_compute(current):
            dquery_acc, dkey_acc, dvalue_acc, relative_bias_tables = current
            key_heads = key_now.reshape(row_count, H, HD)
            weights_now, dscores, ds_low = pair_core(
                query_heads,
                dout_heads,
                log_total,
                row_delta,
                key_heads,
                value_now.reshape(row_count, H, HD),
                relation,
                bias_set,
                scale_factor,
            )
            dquery = jnp.einsum(
                "hqk,khd->qhd", ds_low, key_heads, preferred_element_type=jnp.float32
            ).reshape(row_count, attn_width)
            dkey = jnp.einsum(
                "hqk,qhd->khd", ds_low, query_heads, preferred_element_type=jnp.float32
            ).reshape(row_count, attn_width)
            dvalue = jnp.einsum(
                "hqk,qhd->khd",
                weights_now.astype(jnp.bfloat16),
                dout_heads,
                preferred_element_type=jnp.float32,
            ).reshape(row_count, attn_width)
            return (
                dquery_acc + dquery,
                dkey_acc + dkey,
                dvalue_acc + dvalue,
                add_tables(relative_bias_tables, dscores, relation),
            )

        return lax.cond(relation >= 0, visit_compute, lambda unchanged: unchanged, folded)

    first_state = visit(
        (zero_rows, zero_rows, zero_rows, zero_tables), key_low, value_low, jnp.array(0, jnp.int32)
    )

    def cycle_step(carried, cycle_index):
        key_now, value_now, (dquery_acc, dkey_acc, dvalue_acc, relative_bias_tables) = carried
        key_next, value_next = passed_along((key_now, value_now), "ctx", 1)
        dkey_next, dvalue_next = (
            from_behind(dkey_acc.astype(jnp.bfloat16), "ctx", 1).astype(dkey_acc.dtype),
            from_behind(dvalue_acc.astype(jnp.bfloat16), "ctx", 1).astype(dvalue_acc.dtype),
        )
        relation = jnp.where(position >= cycle_index, cycle_index, -1)
        updated = visit(
            (dquery_acc, dkey_next, dvalue_next, relative_bias_tables),
            key_next,
            value_next,
            relation,
        )
        return ((key_next, value_next, updated), None)

    (
        unused_key,
        unused_value,
        (dquery_total, dkey_part, dvalue_part, relative_bias_tables),
    ), unused = lax.scan(cycle_step, (key_low, value_low, first_state), jnp.arange(1, cycle_size))
    dkey_total, dvalue_total = (
        from_behind(dkey_part.astype(jnp.bfloat16), "ctx", 1).astype(dkey_part.dtype),
        from_behind(dvalue_part.astype(jnp.bfloat16), "ctx", 1).astype(dvalue_part.dtype),
    )
    dquery_low = dquery_total.astype(jnp.bfloat16)
    dkey_low = dkey_total.astype(jnp.bfloat16)
    dvalue_low = dvalue_total.astype(jnp.bfloat16)
    current_bucket_selector, previous_bucket_selector, onehot_far = onehots
    grad_biastable = (
        jnp.einsum(
            "afw,mfw->am",
            current_bucket_selector,
            relative_bias_tables[0],
            precision=strongest_precision,
        )
        + jnp.einsum(
            "afw,mfw->am",
            previous_bucket_selector,
            relative_bias_tables[1],
            precision=strongest_precision,
        )
        + onehot_far[:, None] * relative_bias_tables[2][None, :]
    )
    return dquery_low, dkey_low, dvalue_low, grad_biastable


def heads_forward(tokens, given):
    wa, owners = lax.axis_index("wa"), lax.axis_size("wa")
    table = given["biastable"].astype(F32)
    selector = lax.dynamic_slice_in_dim(line_selector(), wa * table.shape[0], table.shape[0], 0)
    lines = jnp.dot(table.T, selector, precision=strongest_precision).astype(BF)

    def placed(gain):
        row = jnp.zeros((LINE,), BF)
        return lax.dynamic_update_slice(row, gain, (wa * gain.shape[0],))

    gains = jnp.stack([placed(given[name]) for name in GAINS])
    small = jnp.concatenate([lines, gains, jnp.zeros((H - len(GAINS), LINE), BF)], 0)
    shards = [given[LONG_NAMES[name]] for name in GATHERED]
    *wholes, attended_low, low, qh, kh, vh, ot, lse, small = attn_forward(
        lax.axis_size("ctx"), tokens, small, shards
    )
    width = tokens.shape[1]
    gain_of = {name: small[H + g, :width] for g, name in enumerate(GAINS)}
    full = {LONG_NAMES[name]: whole for name, whole in zip(GATHERED, wholes, strict=True)}
    return attended_low, low, full, gain_of, (qh, kh, vh, ot, lse, small[:H])


def heads_backward(state, dout_low, parts, feed_part):
    peers = lax.axis_size("ctx")
    dquery_low, dkey_low, dvalue_low, sums, *shares = attn_backward(
        peers, dout_low, *state, parts, feed_part
    )
    selector = line_selector()
    table = jnp.dot(selector, sums[:2].T, precision=strongest_precision)
    far = jnp.sum(sums[2:4], axis=1)
    table = table + selector[:, WIDE : WIDE + 1] * far[None, :]
    whole = jnp.zeros((NB, H), jnp.float32)
    whole = lax.dynamic_update_slice(whole, table, (0, 2 * lax.axis_index("ctx")))
    return dquery_low, dkey_low, dvalue_low, whole, shares


def cross_pair(groups, keep_ref, q_ref, dx_ref, k_ref, v_ref, dq_ref, dk_ref, dv_ref, q_pad, dx_pad, dq_pad, p):
    lanes = lanes_of(p)
    padded_rows(q_pad, q_ref[:, lanes])
    padded_rows(dx_pad, dx_ref[:, lanes])
    dx_pad[:SPAN, :] = dx_pad[:SPAN, :] * keep_ref[0:1, :]
    for g in range(groups):
        rows = slice(g * 256, (g + 1) * 256)
        query = both_heads(q_pad, g) * BF(HD**-0.5)
        dmixed = both_heads(dx_pad, g)
        keys, values = k_ref[rows, lanes], v_ref[rows, lanes]
        scores = nt_dot(keys, query)
        weights = jnp.exp(scores - jnp.max(scores, axis=0, keepdims=True))
        weights = weights / jnp.sum(weights, axis=0, keepdims=True)
        dweights = nt_dot(values, dmixed)
        dscores = weights * (dweights - jnp.sum(weights * dweights, axis=0, keepdims=True))
        dk_ref[rows, lanes] = nn_dot(dscores.astype(BF), query).astype(BF)
        dv_ref[rows, lanes] = nn_dot(weights.astype(BF), dmixed).astype(BF)
        back = (dscores * HD**-0.5).T.astype(BF)
        dq_pad[g * SPAN : (g + 1) * SPAN, :] = join_heads(nn_dot(back, keys))
    dq_ref[:, lanes] = dq_pad[1 : dq_ref.shape[0] + 1, :].astype(BF)


def middle_kernel(
    keep_ref, q_ref, dx_ref, k_ref, v_ref, near_ref, wk_ref, wv_ref, fin_ref, fout_ref,
    dq_ref, dwk_ref, dwv_ref, near_out, last_out, feed_out,
    dk, dv, q_pad, dx_pad, dq_pad, share, hold, load_sem, ring_send, ring_recv,
):
    ring = Ring(FEED_LANES, ring_send, ring_recv, share=share, hold=hold)
    loads = [
        pltpu.make_async_copy(part, share.at[b], load_sem.at[b])
        for b, part in enumerate((fin_ref, fout_ref))
    ]
    for load in loads:
        load.start()
    meet([{"ctx": ring.after}, {"ctx": ring.before}])
    for load in loads:
        load.wait()
    for lanes in FEED_TURNS:
        ring.scatter(jnp.int32(0), lanes)
    groups = k_ref.shape[0] // 256

    def two_pairs(m, unused):
        for turn, lanes in enumerate(FEED_TURNS):
            cross_pair(
                groups, keep_ref, q_ref, dx_ref, k_ref, v_ref, dq_ref, dk, dv, q_pad, dx_pad, dq_pad,
                2 * m + turn,
            )
            ring.scatter(m + 1, lanes)
        return unused

    pairs = q_ref.shape[1] // (2 * WIDE)
    lax.fori_loop(0, pairs, two_pairs, 0)
    calls = [(step, lanes) for step in range(pairs + 1, HOPS + 1) for lanes in FEED_TURNS]

    def turn():
        if calls:
            step, lanes = calls.pop(0)
            ring.scatter(jnp.int32(step), lanes)

    for g in range(groups):
        rows = slice(g * 256, (g + 1) * 256)
        total = nt_dot(dk[rows, :], wk_ref[...]) + nt_dot(dv[rows, :], wv_ref[...])
        near_out[rows, :] = total.astype(BF)
        if g == groups - 1:
            last_out[...] = total
        if g % 2 == 1:
            turn()
    for c in range(near_ref.shape[1] // WIDE):
        lanes = slice(c * WIDE, (c + 1) * WIDE)
        left = near_ref[:, lanes].astype(F32).T.astype(BF)
        dwk_ref[lanes, :] = nn_dot(left, dk[...]).astype(BF)
        dwv_ref[lanes, :] = nn_dot(left, dv[...]).astype(BF)
        if c % 2 == 1:
            turn()
    while calls:
        turn()
    for lane in range(2):
        feed_out[lane] = share[lane, ring.chunk(lane, 1)]
    ring.finish(lambda lane: share.at[FEED_LANES[lane][0], 0, FEED_LANES[lane][2]])


def middle(keep, query, dmixed, keys, values, near, wk, wv, fin, fout):
    many, width = keys.shape
    wide = near.shape[1]
    low = functools.partial(jax.ShapeDtypeStruct, dtype=BF)
    dma = pltpu.SemaphoreType.DMA
    pad = pltpu.VMEM((many // 256 * SPAN, WIDE), F32)
    return pl.pallas_call(
        middle_kernel,
        out_shape=(
            low(query.shape),
            low(wk.shape),
            low(wv.shape),
            low(near.shape),
            jax.ShapeDtypeStruct((256, wide), F32),
            low((2, *FEED[1:])),
        ),
        in_specs=vmem(8) + [pl.BlockSpec(memory_space=pl.ANY)] * 2,
        out_specs=tuple(vmem(6)),
        scratch_shapes=[
            pltpu.VMEM((many, width), BF),
            pltpu.VMEM((many, width), BF),
            pad,
            pad,
            pad,
            pltpu.VMEM((2, *FEED), BF),
            pltpu.VMEM((2, HOPS, *FEED[1:]), BF),
            dma((2,)),
            dma((len(FEED_LANES), HOPS)),
            dma((len(FEED_LANES), HOPS)),
        ],
        compiler_params=pltpu.CompilerParams(
            collective_id=5, has_side_effects=True, vmem_limit_bytes=56 << 20
        ),
        cost_estimate=lasting(38),
        name="middle",
    )(keep, query, dmixed, keys, values, near, wk, wv, fin.reshape(FEED), fout.reshape(FEED))


NAMES_OF_WEIGHTS = (
    "selfnorm", "selfquery", "selfkey", "selfvalue", "selfout", "biastable", "crossnorm", "crossquery",
    "crosskey", "crossvalue", "crossout", "feednorm", "feedin", "feedbias", "feedout", "outbias",
)
LONG_NAMES = {
    "q": "selfquery",
    "k": "selfkey",
    "v": "selfvalue",
    "so": "selfout",
    "ck": "crosskey",
    "cv": "crossvalue",
    "cq": "crossquery",
    "co": "crossout",
}


def whole_over_wa(shard):
    return lax.all_gather(shard, "wa", axis=0, tiled=True)


def reduce_plain(parts, smalls):
    shares = [
        lax.psum_scatter(part, "wa", scatter_dimension=0, tiled=True).astype(F32)
        for part in parts.values()
    ]
    totals = lax.psum(shares, "ctx")
    return dict(zip(parts, totals, strict=True)), lax.psum(smalls, ("ctx", "wa"))


def per_device(tokens, neighbours, cotangent, *shards):
    given = dict(zip(NAMES_OF_WEIGHTS, shards, strict=True))
    peers = lax.axis_size("ctx")
    position = lax.axis_index("ctx")
    row_count, model_width = tokens.shape[1:]
    split_heads = peers * 2 == H and row_count == BLOCK
    inputs = tokens[0].astype(F32)
    upstream_low = cotangent[0]
    upstream = upstream_low.astype(F32)
    if split_heads:
        attended_low, normed_low, full, small_of, attention_state = heads_forward(tokens[0], given)
        normed_self, back_self = jax.vjp(root_norm, inputs, small_of["selfnorm"])
    else:
        small_of = {name: whole_over_wa(given[name]).astype(F32) for name in GAINS}
        full = {name: whole_over_wa(given[name]) for name in LONG_NAMES.values()}
        normed_self, back_self = jax.vjp(root_norm, inputs, small_of["selfnorm"])
        normed_low = normed_self.astype(BF)
        attended_low, attention_state = ring_forward(
            *(
                forward_product(normed_low, full[name]).astype(BF)
                for name in ("selfquery", "selfkey", "selfvalue")
            ),
            whole_over_wa(given["biastable"]),
        )
    attended_low, feed_in, upstream_low = lax.optimization_barrier(
        (attended_low, given["feedin"], upstream_low)
    )
    upstream_all = lax.all_gather(upstream_low, "wa", axis=0)
    feed_in = lax.all_to_all(feed_in, "wa", 1, 0, tiled=True)
    hidden = inputs + forward_product(attended_low, full["selfout"])

    spans = neighbours.shape[1]
    span_rows = neighbours.shape[2] * neighbours.shape[3]
    own_rows = neighbours[0].reshape(spans * span_rows, model_width)
    before = passed_along(own_rows[-span_rows:], "ctx", 1)
    near_rows = jnp.concatenate([before, own_rows], 0)
    keys_cross = forward_product(near_rows, full["crosskey"]).astype(BF)
    values_cross = forward_product(near_rows, full["crossvalue"]).astype(BF)
    normed_cross, back_cross = jax.vjp(root_norm, hidden, small_of["crossnorm"])
    cross_in = normed_cross.astype(BF)
    query_cross = forward_product(cross_in, full["crossquery"]).astype(BF)
    keep = jnp.full((8, WIDE), jnp.where(position > 0, 1.0, 0.0), F32)
    mixed_low = cross_forward(keep, query_cross, keys_cross, values_cross)
    hidden_two = hidden + forward_product(mixed_low, full["crossout"])

    normed_feed, back_feed = jax.vjp(root_norm, hidden_two, small_of["feednorm"])
    feed_low = normed_feed.astype(BF)
    bias_row = given["feedbias"].astype(F32)[None]
    fed, grad_feed, fin, fout, bias_sums = ffn(
        feed_low, upstream_all, feed_in, given["feedout"], bias_row
    )
    result = (hidden_two + fed + small_of["outbias"]).astype(BF)
    grad_two_part, grad_feednorm = back_feed(grad_feed)
    grad_two = upstream + grad_two_part
    two_low = grad_two.astype(BF)

    grad_mixed = back_product(two_low, full["crossout"]).astype(BF)
    early = {}
    if split_heads:
        grad_query_cross, early["ck"], early["cv"], near_low, near_last, feed_part = middle(
            keep,
            query_cross,
            grad_mixed,
            keys_cross,
            values_cross,
            near_rows,
            full["crosskey"],
            full["crossvalue"],
            fin,
            fout,
        )
    else:
        grad_query_cross, dkeys, dvalues = cross_backward(
            keep, query_cross, grad_mixed, keys_cross, values_cross
        )
        near_grads = back_product(dkeys, full["crosskey"]) + back_product(
            dvalues, full["crossvalue"]
        )
        near_low, near_last = near_grads.astype(BF), near_grads[-span_rows:]
        early["ck"] = outer_product(near_rows, dkeys).astype(BF)
        early["cv"] = outer_product(near_rows, dvalues).astype(BF)
    back = passed_along(near_low[:span_rows], "ctx", -1).astype(F32)
    grad_hidden_part, grad_crossnorm = back_cross(
        back_product(grad_query_cross, full["crossquery"])
    )
    grad_hidden = grad_two + grad_hidden_part
    hidden_low = grad_hidden.astype(BF)
    dout_low = back_product(hidden_low, full["selfout"]).astype(BF)
    early["cq"] = outer_product(cross_in, grad_query_cross).astype(BF)
    early["co"] = outer_product(mixed_low, two_low).astype(BF)
    early["so"] = outer_product(attended_low, hidden_low).astype(BF)
    if split_heads:
        dquery_low, dkey_low, dvalue_low, grad_biastable, shares = heads_backward(
            attention_state, dout_low, [early[name] for name in EARLY], feed_part
        )
        *shares, fin, fout = shares
    else:
        dquery_low, dkey_low, dvalue_low, grad_biastable = ring_backward(attention_state, dout_low)
    grad_normed = (
        back_product(dquery_low, full["selfquery"])
        + back_product(dkey_low, full["selfkey"])
        + back_product(dvalue_low, full["selfvalue"])
    )
    grad_input_part, grad_selfnorm = back_self(grad_normed)
    grad_inputs = (grad_hidden + grad_input_part).astype(BF)

    edge = span_rows * spans
    grad_neigh = (
        jnp.concatenate([near_low[span_rows:edge], (near_last + back).astype(BF)], 0)
        .reshape(neighbours.shape)
    )
    late = {
        "q": outer_product(normed_low, dquery_low).astype(BF),
        "k": outer_product(normed_low, dkey_low).astype(BF),
        "v": outer_product(normed_low, dvalue_low).astype(BF),
    }
    wa, owners = lax.axis_index("wa"), lax.axis_size("wa")
    bias_grad = jnp.sum(bias_sums, axis=0)
    placed = lax.dynamic_update_slice(
        jnp.zeros((owners, bias_grad.size), F32), bias_grad[None], (wa, 0)
    )
    sums = [grad_selfnorm, grad_crossnorm, grad_feednorm, jnp.sum(upstream, axis=0), grad_biastable]
    packed = jnp.concatenate([*(v.reshape(owners, -1) for v in sums), placed], axis=1)
    packed = jnp.pad(packed, ((0, 0), (0, LINE * 2 - packed.shape[1]))).reshape(-1, WIDE)
    if split_heads:
        *reduced, fin = reduce_grads(*shares, packed, [late[name] for name in LATE], fin)
        reduced = dict(zip(NAMES, reduced, strict=True))
        grads, packed = unfold(reduced), reduced["small"]
        fin = jnp.transpose(fin, (1, 0, 2)).reshape(given["feedin"].shape)
        fout = fout.reshape(given["feedout"].shape)
    else:
        grads, packed = reduce_plain(early | late, packed)
        fin, fout = lax.psum((fin, fout), "ctx")
        fin = lax.all_to_all(fin, "wa", 0, 1, tiled=True)
    grads["fin"], grads["fout"] = fin.astype(F32), fout.astype(F32)
    mine = lax.dynamic_index_in_dim(packed.reshape(owners, -1), wa, 0, keepdims=False)
    cuts, start = [], 0
    for v in (*sums, placed):
        cuts.append(mine[start : start + v.size // owners])
        start += v.size // owners
    own_selfnorm, own_crossnorm, own_feednorm, own_outbias, own_table, own_feedbias = cuts
    return (
        result[None],
        grad_inputs[None],
        grad_neigh,
        own_selfnorm,
        grads["q"],
        grads["k"],
        grads["v"],
        grads["so"],
        own_table.reshape(-1, H),
        own_crossnorm,
        grads["cq"],
        grads["ck"],
        grads["cv"],
        grads["co"],
        own_feednorm,
        grads["fin"],
        own_feedbias,
        grads["fout"],
        own_outbias,
    )


def solution(mesh):
    return jax.shard_map(
        per_device,
        mesh=mesh,
        in_specs=(
            P("wa", "ctx", None),
            P("wa", "ctx", None, None, None),
            P("wa", "ctx", None),
            P("wa"),
            P("wa", None),
            P("wa", None),
            P("wa", None),
            P("wa", None),
            P("wa", None),
            P("wa"),
            P("wa", None),
            P("wa", None),
            P("wa", None),
            P("wa", None),
            P("wa"),
            P("wa", None),
            P("wa"),
            P("wa", None),
            P("wa"),
        ),
        out_specs=(
            P("wa", "ctx", None),
            P("wa", "ctx", None),
            P("wa", "ctx", None, None, None),
            P("wa"),
            P("wa", None),
            P("wa", None),
            P("wa", None),
            P("wa", None),
            P("wa", None),
            P("wa"),
            P("wa", None),
            P("wa", None),
            P("wa", None),
            P("wa", None),
            P("wa"),
            P("wa", None),
            P("wa"),
            P("wa", None),
            P("wa"),
        ),
        check_vma=False,
    )
```

```python
import functools
import math

import jax
import jax.numpy as jnp
from jax import lax
from jax.experimental import pallas as pl
from jax.experimental.pallas import tpu as pltpu
from jax.sharding import PartitionSpec as P

H = 16
HD = 64
NB = 32
MAXD = 128
BLOCK = 256
SPAN = 64
MESH = pl.DeviceIdType.MESH
WIDE = 128
LINE = 1024
BF = jnp.bfloat16
F32 = jnp.float32


epsilon = 1e-06
negative = -1e30
strongest_precision = lax.Precision.HIGHEST


def passed_along(value, axis, by):
    peers = lax.axis_size(axis)
    pairs = [(i, i + by) for i in range(peers) if 0 <= i + by < peers]
    return lax.ppermute(value, axis, pairs)


def from_behind(block, axis, distance):
    devices = range(lax.axis_size(axis))
    route = [((i - distance) % len(devices), i) for i in devices]
    return lax.ppermute(block, axis, route)


def bucket_edges():
    half_count = NB // 2
    exact_part = half_count // 2
    edge_list = []
    for level_index in range(exact_part + 1, half_count):
        hits = [
            distance_now
            for distance_now in range(exact_part, MAXD + 1)
            if exact_part
            + int(
                math.log(distance_now / exact_part)
                / math.log(MAXD / exact_part)
                * (half_count - exact_part)
            )
            >= level_index
        ]
        edge_list.append(min(hits + [MAXD]))
    return (half_count, exact_part, edge_list)


def bucket_of(offset_value):
    half_count, exact_part, edge_list = bucket_edges()
    magnitude = jnp.abs(offset_value)
    far_part = exact_part + sum(
        [(magnitude >= edge_value).astype(magnitude.dtype) for edge_value in edge_list],
        jnp.zeros_like(magnitude),
    )
    return jnp.where(offset_value > 0, half_count, 0) + jnp.where(
        magnitude < exact_part, magnitude, far_part
    )


def root_norm(values, gain_vector):
    return (
        values
        * lax.rsqrt(jnp.mean(values * values, axis=-1, keepdims=True) + epsilon)
        * gain_vector
    )


def gelu_tanh(values):
    return jax.nn.gelu(values, approximate=True)


def forward_product(values, weight):
    return jnp.dot(values, weight, preferred_element_type=jnp.float32)


def outer_product(left_side, right_side):
    return lax.dot_general(
        left_side, right_side, (((0,), (0,)), ((), ())), preferred_element_type=jnp.float32
    )


def back_product(grad_low, weight):
    return lax.dot_general(
        grad_low, weight, (((1,), (1,)), ((), ())), preferred_element_type=jnp.float32
    )


def make_bias(bucket_bias_rows, row_count):
    query_place = jnp.arange(row_count)[:, None]
    key_place = jnp.arange(row_count)[None, :]
    levels = jnp.arange(NB)
    current_bucket_selector = (
        bucket_of(key_place - query_place)[None] == levels[:, None, None]
    ).astype(jnp.float32)
    previous_bucket_selector = (
        bucket_of(key_place - row_count - query_place)[None] == levels[:, None, None]
    ).astype(jnp.float32)
    onehot_far = (bucket_of(jnp.array(-MAXD, jnp.int32)) == levels).astype(jnp.float32)
    current_block_bias = jnp.einsum(
        "smz,sj->jmz", current_bucket_selector, bucket_bias_rows, precision=strongest_precision
    )
    previous_block_bias = jnp.einsum(
        "smz,sj->jmz", previous_bucket_selector, bucket_bias_rows, precision=strongest_precision
    )
    bias_far = jnp.dot(onehot_far, bucket_bias_rows, precision=strongest_precision)
    mask_same = key_place // BLOCK <= query_place // BLOCK
    return (
        (current_block_bias, previous_block_bias, bias_far, mask_same),
        (current_bucket_selector, previous_bucket_selector, onehot_far),
    )


def pair_scores(query_heads, key_heads, relation, bias_set, scale_factor):
    current_block_bias, previous_block_bias, bias_far, mask_same = bias_set
    raw_scores = jnp.einsum(
        "qhd,khd->hqk", query_heads, key_heads, preferred_element_type=jnp.float32
    )
    bias_rows = jnp.where(
        relation == 0,
        current_block_bias,
        jnp.where(relation == 1, previous_block_bias, bias_far[:, None, None]),
    )
    allowed = jnp.logical_or(relation > 0, mask_same)
    return jnp.where(allowed[None], raw_scores * scale_factor + bias_rows, negative)


def pair_core(
    query_heads,
    dout_heads,
    log_total,
    row_delta,
    key_heads,
    value_heads,
    relation,
    bias_set,
    scale_factor,
):
    scores = pair_scores(query_heads, key_heads, relation, bias_set, scale_factor)
    weights_now = jnp.exp(scores - log_total[:, :, None])
    grad_weights = jnp.einsum(
        "qhd,khd->hqk", dout_heads, value_heads, preferred_element_type=jnp.float32
    )
    dscores = weights_now * (grad_weights - row_delta[:, :, None])
    return (weights_now, dscores, (dscores * scale_factor).astype(jnp.bfloat16))


def add_tables(relative_bias_tables, dscores, relation):
    same_sum, prev_sum, far_sum = relative_bias_tables
    return (
        same_sum + jnp.where(relation == 0, dscores, 0.0),
        prev_sum + jnp.where(relation == 1, dscores, 0.0),
        far_sum + jnp.where(relation >= 2, jnp.sum(dscores, axis=(1, 2)), 0.0),
    )


def forward_fold(query_heads, position, row_count, bias_set, scale_factor, running, pieces):
    keys_all, values_all = pieces

    def one_shard(folded, shard_step):
        key_heads = lax.dynamic_slice_in_dim(
            keys_all, shard_step * row_count, row_count, 0
        ).reshape(row_count, H, HD)
        value_heads = lax.dynamic_slice_in_dim(
            values_all, shard_step * row_count, row_count, 0
        ).reshape(row_count, H, HD)
        relation = position - shard_step

        def one_compute(current):
            running_max, running_sum, running_acc = current
            scores = pair_scores(query_heads, key_heads, relation, bias_set, scale_factor)
            new_max = jnp.maximum(running_max, jnp.max(scores, axis=-1))
            factor = jnp.exp(running_max - new_max)
            weights_now = jnp.exp(scores - new_max[:, :, None])
            new_sum = running_sum * factor + jnp.sum(weights_now, axis=-1)
            update = jnp.einsum(
                "hqk,khd->qhd",
                weights_now.astype(jnp.bfloat16),
                value_heads,
                preferred_element_type=jnp.float32,
            )
            scaled = running_acc.reshape(row_count, H, HD) * factor.T[:, :, None]
            return (new_max, new_sum, (scaled + update).reshape(row_count, H * HD))

        return (lax.cond(relation >= 0, one_compute, lambda unchanged: unchanged, folded), None)

    running, unused = lax.scan(one_shard, running, jnp.arange(keys_all.shape[0] // row_count))
    return running


def nt_dot(left, right):
    return lax.dot_general(left, right, (((1,), (1,)), ((), ())), preferred_element_type=F32)


def nn_dot(left, right):
    return jnp.dot(left, right, preferred_element_type=F32)


def meet(neighbours):
    barrier = pltpu.get_barrier_semaphore()
    for who in neighbours:
        pl.semaphore_signal(barrier, inc=1, device_id=who, device_id_type=MESH)
    pl.semaphore_wait(barrier, len(neighbours))


def ctx_peers(n):
    me = lax.axis_index("ctx")
    return [{"ctx": lax.rem(me + d, n)} for d in range(1, n)]


def other_wa(me, bit):
    flipped = lax.rem(me // bit, 2)
    return me + bit - 2 * bit * flipped


def remote(src, dst, send_sem, recv_sem, **device):
    return pltpu.make_async_remote_copy(
        src_ref=src,
        dst_ref=dst,
        send_sem=send_sem,
        recv_sem=recv_sem,
        device_id=device,
        device_id_type=MESH,
    )


RING = 8
HOPS = RING - 1


def ring_place(n):
    me = lax.axis_index("ctx")
    half = n // 2

    def at(place):
        return jnp.where(place < half, 2 * place, 2 * (n - 1 - place) + 1)

    place = jnp.where(lax.rem(me, 2) == 0, me // 2, n - 1 - me // 2)
    return place, at(lax.rem(place + 1, n)), at(lax.rem(place + n - 1, n))


class Ring:
    def __init__(self, lanes, send, recv, share=None, hold=None, full=None):
        self.lanes, self.share, self.hold, self.full = lanes, share, hold, full
        self.sems = send, recv
        self.place, self.after, self.before = ring_place(RING)

    def copy(self, lane, src, dst, step):
        send, recv = self.sems
        way = self.lanes[lane][1]
        return remote(
            src, dst, send.at[lane, step], recv.at[lane, step], ctx=self.after if way == 1 else self.before
        )

    def chunk(self, lane, offset):
        here = self.place if self.lanes[lane][1] == 1 else RING - self.place
        return lax.rem(here + offset + 2 * RING, RING)

    def scatter(self, step, which):
        for lane in which:
            b, _, rows = self.lanes[lane]
            share = self.share.at[b, self.chunk(lane, -step), rows]

            @pl.when(step > 0)
            def _():
                there = self.hold.at[b, jnp.maximum(step - 1, 0), rows]
                self.copy(lane, share, there, jnp.maximum(step - 1, 0)).wait_recv()
                share[...] = (share[...].astype(F32) + there[...].astype(F32)).astype(BF)

            @pl.when(step < HOPS)
            def _():
                there = jnp.minimum(step, HOPS - 1)
                self.copy(lane, share, self.hold.at[b, there, rows], there).start()

    def gather(self, step, which):
        for lane in which:
            b, _, rows = self.lanes[lane]
            full = self.full[b].at[self.chunk(lane, 1 - step), rows]

            @pl.when(step > 0)
            def _():
                self.copy(lane, full, full, jnp.maximum(step - 1, 0)).wait_recv()

            @pl.when(step < HOPS)
            def _():
                self.copy(lane, full, full, jnp.minimum(step, HOPS - 1)).start()

    def finish(self, part):
        def one(step, unused):
            for lane in range(len(self.lanes)):
                self.copy(lane, part(lane), part(lane), step).wait_send()
            return unused

        lax.fori_loop(0, HOPS, one, 0)


TALL, FLAT = (224, 1024), (256, 896)
EARLY = ("cq", "ck", "cv", "co", "so")
LATE = ("q", "k", "v")
FEED = (8, 112, 896)
FEED_LANES = (
    (0, 1, slice(0, 64)),
    (1, -1, slice(0, 64)),
    (0, 1, slice(64, 112)),
    (1, -1, slice(64, 112)),
)
FEED_TURNS = ((0, 1), (2, 3))


class Folding:
    def __init__(self, names, parts, scratch):
        self.names = names
        self.parts = parts
        tall, flat, sems = scratch
        self.sets = {TALL: tall, FLAT: flat}
        self.own_sem, self.core_send, self.core_recv, self.x_send, self.x_recv = sems
        self.wa = lax.axis_index("wa")
        self.mate, self.across = other_wa(self.wa, 1), other_wa(self.wa, 2)
        self.core, self.half = lax.rem(self.wa, 2), self.wa // 2
        self.slots, count = {}, {TALL: 0, FLAT: 0}
        for name in names:
            shape = self.shape_of(name)
            self.slots[name] = (count[shape], self.sets[shape])
            count[shape] += 1
        self.own_copies, self.core_copies, self.x_copies = {}, {}, {}

    @staticmethod
    def shape_of(name):
        return FLAT if name in ("co", "so") else TALL

    @classmethod
    def scratch(cls, names):
        shapes = []
        for shape in (TALL, FLAT):
            many = sum(cls.shape_of(name) == shape for name in names)
            if many:
                shapes += [pltpu.VMEM((many, 2, *shape), BF)] * 2 + [pltpu.VMEM((many, *shape), BF)] * 2
        dma = pltpu.SemaphoreType.DMA
        many = len(names)
        return shapes + [dma((many, 2))] * 3 + [dma((many,))] * 2

    def start(self):
        for u, name in enumerate(self.names):
            slot, (own, inn, _, _) = self.slots[name]
            rows = self.shape_of(name)[0]
            for x in range(2):
                mine = pl.ds(pl.multiple_of((2 * x + self.core) * rows, 16), rows)
                theirs = pl.ds(pl.multiple_of((2 * x + 1 - self.core) * rows, 16), rows)
                copy = remote(
                    self.parts[name].at[theirs],
                    inn.at[slot, x],
                    self.core_send.at[u, x],
                    self.core_recv.at[u, x],
                    wa=self.mate,
                )
                copy.start()
                self.core_copies[name, x] = copy
                copy = pltpu.make_async_copy(
                    self.parts[name].at[mine], own.at[slot, x], self.own_sem.at[u, x]
                )
                copy.start()
                self.own_copies[name, x] = copy
            slot, (_, _, out, land) = self.slots[name]
            self.x_copies[name] = remote(
                out.at[slot], land.at[slot], self.x_send.at[u], self.x_recv.at[u], wa=self.across
            )

    def send(self, name):
        self.prepare(name)
        self.x_copies[name].start()

    def prepare(self, name):
        slot, (own, inn, out, _) = self.slots[name]
        for x in range(2):
            self.own_copies[name, x].wait()
            self.core_copies[name, x].wait_recv()
        away = 1 - self.half
        out[slot] = (own[slot, away].astype(F32) + inn[slot, away].astype(F32)).astype(BF)

    def total(self, name):
        slot, (own, inn, _, land) = self.slots[name]
        self.x_copies[name].wait_recv()
        here = self.half
        return (
            own[slot, here].astype(F32) + inn[slot, here].astype(F32) + land[slot].astype(F32)
        ).astype(BF)

    def finish(self):
        for name in self.names:
            for x in range(2):
                self.core_copies[name, x].wait_send()
            self.x_copies[name].wait_send()


def lasting(microseconds):
    return pl.CostEstimate(
        flops=0, bytes_accessed=int(microseconds * 3.0e6), transcendentals=0
    )


def lanes_of(index):
    return pl.ds(pl.multiple_of(index * WIDE, WIDE), WIDE)


def rows_of(index, rows):
    return pl.ds(pl.multiple_of(index * rows, rows), rows)


def to_ctx(src, dst, send_sem, recv_sem, target):
    return pltpu.make_async_remote_copy(
        src_ref=src,
        dst_ref=dst,
        send_sem=send_sem,
        recv_sem=recv_sem,
        device_id={"ctx": target},
        device_id_type=MESH,
    )


def head_mask(h, rows):
    lane = lax.broadcasted_iota(jnp.int32, (rows, WIDE), 1)
    return (lane < HD) if h == 0 else (lane >= HD)


def bias_tiles(bias_ref, me, tiles):
    for h in range(2):
        line = bias_ref[pl.ds(2 * me + h, 1), :]
        rolled = pltpu.roll(
            jnp.broadcast_to(line, (BLOCK, LINE)), 0, 1, stride=1, stride_axis=0
        )
        tiles[h, 0] = rolled[:, :BLOCK]
        tiles[h, 1] = rolled[:, BLOCK : 2 * BLOCK]
        tiles[h, 2] = jnp.broadcast_to(line[:, WIDE : WIDE + BLOCK], (BLOCK, BLOCK))


def spread(n, me, pairs, send, recv, t):
    src, dst = pairs[t]
    for d in range(1, n):
        peer = lax.rem(me + d, n)
        to_ctx(
            src.at[:, lanes_of(peer)], dst.at[rows_of(me, BLOCK)], send.at[t, d], recv.at[t, d], peer
        ).start()
    dst[rows_of(me, BLOCK), :] = src[:, lanes_of(me)]


GATHERED = ("q", "k", "v", "so", "ck", "cv", "cq", "co")
SINGLE = ("cot",)
GAINS = ("selfnorm", "crossnorm", "feednorm", "outbias")


class Gathering:
    def __init__(self, shards, whole, own_sem, send, recv):
        self.names, self.shards, self.whole = tuple(shards), shards, whole
        self.sems = own_sem, send, recv
        self.wa, me = lax.axis_index("wa"), lax.axis_index("ctx")
        self.mate, self.across = other_wa(self.wa, 1), other_wa(self.wa, 2)
        self.y = lax.rem(me, 2)
        self.beside = me + 1 - 2 * self.y
        self.copies = {}

    def start(self):
        own_sem, send, recv = self.sems
        for u, name in enumerate(self.names):
            shard, whole = self.shards[name], self.whole[name]
            rows = shard.shape[0]
            parts = 1 if name in SINGLE else 2
            some = rows // parts
            shift = 0 if parts == 1 else self.y * some

            def at(start, count, ref=whole):
                return ref.at[pl.ds(pl.multiple_of(start, 16), count)]

            mine = at(self.wa * rows, rows)
            theirs = at(self.across * rows, rows)
            theirs_some = at(self.across * rows + shift, some)
            self.copies[name] = {
                "over": remote(
                    at(shift, some, shard), at(self.wa * rows + shift, some), send.at[u, 0], recv.at[u, 0], wa=self.across
                ),
                "near": remote(shard, mine, send.at[u, 1], recv.at[u, 1], wa=self.mate),
                "pass": remote(theirs, theirs, send.at[u, 2], recv.at[u, 2], wa=self.mate),
                "side": remote(theirs_some, theirs_some, send.at[u, 3], recv.at[u, 3], ctx=self.beside),
                "own": pltpu.make_async_copy(shard, mine, own_sem.at[u]),
            }
            self.copies[name]["near"].start()
            self.copies[name]["own"].start()

    def cross(self, *names):
        for name in names:
            self.copies[name]["over"].start()

    def forward(self, *names):
        for name in names:
            self.copies[name]["over"].wait_recv()
            self.copies[name]["pass" if name in SINGLE else "side"].start()

    def land(self, *names):
        for name in names:
            self.copies[name]["side"].wait_recv()
            self.copies[name]["pass"].start()

    def arrive(self, *names):
        for name in names:
            self.copies[name]["near"].wait_recv()
            self.copies[name]["pass"].wait_recv()
            self.copies[name]["own"].wait()

    def finish(self):
        for name, copies in self.copies.items():
            for which in ("over", "near", "pass") + (() if name in SINGLE else ("side",)):
                copies[which].wait_send()


class Columns:
    def __init__(self, gathering, shard, whole, send, recv):
        wa, mate, across, y = gathering.wa, gathering.mate, gathering.across, gathering.y
        both = other_wa(across, 1)
        rows, width = shard.shape[0], whole.shape[1]
        some = rows // 2

        def block(owner, columns):
            return shard.at[owner, pl.ds(pl.multiple_of(columns * width, WIDE), width)]

        def at(start, count):
            return whole.at[pl.ds(pl.multiple_of(start, 16), count)]

        everything = slice(0, rows)
        mine = pl.ds(pl.multiple_of(y * some, 16), some)
        self.own = pltpu.make_async_copy(block(everything, wa), at(wa * rows, rows), send.at[5])
        self.near = remote(block(everything, mate), at(wa * rows, rows), send.at[0], recv.at[0], wa=mate)
        self.over = [
            remote(block(mine, peer), at(wa * rows + y * some, some), send.at[1 + d], recv.at[1 + d], wa=peer)
            for d, peer in enumerate((across, both))
        ]
        self.side = []
        for d, peer in enumerate((across, both)):
            got = at(peer * rows + y * some, some)
            self.side.append(remote(got, got, send.at[3 + d], recv.at[3 + d], ctx=gathering.beside))

    def start(self):
        self.own.start()
        self.near.start()

    def cross(self):
        for copy in self.over:
            copy.start()

    def forward(self):
        for over, side in zip(self.over, self.side, strict=True):
            over.wait_recv()
            side.start()

    def finish(self):
        self.own.wait()
        self.near.wait()
        for over, side in zip(self.over, self.side, strict=True):
            side.wait()
            over.wait_send()


def attn_forward_kernel(n, tokens_ref, small_ref, near_ref, *refs):
    shards = dict(zip((*GATHERED, "cot"), refs[:9], strict=True))
    feed_ref = refs[9]
    wholes = dict(zip((*GATHERED, "cot"), refs[10:19], strict=True))
    feed_whole = refs[19]
    o_ref, low_ref, qh_out, kh_out, vh_out, ot_out, lse_out, small_out, before_ref, keys_ref, values_ref = refs[20:31]
    (
        held_q, held_k, held_v, held_ck, held_cv, proj, small_in, small_mid, qh, kh, vh, vt, oh, land, tiles,
        acc, stat, send, recv, osend, orecv, small_sem, own_sem, out_sem, gather_send, gather_recv, feed_send,
        feed_recv, span_sem,
    ) = refs[31:]
    held = {"q": held_q, "k": held_k, "v": held_v, "ck": held_ck, "cv": held_cv}
    gathering = Gathering(shards, wholes | held, own_sem, gather_send, gather_recv)
    columns = Columns(gathering, feed_ref, feed_whole, feed_send, feed_recv)
    both = other_wa(gathering.across, 1)
    meet([*ctx_peers(n), *({"wa": peer} for peer in (gathering.mate, gathering.across, both))])
    me = lax.axis_index("ctx")
    near = remote(small_ref, small_in.at[0], small_sem.at[0], small_sem.at[1], wa=gathering.mate)
    near.start()
    gathering.start()
    gathering.cross("q")
    columns.start()
    span_rows = before_ref.shape[0]
    span = remote(
        near_ref.at[near_ref.shape[0] - span_rows :],
        before_ref,
        span_sem.at[0],
        span_sem.at[1],
        ctx=lax.rem(me + 1, n),
    )
    over = remote(small_mid, small_in.at[1], small_sem.at[2], small_sem.at[3], wa=gathering.across)
    near.wait_recv()
    small_mid[...] = (small_ref[...].astype(F32) + small_in[0].astype(F32)).astype(BF)
    over.start()
    over.wait_recv()
    small_out[...] = small_mid[...].astype(F32) + small_in[1].astype(F32)
    bias_ref = small_out
    values = tokens_ref[...].astype(F32)
    width = values.shape[1]
    norm = lax.rsqrt(jnp.mean(values * values, axis=1, keepdims=True) + epsilon)
    low_ref[...] = (values * norm * small_out[H : H + 1, :width]).astype(BF)
    bias_tiles(bias_ref, me, tiles)
    pairs = tuple((proj.at[t], dst) for t, dst in enumerate((qh, kh, vh)))
    saving = []

    def save(name):
        copy = pltpu.make_async_copy(held[name], wholes[name], out_sem.at[len(saving)])
        copy.start()
        saving.append(copy)

    def project(t, name):
        gathering.land(name)
        gathering.arrive(name)
        proj[t] = nn_dot(low_ref[...], held[name][...]).astype(BF)
        spread(n, me, pairs, send, recv, t)
        save(name)

    gathering.forward("q")
    gathering.cross("k")
    gathering.forward("k")
    gathering.cross("v")
    project(0, "q")
    gathering.forward("v")
    gathering.cross("so", "ck")
    project(1, "k")
    project(2, "v")

    @pl.when(me < n - 1)
    def _():
        span.start()

    gathering.forward("so", "ck")
    gathering.cross("cv", "cq")

    for d in range(1, n):
        peer = lax.rem(me + n - d, n)
        for t, (src, dst) in enumerate(pairs):
            to_ctx(
                src.at[:, lanes_of(peer)], dst.at[rows_of(peer, BLOCK)], send.at[t, d], recv.at[t, d], peer
            ).wait_recv()
    for i in range(n):
        part = slice(i * BLOCK, (i + 1) * BLOCK)
        vt[:, part] = vh[part, :].astype(F32).T.astype(BF)

    def query_block(step, unused):
        @pl.when(step == 1)
        def _():
            gathering.forward("cv", "cq")
            gathering.land("so", "ck")
            gathering.cross("co")
            columns.cross()

        @pl.when(step == 6)
        def _():
            gathering.land("cv", "cq")
            gathering.forward("co")
            columns.forward()
            gathering.cross("cot")

        i = lax.rem(me + 1 + step, n)
        rows = rows_of(i, BLOCK)
        q_now = qh[rows, :] * BF(HD**-0.5)
        masked = [jnp.where(head_mask(h, BLOCK), q_now, BF(0)) for h in range(2)]

        def fold(j, which, first):
            keys = kh[rows_of(j, BLOCK), :]
            for h in range(2):
                scores = nt_dot(keys, masked[h])
                if which is None:
                    scores = scores + bias_ref[pl.ds(2 * me + h, 1), WIDE : WIDE + BLOCK]
                else:
                    scores = scores + tiles[h, which]
                top = jnp.max(scores, axis=0, keepdims=True)
                if not first:
                    old = stat[h : h + 1, :]
                    top = jnp.maximum(old, top)
                weights = jnp.exp(scores - top)
                total = jnp.sum(weights, axis=0, keepdims=True)
                vals = vt[h * HD : (h + 1) * HD, rows_of(j, BLOCK)]
                mixed = nn_dot(vals, weights.astype(BF))
                if not first:
                    factor = jnp.exp(old - top)
                    total = total + stat[2 + h : 3 + h, :] * factor
                    mixed = mixed + acc[h * HD : (h + 1) * HD, :] * factor
                stat[h : h + 1, :] = top
                stat[2 + h : 3 + h, :] = total
                acc[h * HD : (h + 1) * HD, :] = mixed

        fold(i, 0, True)

        @pl.when(i >= 1)
        def _():
            fold(i - 1, 1, False)

        def far(j, unused):
            fold(j, None, False)
            return unused

        lax.fori_loop(0, i - 1, far, 0)
        for h in range(2):
            total = stat[2 + h : 3 + h, :]
            part = acc[h * HD : (h + 1) * HD, :] / total
            acc[h * HD : (h + 1) * HD, :] = part
            lse_out[h : h + 1, rows] = stat[h : h + 1, :] + jnp.log(total)
        done = acc[...]
        ot_out[:, rows] = done
        oh[rows, :] = done.T.astype(BF)

        @pl.when(i != me)
        def _():
            d = lax.rem(i - me + n, n)
            to_ctx(oh.at[rows], land.at[:, lanes_of(me)], osend.at[d], orecv.at[d], i).start()

        @pl.when(i == me)
        def _():
            land[:, lanes_of(me)] = oh[rows, :]

        return unused

    lax.fori_loop(0, n, query_block, 0)
    qh_out[...] = qh[...]
    kh_out[...] = kh[...]
    vh_out[...] = vh[...]

    @pl.when(me > 0)
    def _():
        span.wait_recv()

    @pl.when(me == 0)
    def _():
        before_ref[...] = jnp.zeros_like(before_ref)

    for name, out_ref in (("ck", keys_ref), ("cv", values_ref)):
        gathering.arrive(name)
        save(name)
        out_ref[:span_rows, :] = nn_dot(before_ref[...], held[name][...]).astype(BF)
        for g in range(near_ref.shape[0] // span_rows):
            rows = slice(g * span_rows, (g + 1) * span_rows)
            there = slice((g + 1) * span_rows, (g + 2) * span_rows)
            out_ref[there, :] = nn_dot(near_ref[rows, :], held[name][...]).astype(BF)
    gathering.land("co")
    gathering.forward("cot")
    for d in range(1, n):
        peer = lax.rem(me + d, n)
        for t, (src, dst) in enumerate(pairs):
            to_ctx(
                src.at[:, lanes_of(peer)], dst.at[rows_of(me, BLOCK)], send.at[t, d], recv.at[t, d], peer
            ).wait_send()
        back = to_ctx(
            oh.at[rows_of(peer, BLOCK)], land.at[:, lanes_of(me)], osend.at[d], orecv.at[d], peer
        )
        back.wait_send()
        back.wait_recv()
    o_ref[...] = land[...]
    gathering.arrive("so", "cq", "co", "cot")
    gathering.finish()
    columns.finish()

    @pl.when(me < n - 1)
    def _():
        span.wait_send()

    near.wait_send()
    over.wait_send()
    for copy in saving:
        copy.wait()


def vmem(count):
    return [pl.BlockSpec(memory_space=pltpu.VMEM)] * count


def attn_forward(n, tokens, small, near, shards, feed):
    rows, seq = tokens.shape[0], n * tokens.shape[0]
    owners = lax.axis_size("wa")
    low = functools.partial(jax.ShapeDtypeStruct, dtype=BF)
    heads = low((seq, WIDE))
    wholes = [low((owners * s.shape[0], s.shape[1])) for s in shards]
    width = wholes[0].shape[1]
    dma = pltpu.SemaphoreType.DMA
    span_rows = 256
    keys = low((span_rows + near.shape[0], width))
    any_spec = pl.BlockSpec(memory_space=pl.ANY)
    return pl.pallas_call(
        functools.partial(attn_forward_kernel, n),
        out_shape=(
            *wholes,
            low((owners * feed.shape[0], feed.shape[1] // owners)),
            low((rows, width)),
            low(tokens.shape),
            heads,
            heads,
            heads,
            jax.ShapeDtypeStruct((WIDE, seq), F32),
            jax.ShapeDtypeStruct((8, seq), F32),
            jax.ShapeDtypeStruct(small.shape, F32),
            low((span_rows, near.shape[1])),
            keys,
            keys,
        ),
        in_specs=vmem(3) + [any_spec] * 10,
        out_specs=tuple([any_spec] * 10 + vmem(11)),
        scratch_shapes=[
            *[pltpu.VMEM(wholes[0].shape, BF)] * 5,
            pltpu.VMEM((3, rows, width), BF),
            pltpu.VMEM((2, *small.shape), BF),
            pltpu.VMEM(small.shape, BF),
            pltpu.VMEM((seq, WIDE), BF),
            pltpu.VMEM((seq, WIDE), BF),
            pltpu.VMEM((seq, WIDE), BF),
            pltpu.VMEM((WIDE, seq), BF),
            pltpu.VMEM((seq, WIDE), BF),
            pltpu.VMEM((rows, width), BF),
            pltpu.VMEM((2, 3, BLOCK, BLOCK), F32),
            pltpu.VMEM((WIDE, BLOCK), F32),
            pltpu.VMEM((8, BLOCK), F32),
            dma((3, n)),
            dma((3, n)),
            dma((n,)),
            dma((n,)),
            dma((4,)),
            dma((9,)),
            dma((5,)),
            dma((9, 4)),
            dma((9, 4)),
            dma((6,)),
            dma((5,)),
            dma((2,)),
        ],
        compiler_params=pltpu.CompilerParams(
            collective_id=1, has_side_effects=True, vmem_limit_bytes=60 << 20
        ),
        cost_estimate=lasting(85),
        name="attn_forward",
    )(tokens, small, near, *shards, feed)


def attn_backward_kernel(
    n, do_ref, qh, kh, vh, ot_ref, lse_ref, bias_ref, *rest
):
    parts = dict(zip(EARLY, rest[:5], strict=True))
    feed_part = rest[5]
    dq_ref, dk_ref, dv_ref, line_ref, tall_pair, tall_one, flat_out = rest[6:13]
    feed_full = rest[13:15]
    (
        doh, kt, stage, land, dk_acc, dv_acc, dq_acc, q_masked, do_masked, delta, tiles, dtiles,
        send, recv, gsend, grecv, ring_send, ring_recv,
    ) = rest[15:33]
    extra = rest[33:]
    fold_wa = Folding(EARLY, parts, (extra[0:4], extra[4:8], extra[8:13]))
    ring = Ring(FEED_LANES, ring_send, ring_recv, full=feed_full)
    for lane in range(2):
        feed_full[lane][ring.chunk(lane, 1)] = feed_part[lane]
    meet([*ctx_peers(n), {"wa": fold_wa.mate}, {"wa": fold_wa.across}])
    me = lax.axis_index("ctx")
    pairs = ((do_ref, doh),)
    spread(n, me, pairs, send, recv, 0)
    fold_wa.start()
    bias_tiles(bias_ref, me, tiles)
    for j in range(n):
        part = slice(j * BLOCK, (j + 1) * BLOCK)
        kt[:, part] = (kh[part, :].astype(F32) * HD**-0.5).T.astype(BF)
    dtiles[...] = jnp.zeros_like(dtiles)
    for name in EARLY[:2]:
        fold_wa.send(name)
    ring.gather(jnp.int32(0), FEED_TURNS[0])
    ring.gather(jnp.int32(0), FEED_TURNS[1])
    dq_acc[...] = jnp.zeros_like(dq_acc)
    for d in range(1, n):
        peer = lax.rem(me + n - d, n)
        to_ctx(
            do_ref.at[:, lanes_of(peer)], doh.at[rows_of(peer, BLOCK)], send.at[0, d], recv.at[0, d], peer
        ).wait_recv()
    for i in range(n):
        rows = slice(i * BLOCK, (i + 1) * BLOCK)
        q_now = qh[rows, :] * BF(HD**-0.5)
        do_now = doh[rows, :]
        products = do_now.astype(F32).T * ot_ref[:, rows]
        for h in range(2):
            mask = head_mask(h, BLOCK)
            q_masked[h, rows, :] = jnp.where(mask, q_now, BF(0))
            do_masked[h, rows, :] = jnp.where(mask, do_now, BF(0))
            delta[h : h + 1, rows] = jnp.sum(
                products[h * HD : (h + 1) * HD], axis=0, keepdims=True
            )

    def pair(t, now):
        i, j = now
        rows, there = rows_of(i, BLOCK), rows_of(j, BLOCK)

        @pl.when(t == 6)
        def _():
            for name in EARLY[2:]:
                fold_wa.send(name)

        for turn, lanes in enumerate(FEED_TURNS):

            @pl.when((lax.rem(t, 4) == 2 * turn + 1) & (t <= 4 * HOPS))
            def _():
                ring.gather(t // 4 + 1, lanes)

        first = i == j
        which = jnp.minimum(i - j, 2)
        keys, vals = kh[there, :], vh[there, :]
        dk_part, dv_part = None, None
        for h in range(2):
            query, dout = q_masked[h, rows, :], do_masked[h, rows, :]
            scores = nt_dot(keys, query)
            weights = jnp.exp(scores + tiles[h, which] - lse_ref[h : h + 1, rows])
            dweights = nt_dot(vals, dout)
            dscores = weights * (dweights - delta[h : h + 1, rows])
            dtiles[h, which] += dscores
            low = dscores.astype(BF)
            dv_now = nn_dot(weights.astype(BF), dout)
            dk_now = nn_dot(low, query)
            dv_part = dv_now if dv_part is None else dv_part + dv_now
            dk_part = dk_now if dk_part is None else dk_part + dk_now
            half = slice(h * HD, (h + 1) * HD)
            dq_acc[half, rows] += nn_dot(kt[half, there], low)

        @pl.when(first)
        def _():
            dk_acc[...] = dk_part
            dv_acc[...] = dv_part

        @pl.when(jnp.logical_not(first))
        def _():
            dk_acc[...] += dk_part
            dv_acc[...] += dv_part

        last = i == n - 1

        @pl.when(last)
        def _():
            stage[1, there, :] = dk_acc[...].astype(BF)
            stage[2, there, :] = dv_acc[...].astype(BF)
            deliver(j, (1, 2))

        after = lax.rem(j + 1, n)
        return jnp.where(last, after, i + 1), jnp.where(last, after, j)

    def deliver(i, arrays):
        rows = rows_of(i, BLOCK)

        @pl.when(i != me)
        def _():
            d = lax.rem(i - me + n, n)
            for t in arrays:
                to_ctx(
                    stage.at[t, rows], land.at[t, :, lanes_of(me)], gsend.at[t, d], grecv.at[t, d], i
                ).start()

        @pl.when(i == me)
        def _():
            for t in arrays:
                land[t, :, lanes_of(me)] = stage[t, rows, :]

    begin = lax.rem(me + 1, n)
    lax.fori_loop(0, n * (n + 1) // 2, pair, (begin, begin))

    def dq_block(step, unused):
        i = lax.rem(me + 1 + step, n)
        rows = rows_of(i, BLOCK)
        stage[0, rows, :] = dq_acc[:, rows].T.astype(BF)
        deliver(i, (0,))
        return unused

    lax.fori_loop(0, n, dq_block, 0)
    ring.finish(lambda lane: feed_full[FEED_LANES[lane][0]].at[0, FEED_LANES[lane][2]])
    tall_pair[:224, :] = fold_wa.total("cq")
    tall_pair[224:, :] = fold_wa.total("ck")
    tall_one[...] = fold_wa.total("cv")
    for at, name in ((0, "co"), (32, "so")):
        flat_out[:, at : at + 32, :] = fold_wa.total(name).reshape(8, 32, 896)
    fold_wa.finish()
    for h in range(2):
        line = jnp.concatenate(
            [dtiles[h, 0], dtiles[h, 1], jnp.zeros((BLOCK, LINE - 2 * BLOCK), F32)], axis=1
        )
        row = lax.broadcasted_iota(jnp.int32, (BLOCK, LINE), 0)
        for bit in range(8):
            moved = pltpu.roll(line, LINE - (1 << bit), 1)
            line = jnp.where((row >> bit) & 1 == 1, moved, line)
        line_ref[h : h + 1, :] = jnp.sum(line, axis=0, keepdims=True)
        line_ref[2 + h : 3 + h, :BLOCK] = jnp.sum(dtiles[h, 2], axis=0, keepdims=True)
    line_ref[2:4, BLOCK:] = jnp.zeros((2, LINE - BLOCK), F32)
    line_ref[4:8, :] = jnp.zeros((4, LINE), F32)
    for d in range(1, n):
        peer = lax.rem(me + d, n)
        to_ctx(
            do_ref.at[:, lanes_of(peer)], doh.at[rows_of(me, BLOCK)], send.at[0, d], recv.at[0, d], peer
        ).wait_send()
        for t in range(3):
            back = to_ctx(
                stage.at[t, rows_of(peer, BLOCK)], land.at[t, :, lanes_of(me)], gsend.at[t, d], grecv.at[t, d], peer
            )
            back.wait_send()
            back.wait_recv()
    dq_ref[...] = land[0]
    dk_ref[...] = land[1]
    dv_ref[...] = land[2]


def attn_backward(n, dout, qh, kh, vh, ot, lse, bias_lines, parts, feed_part):
    rows, seq = dout.shape[0], n * dout.shape[0]
    grads = jax.ShapeDtypeStruct(dout.shape, BF)
    feed = jax.ShapeDtypeStruct(FEED, BF)
    return pl.pallas_call(
        functools.partial(attn_backward_kernel, n),
        out_shape=(
            grads,
            grads,
            grads,
            jax.ShapeDtypeStruct((8, LINE), F32),
            jax.ShapeDtypeStruct((448, 1024), BF),
            jax.ShapeDtypeStruct((224, 1024), BF),
            jax.ShapeDtypeStruct((8, 64, 896), BF),
            feed,
            feed,
        ),
        in_specs=vmem(7) + [pl.BlockSpec(memory_space=pl.ANY)] * 5 + vmem(1),
        out_specs=tuple(vmem(9)),
        scratch_shapes=[
            pltpu.VMEM((seq, WIDE), BF),
            pltpu.VMEM((WIDE, seq), BF),
            pltpu.VMEM((3, seq, WIDE), BF),
            pltpu.VMEM((3, *dout.shape), BF),
            pltpu.VMEM((BLOCK, WIDE), F32),
            pltpu.VMEM((BLOCK, WIDE), F32),
            pltpu.VMEM((WIDE, seq), F32),
            pltpu.VMEM((2, seq, WIDE), BF),
            pltpu.VMEM((2, seq, WIDE), BF),
            pltpu.VMEM((8, seq), F32),
            pltpu.VMEM((2, 3, BLOCK, BLOCK), F32),
            pltpu.VMEM((2, 3, BLOCK, BLOCK), F32),
            pltpu.SemaphoreType.DMA((1, n)),
            pltpu.SemaphoreType.DMA((1, n)),
            pltpu.SemaphoreType.DMA((3, n)),
            pltpu.SemaphoreType.DMA((3, n)),
            pltpu.SemaphoreType.DMA((len(FEED_LANES), HOPS)),
            pltpu.SemaphoreType.DMA((len(FEED_LANES), HOPS)),
            *Folding.scratch(EARLY),
        ],
        compiler_params=pltpu.CompilerParams(
            collective_id=2, has_side_effects=True, vmem_limit_bytes=58 << 20
        ),
        cost_estimate=lasting(100),
        name="attn_backward",
    )(dout, qh, kh, vh, ot, lse, bias_lines, *parts, feed_part)


BUFFERS = {
    "cq": (1, (224, 1024)),
    "cv": (-1, (224, 1024)),
    "ck": (1, (224, 1024)),
    "co": (-1, (8, 32, 896)),
    "so0": (1, (8, 16, 896)),
    "so1": (-1, (8, 16, 896)),
}
NAMES = tuple(BUFFERS)


def chunk_shape(name):
    shape = BUFFERS[name][1]
    return (shape[0], WIDE) if len(shape) == 2 else shape[1:]


def chunk_of(ref, name, c):
    return ref.at[:, lanes_of(c)] if len(BUFFERS[name][1]) == 2 else ref.at[c]


class Grid:
    def __init__(self, u, share, half_in, half, quarters, whole, send, recv):
        self.u, self.share, self.half_in, self.half = u, share, half_in, half
        self.quarters, self.whole, self.sems = quarters, whole, (send, recv)
        me = lax.axis_index("ctx")
        self.y, self.z = lax.rem(me, 2), me // 2
        self.beside = me + 1 - 2 * self.y
        self.column = [lax.rem(self.z + d, 4) for d in range(1, 4)]

    def half_of(self, y):
        return pl.ds(pl.multiple_of(y * 4 * WIDE, WIDE), 4 * WIDE)

    def piece_of(self, z, y=None):
        start = z * WIDE if y is None else (4 * y + z) * WIDE
        return pl.ds(pl.multiple_of(start, WIDE), WIDE)

    def copy(self, number, src, dst, target):
        send, recv = self.sems
        return remote(src, dst, send.at[self.u, number], recv.at[self.u, number], ctx=target)

    def start(self, total):
        self.share[...] = total
        self.first = self.copy(
            0, self.share.at[:, self.half_of(1 - self.y)], self.half_in, self.beside
        )
        self.first.start()

    def spread(self):
        self.first.wait_recv()
        mine = self.share[:, self.half_of(self.y)]
        self.half[...] = (mine.astype(F32) + self.half_in[...].astype(F32)).astype(BF)
        self.out = []
        for d, z in enumerate(self.column):
            copy = self.copy(
                1 + d, self.half.at[:, self.piece_of(z)], self.quarters.at[self.z], 2 * z + self.y
            )
            copy.start()
            self.out.append(copy)
        self.quarters[self.z] = self.half[:, self.piece_of(self.z)]

    def total(self):
        for copy in self.out:
            copy.wait_recv()
        done = self.quarters[0].astype(F32)
        for z in range(1, 4):
            done = done + self.quarters[z].astype(F32)
        piece = self.whole.at[:, self.piece_of(self.z, self.y)]
        piece[...] = done.astype(BF)
        self.back = []
        for d, z in enumerate(self.column):
            copy = self.copy(4 + d, piece, piece, 2 * z + self.y)
            copy.start()
            self.back.append(copy)

    def join(self):
        for copy in self.back:
            copy.wait_recv()
        mine = self.whole.at[:, self.half_of(self.y)]
        self.last = self.copy(7, mine, mine, self.beside)
        self.last.start()

    def finish(self):
        self.last.wait_recv()
        for copy in (self.first, *self.out, *self.back, self.last):
            copy.wait_send()


def reduce_kernel(*refs):
    ca_ref, cb_ref, out_ref, small_ref = refs[:4]
    parts = dict(zip(LATE, refs[4:7], strict=True))
    fin_ref = refs[7]
    count = len(NAMES)
    full = dict(zip(NAMES, refs[8 : 8 + count], strict=True))
    refs = refs[8 + count :]
    late_full = dict(zip(LATE, refs[:3], strict=True))
    small_out, fin_out = refs[3:5]
    refs = refs[5:]
    share = dict(zip(NAMES, refs[:count], strict=True))
    hold = dict(zip(NAMES, refs[count : 2 * count], strict=True))
    refs = refs[2 * count :]
    grid_share, half_in, half, quarters, small_in, small_mid, small_beside, small_column = refs[:8]
    small_send, small_recv, ring_send, ring_recv, grid_send, grid_recv, fin_send, fin_recv = refs[8:16]
    extra = refs[16:]
    fold_wa = Folding(LATE, parts, (extra[0:4], None, extra[4:9]))
    place, after, before = ring_place(RING)
    grids = {
        name: Grid(
            u, grid_share.at[u], half_in.at[u], half.at[u], quarters.at[u], late_full[name], grid_send, grid_recv
        )
        for u, name in enumerate(LATE)
    }
    wa, both = fold_wa.wa, other_wa(fold_wa.across, 1)
    some = grids["q"]
    in_column = [2 * z + some.y for z in some.column]
    meet(
        [{"wa": peer} for peer in (fold_wa.mate, fold_wa.across, both)]
        + [{"ctx": peer} for peer in (after, before, some.beside, *in_column)]
    )
    fold_wa.start()
    near = remote(small_ref, small_in.at[0], small_send.at[0], small_recv.at[0], wa=fold_wa.mate)
    near.start()
    over = remote(small_mid.at[0], small_in.at[1], small_send.at[1], small_recv.at[1], wa=fold_wa.across)
    beside = remote(small_mid.at[1], small_beside, small_send.at[2], small_recv.at[2], ctx=some.beside)
    columns = [
        remote(small_mid.at[2], small_column.at[some.z], small_send.at[3 + d], small_recv.at[3 + d], ctx=peer)
        for d, peer in enumerate(in_column)
    ]
    own_fin = pltpu.make_async_copy(fin_ref.at[wa], fin_out.at[:, columns_of(wa)], fin_send.at[3])
    own_fin.start()
    fin_copies = [
        remote(fin_ref.at[peer], fin_out.at[:, columns_of(wa)], fin_send.at[d], fin_recv.at[d], wa=peer)
        for d, peer in enumerate((fold_wa.across, both, fold_wa.mate))
    ]
    share["cq"][...] = ca_ref[:224]
    share["ck"][...] = ca_ref[224:]
    share["cv"][...] = cb_ref[...]
    share["co"][...] = out_ref[:, :32]
    share["so0"][...] = out_ref[:, 32:48]
    share["so1"][...] = out_ref[:, 48:]
    copies = {}

    def ring_step(b, name, step):
        way = BUFFERS[name][0]
        here = place if way == 1 else RING - place
        target = after if way == 1 else before
        if step > 0:
            copies[name, step - 1].wait_recv()
        if step == 2 * HOPS:
            return
        now = lax.rem(here - step + 3 * RING, RING)
        mine = chunk_of(share[name], name, now)
        done = chunk_of(full[name], name, now)
        if 0 < step <= HOPS:
            total = mine[...].astype(F32) + hold[name][step - 1].astype(F32)
            (mine if step < HOPS else done)[...] = total.astype(BF)
        src, dst = (mine, hold[name].at[step]) if step < HOPS else (done, done)
        copy = remote(src, dst, ring_send.at[b, step], ring_recv.at[b, step], ctx=target)
        copy.start()
        copies[name, step] = copy

    def small_over():
        near.wait_recv()
        small_mid[0] = small_ref[...] + small_in[0]
        over.start()

    def small_next():
        over.wait_recv()
        small_mid[1] = small_mid[0] + small_in[1]
        beside.start()

    def small_last():
        beside.wait_recv()
        small_mid[2] = small_mid[1] + small_beside[...]
        small_column[some.z] = small_mid[2]
        for copy in columns:
            copy.start()

    def begin(name, following=None):
        total = fold_wa.total(name)
        if following:
            fold_wa.x_copies[following].start()
        grids[name].start(total)

    events = {
        0: [
            lambda: fold_wa.send("q"),
            lambda: fold_wa.prepare("k"),
            lambda: fold_wa.prepare("v"),
            small_over,
        ],
        4: [lambda: begin("q", "k"), small_next],
        6: [grids["q"].spread, lambda: begin("k", "v"), small_last],
        8: [grids["q"].total, grids["k"].spread],
        9: [lambda: begin("v"), grids["q"].join, *(copy.start for copy in fin_copies)],
        10: [grids["k"].total],
        11: [grids["v"].spread, grids["k"].join],
        12: [grids["v"].total],
        14: [grids["v"].join],
    }
    for tick in range(2 * HOPS + 1):
        for b, name in enumerate(NAMES):
            ring_step(b, name, tick)
        for event in events.get(tick, ()):
            event()
    for copy in columns:
        copy.wait_recv()
    total = small_column[0]
    for z in range(1, 4):
        total = total + small_column[z]
    small_out[...] = total
    for name in LATE:
        grids[name].finish()
    fold_wa.finish()
    for copy in (near, over, beside, *columns, *copies.values()):
        copy.wait_send()
    own_fin.wait()
    for copy in fin_copies:
        copy.wait()


def columns_of(owner):
    return pl.ds(pl.multiple_of(owner * 896, WIDE), 896)


def reduce_grads(pair, one, flat, small, parts, fin):
    dma = pltpu.SemaphoreType.DMA
    any_spec = pl.BlockSpec(memory_space=pl.ANY)
    late = len(LATE)
    return pl.pallas_call(
        reduce_kernel,
        out_shape=(
            *(jax.ShapeDtypeStruct(BUFFERS[b][1], BF) for b in NAMES),
            *[jax.ShapeDtypeStruct(TALL, BF)] * late,
            jax.ShapeDtypeStruct(small.shape, F32),
            jax.ShapeDtypeStruct((224, 3584), BF),
        ),
        in_specs=vmem(4) + [any_spec] * 4,
        out_specs=(*vmem(len(NAMES) + late + 1), any_spec),
        scratch_shapes=[
            *(pltpu.VMEM(BUFFERS[b][1], BF) for b in NAMES),
            *(pltpu.VMEM((HOPS, *chunk_shape(b)), BF) for b in NAMES),
            pltpu.VMEM((late, *TALL), BF),
            pltpu.VMEM((late, 224, 4 * WIDE), BF),
            pltpu.VMEM((late, 224, 4 * WIDE), BF),
            pltpu.VMEM((late, 4, 224, WIDE), BF),
            pltpu.VMEM((2, *small.shape), F32),
            pltpu.VMEM((3, *small.shape), F32),
            pltpu.VMEM(small.shape, F32),
            pltpu.VMEM((4, *small.shape), F32),
            dma((6,)),
            dma((6,)),
            dma((len(NAMES), 2 * HOPS)),
            dma((len(NAMES), 2 * HOPS)),
            dma((late, 8)),
            dma((late, 8)),
            dma((4,)),
            dma((3,)),
            *Folding.scratch(LATE),
        ],
        compiler_params=pltpu.CompilerParams(
            collective_id=3, has_side_effects=True, vmem_limit_bytes=56 << 20
        ),
        cost_estimate=lasting(90),
        name="reduce_grads",
    )(pair, one, flat, small, *parts, fin.reshape(4, 224, 896))


def unfold(full):
    wide = {name: value.astype(F32) for name, value in full.items()}
    return {
        "co": wide["co"].reshape(FLAT),
        "so": jnp.concatenate([wide["so0"], wide["so1"]], 1).reshape(FLAT),
        **{name: wide[name] for name in ("cq", "ck", "cv", *LATE)},
    }


GELU = (2.0 / math.pi) ** 0.5


def ffn_kernel(
    f_ref, cot_ref, win_ref, wout_ref, bias_ref, res_ref, df_ref, dwin_ref, dwout_ref, dbias_ref,
    f_all, g_all, dul_all, own, kept, out_mate, out_cross, in_mate, in_cross, x_out, x_in,
    f_send, f_recv, p_send, p_recv,
):
    me = lax.axis_index("wa")
    mate, across = other_wa(me, 1), other_wa(me, 2)
    both = other_wa(across, 1)
    barrier = pltpu.get_barrier_semaphore()
    for peer in (mate, across):
        pl.semaphore_signal(barrier, inc=1, device_id={"wa": peer}, device_id_type=MESH)
    pl.semaphore_wait(barrier, 2)
    to_across = remote(f_ref, f_all.at[me], f_send.at[1], f_recv.at[1], wa=across)
    to_across.start()
    to_mate = remote(f_ref, f_all.at[me], f_send.at[0], f_recv.at[0], wa=mate)
    to_mate.start()
    forward = remote(f_all.at[across], f_all.at[across], f_send.at[2], f_recv.at[2], wa=mate)
    f_all[me] = f_ref[...]
    order = (me, mate, across, both)
    dbias_ref[...] = jnp.zeros_like(dbias_ref)
    for k, s in enumerate(order):
        if k == 1:
            to_mate.wait_recv()
        if k == 2:
            to_across.wait_recv()
            forward.start()
        if k == 3:
            forward.wait_recv()
        u = nn_dot(f_all[s], win_ref[...]) + bias_ref[...]
        square = u * u
        t = jnp.tanh(GELU * (u + 0.044715 * (square * u)))
        g_all[s] = (0.5 * u * (1.0 + t)).astype(BF)
        slope = 0.5 * (1.0 + t) + 0.5 * u * (1.0 - t * t) * (GELU * (1.0 + 3 * 0.044715 * square))
        du = nt_dot(cot_ref[s], wout_ref[...]) * slope
        dbias_ref[...] += jnp.sum(du.reshape(32, 8, du.shape[1]), axis=0)
        dul_all[s] = du.astype(BF)

    def scatter(which, product):
        out_cross[which] = product(both).astype(BF)
        cross = remote(
            out_cross.at[which], in_cross.at[which], p_send.at[which, 0], p_recv.at[which, 0], wa=mate
        )
        cross.start()
        kept[...] = product(across)
        cross.wait_recv()
        x_out[which] = (kept[...] + in_cross[which].astype(F32)).astype(BF)
        over = remote(
            x_out.at[which], x_in.at[which], p_send.at[which, 1], p_recv.at[which, 1], wa=across
        )
        over.start()
        out_mate[which] = product(mate).astype(BF)
        near = remote(
            out_mate.at[which], in_mate.at[which], p_send.at[which, 2], p_recv.at[which, 2], wa=mate
        )
        near.start()
        own[which] = product(me)
        return cross, over, near

    def finish(which, copies, out_ref):
        cross, over, near = copies
        near.wait_recv()
        over.wait_recv()
        out_ref[...] = own[which] + in_mate[which].astype(F32) + x_in[which].astype(F32)
        for copy in copies:
            copy.wait_send()

    df_copies = scatter(0, lambda s: nt_dot(dul_all[s], win_ref[...]))
    res_copies = scatter(1, lambda s: nn_dot(g_all[s], wout_ref[...]))
    width = f_ref.shape[1]

    def outer(left_all, right, out_ref):
        for c in range(width // WIDE):
            lanes = slice(c * WIDE, (c + 1) * WIDE)
            total = None
            for s in range(4):
                left = left_all[s, :, lanes].astype(F32).T.astype(BF)
                now = nn_dot(left, right[s])
                total = now if total is None else total + now
            out_ref[lanes, :] = total.astype(BF)

    outer(f_all, dul_all, dwin_ref)
    outer(g_all, cot_ref, dwout_ref)
    finish(0, df_copies, df_ref)
    finish(1, res_copies, res_ref)
    for copy in (to_mate, to_across, forward):
        copy.wait_send()


def ffn(f_low, cot_all, win, wout, bias):
    rows, width = f_low.shape
    hidden = win.shape[1]
    dma = pltpu.SemaphoreType.DMA
    block = (rows, width)
    return pl.pallas_call(
        ffn_kernel,
        out_shape=(
            jax.ShapeDtypeStruct(block, F32),
            jax.ShapeDtypeStruct(block, F32),
            jax.ShapeDtypeStruct(win.shape, BF),
            jax.ShapeDtypeStruct(wout.shape, BF),
            jax.ShapeDtypeStruct((8, hidden), F32),
        ),
        in_specs=vmem(5),
        out_specs=tuple(vmem(5)),
        scratch_shapes=[
            pltpu.VMEM((4, *block), BF),
            pltpu.VMEM((4, rows, hidden), BF),
            pltpu.VMEM((4, rows, hidden), BF),
            pltpu.VMEM((2, *block), F32),
            pltpu.VMEM(block, F32),
            *[pltpu.VMEM((2, *block), BF)] * 6,
            dma((3,)),
            dma((3,)),
            dma((2, 3)),
            dma((2, 3)),
        ],
        compiler_params=pltpu.CompilerParams(
            collective_id=4, has_side_effects=True, vmem_limit_bytes=56 << 20
        ),
        cost_estimate=lasting(44),
        name="feed_forward",
    )(f_low, cot_all, win, wout, bias)


def padded_rows(pad, values):
    rows = values.shape[0]
    pad[...] = jnp.zeros_like(pad)
    pad[1 : rows + 1, :] = values.astype(F32)


def both_heads(pad, g):
    here = pad[g * SPAN : (g + 1) * SPAN, :]
    left = head_mask(0, SPAN)
    return jnp.concatenate([jnp.where(left, here, 0.0), jnp.where(left, 0.0, here)], 0).astype(BF)


def join_heads(stacked):
    return jnp.where(head_mask(0, SPAN), stacked[:SPAN], stacked[SPAN:])


def cross_forward_kernel(groups, keep_ref, q_ref, k_ref, v_ref, x_ref, q_pad, x_pad):
    padded_rows(q_pad, q_ref[...])
    for g in range(groups):
        rows = slice(g * 256, (g + 1) * 256)
        query = both_heads(q_pad, g) * BF(HD**-0.5)
        scores = nt_dot(query, k_ref[rows, :])
        weights = jnp.exp(scores - jnp.max(scores, axis=1, keepdims=True))
        weights = weights / jnp.sum(weights, axis=1, keepdims=True)
        mixed = join_heads(nn_dot(weights.astype(BF), v_ref[rows, :]))
        if g == 0:
            mixed = mixed * keep_ref[0:1, :]
        x_pad[g * SPAN : (g + 1) * SPAN, :] = mixed
    x_ref[...] = x_pad[1 : x_ref.shape[0] + 1, :].astype(BF)


def pair_specs(*rows):
    return [pl.BlockSpec((r, WIDE), lambda p: (0, p)) for r in rows]


def cross_forward(keep, query, keys, values):
    rows, width = query.shape
    many = keys.shape[0]
    groups = many // 256
    return pl.pallas_call(
        functools.partial(cross_forward_kernel, groups),
        grid=(width // WIDE,),
        out_shape=jax.ShapeDtypeStruct(query.shape, BF),
        in_specs=[pl.BlockSpec((8, WIDE), lambda p: (0, 0)), *pair_specs(rows, many, many)],
        out_specs=pair_specs(rows)[0],
        scratch_shapes=[pltpu.VMEM((groups * SPAN, WIDE), F32)] * 2,
        compiler_params=pltpu.CompilerParams(vmem_limit_bytes=16 << 20),
        cost_estimate=lasting(9),
        name="cross_forward",
    )(keep, query, keys, values)


def cross_backward_kernel(
    groups, keep_ref, q_ref, dx_ref, k_ref, v_ref, dq_ref, dk_ref, dv_ref, q_pad, dx_pad, dq_pad
):
    padded_rows(q_pad, q_ref[...])
    padded_rows(dx_pad, dx_ref[...])
    dx_pad[:SPAN, :] = dx_pad[:SPAN, :] * keep_ref[0:1, :]
    for g in range(groups):
        rows = slice(g * 256, (g + 1) * 256)
        query = both_heads(q_pad, g) * BF(HD**-0.5)
        dmixed = both_heads(dx_pad, g)
        keys, values = k_ref[rows, :], v_ref[rows, :]
        scores = nt_dot(keys, query)
        weights = jnp.exp(scores - jnp.max(scores, axis=0, keepdims=True))
        weights = weights / jnp.sum(weights, axis=0, keepdims=True)
        dweights = nt_dot(values, dmixed)
        dscores = weights * (dweights - jnp.sum(weights * dweights, axis=0, keepdims=True))
        dk_ref[rows, :] = nn_dot(dscores.astype(BF), query).astype(BF)
        dv_ref[rows, :] = nn_dot(weights.astype(BF), dmixed).astype(BF)
        back = (dscores * HD**-0.5).T.astype(BF)
        dq_pad[g * SPAN : (g + 1) * SPAN, :] = join_heads(nn_dot(back, keys))
    dq_ref[...] = dq_pad[1 : dq_ref.shape[0] + 1, :].astype(BF)


def cross_backward(keep, query, dmixed, keys, values):
    rows, width = query.shape
    many = keys.shape[0]
    groups = many // 256
    return pl.pallas_call(
        functools.partial(cross_backward_kernel, groups),
        grid=(width // WIDE,),
        out_shape=(
            jax.ShapeDtypeStruct(query.shape, BF),
            jax.ShapeDtypeStruct(keys.shape, BF),
            jax.ShapeDtypeStruct(keys.shape, BF),
        ),
        in_specs=[
            pl.BlockSpec((8, WIDE), lambda p: (0, 0)),
            *pair_specs(rows, rows, many, many),
        ],
        out_specs=tuple(pair_specs(rows, many, many)),
        scratch_shapes=[pltpu.VMEM((groups * SPAN, WIDE), F32)] * 3,
        compiler_params=pltpu.CompilerParams(vmem_limit_bytes=16 << 20),
        cost_estimate=lasting(17),
        name="cross_backward",
    )(keep, query, dmixed, keys, values)


def line_selector():
    place = jnp.arange(LINE)
    offset = jnp.where(place < LINE // 2, -place, LINE - place)
    return (bucket_of(offset)[None, :] == jnp.arange(NB)[:, None]).astype(jnp.float32)


def ring_forward(query_low, key_low, value_low, bucket_table):
    row_count, attn_width = query_low.shape
    position = lax.axis_index("ctx")
    scale_factor = HD ** (-0.5)
    bias_set, onehots = make_bias(bucket_table.astype(jnp.float32), row_count)
    query_heads = query_low.reshape(row_count, H, HD)
    start_state = (
        jnp.full((H, row_count), negative, jnp.float32),
        jnp.zeros((H, row_count), jnp.float32),
        jnp.zeros((row_count, attn_width), jnp.float32),
    )
    running_max, running_sum, running_acc = forward_fold(
        query_heads,
        position,
        row_count,
        bias_set,
        scale_factor,
        start_state,
        (
            lax.all_gather(key_low, "ctx", axis=0, tiled=True),
            lax.all_gather(value_low, "ctx", axis=0, tiled=True),
        ),
    )
    attended = (running_acc.reshape(row_count, H, HD) / running_sum.T[:, :, None]).reshape(
        row_count, attn_width
    )
    log_total = running_max + jnp.log(running_sum)
    state = (query_heads, key_low, value_low, attended, log_total, bias_set, onehots)
    return attended.astype(jnp.bfloat16), state


def ring_backward(state, dout_low):
    query_heads, key_low, value_low, attended, log_total, bias_set, onehots = state
    row_count, attn_width = dout_low.shape
    cycle_size = lax.axis_size("ctx")
    position = lax.axis_index("ctx")
    scale_factor = HD ** (-0.5)
    dout_heads = dout_low.reshape(row_count, H, HD)
    row_delta = jnp.sum(
        (dout_low.astype(jnp.float32) * attended).reshape(row_count, H, HD), axis=-1
    ).T
    zero_rows = jnp.zeros((row_count, attn_width), jnp.float32)
    zero_tables = (
        jnp.zeros((H, row_count, row_count), jnp.float32),
        jnp.zeros((H, row_count, row_count), jnp.float32),
        jnp.zeros((H,), jnp.float32),
    )

    def visit(folded, key_now, value_now, relation):

        def visit_compute(current):
            dquery_acc, dkey_acc, dvalue_acc, relative_bias_tables = current
            key_heads = key_now.reshape(row_count, H, HD)
            weights_now, dscores, ds_low = pair_core(
                query_heads,
                dout_heads,
                log_total,
                row_delta,
                key_heads,
                value_now.reshape(row_count, H, HD),
                relation,
                bias_set,
                scale_factor,
            )
            dquery = jnp.einsum(
                "hqk,khd->qhd", ds_low, key_heads, preferred_element_type=jnp.float32
            ).reshape(row_count, attn_width)
            dkey = jnp.einsum(
                "hqk,qhd->khd", ds_low, query_heads, preferred_element_type=jnp.float32
            ).reshape(row_count, attn_width)
            dvalue = jnp.einsum(
                "hqk,qhd->khd",
                weights_now.astype(jnp.bfloat16),
                dout_heads,
                preferred_element_type=jnp.float32,
            ).reshape(row_count, attn_width)
            return (
                dquery_acc + dquery,
                dkey_acc + dkey,
                dvalue_acc + dvalue,
                add_tables(relative_bias_tables, dscores, relation),
            )

        return lax.cond(relation >= 0, visit_compute, lambda unchanged: unchanged, folded)

    first_state = visit(
        (zero_rows, zero_rows, zero_rows, zero_tables), key_low, value_low, jnp.array(0, jnp.int32)
    )

    def cycle_step(carried, cycle_index):
        key_now, value_now, (dquery_acc, dkey_acc, dvalue_acc, relative_bias_tables) = carried
        key_next, value_next = passed_along((key_now, value_now), "ctx", 1)
        dkey_next, dvalue_next = (
            from_behind(dkey_acc.astype(jnp.bfloat16), "ctx", 1).astype(dkey_acc.dtype),
            from_behind(dvalue_acc.astype(jnp.bfloat16), "ctx", 1).astype(dvalue_acc.dtype),
        )
        relation = jnp.where(position >= cycle_index, cycle_index, -1)
        updated = visit(
            (dquery_acc, dkey_next, dvalue_next, relative_bias_tables),
            key_next,
            value_next,
            relation,
        )
        return ((key_next, value_next, updated), None)

    (
        unused_key,
        unused_value,
        (dquery_total, dkey_part, dvalue_part, relative_bias_tables),
    ), unused = lax.scan(cycle_step, (key_low, value_low, first_state), jnp.arange(1, cycle_size))
    dkey_total, dvalue_total = (
        from_behind(dkey_part.astype(jnp.bfloat16), "ctx", 1).astype(dkey_part.dtype),
        from_behind(dvalue_part.astype(jnp.bfloat16), "ctx", 1).astype(dvalue_part.dtype),
    )
    dquery_low = dquery_total.astype(jnp.bfloat16)
    dkey_low = dkey_total.astype(jnp.bfloat16)
    dvalue_low = dvalue_total.astype(jnp.bfloat16)
    current_bucket_selector, previous_bucket_selector, onehot_far = onehots
    grad_biastable = (
        jnp.einsum(
            "afw,mfw->am",
            current_bucket_selector,
            relative_bias_tables[0],
            precision=strongest_precision,
        )
        + jnp.einsum(
            "afw,mfw->am",
            previous_bucket_selector,
            relative_bias_tables[1],
            precision=strongest_precision,
        )
        + onehot_far[:, None] * relative_bias_tables[2][None, :]
    )
    return dquery_low, dkey_low, dvalue_low, grad_biastable


def heads_forward(tokens, near, cotangent, given):
    wa, owners = lax.axis_index("wa"), lax.axis_size("wa")
    table = given["biastable"].astype(F32)
    selector = lax.dynamic_slice_in_dim(line_selector(), wa * table.shape[0], table.shape[0], 0)
    lines = jnp.dot(table.T, selector, precision=strongest_precision).astype(BF)
    gains = jnp.concatenate([given[name] for name in GAINS]).reshape(len(GAINS), -1)
    small = jnp.zeros((H, LINE), BF)
    small = lax.dynamic_update_slice(small, gains, (0, wa * gains.shape[1]))
    small = jnp.concatenate([lines, small], 0)
    shards = [given[LONG_NAMES[name]] for name in GATHERED]
    *wholes, upstream_all, feed_in, attended_low, low, qh, kh, vh, ot, lse, small, before, keys, values = attn_forward(
        lax.axis_size("ctx"), tokens, small, near, [*shards, cotangent], given["feedin"]
    )
    width = tokens.shape[1]
    gain_of = {name: small[H + g, :width] for g, name in enumerate(GAINS)}
    full = {LONG_NAMES[name]: whole for name, whole in zip(GATHERED, wholes, strict=True)}
    full["feedin"] = feed_in
    upstream_all = upstream_all.reshape(owners, *tokens.shape)
    saved = (qh, kh, vh, ot, lse, small[:H])
    return attended_low, low, full, gain_of, upstream_all, (before, keys, values), saved


def heads_backward(state, dout_low, parts, feed_part):
    peers = lax.axis_size("ctx")
    dquery_low, dkey_low, dvalue_low, sums, *shares = attn_backward(
        peers, dout_low, *state, parts, feed_part
    )
    selector = line_selector()
    table = jnp.dot(selector, sums[:2].T, precision=strongest_precision)
    far = jnp.sum(sums[2:4], axis=1)
    table = table + selector[:, WIDE : WIDE + 1] * far[None, :]
    whole = jnp.zeros((NB, H), jnp.float32)
    whole = lax.dynamic_update_slice(whole, table, (0, 2 * lax.axis_index("ctx")))
    return dquery_low, dkey_low, dvalue_low, whole, shares


def cross_pair(groups, keep_ref, q_ref, dx_ref, k_ref, v_ref, dq_ref, dk_ref, dv_ref, q_pad, dx_pad, dq_pad, p):
    lanes = lanes_of(p)
    padded_rows(q_pad, q_ref[:, lanes])
    padded_rows(dx_pad, dx_ref[:, lanes])
    dx_pad[:SPAN, :] = dx_pad[:SPAN, :] * keep_ref[0:1, :]
    for g in range(groups):
        rows = slice(g * 256, (g + 1) * 256)
        query = both_heads(q_pad, g) * BF(HD**-0.5)
        dmixed = both_heads(dx_pad, g)
        keys, values = k_ref[rows, lanes], v_ref[rows, lanes]
        scores = nt_dot(keys, query)
        weights = jnp.exp(scores - jnp.max(scores, axis=0, keepdims=True))
        weights = weights / jnp.sum(weights, axis=0, keepdims=True)
        dweights = nt_dot(values, dmixed)
        dscores = weights * (dweights - jnp.sum(weights * dweights, axis=0, keepdims=True))
        dk_ref[rows, lanes] = nn_dot(dscores.astype(BF), query).astype(BF)
        dv_ref[rows, lanes] = nn_dot(weights.astype(BF), dmixed).astype(BF)
        back = (dscores * HD**-0.5).T.astype(BF)
        dq_pad[g * SPAN : (g + 1) * SPAN, :] = join_heads(nn_dot(back, keys))
    dq_ref[:, lanes] = dq_pad[1 : dq_ref.shape[0] + 1, :].astype(BF)


def middle_kernel(
    keep_ref, q_ref, dx_ref, k_ref, v_ref, before_ref, near_ref, wk_ref, wv_ref, fin_ref, fout_ref,
    dq_ref, dwk_ref, dwv_ref, first_out, near_out, last_out, feed_out,
    dk, dv, q_pad, dx_pad, dq_pad, share, hold, load_sem, ring_send, ring_recv,
):
    ring = Ring(FEED_LANES, ring_send, ring_recv, share=share, hold=hold)
    loads = [
        pltpu.make_async_copy(part, share.at[b], load_sem.at[b])
        for b, part in enumerate((fin_ref, fout_ref))
    ]
    for load in loads:
        load.start()
    meet([{"ctx": ring.after}, {"ctx": ring.before}])
    for load in loads:
        load.wait()
    for lanes in FEED_TURNS:
        ring.scatter(jnp.int32(0), lanes)
    groups = k_ref.shape[0] // 256

    def two_pairs(m, unused):
        for turn, lanes in enumerate(FEED_TURNS):
            cross_pair(
                groups, keep_ref, q_ref, dx_ref, k_ref, v_ref, dq_ref, dk, dv, q_pad, dx_pad, dq_pad,
                2 * m + turn,
            )
            ring.scatter(m + 1, lanes)
        return unused

    pairs = q_ref.shape[1] // (2 * WIDE)
    lax.fori_loop(0, pairs, two_pairs, 0)
    calls = [(step, lanes) for step in range(pairs + 1, HOPS + 1) for lanes in FEED_TURNS]

    def turn():
        if calls:
            step, lanes = calls.pop(0)
            ring.scatter(jnp.int32(step), lanes)

    for g in range(groups):
        rows = slice(g * 256, (g + 1) * 256)
        total = nt_dot(dk[rows, :], wk_ref[...]) + nt_dot(dv[rows, :], wv_ref[...])
        if g == 0:
            first_out[...] = total.astype(BF)
        elif g == groups - 1:
            last_out[...] = total
        else:
            near_out[(g - 1) * 256 : g * 256, :] = total.astype(BF)
        if g % 2 == 1:
            turn()
    for c in range(near_ref.shape[1] // WIDE):
        lanes = slice(c * WIDE, (c + 1) * WIDE)
        first = before_ref[:, lanes].astype(F32).T.astype(BF)
        left = near_ref[:, lanes].astype(F32).T.astype(BF)
        for grads, out_ref in ((dk, dwk_ref), (dv, dwv_ref)):
            total = nn_dot(first, grads[:256, :]) + nn_dot(left, grads[256:, :])
            out_ref[lanes, :] = total.astype(BF)
        if c % 2 == 1:
            turn()
    while calls:
        turn()
    for lane in range(2):
        feed_out[lane] = share[lane, ring.chunk(lane, 1)]
    ring.finish(lambda lane: share.at[FEED_LANES[lane][0], 0, FEED_LANES[lane][2]])


def middle(keep, query, dmixed, keys, values, before, near, wk, wv, fin, fout):
    many, width = keys.shape
    wide = near.shape[1]
    low = functools.partial(jax.ShapeDtypeStruct, dtype=BF)
    dma = pltpu.SemaphoreType.DMA
    pad = pltpu.VMEM((many // 256 * SPAN, WIDE), F32)
    return pl.pallas_call(
        middle_kernel,
        out_shape=(
            low(query.shape),
            low(wk.shape),
            low(wv.shape),
            low((256, wide)),
            low((many - 512, wide)),
            jax.ShapeDtypeStruct((256, wide), F32),
            low((2, *FEED[1:])),
        ),
        in_specs=vmem(9) + [pl.BlockSpec(memory_space=pl.ANY)] * 2,
        out_specs=tuple(vmem(7)),
        scratch_shapes=[
            pltpu.VMEM((many, width), BF),
            pltpu.VMEM((many, width), BF),
            pad,
            pad,
            pad,
            pltpu.VMEM((2, *FEED), BF),
            pltpu.VMEM((2, HOPS, *FEED[1:]), BF),
            dma((2,)),
            dma((len(FEED_LANES), HOPS)),
            dma((len(FEED_LANES), HOPS)),
        ],
        compiler_params=pltpu.CompilerParams(
            collective_id=5, has_side_effects=True, vmem_limit_bytes=56 << 20
        ),
        cost_estimate=lasting(38),
        name="middle",
    )(keep, query, dmixed, keys, values, before, near, wk, wv, fin.reshape(FEED), fout.reshape(FEED))


NAMES_OF_WEIGHTS = (
    "selfnorm", "selfquery", "selfkey", "selfvalue", "selfout", "biastable", "crossnorm", "crossquery",
    "crosskey", "crossvalue", "crossout", "feednorm", "feedin", "feedbias", "feedout", "outbias",
)
LONG_NAMES = {
    "q": "selfquery",
    "k": "selfkey",
    "v": "selfvalue",
    "so": "selfout",
    "ck": "crosskey",
    "cv": "crossvalue",
    "cq": "crossquery",
    "co": "crossout",
}


def whole_over_wa(shard):
    return lax.all_gather(shard, "wa", axis=0, tiled=True)


def reduce_plain(parts, smalls):
    shares = [
        lax.psum_scatter(part, "wa", scatter_dimension=0, tiled=True).astype(F32)
        for part in parts.values()
    ]
    totals = lax.psum(shares, "ctx")
    return dict(zip(parts, totals, strict=True)), lax.psum(smalls, ("ctx", "wa"))


def per_device(tokens, neighbours, cotangent, *shards):
    given = dict(zip(NAMES_OF_WEIGHTS, shards, strict=True))
    peers = lax.axis_size("ctx")
    position = lax.axis_index("ctx")
    row_count, model_width = tokens.shape[1:]
    split_heads = peers * 2 == H and row_count == BLOCK
    inputs = tokens[0].astype(F32)
    upstream_low = cotangent[0]
    upstream = upstream_low.astype(F32)
    spans = neighbours.shape[1]
    span_rows = neighbours.shape[2] * neighbours.shape[3]
    own_rows = neighbours[0].reshape(spans * span_rows, model_width)
    if split_heads and span_rows == BLOCK:
        attended_low, normed_low, full, small_of, upstream_all, projected, attention_state = (
            heads_forward(tokens[0], own_rows, upstream_low, given)
        )
        before, keys_cross, values_cross = projected
        feed_in = full["feedin"]
        normed_self, back_self = jax.vjp(root_norm, inputs, small_of["selfnorm"])
    else:
        small_of = {name: whole_over_wa(given[name]).astype(F32) for name in GAINS}
        full = {name: whole_over_wa(given[name]) for name in LONG_NAMES.values()}
        normed_self, back_self = jax.vjp(root_norm, inputs, small_of["selfnorm"])
        normed_low = normed_self.astype(BF)
        attended_low, attention_state = ring_forward(
            *(
                forward_product(normed_low, full[name]).astype(BF)
                for name in ("selfquery", "selfkey", "selfvalue")
            ),
            whole_over_wa(given["biastable"]),
        )
        upstream_all = lax.all_gather(upstream_low, "wa", axis=0)
        feed_in = lax.all_to_all(given["feedin"], "wa", 1, 0, tiled=True)
        before = passed_along(own_rows[-span_rows:], "ctx", 1)
        near_rows = jnp.concatenate([before, own_rows], 0)
        keys_cross = forward_product(near_rows, full["crosskey"]).astype(BF)
        values_cross = forward_product(near_rows, full["crossvalue"]).astype(BF)
    hidden = inputs + forward_product(attended_low, full["selfout"])

    normed_cross, back_cross = jax.vjp(root_norm, hidden, small_of["crossnorm"])
    cross_in = normed_cross.astype(BF)
    query_cross = forward_product(cross_in, full["crossquery"]).astype(BF)
    keep = jnp.full((8, WIDE), jnp.where(position > 0, 1.0, 0.0), F32)
    mixed_low = cross_forward(keep, query_cross, keys_cross, values_cross)
    hidden_two = hidden + forward_product(mixed_low, full["crossout"])

    normed_feed, back_feed = jax.vjp(root_norm, hidden_two, small_of["feednorm"])
    feed_low = normed_feed.astype(BF)
    bias_row = given["feedbias"].astype(F32)[None]
    fed, grad_feed, fin, fout, bias_sums = ffn(
        feed_low, upstream_all, feed_in, given["feedout"], bias_row
    )
    result = (hidden_two + fed + small_of["outbias"]).astype(BF)
    grad_two_part, grad_feednorm = back_feed(grad_feed)
    grad_two = upstream + grad_two_part
    two_low = grad_two.astype(BF)

    grad_mixed = back_product(two_low, full["crossout"]).astype(BF)
    early = {}
    if split_heads:
        grad_query_cross, early["ck"], early["cv"], first, near_low, near_last, feed_part = middle(
            keep,
            query_cross,
            grad_mixed,
            keys_cross,
            values_cross,
            before,
            own_rows,
            full["crosskey"],
            full["crossvalue"],
            fin,
            fout,
        )
    else:
        grad_query_cross, dkeys, dvalues = cross_backward(
            keep, query_cross, grad_mixed, keys_cross, values_cross
        )
        near_grads = back_product(dkeys, full["crosskey"]) + back_product(
            dvalues, full["crossvalue"]
        )
        first, near_last = near_grads[:span_rows].astype(BF), near_grads[-span_rows:]
        near_low = near_grads[span_rows:-span_rows].astype(BF)
        early["ck"] = outer_product(near_rows, dkeys).astype(BF)
        early["cv"] = outer_product(near_rows, dvalues).astype(BF)
    back = passed_along(first, "ctx", -1).astype(F32)
    grad_hidden_part, grad_crossnorm = back_cross(
        back_product(grad_query_cross, full["crossquery"])
    )
    grad_hidden = grad_two + grad_hidden_part
    hidden_low = grad_hidden.astype(BF)
    dout_low = back_product(hidden_low, full["selfout"]).astype(BF)
    early["cq"] = outer_product(cross_in, grad_query_cross).astype(BF)
    early["co"] = outer_product(mixed_low, two_low).astype(BF)
    early["so"] = outer_product(attended_low, hidden_low).astype(BF)
    if split_heads:
        dquery_low, dkey_low, dvalue_low, grad_biastable, shares = heads_backward(
            attention_state, dout_low, [early[name] for name in EARLY], feed_part
        )
        *shares, fin, fout = shares
    else:
        dquery_low, dkey_low, dvalue_low, grad_biastable = ring_backward(attention_state, dout_low)
    grad_normed = (
        back_product(dquery_low, full["selfquery"])
        + back_product(dkey_low, full["selfkey"])
        + back_product(dvalue_low, full["selfvalue"])
    )
    grad_input_part, grad_selfnorm = back_self(grad_normed)
    grad_inputs = (grad_hidden + grad_input_part).astype(BF)

    grad_neigh = (
        jnp.concatenate([near_low, (near_last + back).astype(BF)], 0)
        .reshape(neighbours.shape)
    )
    late = {
        "q": outer_product(normed_low, dquery_low).astype(BF),
        "k": outer_product(normed_low, dkey_low).astype(BF),
        "v": outer_product(normed_low, dvalue_low).astype(BF),
    }
    wa, owners = lax.axis_index("wa"), lax.axis_size("wa")
    bias_grad = jnp.sum(bias_sums, axis=0)
    placed = lax.dynamic_update_slice(
        jnp.zeros((owners, bias_grad.size), F32), bias_grad[None], (wa, 0)
    )
    sums = [grad_selfnorm, grad_crossnorm, grad_feednorm, jnp.sum(upstream, axis=0), grad_biastable]
    packed = jnp.concatenate([*(v.reshape(owners, -1) for v in sums), placed], axis=1)
    packed = jnp.pad(packed, ((0, 0), (0, LINE * 2 - packed.shape[1]))).reshape(-1, WIDE)
    if split_heads:
        *reduced, packed, fin = reduce_grads(
            *shares, packed, [late[name] for name in LATE], fin
        )
        grads = unfold(dict(zip((*NAMES, *LATE), reduced, strict=True)))
        fout = fout.reshape(given["feedout"].shape)
    else:
        grads, packed = reduce_plain(early | late, packed)
        fin, fout = lax.psum((fin, fout), "ctx")
        fin = lax.all_to_all(fin, "wa", 0, 1, tiled=True)
    grads["fin"], grads["fout"] = fin.astype(F32), fout.astype(F32)
    mine = lax.dynamic_index_in_dim(packed.reshape(owners, -1), wa, 0, keepdims=False)
    cuts, start = [], 0
    for v in (*sums, placed):
        cuts.append(mine[start : start + v.size // owners])
        start += v.size // owners
    own_selfnorm, own_crossnorm, own_feednorm, own_outbias, own_table, own_feedbias = cuts
    return (
        result[None],
        grad_inputs[None],
        grad_neigh,
        own_selfnorm,
        grads["q"],
        grads["k"],
        grads["v"],
        grads["so"],
        own_table.reshape(-1, H),
        own_crossnorm,
        grads["cq"],
        grads["ck"],
        grads["cv"],
        grads["co"],
        own_feednorm,
        grads["fin"],
        own_feedbias,
        grads["fout"],
        own_outbias,
    )


def solution(mesh):
    return jax.shard_map(
        per_device,
        mesh=mesh,
        in_specs=(
            P("wa", "ctx", None),
            P("wa", "ctx", None, None, None),
            P("wa", "ctx", None),
            P("wa"),
            P("wa", None),
            P("wa", None),
            P("wa", None),
            P("wa", None),
            P("wa", None),
            P("wa"),
            P("wa", None),
            P("wa", None),
            P("wa", None),
            P("wa", None),
            P("wa"),
            P("wa", None),
            P("wa"),
            P("wa", None),
            P("wa"),
        ),
        out_specs=(
            P("wa", "ctx", None),
            P("wa", "ctx", None),
            P("wa", "ctx", None, None, None),
            P("wa"),
            P("wa", None),
            P("wa", None),
            P("wa", None),
            P("wa", None),
            P("wa", None),
            P("wa"),
            P("wa", None),
            P("wa", None),
            P("wa", None),
            P("wa", None),
            P("wa"),
            P("wa", None),
            P("wa"),
            P("wa", None),
            P("wa"),
        ),
        check_vma=False,
    )
```

```python
import functools
import math

import jax
import jax.numpy as jnp
from jax import lax
from jax.experimental import pallas as pl
from jax.experimental.pallas import tpu as pltpu
from jax.sharding import PartitionSpec as P

H = 16
HD = 64
NB = 32
MAXD = 128
BLOCK = 256
SPAN = 64
MESH = pl.DeviceIdType.MESH
WIDE = 128
LINE = 1024
BF = jnp.bfloat16
F32 = jnp.float32


epsilon = 1e-06
negative = -1e30
strongest_precision = lax.Precision.HIGHEST


def passed_along(value, axis, by):
    peers = lax.axis_size(axis)
    pairs = [(i, i + by) for i in range(peers) if 0 <= i + by < peers]
    return lax.ppermute(value, axis, pairs)


def from_behind(block, axis, distance):
    devices = range(lax.axis_size(axis))
    route = [((i - distance) % len(devices), i) for i in devices]
    return lax.ppermute(block, axis, route)


def bucket_edges():
    half_count = NB // 2
    exact_part = half_count // 2
    edge_list = []
    for level_index in range(exact_part + 1, half_count):
        hits = [
            distance_now
            for distance_now in range(exact_part, MAXD + 1)
            if exact_part
            + int(
                math.log(distance_now / exact_part)
                / math.log(MAXD / exact_part)
                * (half_count - exact_part)
            )
            >= level_index
        ]
        edge_list.append(min(hits + [MAXD]))
    return (half_count, exact_part, edge_list)


def bucket_of(offset_value):
    half_count, exact_part, edge_list = bucket_edges()
    magnitude = jnp.abs(offset_value)
    far_part = exact_part + sum(
        [(magnitude >= edge_value).astype(magnitude.dtype) for edge_value in edge_list],
        jnp.zeros_like(magnitude),
    )
    return jnp.where(offset_value > 0, half_count, 0) + jnp.where(
        magnitude < exact_part, magnitude, far_part
    )


def root_norm(values, gain_vector):
    return (
        values
        * lax.rsqrt(jnp.mean(values * values, axis=-1, keepdims=True) + epsilon)
        * gain_vector
    )


def gelu_tanh(values):
    return jax.nn.gelu(values, approximate=True)


def forward_product(values, weight):
    return jnp.dot(values, weight, preferred_element_type=jnp.float32)


def outer_product(left_side, right_side):
    return lax.dot_general(
        left_side, right_side, (((0,), (0,)), ((), ())), preferred_element_type=jnp.float32
    )


def back_product(grad_low, weight):
    return lax.dot_general(
        grad_low, weight, (((1,), (1,)), ((), ())), preferred_element_type=jnp.float32
    )


def make_bias(bucket_bias_rows, row_count):
    query_place = jnp.arange(row_count)[:, None]
    key_place = jnp.arange(row_count)[None, :]
    levels = jnp.arange(NB)
    current_bucket_selector = (
        bucket_of(key_place - query_place)[None] == levels[:, None, None]
    ).astype(jnp.float32)
    previous_bucket_selector = (
        bucket_of(key_place - row_count - query_place)[None] == levels[:, None, None]
    ).astype(jnp.float32)
    onehot_far = (bucket_of(jnp.array(-MAXD, jnp.int32)) == levels).astype(jnp.float32)
    current_block_bias = jnp.einsum(
        "smz,sj->jmz", current_bucket_selector, bucket_bias_rows, precision=strongest_precision
    )
    previous_block_bias = jnp.einsum(
        "smz,sj->jmz", previous_bucket_selector, bucket_bias_rows, precision=strongest_precision
    )
    bias_far = jnp.dot(onehot_far, bucket_bias_rows, precision=strongest_precision)
    mask_same = key_place // BLOCK <= query_place // BLOCK
    return (
        (current_block_bias, previous_block_bias, bias_far, mask_same),
        (current_bucket_selector, previous_bucket_selector, onehot_far),
    )


def pair_scores(query_heads, key_heads, relation, bias_set, scale_factor):
    current_block_bias, previous_block_bias, bias_far, mask_same = bias_set
    raw_scores = jnp.einsum(
        "qhd,khd->hqk", query_heads, key_heads, preferred_element_type=jnp.float32
    )
    bias_rows = jnp.where(
        relation == 0,
        current_block_bias,
        jnp.where(relation == 1, previous_block_bias, bias_far[:, None, None]),
    )
    allowed = jnp.logical_or(relation > 0, mask_same)
    return jnp.where(allowed[None], raw_scores * scale_factor + bias_rows, negative)


def pair_core(
    query_heads,
    dout_heads,
    log_total,
    row_delta,
    key_heads,
    value_heads,
    relation,
    bias_set,
    scale_factor,
):
    scores = pair_scores(query_heads, key_heads, relation, bias_set, scale_factor)
    weights_now = jnp.exp(scores - log_total[:, :, None])
    grad_weights = jnp.einsum(
        "qhd,khd->hqk", dout_heads, value_heads, preferred_element_type=jnp.float32
    )
    dscores = weights_now * (grad_weights - row_delta[:, :, None])
    return (weights_now, dscores, (dscores * scale_factor).astype(jnp.bfloat16))


def add_tables(relative_bias_tables, dscores, relation):
    same_sum, prev_sum, far_sum = relative_bias_tables
    return (
        same_sum + jnp.where(relation == 0, dscores, 0.0),
        prev_sum + jnp.where(relation == 1, dscores, 0.0),
        far_sum + jnp.where(relation >= 2, jnp.sum(dscores, axis=(1, 2)), 0.0),
    )


def forward_fold(query_heads, position, row_count, bias_set, scale_factor, running, pieces):
    keys_all, values_all = pieces

    def one_shard(folded, shard_step):
        key_heads = lax.dynamic_slice_in_dim(
            keys_all, shard_step * row_count, row_count, 0
        ).reshape(row_count, H, HD)
        value_heads = lax.dynamic_slice_in_dim(
            values_all, shard_step * row_count, row_count, 0
        ).reshape(row_count, H, HD)
        relation = position - shard_step

        def one_compute(current):
            running_max, running_sum, running_acc = current
            scores = pair_scores(query_heads, key_heads, relation, bias_set, scale_factor)
            new_max = jnp.maximum(running_max, jnp.max(scores, axis=-1))
            factor = jnp.exp(running_max - new_max)
            weights_now = jnp.exp(scores - new_max[:, :, None])
            new_sum = running_sum * factor + jnp.sum(weights_now, axis=-1)
            update = jnp.einsum(
                "hqk,khd->qhd",
                weights_now.astype(jnp.bfloat16),
                value_heads,
                preferred_element_type=jnp.float32,
            )
            scaled = running_acc.reshape(row_count, H, HD) * factor.T[:, :, None]
            return (new_max, new_sum, (scaled + update).reshape(row_count, H * HD))

        return (lax.cond(relation >= 0, one_compute, lambda unchanged: unchanged, folded), None)

    running, unused = lax.scan(one_shard, running, jnp.arange(keys_all.shape[0] // row_count))
    return running


def nt_dot(left, right):
    return lax.dot_general(left, right, (((1,), (1,)), ((), ())), preferred_element_type=F32)


def nn_dot(left, right):
    return jnp.dot(left, right, preferred_element_type=F32)


def meet(neighbours):
    barrier = pltpu.get_barrier_semaphore()
    for who in neighbours:
        pl.semaphore_signal(barrier, inc=1, device_id=who, device_id_type=MESH)
    pl.semaphore_wait(barrier, len(neighbours))


def ctx_peers(n):
    me = lax.axis_index("ctx")
    return [{"ctx": lax.rem(me + d, n)} for d in range(1, n)]


def other_wa(me, bit):
    flipped = lax.rem(me // bit, 2)
    return me + bit - 2 * bit * flipped


def remote(src, dst, send_sem, recv_sem, **device):
    return pltpu.make_async_remote_copy(
        src_ref=src,
        dst_ref=dst,
        send_sem=send_sem,
        recv_sem=recv_sem,
        device_id=device,
        device_id_type=MESH,
    )


RING = 8
HOPS = RING - 1


def ring_place(n):
    me = lax.axis_index("ctx")
    half = n // 2

    def at(place):
        return jnp.where(place < half, 2 * place, 2 * (n - 1 - place) + 1)

    place = jnp.where(lax.rem(me, 2) == 0, me // 2, n - 1 - me // 2)
    return place, at(lax.rem(place + 1, n)), at(lax.rem(place + n - 1, n))


class Ring:
    def __init__(self, lanes, send, recv, share=None, hold=None, full=None):
        self.lanes, self.share, self.hold, self.full = lanes, share, hold, full
        self.sems = send, recv
        self.place, self.after, self.before = ring_place(RING)

    def copy(self, lane, src, dst, step):
        send, recv = self.sems
        way = self.lanes[lane][1]
        return remote(
            src, dst, send.at[lane, step], recv.at[lane, step], ctx=self.after if way == 1 else self.before
        )

    def chunk(self, lane, offset):
        here = self.place if self.lanes[lane][1] == 1 else RING - self.place
        return lax.rem(here + offset + 2 * RING, RING)

    def scatter(self, step, which):
        for lane in which:
            b, _, rows = self.lanes[lane]
            share = self.share.at[b, self.chunk(lane, -step), rows]

            @pl.when(step > 0)
            def _():
                there = self.hold.at[b, jnp.maximum(step - 1, 0), rows]
                self.copy(lane, share, there, jnp.maximum(step - 1, 0)).wait_recv()
                share[...] = (share[...].astype(F32) + there[...].astype(F32)).astype(BF)

            @pl.when(step < HOPS)
            def _():
                there = jnp.minimum(step, HOPS - 1)
                self.copy(lane, share, self.hold.at[b, there, rows], there).start()

    def gather(self, step, which):
        for lane in which:
            b, _, rows = self.lanes[lane]
            full = self.full[b].at[self.chunk(lane, 1 - step), rows]

            @pl.when(step > 0)
            def _():
                self.copy(lane, full, full, jnp.maximum(step - 1, 0)).wait_recv()

            @pl.when(step < HOPS)
            def _():
                self.copy(lane, full, full, jnp.minimum(step, HOPS - 1)).start()

    def finish(self, part):
        def one(step, unused):
            for lane in range(len(self.lanes)):
                self.copy(lane, part(lane), part(lane), step).wait_send()
            return unused

        lax.fori_loop(0, HOPS, one, 0)


TALL, FLAT = (224, 1024), (256, 896)
EARLY = ("ck", "cv", "cq", "co", "so")
MADE = ("cq", "co", "so")
LATE = ("q", "k", "v")
FEED = (8, 112, 896)
FEED_LANES = (
    (0, 1, slice(0, 64)),
    (1, -1, slice(0, 64)),
    (0, 1, slice(64, 112)),
    (1, -1, slice(64, 112)),
)
FEED_TURNS = ((0, 1), (2, 3))


def product_into(out_ref, left, right):
    for c in range(left.shape[1] // WIDE):
        lanes = slice(c * WIDE, (c + 1) * WIDE)
        turned = left[:, lanes].astype(F32).T.astype(BF)
        out_ref[lanes, :] = nn_dot(turned, right[...]).astype(BF)


class Folding:
    def __init__(self, names, parts, scratch):
        self.names = names
        self.parts = parts
        tall, flat, sems = scratch
        self.sets = {TALL: tall, FLAT: flat}
        self.own_sem, self.core_send, self.core_recv, self.x_send, self.x_recv = sems
        self.wa = lax.axis_index("wa")
        self.mate, self.across = other_wa(self.wa, 1), other_wa(self.wa, 2)
        self.core, self.half = lax.rem(self.wa, 2), self.wa // 2
        self.slots, count = {}, {TALL: 0, FLAT: 0}
        for name in names:
            shape = self.shape_of(name)
            self.slots[name] = (count[shape], self.sets[shape])
            count[shape] += 1
        self.own_copies, self.core_copies, self.x_copies = {}, {}, {}

    @staticmethod
    def shape_of(name):
        return FLAT if name in ("co", "so") else TALL

    @classmethod
    def scratch(cls, names):
        shapes = []
        for shape in (TALL, FLAT):
            many = sum(cls.shape_of(name) == shape for name in names)
            if many:
                shapes += [pltpu.VMEM((many, 2, *shape), BF)] * 2 + [pltpu.VMEM((many, *shape), BF)] * 2
        dma = pltpu.SemaphoreType.DMA
        many = len(names)
        return shapes + [dma((many, 2))] * 3 + [dma((many,))] * 2

    def start(self, *names):
        for name in names:
            u = self.names.index(name)
            slot, (own, inn, _, _) = self.slots[name]
            rows = self.shape_of(name)[0]
            for x in range(2):
                mine = pl.ds(pl.multiple_of((2 * x + self.core) * rows, 16), rows)
                theirs = pl.ds(pl.multiple_of((2 * x + 1 - self.core) * rows, 16), rows)
                copy = remote(
                    self.parts[name].at[theirs],
                    inn.at[slot, x],
                    self.core_send.at[u, x],
                    self.core_recv.at[u, x],
                    wa=self.mate,
                )
                copy.start()
                self.core_copies[name, x] = copy
                copy = pltpu.make_async_copy(
                    self.parts[name].at[mine], own.at[slot, x], self.own_sem.at[u, x]
                )
                copy.start()
                self.own_copies[name, x] = copy
            slot, (_, _, out, land) = self.slots[name]
            self.x_copies[name] = remote(
                out.at[slot], land.at[slot], self.x_send.at[u], self.x_recv.at[u], wa=self.across
            )

    def send(self, name):
        self.prepare(name)
        self.x_copies[name].start()

    def prepare(self, name):
        slot, (own, inn, out, _) = self.slots[name]
        for x in range(2):
            self.own_copies[name, x].wait()
            self.core_copies[name, x].wait_recv()
        away = 1 - self.half
        out[slot] = (own[slot, away].astype(F32) + inn[slot, away].astype(F32)).astype(BF)

    def total(self, name):
        slot, (own, inn, _, land) = self.slots[name]
        self.x_copies[name].wait_recv()
        here = self.half
        return (
            own[slot, here].astype(F32) + inn[slot, here].astype(F32) + land[slot].astype(F32)
        ).astype(BF)

    def finish(self):
        for name in self.names:
            for x in range(2):
                self.core_copies[name, x].wait_send()
            self.x_copies[name].wait_send()


class Moves:
    def __init__(self, sem):
        self.sem, self.count = sem, 0

    def start(self, src, dst):
        copy = pltpu.make_async_copy(src, dst, self.sem.at[self.count])
        copy.start()
        self.count += 1
        return copy


def wait_all(copies):
    for copy in copies:
        copy.wait()


def lasting(microseconds):
    return pl.CostEstimate(
        flops=0, bytes_accessed=int(microseconds * 3.0e6), transcendentals=0
    )


def lanes_of(index):
    return pl.ds(pl.multiple_of(index * WIDE, WIDE), WIDE)


def rows_of(index, rows):
    return pl.ds(pl.multiple_of(index * rows, rows), rows)


def to_ctx(src, dst, send_sem, recv_sem, target):
    return pltpu.make_async_remote_copy(
        src_ref=src,
        dst_ref=dst,
        send_sem=send_sem,
        recv_sem=recv_sem,
        device_id={"ctx": target},
        device_id_type=MESH,
    )


def head_mask(h, rows):
    lane = lax.broadcasted_iota(jnp.int32, (rows, WIDE), 1)
    return (lane < HD) if h == 0 else (lane >= HD)


def bias_tiles(bias_ref, me, tiles):
    for h in range(2):
        line = bias_ref[pl.ds(2 * me + h, 1), :]
        rolled = pltpu.roll(
            jnp.broadcast_to(line, (BLOCK, LINE)), 0, 1, stride=1, stride_axis=0
        )
        tiles[h, 0] = rolled[:, :BLOCK]
        tiles[h, 1] = rolled[:, BLOCK : 2 * BLOCK]
        tiles[h, 2] = jnp.broadcast_to(line[:, WIDE : WIDE + BLOCK], (BLOCK, BLOCK))


def spread(n, me, pairs, send, recv, t):
    src, dst = pairs[t]
    for d in range(1, n):
        peer = lax.rem(me + d, n)
        to_ctx(
            src.at[:, lanes_of(peer)], dst.at[rows_of(me, BLOCK)], send.at[t, d], recv.at[t, d], peer
        ).start()
    dst[rows_of(me, BLOCK), :] = src[:, lanes_of(me)]


GATHERED = ("q", "k", "v", "so", "ck", "cv", "cq", "co")
SINGLE = ("cot",)
GAINS = ("selfnorm", "crossnorm", "feednorm", "outbias")


class Gathering:
    def __init__(self, shards, whole, own_sem, send, recv):
        self.names, self.shards, self.whole = tuple(shards), shards, whole
        self.sems = own_sem, send, recv
        self.wa, me = lax.axis_index("wa"), lax.axis_index("ctx")
        self.mate, self.across = other_wa(self.wa, 1), other_wa(self.wa, 2)
        y, z = lax.rem(me, 2), lax.rem(me // 2, 2)
        self.pairs = ((y, me + 1 - 2 * y), (z, me + 2 - 4 * z))
        self.copies = {}

    def start(self):
        own_sem, send, recv = self.sems
        for u, name in enumerate(self.names):
            part, beside = self.pairs[(u + 1) % 2]
            shard, whole = self.shards[name], self.whole[name]
            rows = shard.shape[0]
            parts = 1 if name in SINGLE else 2
            some = rows // parts
            shift = 0 if parts == 1 else part * some

            def at(start, count, ref=whole):
                return ref.at[pl.ds(pl.multiple_of(start, 16), count)]

            mine = at(self.wa * rows, rows)
            theirs = at(self.across * rows, rows)
            theirs_some = at(self.across * rows + shift, some)
            self.copies[name] = {
                "over": remote(
                    at(shift, some, shard), at(self.wa * rows + shift, some), send.at[u, 0], recv.at[u, 0], wa=self.across
                ),
                "near": remote(shard, mine, send.at[u, 1], recv.at[u, 1], wa=self.mate),
                "pass": remote(theirs, theirs, send.at[u, 2], recv.at[u, 2], wa=self.mate),
                "side": remote(theirs_some, theirs_some, send.at[u, 3], recv.at[u, 3], ctx=beside),
                "own": pltpu.make_async_copy(shard, mine, own_sem.at[u]),
            }
            self.copies[name]["near"].start()
            self.copies[name]["own"].start()

    def cross(self, *names):
        for name in names:
            self.copies[name]["over"].start()

    def forward(self, *names):
        for name in names:
            self.copies[name]["over"].wait_recv()
            self.copies[name]["pass" if name in SINGLE else "side"].start()

    def land(self, *names):
        for name in names:
            self.copies[name]["side"].wait_recv()
            self.copies[name]["pass"].start()

    def arrive(self, *names):
        for name in names:
            self.copies[name]["near"].wait_recv()
            self.copies[name]["pass"].wait_recv()
            self.copies[name]["own"].wait()

    def finish(self):
        for name, copies in self.copies.items():
            for which in ("over", "near", "pass") + (() if name in SINGLE else ("side",)):
                copies[which].wait_send()


class Columns:
    def __init__(self, gathering, shard, whole, send, recv):
        wa, mate, across = gathering.wa, gathering.mate, gathering.across
        both = other_wa(across, 1)
        rows, width = shard.shape[0], whole.shape[1]
        some = rows // 2

        def block(owner, columns):
            return shard.at[owner, pl.ds(pl.multiple_of(columns * width, WIDE), width)]

        def at(start, count):
            return whole.at[pl.ds(pl.multiple_of(start, 16), count)]

        everything = slice(0, rows)
        self.own = pltpu.make_async_copy(block(everything, wa), at(wa * rows, rows), send.at[5])
        self.near = remote(block(everything, mate), at(wa * rows, rows), send.at[0], recv.at[0], wa=mate)
        self.over, self.side = [], []
        for d, peer in enumerate((across, both)):
            part, beside = gathering.pairs[d]
            mine = pl.ds(pl.multiple_of(part * some, 16), some)
            gone, got = at(wa * rows + part * some, some), at(peer * rows + part * some, some)
            self.over.append(remote(block(mine, peer), gone, send.at[1 + d], recv.at[1 + d], wa=peer))
            self.side.append(remote(got, got, send.at[3 + d], recv.at[3 + d], ctx=beside))

    def start(self):
        self.own.start()
        self.near.start()

    def cross(self):
        for copy in self.over:
            copy.start()

    def forward(self):
        for over, side in zip(self.over, self.side, strict=True):
            over.wait_recv()
            side.start()

    def finish(self):
        self.own.wait()
        self.near.wait()
        for over, side in zip(self.over, self.side, strict=True):
            side.wait()
            over.wait_send()


def attn_forward_kernel(n, tokens_ref, small_ref, near_far, *refs):
    shards = dict(zip((*GATHERED, "cot"), refs[:9], strict=True))
    feed_ref = refs[9]
    wholes = dict(zip((*GATHERED, "cot"), refs[10:19], strict=True))
    feed_whole = refs[19]
    o_ref, low_ref, ot_out, lse_out, small_out, before_ref, qh_out, kh_out, vh_out, keys_out, values_out = refs[20:31]
    (
        held_q, held_k, held_v, held_ck, held_cv, proj, small_in, small_mid, qh, kh, vh, vt, oh, land, tiles,
        acc, stat, send, recv, osend, orecv, small_sem, own_sem, out_sem, gather_send, gather_recv, feed_send,
        feed_recv, span_sem, near_ref, keys_ref, values_ref, move_sem,
    ) = refs[31:]
    moves = Moves(move_sem)
    load_near = moves.start(near_far, near_ref)
    held = {"q": held_q, "k": held_k, "v": held_v, "ck": held_ck, "cv": held_cv}
    gathering = Gathering(shards, wholes | held, own_sem, gather_send, gather_recv)
    columns = Columns(gathering, feed_ref, feed_whole, feed_send, feed_recv)
    both = other_wa(gathering.across, 1)
    meet([*ctx_peers(n), *({"wa": peer} for peer in (gathering.mate, gathering.across, both))])
    me = lax.axis_index("ctx")
    near = remote(small_ref, small_in.at[0], small_sem.at[0], small_sem.at[1], wa=gathering.mate)
    near.start()
    gathering.start()
    gathering.cross("q")
    columns.start()
    span_rows = before_ref.shape[0]
    span = remote(
        near_far.at[near_far.shape[0] - span_rows :],
        before_ref,
        span_sem.at[0],
        span_sem.at[1],
        ctx=lax.rem(me + 1, n),
    )
    over = remote(small_mid, small_in.at[1], small_sem.at[2], small_sem.at[3], wa=gathering.across)
    near.wait_recv()
    small_mid[...] = (small_ref[...].astype(F32) + small_in[0].astype(F32)).astype(BF)
    over.start()
    over.wait_recv()
    small_out[...] = small_mid[...].astype(F32) + small_in[1].astype(F32)
    bias_ref = small_out
    values = tokens_ref[...].astype(F32)
    width = values.shape[1]
    norm = lax.rsqrt(jnp.mean(values * values, axis=1, keepdims=True) + epsilon)
    low_ref[...] = (values * norm * small_out[H : H + 1, :width]).astype(BF)
    bias_tiles(bias_ref, me, tiles)
    pairs = tuple((proj.at[t], dst) for t, dst in enumerate((qh, kh, vh)))
    saving = []

    def save(name):
        copy = pltpu.make_async_copy(held[name], wholes[name], out_sem.at[len(saving)])
        copy.start()
        saving.append(copy)

    def project(t, name):
        gathering.land(name)
        gathering.arrive(name)
        proj[t] = nn_dot(low_ref[...], held[name][...]).astype(BF)
        spread(n, me, pairs, send, recv, t)
        save(name)

    gathering.forward("q")
    gathering.cross("k")
    gathering.forward("k")
    gathering.cross("v")
    project(0, "q")
    gathering.forward("v")
    gathering.cross("so", "ck")
    project(1, "k")
    project(2, "v")

    gathering.forward("so", "ck")
    gathering.cross("cv", "cq")

    for d in range(1, n):
        peer = lax.rem(me + n - d, n)
        for t, (src, dst) in enumerate(pairs):
            to_ctx(
                src.at[:, lanes_of(peer)], dst.at[rows_of(peer, BLOCK)], send.at[t, d], recv.at[t, d], peer
            ).wait_recv()
    stores = [moves.start(*pair) for pair in ((qh, qh_out), (kh, kh_out), (vh, vh_out))]
    for i in range(n):
        part = slice(i * BLOCK, (i + 1) * BLOCK)
        vt[:, part] = vh[part, :].astype(F32).T.astype(BF)

    def query_block(step, unused):
        @pl.when((step == 0) & (me < n - 1))
        def _():
            span.start()

        @pl.when(step == 1)
        def _():
            gathering.forward("cv", "cq")
            gathering.land("so", "ck")
            gathering.cross("co")
            columns.cross()

        @pl.when(step == 6)
        def _():
            gathering.land("cv", "cq")
            gathering.forward("co")
            columns.forward()
            gathering.cross("cot")

        i = lax.rem(me + 1 + step, n)
        rows = rows_of(i, BLOCK)
        q_now = qh[rows, :] * BF(HD**-0.5)
        masked = [jnp.where(head_mask(h, BLOCK), q_now, BF(0)) for h in range(2)]

        def fold(j, which, first):
            keys = kh[rows_of(j, BLOCK), :]
            for h in range(2):
                scores = nt_dot(keys, masked[h])
                if which is None:
                    scores = scores + bias_ref[pl.ds(2 * me + h, 1), WIDE : WIDE + BLOCK]
                else:
                    scores = scores + tiles[h, which]
                top = jnp.max(scores, axis=0, keepdims=True)
                if not first:
                    old = stat[h : h + 1, :]
                    top = jnp.maximum(old, top)
                weights = jnp.exp(scores - top)
                total = jnp.sum(weights, axis=0, keepdims=True)
                vals = vt[h * HD : (h + 1) * HD, rows_of(j, BLOCK)]
                mixed = nn_dot(vals, weights.astype(BF))
                if not first:
                    factor = jnp.exp(old - top)
                    total = total + stat[2 + h : 3 + h, :] * factor
                    mixed = mixed + acc[h * HD : (h + 1) * HD, :] * factor
                stat[h : h + 1, :] = top
                stat[2 + h : 3 + h, :] = total
                acc[h * HD : (h + 1) * HD, :] = mixed

        fold(i, 0, True)

        @pl.when(i >= 1)
        def _():
            fold(i - 1, 1, False)

        def far(j, unused):
            fold(j, None, False)
            return unused

        lax.fori_loop(0, i - 1, far, 0)
        for h in range(2):
            total = stat[2 + h : 3 + h, :]
            part = acc[h * HD : (h + 1) * HD, :] / total
            acc[h * HD : (h + 1) * HD, :] = part
            lse_out[h : h + 1, rows] = stat[h : h + 1, :] + jnp.log(total)
        done = acc[...]
        ot_out[:, rows] = done
        oh[rows, :] = done.T.astype(BF)

        @pl.when(i != me)
        def _():
            d = lax.rem(i - me + n, n)
            to_ctx(oh.at[rows], land.at[:, lanes_of(me)], osend.at[d], orecv.at[d], i).start()

        @pl.when(i == me)
        def _():
            land[:, lanes_of(me)] = oh[rows, :]

        return unused

    lax.fori_loop(0, n, query_block, 0)
    load_near.wait()

    @pl.when(me > 0)
    def _():
        span.wait_recv()

    @pl.when(me == 0)
    def _():
        before_ref[...] = jnp.zeros_like(before_ref)

    for name, out_ref, far_ref in (("ck", keys_ref, keys_out), ("cv", values_ref, values_out)):
        gathering.arrive(name)
        save(name)
        out_ref[:span_rows, :] = nn_dot(before_ref[...], held[name][...]).astype(BF)
        for g in range(near_ref.shape[0] // span_rows):
            rows = slice(g * span_rows, (g + 1) * span_rows)
            there = slice((g + 1) * span_rows, (g + 2) * span_rows)
            out_ref[there, :] = nn_dot(near_ref[rows, :], held[name][...]).astype(BF)
        stores.append(moves.start(out_ref, far_ref))
    gathering.land("co")
    gathering.forward("cot")
    for d in range(1, n):
        peer = lax.rem(me + d, n)
        for t, (src, dst) in enumerate(pairs):
            to_ctx(
                src.at[:, lanes_of(peer)], dst.at[rows_of(me, BLOCK)], send.at[t, d], recv.at[t, d], peer
            ).wait_send()
        back = to_ctx(
            oh.at[rows_of(peer, BLOCK)], land.at[:, lanes_of(me)], osend.at[d], orecv.at[d], peer
        )
        back.wait_send()
        back.wait_recv()
    o_ref[...] = land[...]
    gathering.arrive("so", "cq", "co", "cot")
    gathering.finish()
    columns.finish()

    @pl.when(me < n - 1)
    def _():
        span.wait_send()

    near.wait_send()
    over.wait_send()
    wait_all(saving + stores)


def vmem(count):
    return [pl.BlockSpec(memory_space=pltpu.VMEM)] * count


def attn_forward(n, tokens, small, near, shards, feed):
    rows, seq = tokens.shape[0], n * tokens.shape[0]
    owners = lax.axis_size("wa")
    low = functools.partial(jax.ShapeDtypeStruct, dtype=BF)
    heads = low((seq, WIDE))
    wholes = [low((owners * s.shape[0], s.shape[1])) for s in shards]
    width = wholes[0].shape[1]
    dma = pltpu.SemaphoreType.DMA
    span_rows = 256
    keys = low((span_rows + near.shape[0], width))
    any_spec = pl.BlockSpec(memory_space=pl.ANY)
    return pl.pallas_call(
        functools.partial(attn_forward_kernel, n),
        out_shape=(
            *wholes,
            low((owners * feed.shape[0], feed.shape[1] // owners)),
            low((rows, width)),
            low(tokens.shape),
            jax.ShapeDtypeStruct((WIDE, seq), F32),
            jax.ShapeDtypeStruct((8, seq), F32),
            jax.ShapeDtypeStruct(small.shape, F32),
            low((span_rows, near.shape[1])),
            heads,
            heads,
            heads,
            keys,
            keys,
        ),
        in_specs=vmem(2) + [any_spec] * 11,
        out_specs=tuple([any_spec] * 10 + vmem(6) + [any_spec] * 5),
        scratch_shapes=[
            *[pltpu.VMEM(wholes[0].shape, BF)] * 5,
            pltpu.VMEM((3, rows, width), BF),
            pltpu.VMEM((2, *small.shape), BF),
            pltpu.VMEM(small.shape, BF),
            pltpu.VMEM((seq, WIDE), BF),
            pltpu.VMEM((seq, WIDE), BF),
            pltpu.VMEM((seq, WIDE), BF),
            pltpu.VMEM((WIDE, seq), BF),
            pltpu.VMEM((seq, WIDE), BF),
            pltpu.VMEM((rows, width), BF),
            pltpu.VMEM((2, 3, BLOCK, BLOCK), F32),
            pltpu.VMEM((WIDE, BLOCK), F32),
            pltpu.VMEM((8, BLOCK), F32),
            dma((3, n)),
            dma((3, n)),
            dma((n,)),
            dma((n,)),
            dma((4,)),
            dma((9,)),
            dma((5,)),
            dma((9, 4)),
            dma((9, 4)),
            dma((6,)),
            dma((5,)),
            dma((2,)),
            pltpu.VMEM(near.shape, BF),
            pltpu.VMEM(keys.shape, BF),
            pltpu.VMEM(keys.shape, BF),
            dma((6,)),
        ],
        compiler_params=pltpu.CompilerParams(
            collective_id=1, has_side_effects=True, vmem_limit_bytes=60 << 20
        ),
        cost_estimate=lasting(85),
        name="attn_forward",
    )(tokens, small, near, *shards, feed)


def attn_backward_kernel(
    n, do_ref, qh, kh, vh, ot_ref, lse_ref, bias_ref, *rest
):
    given = dict(zip(MADE, zip(rest[2:8:2], rest[3:8:2], strict=True), strict=True))
    feed_part = rest[8]
    dq_ref, dk_ref, dv_ref, line_ref, tall_pair, tall_one, flat_out = rest[9:16]
    feed_full = rest[16:18]
    (
        doh, kt, stage, land, dk_acc, dv_acc, dq_acc, q_masked, do_masked, delta, tiles, dtiles,
        send, recv, gsend, grecv, ring_send, ring_recv,
    ) = rest[18:36]
    made = dict(zip(MADE, rest[36:39], strict=True))
    parts = dict(zip(EARLY, (rest[0], rest[1], *made.values()), strict=True))
    extra = rest[39:]
    fold_wa = Folding(EARLY, parts, (extra[0:4], extra[4:8], extra[8:13]))
    ring = Ring(FEED_LANES, ring_send, ring_recv, full=feed_full)
    for lane in range(2):
        feed_full[lane][ring.chunk(lane, 1)] = feed_part[lane]
    meet([*ctx_peers(n), {"wa": fold_wa.mate}, {"wa": fold_wa.across}])
    me = lax.axis_index("ctx")
    pairs = ((do_ref, doh),)
    spread(n, me, pairs, send, recv, 0)
    fold_wa.start("ck", "cv")
    bias_tiles(bias_ref, me, tiles)
    for j in range(n):
        part = slice(j * BLOCK, (j + 1) * BLOCK)
        kt[:, part] = (kh[part, :].astype(F32) * HD**-0.5).T.astype(BF)
    dtiles[...] = jnp.zeros_like(dtiles)
    for name in EARLY[:2]:
        fold_wa.send(name)
    ring.gather(jnp.int32(0), FEED_TURNS[0])
    ring.gather(jnp.int32(0), FEED_TURNS[1])
    for name in MADE:
        product_into(made[name], *given[name])
        fold_wa.start(name)
    dq_acc[...] = jnp.zeros_like(dq_acc)
    for d in range(1, n):
        peer = lax.rem(me + n - d, n)
        to_ctx(
            do_ref.at[:, lanes_of(peer)], doh.at[rows_of(peer, BLOCK)], send.at[0, d], recv.at[0, d], peer
        ).wait_recv()
    for i in range(n):
        rows = slice(i * BLOCK, (i + 1) * BLOCK)
        q_now = qh[rows, :] * BF(HD**-0.5)
        do_now = doh[rows, :]
        products = do_now.astype(F32).T * ot_ref[:, rows]
        for h in range(2):
            mask = head_mask(h, BLOCK)
            q_masked[h, rows, :] = jnp.where(mask, q_now, BF(0))
            do_masked[h, rows, :] = jnp.where(mask, do_now, BF(0))
            delta[h : h + 1, rows] = jnp.sum(
                products[h * HD : (h + 1) * HD], axis=0, keepdims=True
            )

    def pair(t, now):
        i, j = now
        rows, there = rows_of(i, BLOCK), rows_of(j, BLOCK)

        @pl.when(t == 6)
        def _():
            for name in EARLY[2:]:
                fold_wa.send(name)

        for turn, lanes in enumerate(FEED_TURNS):

            @pl.when((lax.rem(t, 4) == 2 * turn + 1) & (t <= 4 * HOPS))
            def _():
                ring.gather(t // 4 + 1, lanes)

        first = i == j
        which = jnp.minimum(i - j, 2)
        keys, vals = kh[there, :], vh[there, :]
        dk_part, dv_part = None, None
        for h in range(2):
            query, dout = q_masked[h, rows, :], do_masked[h, rows, :]
            scores = nt_dot(keys, query)
            weights = jnp.exp(scores + tiles[h, which] - lse_ref[h : h + 1, rows])
            dweights = nt_dot(vals, dout)
            dscores = weights * (dweights - delta[h : h + 1, rows])
            dtiles[h, which] += dscores
            low = dscores.astype(BF)
            dv_now = nn_dot(weights.astype(BF), dout)
            dk_now = nn_dot(low, query)
            dv_part = dv_now if dv_part is None else dv_part + dv_now
            dk_part = dk_now if dk_part is None else dk_part + dk_now
            half = slice(h * HD, (h + 1) * HD)
            dq_acc[half, rows] += nn_dot(kt[half, there], low)

        @pl.when(first)
        def _():
            dk_acc[...] = dk_part
            dv_acc[...] = dv_part

        @pl.when(jnp.logical_not(first))
        def _():
            dk_acc[...] += dk_part
            dv_acc[...] += dv_part

        last = i == n - 1

        @pl.when(last)
        def _():
            stage[1, there, :] = dk_acc[...].astype(BF)
            stage[2, there, :] = dv_acc[...].astype(BF)
            deliver(j, (1, 2))

        after = lax.rem(j + 1, n)
        return jnp.where(last, after, i + 1), jnp.where(last, after, j)

    def deliver(i, arrays):
        rows = rows_of(i, BLOCK)

        @pl.when(i != me)
        def _():
            d = lax.rem(i - me + n, n)
            for t in arrays:
                to_ctx(
                    stage.at[t, rows], land.at[t, :, lanes_of(me)], gsend.at[t, d], grecv.at[t, d], i
                ).start()

        @pl.when(i == me)
        def _():
            for t in arrays:
                land[t, :, lanes_of(me)] = stage[t, rows, :]

    begin = lax.rem(me + 1, n)
    lax.fori_loop(0, n * (n + 1) // 2, pair, (begin, begin))

    def dq_block(step, unused):
        i = lax.rem(me + 1 + step, n)
        rows = rows_of(i, BLOCK)
        stage[0, rows, :] = dq_acc[:, rows].T.astype(BF)
        deliver(i, (0,))
        return unused

    lax.fori_loop(0, n, dq_block, 0)
    ring.finish(lambda lane: feed_full[FEED_LANES[lane][0]].at[0, FEED_LANES[lane][2]])
    tall_pair[:224, :] = fold_wa.total("cq")
    tall_pair[224:, :] = fold_wa.total("ck")
    tall_one[...] = fold_wa.total("cv")
    for at, name in ((0, "co"), (32, "so")):
        flat_out[:, at : at + 32, :] = fold_wa.total(name).reshape(8, 32, 896)
    fold_wa.finish()
    for h in range(2):
        line = jnp.concatenate(
            [dtiles[h, 0], dtiles[h, 1], jnp.zeros((BLOCK, LINE - 2 * BLOCK), F32)], axis=1
        )
        row = lax.broadcasted_iota(jnp.int32, (BLOCK, LINE), 0)
        for bit in range(8):
            moved = pltpu.roll(line, LINE - (1 << bit), 1)
            line = jnp.where((row >> bit) & 1 == 1, moved, line)
        line_ref[h : h + 1, :] = jnp.sum(line, axis=0, keepdims=True)
        line_ref[2 + h : 3 + h, :BLOCK] = jnp.sum(dtiles[h, 2], axis=0, keepdims=True)
    line_ref[2:4, BLOCK:] = jnp.zeros((2, LINE - BLOCK), F32)
    line_ref[4:8, :] = jnp.zeros((4, LINE), F32)
    for d in range(1, n):
        peer = lax.rem(me + d, n)
        to_ctx(
            do_ref.at[:, lanes_of(peer)], doh.at[rows_of(me, BLOCK)], send.at[0, d], recv.at[0, d], peer
        ).wait_send()
        for t in range(3):
            back = to_ctx(
                stage.at[t, rows_of(peer, BLOCK)], land.at[t, :, lanes_of(me)], gsend.at[t, d], grecv.at[t, d], peer
            )
            back.wait_send()
            back.wait_recv()
    dq_ref[...] = land[0]
    dk_ref[...] = land[1]
    dv_ref[...] = land[2]


def attn_backward(n, dout, qh, kh, vh, ot, lse, bias_lines, parts, feed_part):
    rows, seq = dout.shape[0], n * dout.shape[0]
    grads = jax.ShapeDtypeStruct(dout.shape, BF)
    feed = jax.ShapeDtypeStruct(FEED, BF)
    return pl.pallas_call(
        functools.partial(attn_backward_kernel, n),
        out_shape=(
            grads,
            grads,
            grads,
            jax.ShapeDtypeStruct((8, LINE), F32),
            jax.ShapeDtypeStruct((448, 1024), BF),
            jax.ShapeDtypeStruct((224, 1024), BF),
            jax.ShapeDtypeStruct((8, 64, 896), BF),
            feed,
            feed,
        ),
        in_specs=vmem(7) + [pl.BlockSpec(memory_space=pl.ANY)] * 2 + vmem(7),
        out_specs=tuple(vmem(9)),
        scratch_shapes=[
            pltpu.VMEM((seq, WIDE), BF),
            pltpu.VMEM((WIDE, seq), BF),
            pltpu.VMEM((3, seq, WIDE), BF),
            pltpu.VMEM((3, *dout.shape), BF),
            pltpu.VMEM((BLOCK, WIDE), F32),
            pltpu.VMEM((BLOCK, WIDE), F32),
            pltpu.VMEM((WIDE, seq), F32),
            pltpu.VMEM((2, seq, WIDE), BF),
            pltpu.VMEM((2, seq, WIDE), BF),
            pltpu.VMEM((8, seq), F32),
            pltpu.VMEM((2, 3, BLOCK, BLOCK), F32),
            pltpu.VMEM((2, 3, BLOCK, BLOCK), F32),
            pltpu.SemaphoreType.DMA((1, n)),
            pltpu.SemaphoreType.DMA((1, n)),
            pltpu.SemaphoreType.DMA((3, n)),
            pltpu.SemaphoreType.DMA((3, n)),
            pltpu.SemaphoreType.DMA((len(FEED_LANES), HOPS)),
            pltpu.SemaphoreType.DMA((len(FEED_LANES), HOPS)),
            pltpu.VMEM((896, 1024), BF),
            pltpu.VMEM((1024, 896), BF),
            pltpu.VMEM((1024, 896), BF),
            *Folding.scratch(EARLY),
        ],
        compiler_params=pltpu.CompilerParams(
            collective_id=2, has_side_effects=True, vmem_limit_bytes=60 << 20
        ),
        cost_estimate=lasting(100),
        name="attn_backward",
    )(dout, qh, kh, vh, ot, lse, bias_lines, *parts, feed_part)


BUFFERS = {
    "cq": (1, (224, 1024)),
    "cv": (-1, (224, 1024)),
    "ck": (1, (224, 1024)),
    "co": (-1, (8, 32, 896)),
    "so0": (1, (8, 16, 896)),
    "so1": (-1, (8, 16, 896)),
}
NAMES = tuple(BUFFERS)


def chunk_shape(name):
    shape = BUFFERS[name][1]
    return (shape[0], WIDE) if len(shape) == 2 else shape[1:]


def chunk_of(ref, name, c):
    return ref.at[:, lanes_of(c)] if len(BUFFERS[name][1]) == 2 else ref.at[c]


class Grid:
    def __init__(self, u, share, half_in, half, quarters, whole, send, recv):
        self.u, self.share, self.half_in, self.half = u, share, half_in, half
        self.quarters, self.whole, self.sems = quarters, whole, (send, recv)
        me = lax.axis_index("ctx")
        self.y, self.z = lax.rem(me, 2), me // 2
        self.beside = me + 1 - 2 * self.y
        self.column = [lax.rem(self.z + d, 4) for d in range(1, 4)]

    def half_of(self, y):
        return pl.ds(pl.multiple_of(y * 4 * WIDE, WIDE), 4 * WIDE)

    def piece_of(self, z, y=None):
        start = z * WIDE if y is None else (4 * y + z) * WIDE
        return pl.ds(pl.multiple_of(start, WIDE), WIDE)

    def copy(self, number, src, dst, target):
        send, recv = self.sems
        return remote(src, dst, send.at[self.u, number], recv.at[self.u, number], ctx=target)

    def start(self, total):
        self.share[...] = total
        self.first = self.copy(
            0, self.share.at[:, self.half_of(1 - self.y)], self.half_in, self.beside
        )
        self.first.start()

    def spread(self):
        self.first.wait_recv()
        mine = self.share[:, self.half_of(self.y)]
        self.half[...] = (mine.astype(F32) + self.half_in[...].astype(F32)).astype(BF)
        self.out = []
        for d, z in enumerate(self.column):
            copy = self.copy(
                1 + d, self.half.at[:, self.piece_of(z)], self.quarters.at[self.z], 2 * z + self.y
            )
            copy.start()
            self.out.append(copy)
        self.quarters[self.z] = self.half[:, self.piece_of(self.z)]

    def total(self):
        for copy in self.out:
            copy.wait_recv()
        done = self.quarters[0].astype(F32)
        for z in range(1, 4):
            done = done + self.quarters[z].astype(F32)
        piece = self.whole.at[:, self.piece_of(self.z, self.y)]
        piece[...] = done.astype(BF)
        self.back = []
        for d, z in enumerate(self.column):
            copy = self.copy(4 + d, piece, piece, 2 * z + self.y)
            copy.start()
            self.back.append(copy)

    def join(self):
        for copy in self.back:
            copy.wait_recv()
        mine = self.whole.at[:, self.half_of(self.y)]
        self.last = self.copy(7, mine, mine, self.beside)
        self.last.start()

    def finish(self):
        self.last.wait_recv()
        for copy in (self.first, *self.out, *self.back, self.last):
            copy.wait_send()


def reduce_kernel(*refs):
    ca_ref, cb_ref, out_ref, small_ref, low_ref = refs[:5]
    given = dict(zip(LATE, refs[5:8], strict=True))
    fin_ref = refs[8]
    count = len(NAMES)
    full = dict(zip(NAMES, refs[9 : 9 + count], strict=True))
    refs = refs[9 + count :]
    late_full = dict(zip(LATE, refs[:3], strict=True))
    small_out, fin_out = refs[3:5]
    refs = refs[5:]
    share = dict(zip(NAMES, refs[:count], strict=True))
    hold = dict(zip(NAMES, refs[count : 2 * count], strict=True))
    refs = refs[2 * count :]
    grid_share, half_in, half, quarters, small_in, small_mid, small_beside, small_column = refs[:8]
    small_send, small_recv, ring_send, ring_recv, grid_send, grid_recv, fin_send, fin_recv = refs[8:16]
    made, turned = refs[16:18]
    parts = {name: made.at[u] for u, name in enumerate(LATE)}
    extra = refs[18:]
    fold_wa = Folding(LATE, parts, (extra[0:4], None, extra[4:9]))
    place, after, before = ring_place(RING)
    grids = {
        name: Grid(
            u, grid_share.at[u], half_in.at[u], half.at[u], quarters.at[u], late_full[name], grid_send, grid_recv
        )
        for u, name in enumerate(LATE)
    }
    wa, both = fold_wa.wa, other_wa(fold_wa.across, 1)
    some = grids["q"]
    in_column = [2 * z + some.y for z in some.column]
    meet(
        [{"wa": peer} for peer in (fold_wa.mate, fold_wa.across, both)]
        + [{"ctx": peer} for peer in (after, before, some.beside, *in_column)]
    )
    near = remote(small_ref, small_in.at[0], small_send.at[0], small_recv.at[0], wa=fold_wa.mate)
    near.start()
    over = remote(small_mid.at[0], small_in.at[1], small_send.at[1], small_recv.at[1], wa=fold_wa.across)
    beside = remote(small_mid.at[1], small_beside, small_send.at[2], small_recv.at[2], ctx=some.beside)
    columns = [
        remote(small_mid.at[2], small_column.at[some.z], small_send.at[3 + d], small_recv.at[3 + d], ctx=peer)
        for d, peer in enumerate(in_column)
    ]
    own_fin = pltpu.make_async_copy(fin_ref.at[wa], fin_out.at[:, columns_of(wa)], fin_send.at[3])
    own_fin.start()
    fin_copies = [
        remote(fin_ref.at[peer], fin_out.at[:, columns_of(wa)], fin_send.at[d], fin_recv.at[d], wa=peer)
        for d, peer in enumerate((fold_wa.across, both, fold_wa.mate))
    ]
    share["cq"][...] = ca_ref[:224]
    share["ck"][...] = ca_ref[224:]
    share["cv"][...] = cb_ref[...]
    share["co"][...] = out_ref[:, :32]
    share["so0"][...] = out_ref[:, 32:48]
    share["so1"][...] = out_ref[:, 48:]
    copies = {}

    def ring_step(b, name, step):
        way = BUFFERS[name][0]
        here = place if way == 1 else RING - place
        target = after if way == 1 else before
        if step > 0:
            copies[name, step - 1].wait_recv()
        if step == 2 * HOPS:
            return
        now = lax.rem(here - step + 3 * RING, RING)
        mine = chunk_of(share[name], name, now)
        done = chunk_of(full[name], name, now)
        if 0 < step <= HOPS:
            total = mine[...].astype(F32) + hold[name][step - 1].astype(F32)
            (mine if step < HOPS else done)[...] = total.astype(BF)
        src, dst = (mine, hold[name].at[step]) if step < HOPS else (done, done)
        copy = remote(src, dst, ring_send.at[b, step], ring_recv.at[b, step], ctx=target)
        copy.start()
        copies[name, step] = copy

    def small_over():
        near.wait_recv()
        small_mid[0] = small_ref[...] + small_in[0]
        over.start()

    def small_next():
        over.wait_recv()
        small_mid[1] = small_mid[0] + small_in[1]
        beside.start()

    def small_last():
        beside.wait_recv()
        small_mid[2] = small_mid[1] + small_beside[...]
        small_column[some.z] = small_mid[2]
        for copy in columns:
            copy.start()

    def begin(name, following=None):
        total = fold_wa.total(name)
        if following:
            fold_wa.x_copies[following].start()
        grids[name].start(total)

    def make(name):
        parts[name][...] = nn_dot(turned[...], given[name][...]).astype(BF)
        fold_wa.start(name)

    def make_all():
        turned[...] = low_ref[...].astype(F32).T.astype(BF)
        make("q")
        make("k")
        fold_wa.send("q")
        make("v")
        fold_wa.prepare("k")
        fold_wa.prepare("v")

    events = {
        0: [make_all, small_over],
        4: [lambda: begin("q", "k"), small_next],
        6: [grids["q"].spread, lambda: begin("k", "v"), small_last],
        8: [grids["q"].total, grids["k"].spread],
        9: [lambda: begin("v"), grids["q"].join, *(copy.start for copy in fin_copies)],
        10: [grids["k"].total],
        11: [grids["v"].spread, grids["k"].join],
        12: [grids["v"].total],
        14: [grids["v"].join],
    }
    for tick in range(2 * HOPS + 1):
        for b, name in enumerate(NAMES):
            ring_step(b, name, tick)
        for event in events.get(tick, ()):
            event()
    for copy in columns:
        copy.wait_recv()
    total = small_column[0]
    for z in range(1, 4):
        total = total + small_column[z]
    small_out[...] = total
    for name in LATE:
        grids[name].finish()
    fold_wa.finish()
    for copy in (near, over, beside, *columns, *copies.values()):
        copy.wait_send()
    own_fin.wait()
    for copy in fin_copies:
        copy.wait()


def columns_of(owner):
    return pl.ds(pl.multiple_of(owner * 896, WIDE), 896)


def reduce_grads(pair, one, flat, small, low, grads, fin):
    dma = pltpu.SemaphoreType.DMA
    any_spec = pl.BlockSpec(memory_space=pl.ANY)
    late = len(LATE)
    return pl.pallas_call(
        reduce_kernel,
        out_shape=(
            *(jax.ShapeDtypeStruct(BUFFERS[b][1], BF) for b in NAMES),
            *[jax.ShapeDtypeStruct(TALL, BF)] * late,
            jax.ShapeDtypeStruct(small.shape, F32),
            jax.ShapeDtypeStruct((224, 3584), BF),
        ),
        in_specs=vmem(8) + [any_spec],
        out_specs=(*vmem(len(NAMES) + late + 1), any_spec),
        scratch_shapes=[
            *(pltpu.VMEM(BUFFERS[b][1], BF) for b in NAMES),
            *(pltpu.VMEM((HOPS, *chunk_shape(b)), BF) for b in NAMES),
            pltpu.VMEM((late, *TALL), BF),
            pltpu.VMEM((late, 224, 4 * WIDE), BF),
            pltpu.VMEM((late, 224, 4 * WIDE), BF),
            pltpu.VMEM((late, 4, 224, WIDE), BF),
            pltpu.VMEM((2, *small.shape), F32),
            pltpu.VMEM((3, *small.shape), F32),
            pltpu.VMEM(small.shape, F32),
            pltpu.VMEM((4, *small.shape), F32),
            dma((6,)),
            dma((6,)),
            dma((len(NAMES), 2 * HOPS)),
            dma((len(NAMES), 2 * HOPS)),
            dma((late, 8)),
            dma((late, 8)),
            dma((4,)),
            dma((3,)),
            pltpu.VMEM((late, 896, 1024), BF),
            pltpu.VMEM((896, 256), BF),
            *Folding.scratch(LATE),
        ],
        compiler_params=pltpu.CompilerParams(
            collective_id=3, has_side_effects=True, vmem_limit_bytes=56 << 20
        ),
        cost_estimate=lasting(90),
        name="reduce_grads",
    )(pair, one, flat, small, low, *grads, fin.reshape(4, 224, 896))


def unfold(full):
    wide = {name: value.astype(F32) for name, value in full.items()}
    return {
        "co": wide["co"].reshape(FLAT),
        "so": jnp.concatenate([wide["so0"], wide["so1"]], 1).reshape(FLAT),
        **{name: wide[name] for name in ("cq", "ck", "cv", *LATE)},
    }


GELU = (2.0 / math.pi) ** 0.5


def ffn_kernel(
    late, f_ref, cot_ref, win_ref, wout_ref, bias_ref, res_ref, parts_ref, df_ref, dwin_ref, dwout_ref, dbias_ref,
    f_all, g_all, dul_all, ahead, own, kept, out_mate, out_cross, in_mate, in_cross, x_out, x_in,
    f_send, f_recv, p_send, p_recv,
):
    me = lax.axis_index("wa")
    mate, across = other_wa(me, 1), other_wa(me, 2)
    both = other_wa(across, 1)
    barrier = pltpu.get_barrier_semaphore()
    for peer in (mate, across):
        pl.semaphore_signal(barrier, inc=1, device_id={"wa": peer}, device_id_type=MESH)
    pl.semaphore_wait(barrier, 2)
    to_across = remote(f_ref, f_all.at[me], f_send.at[1], f_recv.at[1], wa=across)
    to_across.start()
    to_mate = remote(f_ref, f_all.at[me], f_send.at[0], f_recv.at[0], wa=mate)
    to_mate.start()
    forward = remote(f_all.at[across], f_all.at[across], f_send.at[2], f_recv.at[2], wa=mate)
    f_all[me] = f_ref[...]
    order = (me, mate, across, both)
    dbias_ref[...] = jnp.zeros_like(dbias_ref)
    for k, s in enumerate(order):
        if k == 1:
            to_mate.wait_recv()
        if k == 2:
            for d in range(2):
                ahead[d] = nt_dot(cot_ref[order[2 + d]], wout_ref[...])
            to_across.wait_recv()
            forward.start()
        if k == 3:
            forward.wait_recv()
        u = nn_dot(f_all[s], win_ref[...]) + bias_ref[...]
        square = u * u
        t = jnp.tanh(GELU * (u + 0.044715 * (square * u)))
        g_all[s] = (0.5 * u * (1.0 + t)).astype(BF)
        slope = 0.5 * (1.0 + t) + 0.5 * u * (1.0 - t * t) * (GELU * (1.0 + 3 * 0.044715 * square))
        du = (nt_dot(cot_ref[s], wout_ref[...]) if k < 2 else ahead[k - 2]) * slope
        dbias_ref[...] += jnp.sum(du.reshape(32, 8, du.shape[1]), axis=0)
        dul_all[s] = du.astype(BF)

    def scatter(which, product):
        out_cross[which] = product(both).astype(BF)
        cross = remote(
            out_cross.at[which], in_cross.at[which], p_send.at[which, 0], p_recv.at[which, 0], wa=mate
        )
        cross.start()
        kept[...] = product(across)
        cross.wait_recv()
        x_out[which] = (kept[...] + in_cross[which].astype(F32)).astype(BF)
        over = remote(
            x_out.at[which], x_in.at[which], p_send.at[which, 1], p_recv.at[which, 1], wa=across
        )
        over.start()
        out_mate[which] = product(mate).astype(BF)
        near = remote(
            out_mate.at[which], in_mate.at[which], p_send.at[which, 2], p_recv.at[which, 2], wa=mate
        )
        near.start()
        own[which] = product(me)
        return cross, over, near

    def finish(which, copies, out_ref):
        cross, over, near = copies
        near.wait_recv()
        over.wait_recv()
        out_ref[...] = own[which] + in_mate[which].astype(F32) + x_in[which].astype(F32)
        for copy in copies:
            copy.wait_send()

    df_copies = scatter(0, lambda s: nt_dot(dul_all[s], win_ref[...]))
    if late:
        res_ref[...] = nn_dot(g_all[me], wout_ref[...])
        for d, s in enumerate(order[1:]):
            parts_ref[d] = nn_dot(g_all[s], wout_ref[...]).astype(BF)
    else:
        res_copies = scatter(1, lambda s: nn_dot(g_all[s], wout_ref[...]))
        parts_ref[...] = jnp.zeros_like(parts_ref)
    width = f_ref.shape[1]

    def outer(left_all, right, out_ref):
        for c in range(width // WIDE):
            lanes = slice(c * WIDE, (c + 1) * WIDE)
            total = None
            for s in range(4):
                left = left_all[s, :, lanes].astype(F32).T.astype(BF)
                now = nn_dot(left, right[s])
                total = now if total is None else total + now
            out_ref[lanes, :] = total.astype(BF)

    outer(f_all, dul_all, dwin_ref)
    outer(g_all, cot_ref, dwout_ref)
    finish(0, df_copies, df_ref)
    if not late:
        finish(1, res_copies, res_ref)
    for copy in (to_mate, to_across, forward):
        copy.wait_send()


def ffn(late, f_low, cot_all, win, wout, bias):
    rows, width = f_low.shape
    hidden = win.shape[1]
    dma = pltpu.SemaphoreType.DMA
    block = (rows, width)
    return pl.pallas_call(
        functools.partial(ffn_kernel, late),
        out_shape=(
            jax.ShapeDtypeStruct(block, F32),
            jax.ShapeDtypeStruct((3, *block), BF),
            jax.ShapeDtypeStruct(block, F32),
            jax.ShapeDtypeStruct(win.shape, BF),
            jax.ShapeDtypeStruct(wout.shape, BF),
            jax.ShapeDtypeStruct((8, hidden), F32),
        ),
        in_specs=vmem(5),
        out_specs=tuple(vmem(6)),
        scratch_shapes=[
            pltpu.VMEM((4, *block), BF),
            pltpu.VMEM((4, rows, hidden), BF),
            pltpu.VMEM((4, rows, hidden), BF),
            pltpu.VMEM((2, rows, hidden), F32),
            pltpu.VMEM((2, *block), F32),
            pltpu.VMEM(block, F32),
            *[pltpu.VMEM((2, *block), BF)] * 6,
            dma((3,)),
            dma((3,)),
            dma((2, 3)),
            dma((2, 3)),
        ],
        compiler_params=pltpu.CompilerParams(
            collective_id=4, has_side_effects=True, vmem_limit_bytes=56 << 20
        ),
        cost_estimate=lasting(44),
        name="feed_forward",
    )(f_low, cot_all, win, wout, bias)


def padded_rows(pad, values):
    rows = values.shape[0]
    pad[...] = jnp.zeros_like(pad)
    pad[1 : rows + 1, :] = values.astype(F32)


def both_heads(pad, g):
    here = pad[g * SPAN : (g + 1) * SPAN, :]
    left = head_mask(0, SPAN)
    return jnp.concatenate([jnp.where(left, here, 0.0), jnp.where(left, 0.0, here)], 0).astype(BF)


def join_heads(stacked):
    return jnp.where(head_mask(0, SPAN), stacked[:SPAN], stacked[SPAN:])


def cross_forward_kernel(groups, keep_ref, q_ref, k_ref, v_ref, x_ref, q_pad, x_pad):
    padded_rows(q_pad, q_ref[...])
    for g in range(groups):
        rows = slice(g * 256, (g + 1) * 256)
        query = both_heads(q_pad, g) * BF(HD**-0.5)
        scores = nt_dot(query, k_ref[rows, :])
        weights = jnp.exp(scores - jnp.max(scores, axis=1, keepdims=True))
        weights = weights / jnp.sum(weights, axis=1, keepdims=True)
        mixed = join_heads(nn_dot(weights.astype(BF), v_ref[rows, :]))
        if g == 0:
            mixed = mixed * keep_ref[0:1, :]
        x_pad[g * SPAN : (g + 1) * SPAN, :] = mixed
    x_ref[...] = x_pad[1 : x_ref.shape[0] + 1, :].astype(BF)


def pair_specs(*rows):
    return [pl.BlockSpec((r, WIDE), lambda p: (0, p)) for r in rows]


def cross_forward(keep, query, keys, values):
    rows, width = query.shape
    many = keys.shape[0]
    groups = many // 256
    return pl.pallas_call(
        functools.partial(cross_forward_kernel, groups),
        grid=(width // WIDE,),
        out_shape=jax.ShapeDtypeStruct(query.shape, BF),
        in_specs=[pl.BlockSpec((8, WIDE), lambda p: (0, 0)), *pair_specs(rows, many, many)],
        out_specs=pair_specs(rows)[0],
        scratch_shapes=[pltpu.VMEM((groups * SPAN, WIDE), F32)] * 2,
        compiler_params=pltpu.CompilerParams(vmem_limit_bytes=16 << 20),
        cost_estimate=lasting(9),
        name="cross_forward",
    )(keep, query, keys, values)


def cross_backward_kernel(
    groups, keep_ref, q_ref, dx_ref, k_ref, v_ref, dq_ref, dk_ref, dv_ref, q_pad, dx_pad, dq_pad
):
    padded_rows(q_pad, q_ref[...])
    padded_rows(dx_pad, dx_ref[...])
    dx_pad[:SPAN, :] = dx_pad[:SPAN, :] * keep_ref[0:1, :]
    for g in range(groups):
        rows = slice(g * 256, (g + 1) * 256)
        query = both_heads(q_pad, g) * BF(HD**-0.5)
        dmixed = both_heads(dx_pad, g)
        keys, values = k_ref[rows, :], v_ref[rows, :]
        scores = nt_dot(keys, query)
        weights = jnp.exp(scores - jnp.max(scores, axis=0, keepdims=True))
        weights = weights / jnp.sum(weights, axis=0, keepdims=True)
        dweights = nt_dot(values, dmixed)
        dscores = weights * (dweights - jnp.sum(weights * dweights, axis=0, keepdims=True))
        dk_ref[rows, :] = nn_dot(dscores.astype(BF), query).astype(BF)
        dv_ref[rows, :] = nn_dot(weights.astype(BF), dmixed).astype(BF)
        back = (dscores * HD**-0.5).T.astype(BF)
        dq_pad[g * SPAN : (g + 1) * SPAN, :] = join_heads(nn_dot(back, keys))
    dq_ref[...] = dq_pad[1 : dq_ref.shape[0] + 1, :].astype(BF)


def cross_backward(keep, query, dmixed, keys, values):
    rows, width = query.shape
    many = keys.shape[0]
    groups = many // 256
    return pl.pallas_call(
        functools.partial(cross_backward_kernel, groups),
        grid=(width // WIDE,),
        out_shape=(
            jax.ShapeDtypeStruct(query.shape, BF),
            jax.ShapeDtypeStruct(keys.shape, BF),
            jax.ShapeDtypeStruct(keys.shape, BF),
        ),
        in_specs=[
            pl.BlockSpec((8, WIDE), lambda p: (0, 0)),
            *pair_specs(rows, rows, many, many),
        ],
        out_specs=tuple(pair_specs(rows, many, many)),
        scratch_shapes=[pltpu.VMEM((groups * SPAN, WIDE), F32)] * 3,
        compiler_params=pltpu.CompilerParams(vmem_limit_bytes=16 << 20),
        cost_estimate=lasting(17),
        name="cross_backward",
    )(keep, query, dmixed, keys, values)


def line_selector():
    place = jnp.arange(LINE)
    offset = jnp.where(place < LINE // 2, -place, LINE - place)
    return (bucket_of(offset)[None, :] == jnp.arange(NB)[:, None]).astype(jnp.float32)


def ring_forward(query_low, key_low, value_low, bucket_table):
    row_count, attn_width = query_low.shape
    position = lax.axis_index("ctx")
    scale_factor = HD ** (-0.5)
    bias_set, onehots = make_bias(bucket_table.astype(jnp.float32), row_count)
    query_heads = query_low.reshape(row_count, H, HD)
    start_state = (
        jnp.full((H, row_count), negative, jnp.float32),
        jnp.zeros((H, row_count), jnp.float32),
        jnp.zeros((row_count, attn_width), jnp.float32),
    )
    running_max, running_sum, running_acc = forward_fold(
        query_heads,
        position,
        row_count,
        bias_set,
        scale_factor,
        start_state,
        (
            lax.all_gather(key_low, "ctx", axis=0, tiled=True),
            lax.all_gather(value_low, "ctx", axis=0, tiled=True),
        ),
    )
    attended = (running_acc.reshape(row_count, H, HD) / running_sum.T[:, :, None]).reshape(
        row_count, attn_width
    )
    log_total = running_max + jnp.log(running_sum)
    state = (query_heads, key_low, value_low, attended, log_total, bias_set, onehots)
    return attended.astype(jnp.bfloat16), state


def ring_backward(state, dout_low):
    query_heads, key_low, value_low, attended, log_total, bias_set, onehots = state
    row_count, attn_width = dout_low.shape
    cycle_size = lax.axis_size("ctx")
    position = lax.axis_index("ctx")
    scale_factor = HD ** (-0.5)
    dout_heads = dout_low.reshape(row_count, H, HD)
    row_delta = jnp.sum(
        (dout_low.astype(jnp.float32) * attended).reshape(row_count, H, HD), axis=-1
    ).T
    zero_rows = jnp.zeros((row_count, attn_width), jnp.float32)
    zero_tables = (
        jnp.zeros((H, row_count, row_count), jnp.float32),
        jnp.zeros((H, row_count, row_count), jnp.float32),
        jnp.zeros((H,), jnp.float32),
    )

    def visit(folded, key_now, value_now, relation):

        def visit_compute(current):
            dquery_acc, dkey_acc, dvalue_acc, relative_bias_tables = current
            key_heads = key_now.reshape(row_count, H, HD)
            weights_now, dscores, ds_low = pair_core(
                query_heads,
                dout_heads,
                log_total,
                row_delta,
                key_heads,
                value_now.reshape(row_count, H, HD),
                relation,
                bias_set,
                scale_factor,
            )
            dquery = jnp.einsum(
                "hqk,khd->qhd", ds_low, key_heads, preferred_element_type=jnp.float32
            ).reshape(row_count, attn_width)
            dkey = jnp.einsum(
                "hqk,qhd->khd", ds_low, query_heads, preferred_element_type=jnp.float32
            ).reshape(row_count, attn_width)
            dvalue = jnp.einsum(
                "hqk,qhd->khd",
                weights_now.astype(jnp.bfloat16),
                dout_heads,
                preferred_element_type=jnp.float32,
            ).reshape(row_count, attn_width)
            return (
                dquery_acc + dquery,
                dkey_acc + dkey,
                dvalue_acc + dvalue,
                add_tables(relative_bias_tables, dscores, relation),
            )

        return lax.cond(relation >= 0, visit_compute, lambda unchanged: unchanged, folded)

    first_state = visit(
        (zero_rows, zero_rows, zero_rows, zero_tables), key_low, value_low, jnp.array(0, jnp.int32)
    )

    def cycle_step(carried, cycle_index):
        key_now, value_now, (dquery_acc, dkey_acc, dvalue_acc, relative_bias_tables) = carried
        key_next, value_next = passed_along((key_now, value_now), "ctx", 1)
        dkey_next, dvalue_next = (
            from_behind(dkey_acc.astype(jnp.bfloat16), "ctx", 1).astype(dkey_acc.dtype),
            from_behind(dvalue_acc.astype(jnp.bfloat16), "ctx", 1).astype(dvalue_acc.dtype),
        )
        relation = jnp.where(position >= cycle_index, cycle_index, -1)
        updated = visit(
            (dquery_acc, dkey_next, dvalue_next, relative_bias_tables),
            key_next,
            value_next,
            relation,
        )
        return ((key_next, value_next, updated), None)

    (
        unused_key,
        unused_value,
        (dquery_total, dkey_part, dvalue_part, relative_bias_tables),
    ), unused = lax.scan(cycle_step, (key_low, value_low, first_state), jnp.arange(1, cycle_size))
    dkey_total, dvalue_total = (
        from_behind(dkey_part.astype(jnp.bfloat16), "ctx", 1).astype(dkey_part.dtype),
        from_behind(dvalue_part.astype(jnp.bfloat16), "ctx", 1).astype(dvalue_part.dtype),
    )
    dquery_low = dquery_total.astype(jnp.bfloat16)
    dkey_low = dkey_total.astype(jnp.bfloat16)
    dvalue_low = dvalue_total.astype(jnp.bfloat16)
    current_bucket_selector, previous_bucket_selector, onehot_far = onehots
    grad_biastable = (
        jnp.einsum(
            "afw,mfw->am",
            current_bucket_selector,
            relative_bias_tables[0],
            precision=strongest_precision,
        )
        + jnp.einsum(
            "afw,mfw->am",
            previous_bucket_selector,
            relative_bias_tables[1],
            precision=strongest_precision,
        )
        + onehot_far[:, None] * relative_bias_tables[2][None, :]
    )
    return dquery_low, dkey_low, dvalue_low, grad_biastable


def heads_forward(tokens, near, cotangent, given):
    wa, owners = lax.axis_index("wa"), lax.axis_size("wa")
    table = given["biastable"].astype(F32)
    selector = lax.dynamic_slice_in_dim(line_selector(), wa * table.shape[0], table.shape[0], 0)
    lines = jnp.dot(table.T, selector, precision=strongest_precision).astype(BF)
    gains = jnp.concatenate([given[name] for name in GAINS]).reshape(len(GAINS), -1)
    small = jnp.zeros((H, LINE), BF)
    small = lax.dynamic_update_slice(small, gains, (0, wa * gains.shape[1]))
    small = jnp.concatenate([lines, small], 0)
    shards = [given[LONG_NAMES[name]] for name in GATHERED]
    *wholes, upstream_all, feed_in, attended_low, low, ot, lse, small, before, qh, kh, vh, keys, values = attn_forward(
        lax.axis_size("ctx"), tokens, small, near, [*shards, cotangent], given["feedin"]
    )
    width = tokens.shape[1]
    gain_of = {name: small[H + g, :width] for g, name in enumerate(GAINS)}
    full = {LONG_NAMES[name]: whole for name, whole in zip(GATHERED, wholes, strict=True)}
    full["feedin"] = feed_in
    upstream_all = upstream_all.reshape(owners, *tokens.shape)
    saved = (qh, kh, vh, ot, lse, small[:H])
    return attended_low, low, full, gain_of, upstream_all, (before, keys, values), saved


def heads_backward(state, dout_low, parts, feed_part):
    peers = lax.axis_size("ctx")
    dquery_low, dkey_low, dvalue_low, sums, *shares = attn_backward(
        peers, dout_low, *state, parts, feed_part
    )
    selector = line_selector()
    table = jnp.dot(selector, sums[:2].T, precision=strongest_precision)
    far = jnp.sum(sums[2:4], axis=1)
    table = table + selector[:, WIDE : WIDE + 1] * far[None, :]
    whole = jnp.zeros((NB, H), jnp.float32)
    whole = lax.dynamic_update_slice(whole, table, (0, 2 * lax.axis_index("ctx")))
    return dquery_low, dkey_low, dvalue_low, whole, shares


def cross_pair(groups, keep_ref, q_ref, dx_ref, k_ref, v_ref, dq_ref, dk_ref, dv_ref, q_pad, dx_pad, dq_pad, p):
    lanes = lanes_of(p)
    padded_rows(q_pad, q_ref[:, lanes])
    padded_rows(dx_pad, dx_ref[:, lanes])
    dx_pad[:SPAN, :] = dx_pad[:SPAN, :] * keep_ref[0:1, :]
    for g in range(groups):
        rows = slice(g * 256, (g + 1) * 256)
        query = both_heads(q_pad, g) * BF(HD**-0.5)
        dmixed = both_heads(dx_pad, g)
        keys, values = k_ref[rows, lanes], v_ref[rows, lanes]
        scores = nt_dot(keys, query)
        weights = jnp.exp(scores - jnp.max(scores, axis=0, keepdims=True))
        weights = weights / jnp.sum(weights, axis=0, keepdims=True)
        dweights = nt_dot(values, dmixed)
        dscores = weights * (dweights - jnp.sum(weights * dweights, axis=0, keepdims=True))
        dk_ref[rows, lanes] = nn_dot(dscores.astype(BF), query).astype(BF)
        dv_ref[rows, lanes] = nn_dot(weights.astype(BF), dmixed).astype(BF)
        back = (dscores * HD**-0.5).T.astype(BF)
        dq_pad[g * SPAN : (g + 1) * SPAN, :] = join_heads(nn_dot(back, keys))
    dq_ref[:, lanes] = dq_pad[1 : dq_ref.shape[0] + 1, :].astype(BF)


def middle_kernel(
    keep_ref, fed_ref, fed_parts, q_far, dx_far, k_far, v_far, before_far, near_far, wk_far, wv_far, fin_ref,
    fout_ref, feed_out, fed_out, dq_out, dwk_out, dwv_out, first_out, near_out, last_out,
    q_ref, dx_ref, k_ref, v_ref, before_ref, near_ref, wk_ref, wv_ref, dq_ref, dwk_ref, dwv_ref, near_low, near_last,
    dk, dv, q_pad, dx_pad, dq_pad, share, hold, in_mate, in_cross, x_out, x_in, load_sem, ring_send, ring_recv,
    fed_send, fed_recv,
):
    ring = Ring(FEED_LANES, ring_send, ring_recv, share=share, hold=hold)
    moves = Moves(load_sem)
    loads = [moves.start(part, share.at[b]) for b, part in enumerate((fin_ref, fout_ref))]
    pair_loads = [
        moves.start(*pair) for pair in ((q_far, q_ref), (dx_far, dx_ref), (k_far, k_ref), (v_far, v_ref))
    ]
    later_loads = [
        moves.start(*pair)
        for pair in ((wk_far, wk_ref), (wv_far, wv_ref), (before_far, before_ref), (near_far, near_ref))
    ]
    wa = lax.axis_index("wa")
    mate, across = other_wa(wa, 1), other_wa(wa, 2)
    meet([{"ctx": ring.after}, {"ctx": ring.before}, {"wa": mate}, {"wa": across}])
    cross = remote(fed_parts.at[2], in_cross, fed_send.at[0], fed_recv.at[0], wa=mate)
    cross.start()
    near = remote(fed_parts.at[0], in_mate, fed_send.at[1], fed_recv.at[1], wa=mate)
    near.start()
    over = remote(x_out, x_in, fed_send.at[2], fed_recv.at[2], wa=across)
    wait_all(loads)
    for lanes in FEED_TURNS:
        ring.scatter(jnp.int32(0), lanes)
    cross.wait_recv()
    x_out[...] = (fed_parts[1].astype(F32) + in_cross[...].astype(F32)).astype(BF)
    over.start()
    groups = k_ref.shape[0] // 256
    wait_all(pair_loads)

    def two_pairs(m, unused):
        for turn, lanes in enumerate(FEED_TURNS):
            cross_pair(
                groups, keep_ref, q_ref, dx_ref, k_ref, v_ref, dq_ref, dk, dv, q_pad, dx_pad, dq_pad,
                2 * m + turn,
            )
            ring.scatter(m + 1, lanes)
        return unused

    pairs = q_ref.shape[1] // (2 * WIDE)
    lax.fori_loop(0, pairs, two_pairs, 0)
    stores = [moves.start(dq_ref, dq_out)]
    wait_all(later_loads)
    calls = [(step, lanes) for step in range(pairs + 1, HOPS + 1) for lanes in FEED_TURNS]

    def turn():
        if calls:
            step, lanes = calls.pop(0)
            ring.scatter(jnp.int32(step), lanes)

    for g in range(groups):
        rows = slice(g * 256, (g + 1) * 256)
        total = nt_dot(dk[rows, :], wk_ref[...]) + nt_dot(dv[rows, :], wv_ref[...])
        if g == groups - 1:
            near_last[...] = total
        else:
            near_low[rows, :] = total.astype(BF)
        if g % 2 == 1:
            turn()
    stores += [
        moves.start(near_low.at[:256], first_out),
        moves.start(near_low.at[256:], near_out),
        moves.start(near_last, last_out),
    ]
    for c in range(near_ref.shape[1] // WIDE):
        lanes = slice(c * WIDE, (c + 1) * WIDE)
        first = before_ref[:, lanes].astype(F32).T.astype(BF)
        left = near_ref[:, lanes].astype(F32).T.astype(BF)
        for grads, out_ref in ((dk, dwk_ref), (dv, dwv_ref)):
            total = nn_dot(first, grads[:256, :]) + nn_dot(left, grads[256:, :])
            out_ref[lanes, :] = total.astype(BF)
        if c % 2 == 1:
            turn()
    stores += [moves.start(dwk_ref, dwk_out), moves.start(dwv_ref, dwv_out)]
    while calls:
        turn()
    near.wait_recv()
    over.wait_recv()
    fed_out[...] = fed_ref[...] + in_mate[...].astype(F32) + x_in[...].astype(F32)
    for copy in (cross, near, over):
        copy.wait_send()
    for lane in range(2):
        feed_out[lane] = share[lane, ring.chunk(lane, 1)]
    ring.finish(lambda lane: share.at[FEED_LANES[lane][0], 0, FEED_LANES[lane][2]])
    wait_all(stores)


def middle(keep, query, dmixed, keys, values, before, near, wk, wv, fed, fed_parts, fin, fout):
    many, width = keys.shape
    wide = near.shape[1]
    rows = query.shape[0]
    low = functools.partial(jax.ShapeDtypeStruct, dtype=BF)
    dma = pltpu.SemaphoreType.DMA
    any_spec = pl.BlockSpec(memory_space=pl.ANY)
    pad = pltpu.VMEM((many // 256 * SPAN, WIDE), F32)
    feed_part, fed, *others = pl.pallas_call(
        middle_kernel,
        out_shape=(
            low((2, *FEED[1:])),
            jax.ShapeDtypeStruct(fed.shape, F32),
            low(query.shape),
            low(wk.shape),
            low(wv.shape),
            low((256, wide)),
            low((many - 512, wide)),
            jax.ShapeDtypeStruct((256, wide), F32),
        ),
        in_specs=vmem(3) + [any_spec] * 10,
        out_specs=tuple(vmem(2) + [any_spec] * 6),
        scratch_shapes=[
            *[pltpu.VMEM((rows, width), BF)] * 2,
            *[pltpu.VMEM((many, width), BF)] * 2,
            pltpu.VMEM((256, wide), BF),
            pltpu.VMEM((many - 256, wide), BF),
            *[pltpu.VMEM(wk.shape, BF)] * 2,
            pltpu.VMEM((rows, width), BF),
            *[pltpu.VMEM(wk.shape, BF)] * 2,
            pltpu.VMEM((many - 256, wide), BF),
            pltpu.VMEM((256, wide), F32),
            pltpu.VMEM((many, width), BF),
            pltpu.VMEM((many, width), BF),
            pad,
            pad,
            pad,
            pltpu.VMEM((2, *FEED), BF),
            pltpu.VMEM((2, HOPS, *FEED[1:]), BF),
            *[pltpu.VMEM(fed.shape, BF)] * 4,
            dma((16,)),
            dma((len(FEED_LANES), HOPS)),
            dma((len(FEED_LANES), HOPS)),
            dma((3,)),
            dma((3,)),
        ],
        compiler_params=pltpu.CompilerParams(
            collective_id=5, has_side_effects=True, vmem_limit_bytes=60 << 20
        ),
        cost_estimate=lasting(38),
        name="middle",
    )(
        keep, fed, fed_parts, query, dmixed, keys, values, before, near, wk, wv,
        fin.reshape(FEED), fout.reshape(FEED),
    )
    return *others, feed_part, fed


NAMES_OF_WEIGHTS = (
    "selfnorm", "selfquery", "selfkey", "selfvalue", "selfout", "biastable", "crossnorm", "crossquery",
    "crosskey", "crossvalue", "crossout", "feednorm", "feedin", "feedbias", "feedout", "outbias",
)
LONG_NAMES = {
    "q": "selfquery",
    "k": "selfkey",
    "v": "selfvalue",
    "so": "selfout",
    "ck": "crosskey",
    "cv": "crossvalue",
    "cq": "crossquery",
    "co": "crossout",
}


def whole_over_wa(shard):
    return lax.all_gather(shard, "wa", axis=0, tiled=True)


def reduce_plain(parts, smalls):
    shares = [
        lax.psum_scatter(part, "wa", scatter_dimension=0, tiled=True).astype(F32)
        for part in parts.values()
    ]
    totals = lax.psum(shares, "ctx")
    return dict(zip(parts, totals, strict=True)), lax.psum(smalls, ("ctx", "wa"))


def per_device(tokens, neighbours, cotangent, *shards):
    given = dict(zip(NAMES_OF_WEIGHTS, shards, strict=True))
    peers = lax.axis_size("ctx")
    position = lax.axis_index("ctx")
    row_count, model_width = tokens.shape[1:]
    split_heads = peers * 2 == H and row_count == BLOCK
    inputs = tokens[0].astype(F32)
    upstream_low = cotangent[0]
    upstream = upstream_low.astype(F32)
    spans = neighbours.shape[1]
    span_rows = neighbours.shape[2] * neighbours.shape[3]
    own_rows = neighbours[0].reshape(spans * span_rows, model_width)
    if split_heads and span_rows == BLOCK:
        attended_low, normed_low, full, small_of, upstream_all, projected, attention_state = (
            heads_forward(tokens[0], own_rows, upstream_low, given)
        )
        before, keys_cross, values_cross = projected
        feed_in = full["feedin"]
        normed_self, back_self = jax.vjp(root_norm, inputs, small_of["selfnorm"])
    else:
        small_of = {name: whole_over_wa(given[name]).astype(F32) for name in GAINS}
        full = {name: whole_over_wa(given[name]) for name in LONG_NAMES.values()}
        normed_self, back_self = jax.vjp(root_norm, inputs, small_of["selfnorm"])
        normed_low = normed_self.astype(BF)
        attended_low, attention_state = ring_forward(
            *(
                forward_product(normed_low, full[name]).astype(BF)
                for name in ("selfquery", "selfkey", "selfvalue")
            ),
            whole_over_wa(given["biastable"]),
        )
        upstream_all = lax.all_gather(upstream_low, "wa", axis=0)
        feed_in = lax.all_to_all(given["feedin"], "wa", 1, 0, tiled=True)
        before = passed_along(own_rows[-span_rows:], "ctx", 1)
        near_rows = jnp.concatenate([before, own_rows], 0)
        keys_cross = forward_product(near_rows, full["crosskey"]).astype(BF)
        values_cross = forward_product(near_rows, full["crossvalue"]).astype(BF)
    hidden = inputs + forward_product(attended_low, full["selfout"])

    normed_cross, back_cross = jax.vjp(root_norm, hidden, small_of["crossnorm"])
    cross_in = normed_cross.astype(BF)
    query_cross = forward_product(cross_in, full["crossquery"]).astype(BF)
    keep = jnp.full((8, WIDE), jnp.where(position > 0, 1.0, 0.0), F32)
    mixed_low = cross_forward(keep, query_cross, keys_cross, values_cross)
    hidden_two = hidden + forward_product(mixed_low, full["crossout"])

    normed_feed, back_feed = jax.vjp(root_norm, hidden_two, small_of["feednorm"])
    feed_low = normed_feed.astype(BF)
    bias_row = given["feedbias"].astype(F32)[None]
    fed, fed_parts, grad_feed, fin, fout, bias_sums = ffn(
        split_heads, feed_low, upstream_all, feed_in, given["feedout"], bias_row
    )
    grad_two_part, grad_feednorm = back_feed(grad_feed)
    grad_two = upstream + grad_two_part
    two_low = grad_two.astype(BF)

    grad_mixed = back_product(two_low, full["crossout"]).astype(BF)
    early = {}
    if split_heads:
        grad_query_cross, early["ck"], early["cv"], first, near_low, near_last, feed_part, fed = middle(
            keep,
            query_cross,
            grad_mixed,
            keys_cross,
            values_cross,
            before,
            own_rows,
            full["crosskey"],
            full["crossvalue"],
            fed,
            fed_parts,
            fin,
            fout,
        )
    else:
        grad_query_cross, dkeys, dvalues = cross_backward(
            keep, query_cross, grad_mixed, keys_cross, values_cross
        )
        near_grads = back_product(dkeys, full["crosskey"]) + back_product(
            dvalues, full["crossvalue"]
        )
        first, near_last = near_grads[:span_rows].astype(BF), near_grads[-span_rows:]
        near_low = near_grads[span_rows:-span_rows].astype(BF)
        early["ck"] = outer_product(near_rows, dkeys).astype(BF)
        early["cv"] = outer_product(near_rows, dvalues).astype(BF)
    result = (hidden_two + fed + small_of["outbias"]).astype(BF)
    back = passed_along(first, "ctx", -1).astype(F32)
    grad_hidden_part, grad_crossnorm = back_cross(
        back_product(grad_query_cross, full["crossquery"])
    )
    grad_hidden = grad_two + grad_hidden_part
    hidden_low = grad_hidden.astype(BF)
    dout_low = back_product(hidden_low, full["selfout"]).astype(BF)
    sides = {
        "cq": (cross_in, grad_query_cross),
        "co": (mixed_low, two_low),
        "so": (attended_low, hidden_low),
    }
    if split_heads:
        parts = [early["ck"], early["cv"], *(side for name in MADE for side in sides[name])]
        dquery_low, dkey_low, dvalue_low, grad_biastable, shares = heads_backward(
            attention_state, dout_low, parts, feed_part
        )
        *shares, fin, fout = shares
    else:
        dquery_low, dkey_low, dvalue_low, grad_biastable = ring_backward(attention_state, dout_low)
    grad_normed = (
        back_product(dquery_low, full["selfquery"])
        + back_product(dkey_low, full["selfkey"])
        + back_product(dvalue_low, full["selfvalue"])
    )
    grad_input_part, grad_selfnorm = back_self(grad_normed)
    grad_inputs = (grad_hidden + grad_input_part).astype(BF)

    grad_neigh = (
        jnp.concatenate([near_low, (near_last + back).astype(BF)], 0)
        .reshape(neighbours.shape)
    )
    late_grads = (dquery_low, dkey_low, dvalue_low)
    wa, owners = lax.axis_index("wa"), lax.axis_size("wa")
    bias_grad = jnp.sum(bias_sums, axis=0)
    placed = lax.dynamic_update_slice(
        jnp.zeros((owners, bias_grad.size), F32), bias_grad[None], (wa, 0)
    )
    sums = [grad_selfnorm, grad_crossnorm, grad_feednorm, jnp.sum(upstream, axis=0), grad_biastable]
    packed = jnp.concatenate([*(v.reshape(owners, -1) for v in sums), placed], axis=1)
    packed = jnp.pad(packed, ((0, 0), (0, LINE * 2 - packed.shape[1]))).reshape(-1, WIDE)
    if split_heads:
        *reduced, packed, fin = reduce_grads(
            *shares, packed, normed_low, late_grads, fin
        )
        grads = unfold(dict(zip((*NAMES, *LATE), reduced, strict=True)))
        fout = fout.reshape(given["feedout"].shape)
    else:
        for name, grad in zip(LATE, late_grads, strict=True):
            sides[name] = (normed_low, grad)
        for name, (left, right) in sides.items():
            early[name] = outer_product(left, right).astype(BF)
        grads, packed = reduce_plain(early, packed)
        fin, fout = lax.psum((fin, fout), "ctx")
        fin = lax.all_to_all(fin, "wa", 0, 1, tiled=True)
    grads["fin"], grads["fout"] = fin.astype(F32), fout.astype(F32)
    mine = lax.dynamic_index_in_dim(packed.reshape(owners, -1), wa, 0, keepdims=False)
    cuts, start = [], 0
    for v in (*sums, placed):
        cuts.append(mine[start : start + v.size // owners])
        start += v.size // owners
    own_selfnorm, own_crossnorm, own_feednorm, own_outbias, own_table, own_feedbias = cuts
    return (
        result[None],
        grad_inputs[None],
        grad_neigh,
        own_selfnorm,
        grads["q"],
        grads["k"],
        grads["v"],
        grads["so"],
        own_table.reshape(-1, H),
        own_crossnorm,
        grads["cq"],
        grads["ck"],
        grads["cv"],
        grads["co"],
        own_feednorm,
        grads["fin"],
        own_feedbias,
        grads["fout"],
        own_outbias,
    )


def solution(mesh):
    return jax.shard_map(
        per_device,
        mesh=mesh,
        in_specs=(
            P("wa", "ctx", None),
            P("wa", "ctx", None, None, None),
            P("wa", "ctx", None),
            P("wa"),
            P("wa", None),
            P("wa", None),
            P("wa", None),
            P("wa", None),
            P("wa", None),
            P("wa"),
            P("wa", None),
            P("wa", None),
            P("wa", None),
            P("wa", None),
            P("wa"),
            P("wa", None),
            P("wa"),
            P("wa", None),
            P("wa"),
        ),
        out_specs=(
            P("wa", "ctx", None),
            P("wa", "ctx", None),
            P("wa", "ctx", None, None, None),
            P("wa"),
            P("wa", None),
            P("wa", None),
            P("wa", None),
            P("wa", None),
            P("wa", None),
            P("wa"),
            P("wa", None),
            P("wa", None),
            P("wa", None),
            P("wa", None),
            P("wa"),
            P("wa", None),
            P("wa"),
            P("wa", None),
            P("wa"),
        ),
        check_vma=False,
    )
```

```python
import functools
import math

import jax
import jax.numpy as jnp
from jax import lax
from jax.experimental import pallas as pl
from jax.experimental.pallas import tpu as pltpu
from jax.sharding import PartitionSpec as P

H = 16
HD = 64
NB = 32
MAXD = 128
BLOCK = 256
SPAN = 64
MESH = pl.DeviceIdType.MESH
WIDE = 128
LINE = 1024
BF = jnp.bfloat16
F32 = jnp.float32


epsilon = 1e-06
negative = -1e30
strongest_precision = lax.Precision.HIGHEST


def passed_along(value, axis, by):
    peers = lax.axis_size(axis)
    pairs = [(i, i + by) for i in range(peers) if 0 <= i + by < peers]
    return lax.ppermute(value, axis, pairs)


def from_behind(block, axis, distance):
    devices = range(lax.axis_size(axis))
    route = [((i - distance) % len(devices), i) for i in devices]
    return lax.ppermute(block, axis, route)


def bucket_edges():
    half_count = NB // 2
    exact_part = half_count // 2
    edge_list = []
    for level_index in range(exact_part + 1, half_count):
        hits = [
            distance_now
            for distance_now in range(exact_part, MAXD + 1)
            if exact_part
            + int(
                math.log(distance_now / exact_part)
                / math.log(MAXD / exact_part)
                * (half_count - exact_part)
            )
            >= level_index
        ]
        edge_list.append(min(hits + [MAXD]))
    return (half_count, exact_part, edge_list)


def bucket_of(offset_value):
    half_count, exact_part, edge_list = bucket_edges()
    magnitude = jnp.abs(offset_value)
    far_part = exact_part + sum(
        [(magnitude >= edge_value).astype(magnitude.dtype) for edge_value in edge_list],
        jnp.zeros_like(magnitude),
    )
    return jnp.where(offset_value > 0, half_count, 0) + jnp.where(
        magnitude < exact_part, magnitude, far_part
    )


def root_norm(values, gain_vector):
    return (
        values
        * lax.rsqrt(jnp.mean(values * values, axis=-1, keepdims=True) + epsilon)
        * gain_vector
    )


def gelu_tanh(values):
    return jax.nn.gelu(values, approximate=True)


def forward_product(values, weight):
    return jnp.dot(values, weight, preferred_element_type=jnp.float32)


def outer_product(left_side, right_side):
    return lax.dot_general(
        left_side, right_side, (((0,), (0,)), ((), ())), preferred_element_type=jnp.float32
    )


def back_product(grad_low, weight):
    return lax.dot_general(
        grad_low, weight, (((1,), (1,)), ((), ())), preferred_element_type=jnp.float32
    )


def make_bias(bucket_bias_rows, row_count):
    query_place = jnp.arange(row_count)[:, None]
    key_place = jnp.arange(row_count)[None, :]
    levels = jnp.arange(NB)
    current_bucket_selector = (
        bucket_of(key_place - query_place)[None] == levels[:, None, None]
    ).astype(jnp.float32)
    previous_bucket_selector = (
        bucket_of(key_place - row_count - query_place)[None] == levels[:, None, None]
    ).astype(jnp.float32)
    onehot_far = (bucket_of(jnp.array(-MAXD, jnp.int32)) == levels).astype(jnp.float32)
    current_block_bias = jnp.einsum(
        "smz,sj->jmz", current_bucket_selector, bucket_bias_rows, precision=strongest_precision
    )
    previous_block_bias = jnp.einsum(
        "smz,sj->jmz", previous_bucket_selector, bucket_bias_rows, precision=strongest_precision
    )
    bias_far = jnp.dot(onehot_far, bucket_bias_rows, precision=strongest_precision)
    mask_same = key_place // BLOCK <= query_place // BLOCK
    return (
        (current_block_bias, previous_block_bias, bias_far, mask_same),
        (current_bucket_selector, previous_bucket_selector, onehot_far),
    )


def pair_scores(query_heads, key_heads, relation, bias_set, scale_factor):
    current_block_bias, previous_block_bias, bias_far, mask_same = bias_set
    raw_scores = jnp.einsum(
        "qhd,khd->hqk", query_heads, key_heads, preferred_element_type=jnp.float32
    )
    bias_rows = jnp.where(
        relation == 0,
        current_block_bias,
        jnp.where(relation == 1, previous_block_bias, bias_far[:, None, None]),
    )
    allowed = jnp.logical_or(relation > 0, mask_same)
    return jnp.where(allowed[None], raw_scores * scale_factor + bias_rows, negative)


def pair_core(
    query_heads,
    dout_heads,
    log_total,
    row_delta,
    key_heads,
    value_heads,
    relation,
    bias_set,
    scale_factor,
):
    scores = pair_scores(query_heads, key_heads, relation, bias_set, scale_factor)
    weights_now = jnp.exp(scores - log_total[:, :, None])
    grad_weights = jnp.einsum(
        "qhd,khd->hqk", dout_heads, value_heads, preferred_element_type=jnp.float32
    )
    dscores = weights_now * (grad_weights - row_delta[:, :, None])
    return (weights_now, dscores, (dscores * scale_factor).astype(jnp.bfloat16))


def add_tables(relative_bias_tables, dscores, relation):
    same_sum, prev_sum, far_sum = relative_bias_tables
    return (
        same_sum + jnp.where(relation == 0, dscores, 0.0),
        prev_sum + jnp.where(relation == 1, dscores, 0.0),
        far_sum + jnp.where(relation >= 2, jnp.sum(dscores, axis=(1, 2)), 0.0),
    )


def forward_fold(query_heads, position, row_count, bias_set, scale_factor, running, pieces):
    keys_all, values_all = pieces

    def one_shard(folded, shard_step):
        key_heads = lax.dynamic_slice_in_dim(
            keys_all, shard_step * row_count, row_count, 0
        ).reshape(row_count, H, HD)
        value_heads = lax.dynamic_slice_in_dim(
            values_all, shard_step * row_count, row_count, 0
        ).reshape(row_count, H, HD)
        relation = position - shard_step

        def one_compute(current):
            running_max, running_sum, running_acc = current
            scores = pair_scores(query_heads, key_heads, relation, bias_set, scale_factor)
            new_max = jnp.maximum(running_max, jnp.max(scores, axis=-1))
            factor = jnp.exp(running_max - new_max)
            weights_now = jnp.exp(scores - new_max[:, :, None])
            new_sum = running_sum * factor + jnp.sum(weights_now, axis=-1)
            update = jnp.einsum(
                "hqk,khd->qhd",
                weights_now.astype(jnp.bfloat16),
                value_heads,
                preferred_element_type=jnp.float32,
            )
            scaled = running_acc.reshape(row_count, H, HD) * factor.T[:, :, None]
            return (new_max, new_sum, (scaled + update).reshape(row_count, H * HD))

        return (lax.cond(relation >= 0, one_compute, lambda unchanged: unchanged, folded), None)

    running, unused = lax.scan(one_shard, running, jnp.arange(keys_all.shape[0] // row_count))
    return running


def nt_dot(left, right):
    return lax.dot_general(left, right, (((1,), (1,)), ((), ())), preferred_element_type=F32)


def nn_dot(left, right):
    return jnp.dot(left, right, preferred_element_type=F32)


def meet(neighbours):
    barrier = pltpu.get_barrier_semaphore()
    for who in neighbours:
        pl.semaphore_signal(barrier, inc=1, device_id=who, device_id_type=MESH)
    pl.semaphore_wait(barrier, len(neighbours))


def ctx_peers(n):
    me = lax.axis_index("ctx")
    return [{"ctx": lax.rem(me + d, n)} for d in range(1, n)]


def other_wa(me, bit):
    flipped = lax.rem(me // bit, 2)
    return me + bit - 2 * bit * flipped


def remote(src, dst, send_sem, recv_sem, **device):
    return pltpu.make_async_remote_copy(
        src_ref=src,
        dst_ref=dst,
        send_sem=send_sem,
        recv_sem=recv_sem,
        device_id=device,
        device_id_type=MESH,
    )


RING = 8
HOPS = RING - 1


def ring_place(n):
    me = lax.axis_index("ctx")
    half = n // 2

    def at(place):
        return jnp.where(place < half, 2 * place, 2 * (n - 1 - place) + 1)

    place = jnp.where(lax.rem(me, 2) == 0, me // 2, n - 1 - me // 2)
    return place, at(lax.rem(place + 1, n)), at(lax.rem(place + n - 1, n))


class Ring:
    def __init__(self, lanes, send, recv, share=None, hold=None, full=None):
        self.lanes, self.share, self.hold, self.full = lanes, share, hold, full
        self.sems = send, recv
        self.place, self.after, self.before = ring_place(RING)

    def copy(self, lane, src, dst, step):
        send, recv = self.sems
        way = self.lanes[lane][1]
        return remote(
            src, dst, send.at[lane, step], recv.at[lane, step], ctx=self.after if way == 1 else self.before
        )

    def chunk(self, lane, offset):
        here = self.place if self.lanes[lane][1] == 1 else RING - self.place
        return lax.rem(here + offset + 2 * RING, RING)

    def scatter(self, step, which):
        for lane in which:
            b, _, rows = self.lanes[lane]
            share = self.share.at[b, self.chunk(lane, -step), rows]

            @pl.when(step > 0)
            def _():
                there = self.hold.at[b, jnp.maximum(step - 1, 0), rows]
                self.copy(lane, share, there, jnp.maximum(step - 1, 0)).wait_recv()
                share[...] = (share[...].astype(F32) + there[...].astype(F32)).astype(BF)

            @pl.when(step < HOPS)
            def _():
                there = jnp.minimum(step, HOPS - 1)
                self.copy(lane, share, self.hold.at[b, there, rows], there).start()

    def gather(self, step, which):
        for lane in which:
            b, _, rows = self.lanes[lane]
            full = self.full[b].at[self.chunk(lane, 1 - step), rows]

            @pl.when(step > 0)
            def _():
                self.copy(lane, full, full, jnp.maximum(step - 1, 0)).wait_recv()

            @pl.when(step < HOPS)
            def _():
                self.copy(lane, full, full, jnp.minimum(step, HOPS - 1)).start()

    def finish(self, part):
        def one(step, unused):
            for lane in range(len(self.lanes)):
                self.copy(lane, part(lane), part(lane), step).wait_send()
            return unused

        lax.fori_loop(0, HOPS, one, 0)


TALL, FLAT = (224, 1024), (256, 896)
EARLY = ("ck", "cv", "cq", "co", "so")
MADE = ("cq", "co", "so")
LATE = ("q", "k", "v")
FEED = (8, 112, 896)
FEED_LANES = (
    (0, 1, slice(0, 64)),
    (1, -1, slice(0, 64)),
    (0, 1, slice(64, 112)),
    (1, -1, slice(64, 112)),
)
FEED_TURNS = ((0, 1), (2, 3))


def product_into(out_ref, left, right):
    for c in range(left.shape[1] // WIDE):
        lanes = slice(c * WIDE, (c + 1) * WIDE)
        turned = left[:, lanes].astype(F32).T.astype(BF)
        out_ref[lanes, :] = nn_dot(turned, right[...]).astype(BF)


class Folding:
    def __init__(self, names, parts, scratch):
        self.names = names
        self.parts = parts
        tall, flat, sems = scratch
        self.sets = {TALL: tall, FLAT: flat}
        self.own_sem, self.core_send, self.core_recv, self.x_send, self.x_recv = sems
        self.wa = lax.axis_index("wa")
        self.mate, self.across = other_wa(self.wa, 1), other_wa(self.wa, 2)
        self.core, self.half = lax.rem(self.wa, 2), self.wa // 2
        self.slots, count = {}, {TALL: 0, FLAT: 0}
        for name in names:
            shape = self.shape_of(name)
            self.slots[name] = (count[shape], self.sets[shape])
            count[shape] += 1
        self.own_copies, self.core_copies, self.x_copies = {}, {}, {}

    @staticmethod
    def shape_of(name):
        return FLAT if name in ("co", "so") else TALL

    @classmethod
    def scratch(cls, names):
        shapes = []
        for shape in (TALL, FLAT):
            many = sum(cls.shape_of(name) == shape for name in names)
            if many:
                shapes += [pltpu.VMEM((many, 2, *shape), BF)] * 2 + [pltpu.VMEM((many, *shape), BF)] * 2
        dma = pltpu.SemaphoreType.DMA
        many = len(names)
        return shapes + [dma((many, 2))] * 3 + [dma((many,))] * 2

    def start(self, *names):
        for name in names:
            u = self.names.index(name)
            slot, (own, inn, _, _) = self.slots[name]
            rows = self.shape_of(name)[0]
            for x in range(2):
                mine = pl.ds(pl.multiple_of((2 * x + self.core) * rows, 16), rows)
                theirs = pl.ds(pl.multiple_of((2 * x + 1 - self.core) * rows, 16), rows)
                copy = remote(
                    self.parts[name].at[theirs],
                    inn.at[slot, x],
                    self.core_send.at[u, x],
                    self.core_recv.at[u, x],
                    wa=self.mate,
                )
                copy.start()
                self.core_copies[name, x] = copy
                copy = pltpu.make_async_copy(
                    self.parts[name].at[mine], own.at[slot, x], self.own_sem.at[u, x]
                )
                copy.start()
                self.own_copies[name, x] = copy
            slot, (_, _, out, land) = self.slots[name]
            self.x_copies[name] = remote(
                out.at[slot], land.at[slot], self.x_send.at[u], self.x_recv.at[u], wa=self.across
            )

    def send(self, name):
        self.prepare(name)
        self.x_copies[name].start()

    def prepare(self, name):
        slot, (own, inn, out, _) = self.slots[name]
        for x in range(2):
            self.own_copies[name, x].wait()
            self.core_copies[name, x].wait_recv()
        away = 1 - self.half
        out[slot] = (own[slot, away].astype(F32) + inn[slot, away].astype(F32)).astype(BF)

    def total(self, name):
        slot, (own, inn, _, land) = self.slots[name]
        self.x_copies[name].wait_recv()
        here = self.half
        return (
            own[slot, here].astype(F32) + inn[slot, here].astype(F32) + land[slot].astype(F32)
        ).astype(BF)

    def finish(self):
        for name in self.names:
            for x in range(2):
                self.core_copies[name, x].wait_send()
            self.x_copies[name].wait_send()


class Moves:
    def __init__(self, sem):
        self.sem, self.count = sem, 0

    def start(self, src, dst):
        copy = pltpu.make_async_copy(src, dst, self.sem.at[self.count])
        copy.start()
        self.count += 1
        return copy


def wait_all(copies):
    for copy in copies:
        copy.wait()


def lasting(microseconds):
    return pl.CostEstimate(
        flops=0, bytes_accessed=int(microseconds * 3.0e6), transcendentals=0
    )


def lanes_of(index):
    return pl.ds(pl.multiple_of(index * WIDE, WIDE), WIDE)


def rows_of(index, rows):
    return pl.ds(pl.multiple_of(index * rows, rows), rows)


def to_ctx(src, dst, send_sem, recv_sem, target):
    return pltpu.make_async_remote_copy(
        src_ref=src,
        dst_ref=dst,
        send_sem=send_sem,
        recv_sem=recv_sem,
        device_id={"ctx": target},
        device_id_type=MESH,
    )


def head_mask(h, rows):
    lane = lax.broadcasted_iota(jnp.int32, (rows, WIDE), 1)
    return (lane < HD) if h == 0 else (lane >= HD)


def bias_tiles(bias_ref, me, tiles):
    for h in range(2):
        line = bias_ref[pl.ds(2 * me + h, 1), :]
        rolled = pltpu.roll(
            jnp.broadcast_to(line, (BLOCK, LINE)), 0, 1, stride=1, stride_axis=0
        )
        tiles[h, 0] = rolled[:, :BLOCK]
        tiles[h, 1] = rolled[:, BLOCK : 2 * BLOCK]
        tiles[h, 2] = jnp.broadcast_to(line[:, WIDE : WIDE + BLOCK], (BLOCK, BLOCK))


def spread(n, me, pairs, send, recv, t):
    src, dst = pairs[t]
    for d in range(1, n):
        peer = lax.rem(me + d, n)
        to_ctx(
            src.at[:, lanes_of(peer)], dst.at[rows_of(me, BLOCK)], send.at[t, d], recv.at[t, d], peer
        ).start()
    dst[rows_of(me, BLOCK), :] = src[:, lanes_of(me)]


GATHERED = ("q", "k", "v", "so", "ck", "cv", "cq", "co")
SINGLE = ("cot",)
GAINS = ("selfnorm", "crossnorm", "feednorm", "outbias")


class Gathering:
    def __init__(self, shards, whole, own_sem, send, recv):
        self.names, self.shards, self.whole = tuple(shards), shards, whole
        self.sems = own_sem, send, recv
        self.wa, me = lax.axis_index("wa"), lax.axis_index("ctx")
        self.mate, self.across = other_wa(self.wa, 1), other_wa(self.wa, 2)
        y, z = lax.rem(me, 2), lax.rem(me // 2, 2)
        self.pairs = ((y, me + 1 - 2 * y), (z, me + 2 - 4 * z))
        self.copies = {}

    def start(self):
        own_sem, send, recv = self.sems
        for u, name in enumerate(self.names):
            part, beside = self.pairs[(u + 1) % 2]
            shard, whole = self.shards[name], self.whole[name]
            rows = shard.shape[0]
            parts = 1 if name in SINGLE else 2
            some = rows // parts
            shift = 0 if parts == 1 else part * some

            def at(start, count, ref=whole):
                return ref.at[pl.ds(pl.multiple_of(start, 16), count)]

            mine = at(self.wa * rows, rows)
            theirs = at(self.across * rows, rows)
            theirs_some = at(self.across * rows + shift, some)
            self.copies[name] = {
                "over": remote(
                    at(shift, some, shard), at(self.wa * rows + shift, some), send.at[u, 0], recv.at[u, 0], wa=self.across
                ),
                "near": remote(shard, mine, send.at[u, 1], recv.at[u, 1], wa=self.mate),
                "pass": remote(theirs, theirs, send.at[u, 2], recv.at[u, 2], wa=self.mate),
                "side": remote(theirs_some, theirs_some, send.at[u, 3], recv.at[u, 3], ctx=beside),
                "own": pltpu.make_async_copy(shard, mine, own_sem.at[u]),
            }
            self.copies[name]["near"].start()
            self.copies[name]["own"].start()

    def cross(self, *names):
        for name in names:
            self.copies[name]["over"].start()

    def forward(self, *names):
        for name in names:
            self.copies[name]["over"].wait_recv()
            self.copies[name]["pass" if name in SINGLE else "side"].start()

    def land(self, *names):
        for name in names:
            self.copies[name]["side"].wait_recv()
            self.copies[name]["pass"].start()

    def arrive(self, *names):
        for name in names:
            self.copies[name]["near"].wait_recv()
            self.copies[name]["pass"].wait_recv()
            self.copies[name]["own"].wait()

    def finish(self):
        for name, copies in self.copies.items():
            for which in ("over", "near", "pass") + (() if name in SINGLE else ("side",)):
                copies[which].wait_send()


class Columns:
    def __init__(self, gathering, shard, whole, send, recv):
        wa, mate, across = gathering.wa, gathering.mate, gathering.across
        both = other_wa(across, 1)
        rows, width = shard.shape[0], whole.shape[1]
        some = rows // 2

        def block(owner, columns):
            return shard.at[owner, pl.ds(pl.multiple_of(columns * width, WIDE), width)]

        def at(start, count):
            return whole.at[pl.ds(pl.multiple_of(start, 16), count)]

        everything = slice(0, rows)
        self.own = pltpu.make_async_copy(block(everything, wa), at(wa * rows, rows), send.at[5])
        self.near = remote(block(everything, mate), at(wa * rows, rows), send.at[0], recv.at[0], wa=mate)
        self.over, self.side = [], []
        for d, peer in enumerate((across, both)):
            part, beside = gathering.pairs[d]
            mine = pl.ds(pl.multiple_of(part * some, 16), some)
            gone, got = at(wa * rows + part * some, some), at(peer * rows + part * some, some)
            self.over.append(remote(block(mine, peer), gone, send.at[1 + d], recv.at[1 + d], wa=peer))
            self.side.append(remote(got, got, send.at[3 + d], recv.at[3 + d], ctx=beside))

    def start(self):
        self.own.start()
        self.near.start()

    def cross(self):
        for copy in self.over:
            copy.start()

    def forward(self):
        for over, side in zip(self.over, self.side, strict=True):
            over.wait_recv()
            side.start()

    def finish(self):
        self.own.wait()
        self.near.wait()
        for over, side in zip(self.over, self.side, strict=True):
            side.wait()
            over.wait_send()


def attn_forward_kernel(n, tokens_ref, small_ref, near_far, *refs):
    shards = dict(zip((*GATHERED, "cot"), refs[:9], strict=True))
    feed_ref = refs[9]
    wholes = dict(zip((*GATHERED, "cot"), refs[10:19], strict=True))
    feed_whole = refs[19]
    o_ref, low_ref, ot_out, lse_out, small_out, before_ref, qh_out, kh_out, vh_out, keys_out, values_out = refs[20:31]
    (
        held_q, held_k, held_v, held_ck, held_cv, proj, small_in, small_mid, qh, kh, vh, vt, oh, land, tiles,
        acc, stat, send, recv, osend, orecv, small_sem, own_sem, out_sem, gather_send, gather_recv, feed_send,
        feed_recv, span_sem, near_ref, keys_ref, values_ref, move_sem,
    ) = refs[31:]
    moves = Moves(move_sem)
    load_near = moves.start(near_far, near_ref)
    held = {"q": held_q, "k": held_k, "v": held_v, "ck": held_ck, "cv": held_cv}
    gathering = Gathering(shards, wholes | held, own_sem, gather_send, gather_recv)
    columns = Columns(gathering, feed_ref, feed_whole, feed_send, feed_recv)
    both = other_wa(gathering.across, 1)
    meet([*ctx_peers(n), *({"wa": peer} for peer in (gathering.mate, gathering.across, both))])
    me = lax.axis_index("ctx")
    near = remote(small_ref, small_in.at[0], small_sem.at[0], small_sem.at[1], wa=gathering.mate)
    near.start()
    gathering.start()
    gathering.cross("q")
    columns.start()
    span_rows = before_ref.shape[0]
    span = remote(
        near_far.at[near_far.shape[0] - span_rows :],
        before_ref,
        span_sem.at[0],
        span_sem.at[1],
        ctx=lax.rem(me + 1, n),
    )
    over = remote(small_mid, small_in.at[1], small_sem.at[2], small_sem.at[3], wa=gathering.across)
    near.wait_recv()
    small_mid[...] = (small_ref[...].astype(F32) + small_in[0].astype(F32)).astype(BF)
    over.start()
    over.wait_recv()
    small_out[...] = small_mid[...].astype(F32) + small_in[1].astype(F32)
    bias_ref = small_out
    values = tokens_ref[...].astype(F32)
    width = values.shape[1]
    norm = lax.rsqrt(jnp.mean(values * values, axis=1, keepdims=True) + epsilon)
    low_ref[...] = (values * norm * small_out[H : H + 1, :width]).astype(BF)
    bias_tiles(bias_ref, me, tiles)
    pairs = tuple((proj.at[t], dst) for t, dst in enumerate((qh, kh, vh)))
    saving = []

    def save(name):
        copy = pltpu.make_async_copy(held[name], wholes[name], out_sem.at[len(saving)])
        copy.start()
        saving.append(copy)

    def project(t, name):
        gathering.land(name)
        gathering.arrive(name)
        proj[t] = nn_dot(low_ref[...], held[name][...]).astype(BF)
        spread(n, me, pairs, send, recv, t)
        save(name)

    gathering.forward("q")
    gathering.cross("k")
    gathering.forward("k")
    gathering.cross("v")
    project(0, "q")
    gathering.forward("v")
    gathering.cross("so", "ck")
    project(1, "k")
    project(2, "v")

    gathering.forward("so", "ck")
    gathering.cross("cv", "cq")

    for d in range(1, n):
        peer = lax.rem(me + n - d, n)
        for t, (src, dst) in enumerate(pairs):
            to_ctx(
                src.at[:, lanes_of(peer)], dst.at[rows_of(peer, BLOCK)], send.at[t, d], recv.at[t, d], peer
            ).wait_recv()
    stores = [moves.start(*pair) for pair in ((qh, qh_out), (kh, kh_out), (vh, vh_out))]
    for i in range(n):
        part = slice(i * BLOCK, (i + 1) * BLOCK)
        vt[:, part] = vh[part, :].astype(F32).T.astype(BF)

    def query_block(step, unused):
        @pl.when((step == 0) & (me < n - 1))
        def _():
            span.start()

        @pl.when(step == 1)
        def _():
            gathering.forward("cv", "cq")
            gathering.land("so", "ck")
            gathering.cross("co")
            columns.cross()

        @pl.when(step == 6)
        def _():
            gathering.land("cv", "cq")
            gathering.forward("co")
            columns.forward()
            gathering.cross("cot")

        i = lax.rem(me + 1 + step, n)
        rows = rows_of(i, BLOCK)
        q_now = qh[rows, :] * BF(HD**-0.5)
        masked = [jnp.where(head_mask(h, BLOCK), q_now, BF(0)) for h in range(2)]

        def fold(j, which, first):
            keys = kh[rows_of(j, BLOCK), :]
            for h in range(2):
                scores = nt_dot(keys, masked[h])
                if which is None:
                    scores = scores + bias_ref[pl.ds(2 * me + h, 1), WIDE : WIDE + BLOCK]
                else:
                    scores = scores + tiles[h, which]
                top = jnp.max(scores, axis=0, keepdims=True)
                if not first:
                    old = stat[h : h + 1, :]
                    top = jnp.maximum(old, top)
                weights = jnp.exp(scores - top)
                total = jnp.sum(weights, axis=0, keepdims=True)
                vals = vt[h * HD : (h + 1) * HD, rows_of(j, BLOCK)]
                mixed = nn_dot(vals, weights.astype(BF))
                if not first:
                    factor = jnp.exp(old - top)
                    total = total + stat[2 + h : 3 + h, :] * factor
                    mixed = mixed + acc[h * HD : (h + 1) * HD, :] * factor
                stat[h : h + 1, :] = top
                stat[2 + h : 3 + h, :] = total
                acc[h * HD : (h + 1) * HD, :] = mixed

        fold(i, 0, True)

        @pl.when(i >= 1)
        def _():
            fold(i - 1, 1, False)

        def far(j, unused):
            fold(j, None, False)
            return unused

        lax.fori_loop(0, i - 1, far, 0)
        for h in range(2):
            total = stat[2 + h : 3 + h, :]
            part = acc[h * HD : (h + 1) * HD, :] / total
            acc[h * HD : (h + 1) * HD, :] = part
            lse_out[h : h + 1, rows] = stat[h : h + 1, :] + jnp.log(total)
        done = acc[...]
        ot_out[:, rows] = done
        oh[rows, :] = done.T.astype(BF)

        @pl.when(i != me)
        def _():
            d = lax.rem(i - me + n, n)
            to_ctx(oh.at[rows], land.at[:, lanes_of(me)], osend.at[d], orecv.at[d], i).start()

        @pl.when(i == me)
        def _():
            land[:, lanes_of(me)] = oh[rows, :]

        return unused

    lax.fori_loop(0, n, query_block, 0)
    load_near.wait()

    @pl.when(me > 0)
    def _():
        span.wait_recv()

    @pl.when(me == 0)
    def _():
        before_ref[...] = jnp.zeros_like(before_ref)

    for name, out_ref, far_ref in (("ck", keys_ref, keys_out), ("cv", values_ref, values_out)):
        gathering.arrive(name)
        save(name)
        out_ref[:span_rows, :] = nn_dot(before_ref[...], held[name][...]).astype(BF)
        for g in range(near_ref.shape[0] // span_rows):
            rows = slice(g * span_rows, (g + 1) * span_rows)
            there = slice((g + 1) * span_rows, (g + 2) * span_rows)
            out_ref[there, :] = nn_dot(near_ref[rows, :], held[name][...]).astype(BF)
        stores.append(moves.start(out_ref, far_ref))
    gathering.land("co")
    gathering.forward("cot")
    for d in range(1, n):
        peer = lax.rem(me + d, n)
        for t, (src, dst) in enumerate(pairs):
            to_ctx(
                src.at[:, lanes_of(peer)], dst.at[rows_of(me, BLOCK)], send.at[t, d], recv.at[t, d], peer
            ).wait_send()
        back = to_ctx(
            oh.at[rows_of(peer, BLOCK)], land.at[:, lanes_of(me)], osend.at[d], orecv.at[d], peer
        )
        back.wait_send()
        back.wait_recv()
    o_ref[...] = land[...]
    gathering.arrive("so", "cq", "co", "cot")
    gathering.finish()
    columns.finish()

    @pl.when(me < n - 1)
    def _():
        span.wait_send()

    near.wait_send()
    over.wait_send()
    wait_all(saving + stores)


def vmem(count):
    return [pl.BlockSpec(memory_space=pltpu.VMEM)] * count


def attn_forward(n, tokens, small, near, shards, feed):
    rows, seq = tokens.shape[0], n * tokens.shape[0]
    owners = lax.axis_size("wa")
    low = functools.partial(jax.ShapeDtypeStruct, dtype=BF)
    heads = low((seq, WIDE))
    wholes = [low((owners * s.shape[0], s.shape[1])) for s in shards]
    width = wholes[0].shape[1]
    dma = pltpu.SemaphoreType.DMA
    span_rows = 256
    keys = low((span_rows + near.shape[0], width))
    any_spec = pl.BlockSpec(memory_space=pl.ANY)
    return pl.pallas_call(
        functools.partial(attn_forward_kernel, n),
        out_shape=(
            *wholes,
            low((owners * feed.shape[0], feed.shape[1] // owners)),
            low((rows, width)),
            low(tokens.shape),
            jax.ShapeDtypeStruct((WIDE, seq), F32),
            jax.ShapeDtypeStruct((8, seq), F32),
            jax.ShapeDtypeStruct(small.shape, F32),
            low((span_rows, near.shape[1])),
            heads,
            heads,
            heads,
            keys,
            keys,
        ),
        in_specs=vmem(2) + [any_spec] * 11,
        out_specs=tuple([any_spec] * 10 + vmem(6) + [any_spec] * 5),
        scratch_shapes=[
            *[pltpu.VMEM(wholes[0].shape, BF)] * 5,
            pltpu.VMEM((3, rows, width), BF),
            pltpu.VMEM((2, *small.shape), BF),
            pltpu.VMEM(small.shape, BF),
            pltpu.VMEM((seq, WIDE), BF),
            pltpu.VMEM((seq, WIDE), BF),
            pltpu.VMEM((seq, WIDE), BF),
            pltpu.VMEM((WIDE, seq), BF),
            pltpu.VMEM((seq, WIDE), BF),
            pltpu.VMEM((rows, width), BF),
            pltpu.VMEM((2, 3, BLOCK, BLOCK), F32),
            pltpu.VMEM((WIDE, BLOCK), F32),
            pltpu.VMEM((8, BLOCK), F32),
            dma((3, n)),
            dma((3, n)),
            dma((n,)),
            dma((n,)),
            dma((4,)),
            dma((9,)),
            dma((5,)),
            dma((9, 4)),
            dma((9, 4)),
            dma((6,)),
            dma((5,)),
            dma((2,)),
            pltpu.VMEM(near.shape, BF),
            pltpu.VMEM(keys.shape, BF),
            pltpu.VMEM(keys.shape, BF),
            dma((6,)),
        ],
        compiler_params=pltpu.CompilerParams(
            collective_id=1, has_side_effects=True, vmem_limit_bytes=60 << 20
        ),
        cost_estimate=lasting(85),
        name="attn_forward",
    )(tokens, small, near, *shards, feed)


def attn_backward_kernel(n, do_ref, lse_ref, bias_ref, feed_part, *rest):
    far = rest[:10]
    sides_far = far[4:]
    line_ref, *outs = rest[12:21]
    near = rest[21:31]
    kh, qh, ot_ref, vh = near[:4]
    given = dict(zip(MADE, zip(near[4::2], near[5::2], strict=True), strict=True))
    tall_pair, tall_one, flat_out, *feed_full, move_sem = rest[31:37]
    (
        doh, kt, stage, land, dk_acc, dv_acc, dq_acc, q_masked, do_masked, delta, tiles, dtiles,
        send, recv, gsend, grecv, ring_send, ring_recv,
    ) = rest[37:55]
    made = dict(zip(MADE, rest[55:58], strict=True))
    parts = dict(zip(EARLY, (rest[10], rest[11], *made.values()), strict=True))
    extra = rest[58:]
    moves = Moves(move_sem)
    loads = [moves.start(*pair) for pair in zip(far, near, strict=True)]
    fold_wa = Folding(EARLY, parts, (extra[0:4], extra[4:8], extra[8:13]))
    ring = Ring(FEED_LANES, ring_send, ring_recv, full=feed_full)
    for lane in range(2):
        feed_full[lane][ring.chunk(lane, 1)] = feed_part[lane]
    meet([*ctx_peers(n), {"wa": fold_wa.mate}, {"wa": fold_wa.across}])
    me = lax.axis_index("ctx")
    pairs = ((do_ref, doh),)
    spread(n, me, pairs, send, recv, 0)
    fold_wa.start("ck", "cv")
    bias_tiles(bias_ref, me, tiles)
    loads[0].wait()
    for j in range(n):
        part = slice(j * BLOCK, (j + 1) * BLOCK)
        kt[:, part] = (kh[part, :].astype(F32) * HD**-0.5).T.astype(BF)
    dtiles[...] = jnp.zeros_like(dtiles)
    for name in EARLY[:2]:
        fold_wa.send(name)
    ring.gather(jnp.int32(0), FEED_TURNS[0])
    ring.gather(jnp.int32(0), FEED_TURNS[1])
    wait_all(loads[1:])
    for name in MADE:
        product_into(made[name], *given[name])
        fold_wa.start(name)
    dq_acc[...] = jnp.zeros_like(dq_acc)
    for d in range(1, n):
        peer = lax.rem(me + n - d, n)
        to_ctx(
            do_ref.at[:, lanes_of(peer)], doh.at[rows_of(peer, BLOCK)], send.at[0, d], recv.at[0, d], peer
        ).wait_recv()
    for i in range(n):
        rows = slice(i * BLOCK, (i + 1) * BLOCK)
        q_now = qh[rows, :] * BF(HD**-0.5)
        do_now = doh[rows, :]
        products = do_now.astype(F32).T * ot_ref[:, rows]
        for h in range(2):
            mask = head_mask(h, BLOCK)
            q_masked[h, rows, :] = jnp.where(mask, q_now, BF(0))
            do_masked[h, rows, :] = jnp.where(mask, do_now, BF(0))
            delta[h : h + 1, rows] = jnp.sum(
                products[h * HD : (h + 1) * HD], axis=0, keepdims=True
            )

    def pair(t, now):
        i, j = now
        rows, there = rows_of(i, BLOCK), rows_of(j, BLOCK)

        @pl.when(t == 6)
        def _():
            for name in EARLY[2:]:
                fold_wa.send(name)

        for turn, lanes in enumerate(FEED_TURNS):

            @pl.when((lax.rem(t, 4) == 2 * turn + 1) & (t <= 4 * HOPS))
            def _():
                ring.gather(t // 4 + 1, lanes)

        first = i == j
        which = jnp.minimum(i - j, 2)
        keys, vals = kh[there, :], vh[there, :]
        dk_part, dv_part = None, None
        for h in range(2):
            query, dout = q_masked[h, rows, :], do_masked[h, rows, :]
            scores = nt_dot(keys, query)
            weights = jnp.exp(scores + tiles[h, which] - lse_ref[h : h + 1, rows])
            dweights = nt_dot(vals, dout)
            dscores = weights * (dweights - delta[h : h + 1, rows])
            dtiles[h, which] += dscores
            low = dscores.astype(BF)
            dv_now = nn_dot(weights.astype(BF), dout)
            dk_now = nn_dot(low, query)
            dv_part = dv_now if dv_part is None else dv_part + dv_now
            dk_part = dk_now if dk_part is None else dk_part + dk_now
            half = slice(h * HD, (h + 1) * HD)
            dq_acc[half, rows] += nn_dot(kt[half, there], low)

        @pl.when(first)
        def _():
            dk_acc[...] = dk_part
            dv_acc[...] = dv_part

        @pl.when(jnp.logical_not(first))
        def _():
            dk_acc[...] += dk_part
            dv_acc[...] += dv_part

        last = i == n - 1

        @pl.when(last)
        def _():
            stage[1, there, :] = dk_acc[...].astype(BF)
            stage[2, there, :] = dv_acc[...].astype(BF)
            deliver(j, (1, 2))

        after = lax.rem(j + 1, n)
        return jnp.where(last, after, i + 1), jnp.where(last, after, j)

    def deliver(i, arrays):
        rows = rows_of(i, BLOCK)

        @pl.when(i != me)
        def _():
            d = lax.rem(i - me + n, n)
            for t in arrays:
                to_ctx(
                    stage.at[t, rows], land.at[t, :, lanes_of(me)], gsend.at[t, d], grecv.at[t, d], i
                ).start()

        @pl.when(i == me)
        def _():
            for t in arrays:
                land[t, :, lanes_of(me)] = stage[t, rows, :]

    begin = lax.rem(me + 1, n)
    lax.fori_loop(0, n * (n + 1) // 2, pair, (begin, begin))

    def dq_block(step, unused):
        i = lax.rem(me + 1 + step, n)
        rows = rows_of(i, BLOCK)
        stage[0, rows, :] = dq_acc[:, rows].T.astype(BF)
        deliver(i, (0,))
        return unused

    lax.fori_loop(0, n, dq_block, 0)
    ring.finish(lambda lane: feed_full[FEED_LANES[lane][0]].at[0, FEED_LANES[lane][2]])
    stores = [moves.start(full, out) for full, out in zip(feed_full, outs[6:8], strict=True)]
    tall_pair[:224, :] = fold_wa.total("cq")
    tall_pair[224:, :] = fold_wa.total("ck")
    tall_one[...] = fold_wa.total("cv")
    for at, name in ((0, "co"), (32, "so")):
        flat_out[:, at : at + 32, :] = fold_wa.total(name).reshape(8, 32, 896)
    stores += [
        moves.start(tall_pair, outs[3]),
        moves.start(tall_one, outs[4]),
        moves.start(flat_out, outs[5]),
    ]
    fold_wa.finish()
    for h in range(2):
        line = jnp.concatenate(
            [dtiles[h, 0], dtiles[h, 1], jnp.zeros((BLOCK, LINE - 2 * BLOCK), F32)], axis=1
        )
        row = lax.broadcasted_iota(jnp.int32, (BLOCK, LINE), 0)
        for bit in range(8):
            moved = pltpu.roll(line, LINE - (1 << bit), 1)
            line = jnp.where((row >> bit) & 1 == 1, moved, line)
        line_ref[h : h + 1, :] = jnp.sum(line, axis=0, keepdims=True)
        line_ref[2 + h : 3 + h, :BLOCK] = jnp.sum(dtiles[h, 2], axis=0, keepdims=True)
    line_ref[2:4, BLOCK:] = jnp.zeros((2, LINE - BLOCK), F32)
    line_ref[4:8, :] = jnp.zeros((4, LINE), F32)
    for d in range(1, n):
        peer = lax.rem(me + d, n)
        to_ctx(
            do_ref.at[:, lanes_of(peer)], doh.at[rows_of(me, BLOCK)], send.at[0, d], recv.at[0, d], peer
        ).wait_send()
        for t in range(3):
            back = to_ctx(
                stage.at[t, rows_of(peer, BLOCK)], land.at[t, :, lanes_of(me)], gsend.at[t, d], grecv.at[t, d], peer
            )
            back.wait_send()
            back.wait_recv()
    wait_all(stores + [moves.start(land.at[t], outs[t]) for t in range(3)])


def attn_backward(n, dout, qh, kh, vh, ot, lse, bias_lines, parts, feed_part):
    rows, seq = dout.shape[0], n * dout.shape[0]
    grads = jax.ShapeDtypeStruct(dout.shape, BF)
    feed = jax.ShapeDtypeStruct(FEED, BF)
    low = functools.partial(jax.ShapeDtypeStruct, dtype=BF)
    any_spec = pl.BlockSpec(memory_space=pl.ANY)
    far = (kh, qh, ot, vh, *parts[2:])
    shares = (low((448, 1024)), low((224, 1024)), low((8, 64, 896)))
    line, *outs = pl.pallas_call(
        functools.partial(attn_backward_kernel, n),
        out_shape=(jax.ShapeDtypeStruct((8, LINE), F32), grads, grads, grads, *shares, feed, feed),
        in_specs=vmem(4) + [any_spec] * 12,
        out_specs=tuple(vmem(1) + [any_spec] * 8),
        scratch_shapes=[
            *(pltpu.VMEM(v.shape, v.dtype) for v in far),
            *(pltpu.VMEM(v.shape, v.dtype) for v in (*shares, feed, feed)),
            pltpu.SemaphoreType.DMA((18,)),
            pltpu.VMEM((seq, WIDE), BF),
            pltpu.VMEM((WIDE, seq), BF),
            pltpu.VMEM((3, seq, WIDE), BF),
            pltpu.VMEM((3, *dout.shape), BF),
            pltpu.VMEM((BLOCK, WIDE), F32),
            pltpu.VMEM((BLOCK, WIDE), F32),
            pltpu.VMEM((WIDE, seq), F32),
            pltpu.VMEM((2, seq, WIDE), BF),
            pltpu.VMEM((2, seq, WIDE), BF),
            pltpu.VMEM((8, seq), F32),
            pltpu.VMEM((2, 3, BLOCK, BLOCK), F32),
            pltpu.VMEM((2, 3, BLOCK, BLOCK), F32),
            pltpu.SemaphoreType.DMA((1, n)),
            pltpu.SemaphoreType.DMA((1, n)),
            pltpu.SemaphoreType.DMA((3, n)),
            pltpu.SemaphoreType.DMA((3, n)),
            pltpu.SemaphoreType.DMA((len(FEED_LANES), HOPS)),
            pltpu.SemaphoreType.DMA((len(FEED_LANES), HOPS)),
            pltpu.VMEM((896, 1024), BF),
            pltpu.VMEM((1024, 896), BF),
            pltpu.VMEM((1024, 896), BF),
            *Folding.scratch(EARLY),
        ],
        compiler_params=pltpu.CompilerParams(
            collective_id=2, has_side_effects=True, vmem_limit_bytes=60 << 20
        ),
        cost_estimate=lasting(100),
        name="attn_backward",
    )(dout, lse, bias_lines, feed_part, *far, *parts[:2])
    return *outs[:3], line, *outs[3:]


BUFFERS = {
    "cq": (1, (224, 1024)),
    "cv": (-1, (224, 1024)),
    "ck": (1, (224, 1024)),
    "co": (-1, (8, 32, 896)),
    "so0": (1, (8, 16, 896)),
    "so1": (-1, (8, 16, 896)),
}
NAMES = tuple(BUFFERS)


def chunk_shape(name):
    shape = BUFFERS[name][1]
    return (shape[0], WIDE) if len(shape) == 2 else shape[1:]


def chunk_of(ref, name, c):
    return ref.at[:, lanes_of(c)] if len(BUFFERS[name][1]) == 2 else ref.at[c]


class Grid:
    def __init__(self, u, share, half_in, half, quarters, whole, send, recv):
        self.u, self.share, self.half_in, self.half = u, share, half_in, half
        self.quarters, self.whole, self.sems = quarters, whole, (send, recv)
        me = lax.axis_index("ctx")
        self.y, self.z = lax.rem(me, 2), me // 2
        self.beside = me + 1 - 2 * self.y
        self.column = [lax.rem(self.z + d, 4) for d in range(1, 4)]

    def half_of(self, y):
        return pl.ds(pl.multiple_of(y * 4 * WIDE, WIDE), 4 * WIDE)

    def piece_of(self, z, y=None):
        start = z * WIDE if y is None else (4 * y + z) * WIDE
        return pl.ds(pl.multiple_of(start, WIDE), WIDE)

    def copy(self, number, src, dst, target):
        send, recv = self.sems
        return remote(src, dst, send.at[self.u, number], recv.at[self.u, number], ctx=target)

    def start(self, total):
        self.share[...] = total
        self.first = self.copy(
            0, self.share.at[:, self.half_of(1 - self.y)], self.half_in, self.beside
        )
        self.first.start()

    def spread(self):
        self.first.wait_recv()
        mine = self.share[:, self.half_of(self.y)]
        self.half[...] = (mine.astype(F32) + self.half_in[...].astype(F32)).astype(BF)
        self.out = []
        for d, z in enumerate(self.column):
            copy = self.copy(
                1 + d, self.half.at[:, self.piece_of(z)], self.quarters.at[self.z], 2 * z + self.y
            )
            copy.start()
            self.out.append(copy)
        self.quarters[self.z] = self.half[:, self.piece_of(self.z)]

    def total(self):
        for copy in self.out:
            copy.wait_recv()
        done = self.quarters[0].astype(F32)
        for z in range(1, 4):
            done = done + self.quarters[z].astype(F32)
        piece = self.whole.at[:, self.piece_of(self.z, self.y)]
        piece[...] = done.astype(BF)
        self.back = []
        for d, z in enumerate(self.column):
            copy = self.copy(4 + d, piece, piece, 2 * z + self.y)
            copy.start()
            self.back.append(copy)

    def join(self):
        for copy in self.back:
            copy.wait_recv()
        mine = self.whole.at[:, self.half_of(self.y)]
        self.last = self.copy(7, mine, mine, self.beside)
        self.last.start()

    def finish(self):
        self.last.wait_recv()
        for copy in (self.first, *self.out, *self.back, self.last):
            copy.wait_send()


def reduce_kernel(*refs):
    small_ref, ca_far, cb_far, out_far = refs[:4]
    sides_far, fin_ref = refs[4:8], refs[8]
    count = len(NAMES)
    small_out = refs[9]
    full_out = dict(zip((*NAMES, *LATE), refs[10 : 13 + count], strict=True))
    fin_out = refs[13 + count]
    refs = refs[14 + count :]
    low_ref, *sides = refs[:4]
    given = dict(zip(LATE, sides, strict=True))
    full = dict(zip((*NAMES, *LATE), refs[4 : 7 + count], strict=True))
    late_full = full
    move_sem = refs[7 + count]
    refs = refs[8 + count :]
    share = dict(zip(NAMES, refs[:count], strict=True))
    hold = dict(zip(NAMES, refs[count : 2 * count], strict=True))
    refs = refs[2 * count :]
    grid_share, half_in, half, quarters, small_in, small_mid, small_beside, small_column = refs[:8]
    small_send, small_recv, ring_send, ring_recv, grid_send, grid_recv, fin_send, fin_recv = refs[8:16]
    made, turned = refs[16:18]
    moves = Moves(move_sem)
    share_loads = [
        moves.start(*pair)
        for pair in (
            (ca_far.at[:224], share["cq"]),
            (cb_far, share["cv"]),
            (ca_far.at[224:], share["ck"]),
            (out_far.at[:, :32], share["co"]),
            (out_far.at[:, 32:48], share["so0"]),
            (out_far.at[:, 48:], share["so1"]),
        )
    ]
    side_loads = [moves.start(*pair) for pair in zip(sides_far, (low_ref, *sides), strict=True)]
    parts = {name: made.at[u] for u, name in enumerate(LATE)}
    extra = refs[18:]
    fold_wa = Folding(LATE, parts, (extra[0:4], None, extra[4:9]))
    place, after, before = ring_place(RING)
    grids = {
        name: Grid(
            u, grid_share.at[u], half_in.at[u], half.at[u], quarters.at[u], late_full[name], grid_send, grid_recv
        )
        for u, name in enumerate(LATE)
    }
    wa, both = fold_wa.wa, other_wa(fold_wa.across, 1)
    some = grids["q"]
    in_column = [2 * z + some.y for z in some.column]
    meet(
        [{"wa": peer} for peer in (fold_wa.mate, fold_wa.across, both)]
        + [{"ctx": peer} for peer in (after, before, some.beside, *in_column)]
    )
    near = remote(small_ref, small_in.at[0], small_send.at[0], small_recv.at[0], wa=fold_wa.mate)
    near.start()
    over = remote(small_mid.at[0], small_in.at[1], small_send.at[1], small_recv.at[1], wa=fold_wa.across)
    beside = remote(small_mid.at[1], small_beside, small_send.at[2], small_recv.at[2], ctx=some.beside)
    columns = [
        remote(small_mid.at[2], small_column.at[some.z], small_send.at[3 + d], small_recv.at[3 + d], ctx=peer)
        for d, peer in enumerate(in_column)
    ]
    own_fin = pltpu.make_async_copy(fin_ref.at[wa], fin_out.at[:, columns_of(wa)], fin_send.at[3])
    own_fin.start()
    fin_copies = [
        remote(fin_ref.at[peer], fin_out.at[:, columns_of(wa)], fin_send.at[d], fin_recv.at[d], wa=peer)
        for d, peer in enumerate((fold_wa.across, both, fold_wa.mate))
    ]
    wait_all(share_loads)
    copies = {}

    def ring_step(b, name, step):
        way = BUFFERS[name][0]
        here = place if way == 1 else RING - place
        target = after if way == 1 else before
        if step > 0:
            copies[name, step - 1].wait_recv()
        if step == 2 * HOPS:
            return
        now = lax.rem(here - step + 3 * RING, RING)
        mine = chunk_of(share[name], name, now)
        done = chunk_of(full[name], name, now)
        if 0 < step <= HOPS:
            total = mine[...].astype(F32) + hold[name][step - 1].astype(F32)
            (mine if step < HOPS else done)[...] = total.astype(BF)
        src, dst = (mine, hold[name].at[step]) if step < HOPS else (done, done)
        copy = remote(src, dst, ring_send.at[b, step], ring_recv.at[b, step], ctx=target)
        copy.start()
        copies[name, step] = copy

    def small_over():
        near.wait_recv()
        small_mid[0] = small_ref[...] + small_in[0]
        over.start()

    def small_next():
        over.wait_recv()
        small_mid[1] = small_mid[0] + small_in[1]
        beside.start()

    def small_last():
        beside.wait_recv()
        small_mid[2] = small_mid[1] + small_beside[...]
        small_column[some.z] = small_mid[2]
        for copy in columns:
            copy.start()

    def begin(name, following=None):
        total = fold_wa.total(name)
        if following:
            fold_wa.x_copies[following].start()
        grids[name].start(total)

    def make(name):
        parts[name][...] = nn_dot(turned[...], given[name][...]).astype(BF)
        fold_wa.start(name)

    def make_all():
        wait_all(side_loads)
        turned[...] = low_ref[...].astype(F32).T.astype(BF)
        make("q")
        make("k")
        fold_wa.send("q")
        make("v")
        fold_wa.prepare("k")
        fold_wa.prepare("v")

    events = {
        0: [make_all, small_over],
        4: [lambda: begin("q", "k"), small_next],
        6: [grids["q"].spread, lambda: begin("k", "v"), small_last],
        8: [grids["q"].total, grids["k"].spread],
        9: [lambda: begin("v"), grids["q"].join, *(copy.start for copy in fin_copies)],
        10: [grids["k"].total],
        11: [grids["v"].spread, grids["k"].join],
        12: [grids["v"].total],
        14: [grids["v"].join],
    }
    for tick in range(2 * HOPS + 1):
        for b, name in enumerate(NAMES):
            ring_step(b, name, tick)
        for event in events.get(tick, ()):
            event()
    stores = [moves.start(full[name], full_out[name]) for name in NAMES]
    for copy in columns:
        copy.wait_recv()
    total = small_column[0]
    for z in range(1, 4):
        total = total + small_column[z]
    small_out[...] = total
    for name in LATE:
        grids[name].finish()
        stores.append(moves.start(full[name], full_out[name]))
    fold_wa.finish()
    for copy in (near, over, beside, *columns, *copies.values()):
        copy.wait_send()
    own_fin.wait()
    for copy in fin_copies:
        copy.wait()
    wait_all(stores)


def columns_of(owner):
    return pl.ds(pl.multiple_of(owner * 896, WIDE), 896)


def reduce_grads(pair, one, flat, small, low, grads, fin):
    dma = pltpu.SemaphoreType.DMA
    any_spec = pl.BlockSpec(memory_space=pl.ANY)
    late = len(LATE)
    shapes = [*(BUFFERS[b][1] for b in NAMES), *[TALL] * late]
    small, *others = pl.pallas_call(
        reduce_kernel,
        out_shape=(
            jax.ShapeDtypeStruct(small.shape, F32),
            *(jax.ShapeDtypeStruct(shape, BF) for shape in shapes),
            jax.ShapeDtypeStruct((224, 3584), BF),
        ),
        in_specs=vmem(1) + [any_spec] * 8,
        out_specs=tuple(vmem(1) + [any_spec] * (len(shapes) + 1)),
        scratch_shapes=[
            pltpu.VMEM(low.shape, BF),
            *(pltpu.VMEM(grad.shape, BF) for grad in grads),
            *(pltpu.VMEM(shape, BF) for shape in shapes),
            dma((10 + len(shapes),)),
            *(pltpu.VMEM(BUFFERS[b][1], BF) for b in NAMES),
            *(pltpu.VMEM((HOPS, *chunk_shape(b)), BF) for b in NAMES),
            pltpu.VMEM((late, *TALL), BF),
            pltpu.VMEM((late, 224, 4 * WIDE), BF),
            pltpu.VMEM((late, 224, 4 * WIDE), BF),
            pltpu.VMEM((late, 4, 224, WIDE), BF),
            pltpu.VMEM((2, *small.shape), F32),
            pltpu.VMEM((3, *small.shape), F32),
            pltpu.VMEM(small.shape, F32),
            pltpu.VMEM((4, *small.shape), F32),
            dma((6,)),
            dma((6,)),
            dma((len(NAMES), 2 * HOPS)),
            dma((len(NAMES), 2 * HOPS)),
            dma((late, 8)),
            dma((late, 8)),
            dma((4,)),
            dma((3,)),
            pltpu.VMEM((late, 896, 1024), BF),
            pltpu.VMEM((896, 256), BF),
            *Folding.scratch(LATE),
        ],
        compiler_params=pltpu.CompilerParams(
            collective_id=3, has_side_effects=True, vmem_limit_bytes=56 << 20
        ),
        cost_estimate=lasting(90),
        name="reduce_grads",
    )(small, pair, one, flat, low, *grads, fin.reshape(4, 224, 896))
    return *others[:-1], small, others[-1]


def unfold(full):
    wide = {name: value.astype(F32) for name, value in full.items()}
    return {
        "co": wide["co"].reshape(FLAT),
        "so": jnp.concatenate([wide["so0"], wide["so1"]], 1).reshape(FLAT),
        **{name: wide[name] for name in ("cq", "ck", "cv", *LATE)},
    }


GELU = (2.0 / math.pi) ** 0.5


def ffn_kernel(
    late, f_ref, bias_ref, win_far, cot_far, wout_far, df_ref, dbias_ref, res_out, parts_out, dwin_out, dwout_out,
    win_ref, cot_ref, wout_ref, res_ref, parts_ref, dwin_ref, dwout_ref, move_sem, f_all, g_all, dul_all, ahead, own, kept, out_mate, out_cross, in_mate, in_cross, x_out, x_in,
    f_send, f_recv, p_send, p_recv,
):
    moves = Moves(move_sem)
    load_in, load_cot, load_out = (
        moves.start(*pair) for pair in ((win_far, win_ref), (cot_far, cot_ref), (wout_far, wout_ref))
    )
    me = lax.axis_index("wa")
    mate, across = other_wa(me, 1), other_wa(me, 2)
    both = other_wa(across, 1)
    barrier = pltpu.get_barrier_semaphore()
    for peer in (mate, across):
        pl.semaphore_signal(barrier, inc=1, device_id={"wa": peer}, device_id_type=MESH)
    pl.semaphore_wait(barrier, 2)
    to_across = remote(f_ref, f_all.at[me], f_send.at[1], f_recv.at[1], wa=across)
    to_across.start()
    to_mate = remote(f_ref, f_all.at[me], f_send.at[0], f_recv.at[0], wa=mate)
    to_mate.start()
    forward = remote(f_all.at[across], f_all.at[across], f_send.at[2], f_recv.at[2], wa=mate)
    f_all[me] = f_ref[...]
    order = (me, mate, across, both)
    dbias_ref[...] = jnp.zeros_like(dbias_ref)
    load_in.wait()
    for k, s in enumerate(order):
        if k == 1:
            to_mate.wait_recv()
        if k == 2:
            for d in range(2):
                ahead[d] = nt_dot(cot_ref[order[2 + d]], wout_ref[...])
            to_across.wait_recv()
            forward.start()
        if k == 3:
            forward.wait_recv()
        u = nn_dot(f_all[s], win_ref[...]) + bias_ref[...]
        square = u * u
        t = jnp.tanh(GELU * (u + 0.044715 * (square * u)))
        g_all[s] = (0.5 * u * (1.0 + t)).astype(BF)
        if k == 0:
            load_cot.wait()
            load_out.wait()
        slope = 0.5 * (1.0 + t) + 0.5 * u * (1.0 - t * t) * (GELU * (1.0 + 3 * 0.044715 * square))
        du = (nt_dot(cot_ref[s], wout_ref[...]) if k < 2 else ahead[k - 2]) * slope
        dbias_ref[...] += jnp.sum(du.reshape(32, 8, du.shape[1]), axis=0)
        dul_all[s] = du.astype(BF)

    def scatter(which, product):
        out_cross[which] = product(both).astype(BF)
        cross = remote(
            out_cross.at[which], in_cross.at[which], p_send.at[which, 0], p_recv.at[which, 0], wa=mate
        )
        cross.start()
        kept[...] = product(across)
        cross.wait_recv()
        x_out[which] = (kept[...] + in_cross[which].astype(F32)).astype(BF)
        over = remote(
            x_out.at[which], x_in.at[which], p_send.at[which, 1], p_recv.at[which, 1], wa=across
        )
        over.start()
        out_mate[which] = product(mate).astype(BF)
        near = remote(
            out_mate.at[which], in_mate.at[which], p_send.at[which, 2], p_recv.at[which, 2], wa=mate
        )
        near.start()
        own[which] = product(me)
        return cross, over, near

    def finish(which, copies, out_ref):
        cross, over, near = copies
        near.wait_recv()
        over.wait_recv()
        out_ref[...] = own[which] + in_mate[which].astype(F32) + x_in[which].astype(F32)
        for copy in copies:
            copy.wait_send()

    df_copies = scatter(0, lambda s: nt_dot(dul_all[s], win_ref[...]))
    if late:
        res_ref[...] = nn_dot(g_all[me], wout_ref[...])
        for d, s in enumerate(order[1:]):
            parts_ref[d] = nn_dot(g_all[s], wout_ref[...]).astype(BF)
    else:
        res_copies = scatter(1, lambda s: nn_dot(g_all[s], wout_ref[...]))
        parts_ref[...] = jnp.zeros_like(parts_ref)
    stores = []
    if late:
        stores += [moves.start(res_ref, res_out), moves.start(parts_ref, parts_out)]
    width = f_ref.shape[1]

    def outer(left_all, right, out_ref):
        for c in range(width // WIDE):
            lanes = slice(c * WIDE, (c + 1) * WIDE)
            total = None
            for s in range(4):
                left = left_all[s, :, lanes].astype(F32).T.astype(BF)
                now = nn_dot(left, right[s])
                total = now if total is None else total + now
            out_ref[lanes, :] = total.astype(BF)

    outer(f_all, dul_all, dwin_ref)
    stores.append(moves.start(dwin_ref, dwin_out))
    outer(g_all, cot_ref, dwout_ref)
    stores.append(moves.start(dwout_ref, dwout_out))
    finish(0, df_copies, df_ref)
    if not late:
        finish(1, res_copies, res_ref)
        stores += [moves.start(res_ref, res_out), moves.start(parts_ref, parts_out)]
    wait_all(stores)
    for copy in (to_mate, to_across, forward):
        copy.wait_send()


def ffn(late, f_low, cot_all, win, wout, bias):
    rows, width = f_low.shape
    hidden = win.shape[1]
    dma = pltpu.SemaphoreType.DMA
    block = (rows, width)
    any_spec = pl.BlockSpec(memory_space=pl.ANY)
    df, dbias, *others = pl.pallas_call(
        functools.partial(ffn_kernel, late),
        out_shape=(
            jax.ShapeDtypeStruct(block, F32),
            jax.ShapeDtypeStruct((8, hidden), F32),
            jax.ShapeDtypeStruct(block, F32),
            jax.ShapeDtypeStruct((3, *block), BF),
            jax.ShapeDtypeStruct(win.shape, BF),
            jax.ShapeDtypeStruct(wout.shape, BF),
        ),
        in_specs=vmem(2) + [any_spec] * 3,
        out_specs=tuple(vmem(2) + [any_spec] * 4),
        scratch_shapes=[
            pltpu.VMEM(win.shape, BF),
            pltpu.VMEM((4, *block), BF),
            pltpu.VMEM(wout.shape, BF),
            pltpu.VMEM(block, F32),
            pltpu.VMEM((3, *block), BF),
            pltpu.VMEM(win.shape, BF),
            pltpu.VMEM(wout.shape, BF),
            dma((7,)),
            pltpu.VMEM((4, *block), BF),
            pltpu.VMEM((4, rows, hidden), BF),
            pltpu.VMEM((4, rows, hidden), BF),
            pltpu.VMEM((2, rows, hidden), F32),
            pltpu.VMEM((2, *block), F32),
            pltpu.VMEM(block, F32),
            *[pltpu.VMEM((2, *block), BF)] * 6,
            dma((3,)),
            dma((3,)),
            dma((2, 3)),
            dma((2, 3)),
        ],
        compiler_params=pltpu.CompilerParams(
            collective_id=4, has_side_effects=True, vmem_limit_bytes=60 << 20
        ),
        cost_estimate=lasting(44),
        name="feed_forward",
    )(f_low, bias, win, cot_all, wout)
    res, parts, dwin, dwout = others
    return res, parts, df, dwin, dwout, dbias


def padded_rows(pad, values):
    rows = values.shape[0]
    pad[...] = jnp.zeros_like(pad)
    pad[1 : rows + 1, :] = values.astype(F32)


def both_heads(pad, g):
    here = pad[g * SPAN : (g + 1) * SPAN, :]
    left = head_mask(0, SPAN)
    return jnp.concatenate([jnp.where(left, here, 0.0), jnp.where(left, 0.0, here)], 0).astype(BF)


def join_heads(stacked):
    return jnp.where(head_mask(0, SPAN), stacked[:SPAN], stacked[SPAN:])


def cross_forward_kernel(groups, keep_ref, q_ref, k_ref, v_ref, x_ref, q_pad, x_pad):
    padded_rows(q_pad, q_ref[...])
    for g in range(groups):
        rows = slice(g * 256, (g + 1) * 256)
        query = both_heads(q_pad, g) * BF(HD**-0.5)
        scores = nt_dot(query, k_ref[rows, :])
        weights = jnp.exp(scores - jnp.max(scores, axis=1, keepdims=True))
        weights = weights / jnp.sum(weights, axis=1, keepdims=True)
        mixed = join_heads(nn_dot(weights.astype(BF), v_ref[rows, :]))
        if g == 0:
            mixed = mixed * keep_ref[0:1, :]
        x_pad[g * SPAN : (g + 1) * SPAN, :] = mixed
    x_ref[...] = x_pad[1 : x_ref.shape[0] + 1, :].astype(BF)


def pair_specs(*rows):
    return [pl.BlockSpec((r, WIDE), lambda p: (0, p)) for r in rows]


def cross_forward(keep, query, keys, values):
    rows, width = query.shape
    many = keys.shape[0]
    groups = many // 256
    return pl.pallas_call(
        functools.partial(cross_forward_kernel, groups),
        grid=(width // WIDE,),
        out_shape=jax.ShapeDtypeStruct(query.shape, BF),
        in_specs=[pl.BlockSpec((8, WIDE), lambda p: (0, 0)), *pair_specs(rows, many, many)],
        out_specs=pair_specs(rows)[0],
        scratch_shapes=[pltpu.VMEM((groups * SPAN, WIDE), F32)] * 2,
        compiler_params=pltpu.CompilerParams(vmem_limit_bytes=16 << 20),
        cost_estimate=lasting(9),
        name="cross_forward",
    )(keep, query, keys, values)


def cross_backward_kernel(
    groups, keep_ref, q_ref, dx_ref, k_ref, v_ref, dq_ref, dk_ref, dv_ref, q_pad, dx_pad, dq_pad
):
    padded_rows(q_pad, q_ref[...])
    padded_rows(dx_pad, dx_ref[...])
    dx_pad[:SPAN, :] = dx_pad[:SPAN, :] * keep_ref[0:1, :]
    for g in range(groups):
        rows = slice(g * 256, (g + 1) * 256)
        query = both_heads(q_pad, g) * BF(HD**-0.5)
        dmixed = both_heads(dx_pad, g)
        keys, values = k_ref[rows, :], v_ref[rows, :]
        scores = nt_dot(keys, query)
        weights = jnp.exp(scores - jnp.max(scores, axis=0, keepdims=True))
        weights = weights / jnp.sum(weights, axis=0, keepdims=True)
        dweights = nt_dot(values, dmixed)
        dscores = weights * (dweights - jnp.sum(weights * dweights, axis=0, keepdims=True))
        dk_ref[rows, :] = nn_dot(dscores.astype(BF), query).astype(BF)
        dv_ref[rows, :] = nn_dot(weights.astype(BF), dmixed).astype(BF)
        back = (dscores * HD**-0.5).T.astype(BF)
        dq_pad[g * SPAN : (g + 1) * SPAN, :] = join_heads(nn_dot(back, keys))
    dq_ref[...] = dq_pad[1 : dq_ref.shape[0] + 1, :].astype(BF)


def cross_backward(keep, query, dmixed, keys, values):
    rows, width = query.shape
    many = keys.shape[0]
    groups = many // 256
    return pl.pallas_call(
        functools.partial(cross_backward_kernel, groups),
        grid=(width // WIDE,),
        out_shape=(
            jax.ShapeDtypeStruct(query.shape, BF),
            jax.ShapeDtypeStruct(keys.shape, BF),
            jax.ShapeDtypeStruct(keys.shape, BF),
        ),
        in_specs=[
            pl.BlockSpec((8, WIDE), lambda p: (0, 0)),
            *pair_specs(rows, rows, many, many),
        ],
        out_specs=tuple(pair_specs(rows, many, many)),
        scratch_shapes=[pltpu.VMEM((groups * SPAN, WIDE), F32)] * 3,
        compiler_params=pltpu.CompilerParams(vmem_limit_bytes=16 << 20),
        cost_estimate=lasting(17),
        name="cross_backward",
    )(keep, query, dmixed, keys, values)


def line_selector():
    place = jnp.arange(LINE)
    offset = jnp.where(place < LINE // 2, -place, LINE - place)
    return (bucket_of(offset)[None, :] == jnp.arange(NB)[:, None]).astype(jnp.float32)


def ring_forward(query_low, key_low, value_low, bucket_table):
    row_count, attn_width = query_low.shape
    position = lax.axis_index("ctx")
    scale_factor = HD ** (-0.5)
    bias_set, onehots = make_bias(bucket_table.astype(jnp.float32), row_count)
    query_heads = query_low.reshape(row_count, H, HD)
    start_state = (
        jnp.full((H, row_count), negative, jnp.float32),
        jnp.zeros((H, row_count), jnp.float32),
        jnp.zeros((row_count, attn_width), jnp.float32),
    )
    running_max, running_sum, running_acc = forward_fold(
        query_heads,
        position,
        row_count,
        bias_set,
        scale_factor,
        start_state,
        (
            lax.all_gather(key_low, "ctx", axis=0, tiled=True),
            lax.all_gather(value_low, "ctx", axis=0, tiled=True),
        ),
    )
    attended = (running_acc.reshape(row_count, H, HD) / running_sum.T[:, :, None]).reshape(
        row_count, attn_width
    )
    log_total = running_max + jnp.log(running_sum)
    state = (query_heads, key_low, value_low, attended, log_total, bias_set, onehots)
    return attended.astype(jnp.bfloat16), state


def ring_backward(state, dout_low):
    query_heads, key_low, value_low, attended, log_total, bias_set, onehots = state
    row_count, attn_width = dout_low.shape
    cycle_size = lax.axis_size("ctx")
    position = lax.axis_index("ctx")
    scale_factor = HD ** (-0.5)
    dout_heads = dout_low.reshape(row_count, H, HD)
    row_delta = jnp.sum(
        (dout_low.astype(jnp.float32) * attended).reshape(row_count, H, HD), axis=-1
    ).T
    zero_rows = jnp.zeros((row_count, attn_width), jnp.float32)
    zero_tables = (
        jnp.zeros((H, row_count, row_count), jnp.float32),
        jnp.zeros((H, row_count, row_count), jnp.float32),
        jnp.zeros((H,), jnp.float32),
    )

    def visit(folded, key_now, value_now, relation):

        def visit_compute(current):
            dquery_acc, dkey_acc, dvalue_acc, relative_bias_tables = current
            key_heads = key_now.reshape(row_count, H, HD)
            weights_now, dscores, ds_low = pair_core(
                query_heads,
                dout_heads,
                log_total,
                row_delta,
                key_heads,
                value_now.reshape(row_count, H, HD),
                relation,
                bias_set,
                scale_factor,
            )
            dquery = jnp.einsum(
                "hqk,khd->qhd", ds_low, key_heads, preferred_element_type=jnp.float32
            ).reshape(row_count, attn_width)
            dkey = jnp.einsum(
                "hqk,qhd->khd", ds_low, query_heads, preferred_element_type=jnp.float32
            ).reshape(row_count, attn_width)
            dvalue = jnp.einsum(
                "hqk,qhd->khd",
                weights_now.astype(jnp.bfloat16),
                dout_heads,
                preferred_element_type=jnp.float32,
            ).reshape(row_count, attn_width)
            return (
                dquery_acc + dquery,
                dkey_acc + dkey,
                dvalue_acc + dvalue,
                add_tables(relative_bias_tables, dscores, relation),
            )

        return lax.cond(relation >= 0, visit_compute, lambda unchanged: unchanged, folded)

    first_state = visit(
        (zero_rows, zero_rows, zero_rows, zero_tables), key_low, value_low, jnp.array(0, jnp.int32)
    )

    def cycle_step(carried, cycle_index):
        key_now, value_now, (dquery_acc, dkey_acc, dvalue_acc, relative_bias_tables) = carried
        key_next, value_next = passed_along((key_now, value_now), "ctx", 1)
        dkey_next, dvalue_next = (
            from_behind(dkey_acc.astype(jnp.bfloat16), "ctx", 1).astype(dkey_acc.dtype),
            from_behind(dvalue_acc.astype(jnp.bfloat16), "ctx", 1).astype(dvalue_acc.dtype),
        )
        relation = jnp.where(position >= cycle_index, cycle_index, -1)
        updated = visit(
            (dquery_acc, dkey_next, dvalue_next, relative_bias_tables),
            key_next,
            value_next,
            relation,
        )
        return ((key_next, value_next, updated), None)

    (
        unused_key,
        unused_value,
        (dquery_total, dkey_part, dvalue_part, relative_bias_tables),
    ), unused = lax.scan(cycle_step, (key_low, value_low, first_state), jnp.arange(1, cycle_size))
    dkey_total, dvalue_total = (
        from_behind(dkey_part.astype(jnp.bfloat16), "ctx", 1).astype(dkey_part.dtype),
        from_behind(dvalue_part.astype(jnp.bfloat16), "ctx", 1).astype(dvalue_part.dtype),
    )
    dquery_low = dquery_total.astype(jnp.bfloat16)
    dkey_low = dkey_total.astype(jnp.bfloat16)
    dvalue_low = dvalue_total.astype(jnp.bfloat16)
    current_bucket_selector, previous_bucket_selector, onehot_far = onehots
    grad_biastable = (
        jnp.einsum(
            "afw,mfw->am",
            current_bucket_selector,
            relative_bias_tables[0],
            precision=strongest_precision,
        )
        + jnp.einsum(
            "afw,mfw->am",
            previous_bucket_selector,
            relative_bias_tables[1],
            precision=strongest_precision,
        )
        + onehot_far[:, None] * relative_bias_tables[2][None, :]
    )
    return dquery_low, dkey_low, dvalue_low, grad_biastable


def heads_forward(tokens, near, cotangent, given):
    wa, owners = lax.axis_index("wa"), lax.axis_size("wa")
    table = given["biastable"].astype(F32)
    selector = lax.dynamic_slice_in_dim(line_selector(), wa * table.shape[0], table.shape[0], 0)
    lines = jnp.dot(table.T, selector, precision=strongest_precision).astype(BF)
    gains = jnp.concatenate([given[name] for name in GAINS]).reshape(len(GAINS), -1)
    small = jnp.zeros((H, LINE), BF)
    small = lax.dynamic_update_slice(small, gains, (0, wa * gains.shape[1]))
    small = jnp.concatenate([lines, small], 0)
    shards = [given[LONG_NAMES[name]] for name in GATHERED]
    *wholes, upstream_all, feed_in, attended_low, low, ot, lse, small, before, qh, kh, vh, keys, values = attn_forward(
        lax.axis_size("ctx"), tokens, small, near, [*shards, cotangent], given["feedin"]
    )
    width = tokens.shape[1]
    gain_of = {name: small[H + g, :width] for g, name in enumerate(GAINS)}
    full = {LONG_NAMES[name]: whole for name, whole in zip(GATHERED, wholes, strict=True)}
    full["feedin"] = feed_in
    upstream_all = upstream_all.reshape(owners, *tokens.shape)
    saved = (qh, kh, vh, ot, lse, small[:H])
    return attended_low, low, full, gain_of, upstream_all, (before, keys, values), saved


def heads_backward(state, dout_low, parts, feed_part):
    peers = lax.axis_size("ctx")
    dquery_low, dkey_low, dvalue_low, sums, *shares = attn_backward(
        peers, dout_low, *state, parts, feed_part
    )
    selector = line_selector()
    table = jnp.dot(selector, sums[:2].T, precision=strongest_precision)
    far = jnp.sum(sums[2:4], axis=1)
    table = table + selector[:, WIDE : WIDE + 1] * far[None, :]
    whole = jnp.zeros((NB, H), jnp.float32)
    whole = lax.dynamic_update_slice(whole, table, (0, 2 * lax.axis_index("ctx")))
    return dquery_low, dkey_low, dvalue_low, whole, shares


def cross_pair(groups, keep_ref, q_ref, dx_ref, k_ref, v_ref, dq_ref, dk_ref, dv_ref, q_pad, dx_pad, dq_pad, p):
    lanes = lanes_of(p)
    padded_rows(q_pad, q_ref[:, lanes])
    padded_rows(dx_pad, dx_ref[:, lanes])
    dx_pad[:SPAN, :] = dx_pad[:SPAN, :] * keep_ref[0:1, :]
    for g in range(groups):
        rows = slice(g * 256, (g + 1) * 256)
        query = both_heads(q_pad, g) * BF(HD**-0.5)
        dmixed = both_heads(dx_pad, g)
        keys, values = k_ref[rows, lanes], v_ref[rows, lanes]
        scores = nt_dot(keys, query)
        weights = jnp.exp(scores - jnp.max(scores, axis=0, keepdims=True))
        weights = weights / jnp.sum(weights, axis=0, keepdims=True)
        dweights = nt_dot(values, dmixed)
        dscores = weights * (dweights - jnp.sum(weights * dweights, axis=0, keepdims=True))
        dk_ref[rows, lanes] = nn_dot(dscores.astype(BF), query).astype(BF)
        dv_ref[rows, lanes] = nn_dot(weights.astype(BF), dmixed).astype(BF)
        back = (dscores * HD**-0.5).T.astype(BF)
        dq_pad[g * SPAN : (g + 1) * SPAN, :] = join_heads(nn_dot(back, keys))
    dq_ref[:, lanes] = dq_pad[1 : dq_ref.shape[0] + 1, :].astype(BF)


def middle_kernel(
    keep_ref, fed_ref, fed_parts, q_far, dx_far, k_far, v_far, before_far, near_far, wk_far, wv_far, fin_ref,
    fout_ref, feed_out, fed_out, dq_out, dwk_out, dwv_out, first_out, near_out, last_out,
    q_ref, dx_ref, k_ref, v_ref, before_ref, near_ref, wk_ref, wv_ref, dq_ref, dwk_ref, dwv_ref, near_low, near_last,
    dk, dv, q_pad, dx_pad, dq_pad, share, hold, in_mate, in_cross, x_out, x_in, load_sem, ring_send, ring_recv,
    fed_send, fed_recv,
):
    ring = Ring(FEED_LANES, ring_send, ring_recv, share=share, hold=hold)
    moves = Moves(load_sem)
    loads = [moves.start(part, share.at[b]) for b, part in enumerate((fin_ref, fout_ref))]
    pair_loads = [
        moves.start(*pair) for pair in ((q_far, q_ref), (dx_far, dx_ref), (k_far, k_ref), (v_far, v_ref))
    ]
    later_loads = [
        moves.start(*pair)
        for pair in ((wk_far, wk_ref), (wv_far, wv_ref), (before_far, before_ref), (near_far, near_ref))
    ]
    wa = lax.axis_index("wa")
    mate, across = other_wa(wa, 1), other_wa(wa, 2)
    meet([{"ctx": ring.after}, {"ctx": ring.before}, {"wa": mate}, {"wa": across}])
    cross = remote(fed_parts.at[2], in_cross, fed_send.at[0], fed_recv.at[0], wa=mate)
    cross.start()
    near = remote(fed_parts.at[0], in_mate, fed_send.at[1], fed_recv.at[1], wa=mate)
    near.start()
    over = remote(x_out, x_in, fed_send.at[2], fed_recv.at[2], wa=across)
    wait_all(loads)
    for lanes in FEED_TURNS:
        ring.scatter(jnp.int32(0), lanes)
    cross.wait_recv()
    x_out[...] = (fed_parts[1].astype(F32) + in_cross[...].astype(F32)).astype(BF)
    over.start()
    groups = k_ref.shape[0] // 256
    wait_all(pair_loads)

    def two_pairs(m, unused):
        for turn, lanes in enumerate(FEED_TURNS):
            cross_pair(
                groups, keep_ref, q_ref, dx_ref, k_ref, v_ref, dq_ref, dk, dv, q_pad, dx_pad, dq_pad,
                2 * m + turn,
            )
            ring.scatter(m + 1, lanes)
        return unused

    pairs = q_ref.shape[1] // (2 * WIDE)
    lax.fori_loop(0, pairs, two_pairs, 0)
    stores = [moves.start(dq_ref, dq_out)]
    wait_all(later_loads)
    calls = [(step, lanes) for step in range(pairs + 1, HOPS + 1) for lanes in FEED_TURNS]

    def turn():
        if calls:
            step, lanes = calls.pop(0)
            ring.scatter(jnp.int32(step), lanes)

    for g in range(groups):
        rows = slice(g * 256, (g + 1) * 256)
        total = nt_dot(dk[rows, :], wk_ref[...]) + nt_dot(dv[rows, :], wv_ref[...])
        if g == groups - 1:
            near_last[...] = total
        else:
            near_low[rows, :] = total.astype(BF)
        if g % 2 == 1:
            turn()
    stores += [
        moves.start(near_low.at[:256], first_out),
        moves.start(near_low.at[256:], near_out),
        moves.start(near_last, last_out),
    ]
    for c in range(near_ref.shape[1] // WIDE):
        lanes = slice(c * WIDE, (c + 1) * WIDE)
        first = before_ref[:, lanes].astype(F32).T.astype(BF)
        left = near_ref[:, lanes].astype(F32).T.astype(BF)
        for grads, out_ref in ((dk, dwk_ref), (dv, dwv_ref)):
            total = nn_dot(first, grads[:256, :]) + nn_dot(left, grads[256:, :])
            out_ref[lanes, :] = total.astype(BF)
        if c % 2 == 1:
            turn()
    stores += [moves.start(dwk_ref, dwk_out), moves.start(dwv_ref, dwv_out)]
    while calls:
        turn()
    near.wait_recv()
    over.wait_recv()
    fed_out[...] = fed_ref[...] + in_mate[...].astype(F32) + x_in[...].astype(F32)
    for copy in (cross, near, over):
        copy.wait_send()
    for lane in range(2):
        feed_out[lane] = share[lane, ring.chunk(lane, 1)]
    ring.finish(lambda lane: share.at[FEED_LANES[lane][0], 0, FEED_LANES[lane][2]])
    wait_all(stores)


def middle(keep, query, dmixed, keys, values, before, near, wk, wv, fed, fed_parts, fin, fout):
    many, width = keys.shape
    wide = near.shape[1]
    rows = query.shape[0]
    low = functools.partial(jax.ShapeDtypeStruct, dtype=BF)
    dma = pltpu.SemaphoreType.DMA
    any_spec = pl.BlockSpec(memory_space=pl.ANY)
    pad = pltpu.VMEM((many // 256 * SPAN, WIDE), F32)
    feed_part, fed, *others = pl.pallas_call(
        middle_kernel,
        out_shape=(
            low((2, *FEED[1:])),
            jax.ShapeDtypeStruct(fed.shape, F32),
            low(query.shape),
            low(wk.shape),
            low(wv.shape),
            low((256, wide)),
            low((many - 512, wide)),
            jax.ShapeDtypeStruct((256, wide), F32),
        ),
        in_specs=vmem(3) + [any_spec] * 10,
        out_specs=tuple(vmem(2) + [any_spec] * 6),
        scratch_shapes=[
            *[pltpu.VMEM((rows, width), BF)] * 2,
            *[pltpu.VMEM((many, width), BF)] * 2,
            pltpu.VMEM((256, wide), BF),
            pltpu.VMEM((many - 256, wide), BF),
            *[pltpu.VMEM(wk.shape, BF)] * 2,
            pltpu.VMEM((rows, width), BF),
            *[pltpu.VMEM(wk.shape, BF)] * 2,
            pltpu.VMEM((many - 256, wide), BF),
            pltpu.VMEM((256, wide), F32),
            pltpu.VMEM((many, width), BF),
            pltpu.VMEM((many, width), BF),
            pad,
            pad,
            pad,
            pltpu.VMEM((2, *FEED), BF),
            pltpu.VMEM((2, HOPS, *FEED[1:]), BF),
            *[pltpu.VMEM(fed.shape, BF)] * 4,
            dma((16,)),
            dma((len(FEED_LANES), HOPS)),
            dma((len(FEED_LANES), HOPS)),
            dma((3,)),
            dma((3,)),
        ],
        compiler_params=pltpu.CompilerParams(
            collective_id=5, has_side_effects=True, vmem_limit_bytes=60 << 20
        ),
        cost_estimate=lasting(38),
        name="middle",
    )(
        keep, fed, fed_parts, query, dmixed, keys, values, before, near, wk, wv,
        fin.reshape(FEED), fout.reshape(FEED),
    )
    return *others, feed_part, fed


NAMES_OF_WEIGHTS = (
    "selfnorm", "selfquery", "selfkey", "selfvalue", "selfout", "biastable", "crossnorm", "crossquery",
    "crosskey", "crossvalue", "crossout", "feednorm", "feedin", "feedbias", "feedout", "outbias",
)
LONG_NAMES = {
    "q": "selfquery",
    "k": "selfkey",
    "v": "selfvalue",
    "so": "selfout",
    "ck": "crosskey",
    "cv": "crossvalue",
    "cq": "crossquery",
    "co": "crossout",
}


def whole_over_wa(shard):
    return lax.all_gather(shard, "wa", axis=0, tiled=True)


def reduce_plain(parts, smalls):
    shares = [
        lax.psum_scatter(part, "wa", scatter_dimension=0, tiled=True).astype(F32)
        for part in parts.values()
    ]
    totals = lax.psum(shares, "ctx")
    return dict(zip(parts, totals, strict=True)), lax.psum(smalls, ("ctx", "wa"))


def per_device(tokens, neighbours, cotangent, *shards):
    given = dict(zip(NAMES_OF_WEIGHTS, shards, strict=True))
    peers = lax.axis_size("ctx")
    position = lax.axis_index("ctx")
    row_count, model_width = tokens.shape[1:]
    split_heads = peers * 2 == H and row_count == BLOCK
    inputs = tokens[0].astype(F32)
    upstream_low = cotangent[0]
    upstream = upstream_low.astype(F32)
    spans = neighbours.shape[1]
    span_rows = neighbours.shape[2] * neighbours.shape[3]
    own_rows = neighbours[0].reshape(spans * span_rows, model_width)
    if split_heads and span_rows == BLOCK:
        attended_low, normed_low, full, small_of, upstream_all, projected, attention_state = (
            heads_forward(tokens[0], own_rows, upstream_low, given)
        )
        before, keys_cross, values_cross = projected
        feed_in = full["feedin"]
        normed_self, back_self = jax.vjp(root_norm, inputs, small_of["selfnorm"])
    else:
        small_of = {name: whole_over_wa(given[name]).astype(F32) for name in GAINS}
        full = {name: whole_over_wa(given[name]) for name in LONG_NAMES.values()}
        normed_self, back_self = jax.vjp(root_norm, inputs, small_of["selfnorm"])
        normed_low = normed_self.astype(BF)
        attended_low, attention_state = ring_forward(
            *(
                forward_product(normed_low, full[name]).astype(BF)
                for name in ("selfquery", "selfkey", "selfvalue")
            ),
            whole_over_wa(given["biastable"]),
        )
        upstream_all = lax.all_gather(upstream_low, "wa", axis=0)
        feed_in = lax.all_to_all(given["feedin"], "wa", 1, 0, tiled=True)
        before = passed_along(own_rows[-span_rows:], "ctx", 1)
        near_rows = jnp.concatenate([before, own_rows], 0)
        keys_cross = forward_product(near_rows, full["crosskey"]).astype(BF)
        values_cross = forward_product(near_rows, full["crossvalue"]).astype(BF)
    hidden = inputs + forward_product(attended_low, full["selfout"])

    normed_cross, back_cross = jax.vjp(root_norm, hidden, small_of["crossnorm"])
    cross_in = normed_cross.astype(BF)
    query_cross = forward_product(cross_in, full["crossquery"]).astype(BF)
    keep = jnp.full((8, WIDE), jnp.where(position > 0, 1.0, 0.0), F32)
    mixed_low = cross_forward(keep, query_cross, keys_cross, values_cross)
    hidden_two = hidden + forward_product(mixed_low, full["crossout"])

    normed_feed, back_feed = jax.vjp(root_norm, hidden_two, small_of["feednorm"])
    feed_low = normed_feed.astype(BF)
    bias_row = given["feedbias"].astype(F32)[None]
    fed, fed_parts, grad_feed, fin, fout, bias_sums = ffn(
        split_heads, feed_low, upstream_all, feed_in, given["feedout"], bias_row
    )
    grad_two_part, grad_feednorm = back_feed(grad_feed)
    grad_two = upstream + grad_two_part
    two_low = grad_two.astype(BF)

    grad_mixed = back_product(two_low, full["crossout"]).astype(BF)
    early = {}
    if split_heads:
        grad_query_cross, early["ck"], early["cv"], first, near_low, near_last, feed_part, fed = middle(
            keep,
            query_cross,
            grad_mixed,
            keys_cross,
            values_cross,
            before,
            own_rows,
            full["crosskey"],
            full["crossvalue"],
            fed,
            fed_parts,
            fin,
            fout,
        )
    else:
        grad_query_cross, dkeys, dvalues = cross_backward(
            keep, query_cross, grad_mixed, keys_cross, values_cross
        )
        near_grads = back_product(dkeys, full["crosskey"]) + back_product(
            dvalues, full["crossvalue"]
        )
        first, near_last = near_grads[:span_rows].astype(BF), near_grads[-span_rows:]
        near_low = near_grads[span_rows:-span_rows].astype(BF)
        early["ck"] = outer_product(near_rows, dkeys).astype(BF)
        early["cv"] = outer_product(near_rows, dvalues).astype(BF)
    result = (hidden_two + fed + small_of["outbias"]).astype(BF)
    back = passed_along(first, "ctx", -1).astype(F32)
    grad_hidden_part, grad_crossnorm = back_cross(
        back_product(grad_query_cross, full["crossquery"])
    )
    grad_hidden = grad_two + grad_hidden_part
    hidden_low = grad_hidden.astype(BF)
    dout_low = back_product(hidden_low, full["selfout"]).astype(BF)
    sides = {
        "cq": (cross_in, grad_query_cross),
        "co": (mixed_low, two_low),
        "so": (attended_low, hidden_low),
    }
    if split_heads:
        parts = [early["ck"], early["cv"], *(side for name in MADE for side in sides[name])]
        dquery_low, dkey_low, dvalue_low, grad_biastable, shares = heads_backward(
            attention_state, dout_low, parts, feed_part
        )
        *shares, fin, fout = shares
    else:
        dquery_low, dkey_low, dvalue_low, grad_biastable = ring_backward(attention_state, dout_low)
    grad_normed = (
        back_product(dquery_low, full["selfquery"])
        + back_product(dkey_low, full["selfkey"])
        + back_product(dvalue_low, full["selfvalue"])
    )
    grad_input_part, grad_selfnorm = back_self(grad_normed)
    grad_inputs = (grad_hidden + grad_input_part).astype(BF)

    grad_neigh = (
        jnp.concatenate([near_low, (near_last + back).astype(BF)], 0)
        .reshape(neighbours.shape)
    )
    late_grads = (dquery_low, dkey_low, dvalue_low)
    wa, owners = lax.axis_index("wa"), lax.axis_size("wa")
    bias_grad = jnp.sum(bias_sums, axis=0)
    placed = lax.dynamic_update_slice(
        jnp.zeros((owners, bias_grad.size), F32), bias_grad[None], (wa, 0)
    )
    sums = [grad_selfnorm, grad_crossnorm, grad_feednorm, jnp.sum(upstream, axis=0), grad_biastable]
    packed = jnp.concatenate([*(v.reshape(owners, -1) for v in sums), placed], axis=1)
    packed = jnp.pad(packed, ((0, 0), (0, LINE * 2 - packed.shape[1]))).reshape(-1, WIDE)
    if split_heads:
        *reduced, packed, fin = reduce_grads(
            *shares, packed, normed_low, late_grads, fin
        )
        grads = unfold(dict(zip((*NAMES, *LATE), reduced, strict=True)))
        fout = fout.reshape(given["feedout"].shape)
    else:
        for name, grad in zip(LATE, late_grads, strict=True):
            sides[name] = (normed_low, grad)
        for name, (left, right) in sides.items():
            early[name] = outer_product(left, right).astype(BF)
        grads, packed = reduce_plain(early, packed)
        fin, fout = lax.psum((fin, fout), "ctx")
        fin = lax.all_to_all(fin, "wa", 0, 1, tiled=True)
    grads["fin"], grads["fout"] = fin.astype(F32), fout.astype(F32)
    mine = lax.dynamic_index_in_dim(packed.reshape(owners, -1), wa, 0, keepdims=False)
    cuts, start = [], 0
    for v in (*sums, placed):
        cuts.append(mine[start : start + v.size // owners])
        start += v.size // owners
    own_selfnorm, own_crossnorm, own_feednorm, own_outbias, own_table, own_feedbias = cuts
    return (
        result[None],
        grad_inputs[None],
        grad_neigh,
        own_selfnorm,
        grads["q"],
        grads["k"],
        grads["v"],
        grads["so"],
        own_table.reshape(-1, H),
        own_crossnorm,
        grads["cq"],
        grads["ck"],
        grads["cv"],
        grads["co"],
        own_feednorm,
        grads["fin"],
        own_feedbias,
        grads["fout"],
        own_outbias,
    )


def solution(mesh):
    return jax.shard_map(
        per_device,
        mesh=mesh,
        in_specs=(
            P("wa", "ctx", None),
            P("wa", "ctx", None, None, None),
            P("wa", "ctx", None),
            P("wa"),
            P("wa", None),
            P("wa", None),
            P("wa", None),
            P("wa", None),
            P("wa", None),
            P("wa"),
            P("wa", None),
            P("wa", None),
            P("wa", None),
            P("wa", None),
            P("wa"),
            P("wa", None),
            P("wa"),
            P("wa", None),
            P("wa"),
        ),
        out_specs=(
            P("wa", "ctx", None),
            P("wa", "ctx", None),
            P("wa", "ctx", None, None, None),
            P("wa"),
            P("wa", None),
            P("wa", None),
            P("wa", None),
            P("wa", None),
            P("wa", None),
            P("wa"),
            P("wa", None),
            P("wa", None),
            P("wa", None),
            P("wa", None),
            P("wa"),
            P("wa", None),
            P("wa"),
            P("wa", None),
            P("wa"),
        ),
        check_vma=False,
    )
```

```python
import functools
import math

import jax
import jax.numpy as jnp
from jax import lax
from jax.experimental import pallas as pl
from jax.experimental.pallas import tpu as pltpu
from jax.sharding import PartitionSpec as P

H = 16
HD = 64
NB = 32
MAXD = 128
BLOCK = 256
SPAN = 64
MESH = pl.DeviceIdType.MESH
WIDE = 128
LINE = 1024
BF = jnp.bfloat16
F32 = jnp.float32


epsilon = 1e-06
negative = -1e30
strongest_precision = lax.Precision.HIGHEST


def passed_along(value, axis, by):
    peers = lax.axis_size(axis)
    pairs = [(i, i + by) for i in range(peers) if 0 <= i + by < peers]
    return lax.ppermute(value, axis, pairs)


def from_behind(block, axis, distance):
    devices = range(lax.axis_size(axis))
    route = [((i - distance) % len(devices), i) for i in devices]
    return lax.ppermute(block, axis, route)


def bucket_edges():
    half_count = NB // 2
    exact_part = half_count // 2
    edge_list = []
    for level_index in range(exact_part + 1, half_count):
        hits = [
            distance_now
            for distance_now in range(exact_part, MAXD + 1)
            if exact_part
            + int(
                math.log(distance_now / exact_part)
                / math.log(MAXD / exact_part)
                * (half_count - exact_part)
            )
            >= level_index
        ]
        edge_list.append(min(hits + [MAXD]))
    return (half_count, exact_part, edge_list)


def bucket_of(offset_value):
    half_count, exact_part, edge_list = bucket_edges()
    magnitude = jnp.abs(offset_value)
    far_part = exact_part + sum(
        [(magnitude >= edge_value).astype(magnitude.dtype) for edge_value in edge_list],
        jnp.zeros_like(magnitude),
    )
    return jnp.where(offset_value > 0, half_count, 0) + jnp.where(
        magnitude < exact_part, magnitude, far_part
    )


def root_norm(values, gain_vector):
    return (
        values
        * lax.rsqrt(jnp.mean(values * values, axis=-1, keepdims=True) + epsilon)
        * gain_vector
    )


def gelu_tanh(values):
    return jax.nn.gelu(values, approximate=True)


def forward_product(values, weight):
    return jnp.dot(values, weight, preferred_element_type=jnp.float32)


def outer_product(left_side, right_side):
    return lax.dot_general(
        left_side, right_side, (((0,), (0,)), ((), ())), preferred_element_type=jnp.float32
    )


def back_product(grad_low, weight):
    return lax.dot_general(
        grad_low, weight, (((1,), (1,)), ((), ())), preferred_element_type=jnp.float32
    )


def make_bias(bucket_bias_rows, row_count):
    query_place = jnp.arange(row_count)[:, None]
    key_place = jnp.arange(row_count)[None, :]
    levels = jnp.arange(NB)
    current_bucket_selector = (
        bucket_of(key_place - query_place)[None] == levels[:, None, None]
    ).astype(jnp.float32)
    previous_bucket_selector = (
        bucket_of(key_place - row_count - query_place)[None] == levels[:, None, None]
    ).astype(jnp.float32)
    onehot_far = (bucket_of(jnp.array(-MAXD, jnp.int32)) == levels).astype(jnp.float32)
    current_block_bias = jnp.einsum(
        "smz,sj->jmz", current_bucket_selector, bucket_bias_rows, precision=strongest_precision
    )
    previous_block_bias = jnp.einsum(
        "smz,sj->jmz", previous_bucket_selector, bucket_bias_rows, precision=strongest_precision
    )
    bias_far = jnp.dot(onehot_far, bucket_bias_rows, precision=strongest_precision)
    mask_same = key_place // BLOCK <= query_place // BLOCK
    return (
        (current_block_bias, previous_block_bias, bias_far, mask_same),
        (current_bucket_selector, previous_bucket_selector, onehot_far),
    )


def pair_scores(query_heads, key_heads, relation, bias_set, scale_factor):
    current_block_bias, previous_block_bias, bias_far, mask_same = bias_set
    raw_scores = jnp.einsum(
        "qhd,khd->hqk", query_heads, key_heads, preferred_element_type=jnp.float32
    )
    bias_rows = jnp.where(
        relation == 0,
        current_block_bias,
        jnp.where(relation == 1, previous_block_bias, bias_far[:, None, None]),
    )
    allowed = jnp.logical_or(relation > 0, mask_same)
    return jnp.where(allowed[None], raw_scores * scale_factor + bias_rows, negative)


def pair_core(
    query_heads,
    dout_heads,
    log_total,
    row_delta,
    key_heads,
    value_heads,
    relation,
    bias_set,
    scale_factor,
):
    scores = pair_scores(query_heads, key_heads, relation, bias_set, scale_factor)
    weights_now = jnp.exp(scores - log_total[:, :, None])
    grad_weights = jnp.einsum(
        "qhd,khd->hqk", dout_heads, value_heads, preferred_element_type=jnp.float32
    )
    dscores = weights_now * (grad_weights - row_delta[:, :, None])
    return (weights_now, dscores, (dscores * scale_factor).astype(jnp.bfloat16))


def add_tables(relative_bias_tables, dscores, relation):
    same_sum, prev_sum, far_sum = relative_bias_tables
    return (
        same_sum + jnp.where(relation == 0, dscores, 0.0),
        prev_sum + jnp.where(relation == 1, dscores, 0.0),
        far_sum + jnp.where(relation >= 2, jnp.sum(dscores, axis=(1, 2)), 0.0),
    )


def forward_fold(query_heads, position, row_count, bias_set, scale_factor, running, pieces):
    keys_all, values_all = pieces

    def one_shard(folded, shard_step):
        key_heads = lax.dynamic_slice_in_dim(
            keys_all, shard_step * row_count, row_count, 0
        ).reshape(row_count, H, HD)
        value_heads = lax.dynamic_slice_in_dim(
            values_all, shard_step * row_count, row_count, 0
        ).reshape(row_count, H, HD)
        relation = position - shard_step

        def one_compute(current):
            running_max, running_sum, running_acc = current
            scores = pair_scores(query_heads, key_heads, relation, bias_set, scale_factor)
            new_max = jnp.maximum(running_max, jnp.max(scores, axis=-1))
            factor = jnp.exp(running_max - new_max)
            weights_now = jnp.exp(scores - new_max[:, :, None])
            new_sum = running_sum * factor + jnp.sum(weights_now, axis=-1)
            update = jnp.einsum(
                "hqk,khd->qhd",
                weights_now.astype(jnp.bfloat16),
                value_heads,
                preferred_element_type=jnp.float32,
            )
            scaled = running_acc.reshape(row_count, H, HD) * factor.T[:, :, None]
            return (new_max, new_sum, (scaled + update).reshape(row_count, H * HD))

        return (lax.cond(relation >= 0, one_compute, lambda unchanged: unchanged, folded), None)

    running, unused = lax.scan(one_shard, running, jnp.arange(keys_all.shape[0] // row_count))
    return running


def nt_dot(left, right):
    return lax.dot_general(left, right, (((1,), (1,)), ((), ())), preferred_element_type=F32)


def nn_dot(left, right):
    return jnp.dot(left, right, preferred_element_type=F32)


def meet(neighbours):
    barrier = pltpu.get_barrier_semaphore()
    for who in neighbours:
        pl.semaphore_signal(barrier, inc=1, device_id=who, device_id_type=MESH)
    pl.semaphore_wait(barrier, len(neighbours))


def ctx_peers(n):
    me = lax.axis_index("ctx")
    return [{"ctx": lax.rem(me + d, n)} for d in range(1, n)]


def other_wa(me, bit):
    flipped = lax.rem(me // bit, 2)
    return me + bit - 2 * bit * flipped


def remote(src, dst, send_sem, recv_sem, **device):
    return pltpu.make_async_remote_copy(
        src_ref=src,
        dst_ref=dst,
        send_sem=send_sem,
        recv_sem=recv_sem,
        device_id=device,
        device_id_type=MESH,
    )


RING = 8
HOPS = RING - 1


def ring_place(n):
    me = lax.axis_index("ctx")
    half = n // 2

    def at(place):
        return jnp.where(place < half, 2 * place, 2 * (n - 1 - place) + 1)

    place = jnp.where(lax.rem(me, 2) == 0, me // 2, n - 1 - me // 2)
    return place, at(lax.rem(place + 1, n)), at(lax.rem(place + n - 1, n))


class Ring:
    def __init__(self, lanes, send, recv, share=None, hold=None, full=None):
        self.lanes, self.share, self.hold, self.full = lanes, share, hold, full
        self.sems = send, recv
        self.place, self.after, self.before = ring_place(RING)

    def copy(self, lane, src, dst, step):
        send, recv = self.sems
        way = self.lanes[lane][1]
        return remote(
            src, dst, send.at[lane, step], recv.at[lane, step], ctx=self.after if way == 1 else self.before
        )

    def chunk(self, lane, offset):
        here = self.place if self.lanes[lane][1] == 1 else RING - self.place
        return lax.rem(here + offset + 2 * RING, RING)

    def scatter(self, step, which):
        for lane in which:
            b, _, rows = self.lanes[lane]
            share = self.share.at[b, self.chunk(lane, -step), rows]

            @pl.when(step > 0)
            def _():
                there = self.hold.at[b, jnp.maximum(step - 1, 0), rows]
                self.copy(lane, share, there, jnp.maximum(step - 1, 0)).wait_recv()
                share[...] = (share[...].astype(F32) + there[...].astype(F32)).astype(BF)

            @pl.when(step < HOPS)
            def _():
                there = jnp.minimum(step, HOPS - 1)
                self.copy(lane, share, self.hold.at[b, there, rows], there).start()

    def gather(self, step, which):
        for lane in which:
            b, _, rows = self.lanes[lane]
            full = self.full[b].at[self.chunk(lane, 1 - step), rows]

            @pl.when(step > 0)
            def _():
                self.copy(lane, full, full, jnp.maximum(step - 1, 0)).wait_recv()

            @pl.when(step < HOPS)
            def _():
                self.copy(lane, full, full, jnp.minimum(step, HOPS - 1)).start()

    def finish(self, part):
        def one(step, unused):
            for lane in range(len(self.lanes)):
                self.copy(lane, part(lane), part(lane), step).wait_send()
            return unused

        lax.fori_loop(0, HOPS, one, 0)


TALL, FLAT = (224, 1024), (256, 896)
EARLY = ("ck", "cv", "cq", "co", "so")
MADE = ("cq", "co", "so")
LATE = ("q", "k", "v")
FEED = (8, 112, 896)
FEED_LANES = (
    (0, 1, slice(0, 64)),
    (1, -1, slice(0, 64)),
    (0, 1, slice(64, 112)),
    (1, -1, slice(64, 112)),
)
FEED_TURNS = ((0, 1), (2, 3))


def product_into(out_ref, left, right):
    for c in range(left.shape[1] // WIDE):
        lanes = slice(c * WIDE, (c + 1) * WIDE)
        turned = left[:, lanes].astype(F32).T.astype(BF)
        out_ref[lanes, :] = nn_dot(turned, right[...]).astype(BF)


class Folding:
    def __init__(self, names, parts, scratch):
        self.names = names
        self.parts = parts
        tall, flat, sems = scratch
        self.sets = {TALL: tall, FLAT: flat}
        self.own_sem, self.core_send, self.core_recv, self.x_send, self.x_recv = sems
        self.wa = lax.axis_index("wa")
        self.mate, self.across = other_wa(self.wa, 1), other_wa(self.wa, 2)
        self.core, self.half = lax.rem(self.wa, 2), self.wa // 2
        self.slots, count = {}, {TALL: 0, FLAT: 0}
        for name in names:
            shape = self.shape_of(name)
            self.slots[name] = (count[shape], self.sets[shape])
            count[shape] += 1
        self.own_copies, self.core_copies, self.x_copies = {}, {}, {}

    @staticmethod
    def shape_of(name):
        return FLAT if name in ("co", "so") else TALL

    @classmethod
    def scratch(cls, names):
        shapes = []
        for shape in (TALL, FLAT):
            many = sum(cls.shape_of(name) == shape for name in names)
            if many:
                shapes += [pltpu.VMEM((many, 2, *shape), BF)] * 2 + [pltpu.VMEM((many, *shape), BF)] * 2
        dma = pltpu.SemaphoreType.DMA
        many = len(names)
        return shapes + [dma((many, 2))] * 3 + [dma((many,))] * 2

    def start(self, *names):
        for name in names:
            u = self.names.index(name)
            slot, (own, inn, _, _) = self.slots[name]
            rows = self.shape_of(name)[0]
            for x in range(2):
                mine = pl.ds(pl.multiple_of((2 * x + self.core) * rows, 16), rows)
                theirs = pl.ds(pl.multiple_of((2 * x + 1 - self.core) * rows, 16), rows)
                copy = remote(
                    self.parts[name].at[theirs],
                    inn.at[slot, x],
                    self.core_send.at[u, x],
                    self.core_recv.at[u, x],
                    wa=self.mate,
                )
                copy.start()
                self.core_copies[name, x] = copy
                copy = pltpu.make_async_copy(
                    self.parts[name].at[mine], own.at[slot, x], self.own_sem.at[u, x]
                )
                copy.start()
                self.own_copies[name, x] = copy
            slot, (_, _, out, land) = self.slots[name]
            self.x_copies[name] = remote(
                out.at[slot], land.at[slot], self.x_send.at[u], self.x_recv.at[u], wa=self.across
            )

    def send(self, name):
        self.prepare(name)
        self.x_copies[name].start()

    def prepare(self, name):
        slot, (own, inn, out, _) = self.slots[name]
        for x in range(2):
            self.own_copies[name, x].wait()
            self.core_copies[name, x].wait_recv()
        away = 1 - self.half
        out[slot] = (own[slot, away].astype(F32) + inn[slot, away].astype(F32)).astype(BF)

    def total(self, name):
        slot, (own, inn, _, land) = self.slots[name]
        self.x_copies[name].wait_recv()
        here = self.half
        return (
            own[slot, here].astype(F32) + inn[slot, here].astype(F32) + land[slot].astype(F32)
        ).astype(BF)

    def finish(self):
        for name in self.names:
            for x in range(2):
                self.core_copies[name, x].wait_send()
            self.x_copies[name].wait_send()


class Moves:
    def __init__(self, sem):
        self.sem, self.count = sem, 0

    def start(self, src, dst):
        copy = pltpu.make_async_copy(src, dst, self.sem.at[self.count])
        copy.start()
        self.count += 1
        return copy


def wait_all(copies):
    for copy in copies:
        copy.wait()


def lasting(microseconds):
    return pl.CostEstimate(
        flops=0, bytes_accessed=int(microseconds * 3.0e6), transcendentals=0
    )


def lanes_of(index):
    return pl.ds(pl.multiple_of(index * WIDE, WIDE), WIDE)


def rows_of(index, rows):
    return pl.ds(pl.multiple_of(index * rows, rows), rows)


def to_ctx(src, dst, send_sem, recv_sem, target):
    return pltpu.make_async_remote_copy(
        src_ref=src,
        dst_ref=dst,
        send_sem=send_sem,
        recv_sem=recv_sem,
        device_id={"ctx": target},
        device_id_type=MESH,
    )


def head_mask(h, rows):
    lane = lax.broadcasted_iota(jnp.int32, (rows, WIDE), 1)
    return (lane < HD) if h == 0 else (lane >= HD)


def bias_tiles(bias_ref, me, tiles):
    for h in range(2):
        line = bias_ref[pl.ds(2 * me + h, 1), :]
        rolled = pltpu.roll(
            jnp.broadcast_to(line, (BLOCK, LINE)), 0, 1, stride=1, stride_axis=0
        )
        tiles[h, 0] = rolled[:, :BLOCK]
        tiles[h, 1] = rolled[:, BLOCK : 2 * BLOCK]
        tiles[h, 2] = jnp.broadcast_to(line[:, WIDE : WIDE + BLOCK], (BLOCK, BLOCK))


def spread(n, me, pairs, send, recv, t):
    src, dst = pairs[t]
    for d in range(1, n):
        peer = lax.rem(me + d, n)
        to_ctx(
            src.at[:, lanes_of(peer)], dst.at[rows_of(me, BLOCK)], send.at[t, d], recv.at[t, d], peer
        ).start()
    dst[rows_of(me, BLOCK), :] = src[:, lanes_of(me)]


GATHERED = ("q", "k", "v", "so", "ck", "cv", "cq", "co")
SINGLE = ("cot",)
GAINS = ("selfnorm", "crossnorm", "feednorm", "outbias")


class Gathering:
    def __init__(self, shards, whole, own_sem, send, recv):
        self.names, self.shards, self.whole = tuple(shards), shards, whole
        self.sems = own_sem, send, recv
        self.wa, me = lax.axis_index("wa"), lax.axis_index("ctx")
        self.mate, self.across = other_wa(self.wa, 1), other_wa(self.wa, 2)
        y, z = lax.rem(me, 2), lax.rem(me // 2, 2)
        self.pairs = ((y, me + 1 - 2 * y), (z, me + 2 - 4 * z))
        self.copies = {}

    def start(self):
        own_sem, send, recv = self.sems
        for u, name in enumerate(self.names):
            part, beside = self.pairs[(u + 1) % 2]
            shard, whole = self.shards[name], self.whole[name]
            rows = shard.shape[0]
            parts = 1 if name in SINGLE else 2
            some = rows // parts
            shift = 0 if parts == 1 else part * some

            def at(start, count, ref=whole):
                return ref.at[pl.ds(pl.multiple_of(start, 16), count)]

            mine = at(self.wa * rows, rows)
            theirs = at(self.across * rows, rows)
            theirs_some = at(self.across * rows + shift, some)
            self.copies[name] = {
                "over": remote(
                    at(shift, some, shard), at(self.wa * rows + shift, some), send.at[u, 0], recv.at[u, 0], wa=self.across
                ),
                "near": remote(shard, mine, send.at[u, 1], recv.at[u, 1], wa=self.mate),
                "pass": remote(theirs, theirs, send.at[u, 2], recv.at[u, 2], wa=self.mate),
                "side": remote(theirs_some, theirs_some, send.at[u, 3], recv.at[u, 3], ctx=beside),
                "own": pltpu.make_async_copy(shard, mine, own_sem.at[u]),
            }
            self.copies[name]["near"].start()
            self.copies[name]["own"].start()

    def cross(self, *names):
        for name in names:
            self.copies[name]["over"].start()

    def forward(self, *names):
        for name in names:
            self.copies[name]["over"].wait_recv()
            self.copies[name]["pass" if name in SINGLE else "side"].start()

    def land(self, *names):
        for name in names:
            self.copies[name]["side"].wait_recv()
            self.copies[name]["pass"].start()

    def arrive(self, *names):
        for name in names:
            self.copies[name]["near"].wait_recv()
            self.copies[name]["pass"].wait_recv()
            self.copies[name]["own"].wait()

    def finish(self):
        for name, copies in self.copies.items():
            for which in ("over", "near", "pass") + (() if name in SINGLE else ("side",)):
                copies[which].wait_send()


class Columns:
    def __init__(self, gathering, shard, whole, send, recv):
        wa, mate, across = gathering.wa, gathering.mate, gathering.across
        both = other_wa(across, 1)
        rows, width = shard.shape[0], whole.shape[1]
        some = rows // 2

        def block(owner, columns):
            return shard.at[owner, pl.ds(pl.multiple_of(columns * width, WIDE), width)]

        def at(start, count):
            return whole.at[pl.ds(pl.multiple_of(start, 16), count)]

        everything = slice(0, rows)
        self.own = pltpu.make_async_copy(block(everything, wa), at(wa * rows, rows), send.at[5])
        self.near = remote(block(everything, mate), at(wa * rows, rows), send.at[0], recv.at[0], wa=mate)
        self.over, self.side = [], []
        for d, peer in enumerate((across, both)):
            part, beside = gathering.pairs[d]
            mine = pl.ds(pl.multiple_of(part * some, 16), some)
            gone, got = at(wa * rows + part * some, some), at(peer * rows + part * some, some)
            self.over.append(remote(block(mine, peer), gone, send.at[1 + d], recv.at[1 + d], wa=peer))
            self.side.append(remote(got, got, send.at[3 + d], recv.at[3 + d], ctx=beside))

    def start(self):
        self.own.start()
        self.near.start()

    def cross(self):
        for copy in self.over:
            copy.start()

    def forward(self):
        for over, side in zip(self.over, self.side, strict=True):
            over.wait_recv()
            side.start()

    def finish(self):
        self.own.wait()
        self.near.wait()
        for over, side in zip(self.over, self.side, strict=True):
            side.wait()
            over.wait_send()


def attn_forward_kernel(n, tokens_ref, small_ref, near_far, *refs):
    shards = dict(zip((*GATHERED, "cot"), refs[:9], strict=True))
    feed_ref = refs[9]
    wholes = dict(zip((*GATHERED, "cot"), refs[10:19], strict=True))
    feed_whole = refs[19]
    o_ref, low_ref, ot_out, lse_out, small_out, before_ref, qh_out, kh_out, vh_out, keys_out, values_out = refs[20:31]
    (
        held_q, held_k, held_v, held_ck, held_cv, proj, small_in, small_mid, qh, kh, vh, vt, oh, land, tiles,
        acc, stat, send, recv, osend, orecv, small_sem, own_sem, out_sem, gather_send, gather_recv, feed_send,
        feed_recv, span_sem, near_ref, keys_ref, values_ref, move_sem,
    ) = refs[31:]
    moves = Moves(move_sem)
    load_near = moves.start(near_far, near_ref)
    held = {"q": held_q, "k": held_k, "v": held_v, "ck": held_ck, "cv": held_cv}
    gathering = Gathering(shards, wholes | held, own_sem, gather_send, gather_recv)
    columns = Columns(gathering, feed_ref, feed_whole, feed_send, feed_recv)
    both = other_wa(gathering.across, 1)
    meet([*ctx_peers(n), *({"wa": peer} for peer in (gathering.mate, gathering.across, both))])
    me = lax.axis_index("ctx")
    near = remote(small_ref, small_in.at[0], small_sem.at[0], small_sem.at[1], wa=gathering.mate)
    near.start()
    gathering.start()
    gathering.cross("q")
    columns.start()
    span_rows = before_ref.shape[0]
    span = remote(
        near_far.at[near_far.shape[0] - span_rows :],
        before_ref,
        span_sem.at[0],
        span_sem.at[1],
        ctx=lax.rem(me + 1, n),
    )
    over = remote(small_mid, small_in.at[1], small_sem.at[2], small_sem.at[3], wa=gathering.across)
    near.wait_recv()
    small_mid[...] = (small_ref[...].astype(F32) + small_in[0].astype(F32)).astype(BF)
    over.start()
    over.wait_recv()
    small_out[...] = small_mid[...].astype(F32) + small_in[1].astype(F32)
    bias_ref = small_out
    values = tokens_ref[...].astype(F32)
    width = values.shape[1]
    norm = lax.rsqrt(jnp.mean(values * values, axis=1, keepdims=True) + epsilon)
    low_ref[...] = (values * norm * small_out[H : H + 1, :width]).astype(BF)
    bias_tiles(bias_ref, me, tiles)
    pairs = tuple((proj.at[t], dst) for t, dst in enumerate((qh, kh, vh)))
    saving = []

    def save(name):
        copy = pltpu.make_async_copy(held[name], wholes[name], out_sem.at[len(saving)])
        copy.start()
        saving.append(copy)

    def project(t, name):
        gathering.land(name)
        gathering.arrive(name)
        proj[t] = nn_dot(low_ref[...], held[name][...]).astype(BF)
        spread(n, me, pairs, send, recv, t)
        save(name)

    gathering.forward("q")
    gathering.cross("k")
    gathering.forward("k")
    gathering.cross("v")
    project(0, "q")
    gathering.forward("v")
    gathering.cross("so", "ck")
    project(1, "k")
    project(2, "v")

    gathering.forward("so", "ck")
    gathering.cross("cv", "cq")

    for d in range(1, n):
        peer = lax.rem(me + n - d, n)
        for t, (src, dst) in enumerate(pairs):
            to_ctx(
                src.at[:, lanes_of(peer)], dst.at[rows_of(peer, BLOCK)], send.at[t, d], recv.at[t, d], peer
            ).wait_recv()
    stores = [moves.start(*pair) for pair in ((qh, qh_out), (kh, kh_out), (vh, vh_out))]
    for i in range(n):
        part = slice(i * BLOCK, (i + 1) * BLOCK)
        vt[:, part] = vh[part, :].astype(F32).T.astype(BF)

    def query_block(step, unused):
        @pl.when((step == 0) & (me < n - 1))
        def _():
            span.start()

        @pl.when(step == 1)
        def _():
            gathering.forward("cv", "cq")
            gathering.land("so", "ck")
            gathering.cross("co")
            columns.cross()

        @pl.when(step == 6)
        def _():
            gathering.land("cv", "cq")
            gathering.forward("co")
            columns.forward()
            gathering.cross("cot")

        i = lax.rem(me + 1 + step, n)
        rows = rows_of(i, BLOCK)
        q_now = qh[rows, :] * BF(HD**-0.5)
        masked = [jnp.where(head_mask(h, BLOCK), q_now, BF(0)) for h in range(2)]

        def fold(j, which, first):
            keys = kh[rows_of(j, BLOCK), :]
            for h in range(2):
                scores = nt_dot(keys, masked[h])
                if which is None:
                    scores = scores + bias_ref[pl.ds(2 * me + h, 1), WIDE : WIDE + BLOCK]
                else:
                    scores = scores + tiles[h, which]
                top = jnp.max(scores, axis=0, keepdims=True)
                if not first:
                    old = stat[h : h + 1, :]
                    top = jnp.maximum(old, top)
                weights = jnp.exp(scores - top)
                total = jnp.sum(weights, axis=0, keepdims=True)
                vals = vt[h * HD : (h + 1) * HD, rows_of(j, BLOCK)]
                mixed = nn_dot(vals, weights.astype(BF))
                if not first:
                    factor = jnp.exp(old - top)
                    total = total + stat[2 + h : 3 + h, :] * factor
                    mixed = mixed + acc[h * HD : (h + 1) * HD, :] * factor
                stat[h : h + 1, :] = top
                stat[2 + h : 3 + h, :] = total
                acc[h * HD : (h + 1) * HD, :] = mixed

        fold(i, 0, True)

        @pl.when(i >= 1)
        def _():
            fold(i - 1, 1, False)

        def far(j, unused):
            fold(j, None, False)
            return unused

        lax.fori_loop(0, i - 1, far, 0)
        for h in range(2):
            total = stat[2 + h : 3 + h, :]
            part = acc[h * HD : (h + 1) * HD, :] / total
            acc[h * HD : (h + 1) * HD, :] = part
            lse_out[h : h + 1, rows] = stat[h : h + 1, :] + jnp.log(total)
        done = acc[...]
        ot_out[:, rows] = done
        oh[rows, :] = done.T.astype(BF)

        @pl.when(i != me)
        def _():
            d = lax.rem(i - me + n, n)
            to_ctx(oh.at[rows], land.at[:, lanes_of(me)], osend.at[d], orecv.at[d], i).start()

        @pl.when(i == me)
        def _():
            land[:, lanes_of(me)] = oh[rows, :]

        return unused

    lax.fori_loop(0, n, query_block, 0)
    load_near.wait()

    @pl.when(me > 0)
    def _():
        span.wait_recv()

    @pl.when(me == 0)
    def _():
        before_ref[...] = jnp.zeros_like(before_ref)

    for name, out_ref, far_ref in (("ck", keys_ref, keys_out), ("cv", values_ref, values_out)):
        gathering.arrive(name)
        save(name)
        out_ref[:span_rows, :] = nn_dot(before_ref[...], held[name][...]).astype(BF)
        for g in range(near_ref.shape[0] // span_rows):
            rows = slice(g * span_rows, (g + 1) * span_rows)
            there = slice((g + 1) * span_rows, (g + 2) * span_rows)
            out_ref[there, :] = nn_dot(near_ref[rows, :], held[name][...]).astype(BF)
        stores.append(moves.start(out_ref, far_ref))
    gathering.land("co")
    gathering.forward("cot")
    for d in range(1, n):
        peer = lax.rem(me + d, n)
        for t, (src, dst) in enumerate(pairs):
            to_ctx(
                src.at[:, lanes_of(peer)], dst.at[rows_of(me, BLOCK)], send.at[t, d], recv.at[t, d], peer
            ).wait_send()
        back = to_ctx(
            oh.at[rows_of(peer, BLOCK)], land.at[:, lanes_of(me)], osend.at[d], orecv.at[d], peer
        )
        back.wait_send()
        back.wait_recv()
    o_ref[...] = land[...]
    gathering.arrive("so", "cq", "co", "cot")
    gathering.finish()
    columns.finish()

    @pl.when(me < n - 1)
    def _():
        span.wait_send()

    near.wait_send()
    over.wait_send()
    wait_all(saving + stores)


def vmem(count):
    return [pl.BlockSpec(memory_space=pltpu.VMEM)] * count


def attn_forward(n, tokens, small, near, shards, feed):
    rows, seq = tokens.shape[0], n * tokens.shape[0]
    owners = lax.axis_size("wa")
    low = functools.partial(jax.ShapeDtypeStruct, dtype=BF)
    heads = low((seq, WIDE))
    wholes = [low((owners * s.shape[0], s.shape[1])) for s in shards]
    width = wholes[0].shape[1]
    dma = pltpu.SemaphoreType.DMA
    span_rows = 256
    keys = low((span_rows + near.shape[0], width))
    any_spec = pl.BlockSpec(memory_space=pl.ANY)
    return pl.pallas_call(
        functools.partial(attn_forward_kernel, n),
        out_shape=(
            *wholes,
            low((owners * feed.shape[0], feed.shape[1] // owners)),
            low((rows, width)),
            low(tokens.shape),
            jax.ShapeDtypeStruct((WIDE, seq), F32),
            jax.ShapeDtypeStruct((8, seq), F32),
            jax.ShapeDtypeStruct(small.shape, F32),
            low((span_rows, near.shape[1])),
            heads,
            heads,
            heads,
            keys,
            keys,
        ),
        in_specs=vmem(2) + [any_spec] * 11,
        out_specs=tuple([any_spec] * 10 + vmem(6) + [any_spec] * 5),
        scratch_shapes=[
            *[pltpu.VMEM(wholes[0].shape, BF)] * 5,
            pltpu.VMEM((3, rows, width), BF),
            pltpu.VMEM((2, *small.shape), BF),
            pltpu.VMEM(small.shape, BF),
            pltpu.VMEM((seq, WIDE), BF),
            pltpu.VMEM((seq, WIDE), BF),
            pltpu.VMEM((seq, WIDE), BF),
            pltpu.VMEM((WIDE, seq), BF),
            pltpu.VMEM((seq, WIDE), BF),
            pltpu.VMEM((rows, width), BF),
            pltpu.VMEM((2, 3, BLOCK, BLOCK), F32),
            pltpu.VMEM((WIDE, BLOCK), F32),
            pltpu.VMEM((8, BLOCK), F32),
            dma((3, n)),
            dma((3, n)),
            dma((n,)),
            dma((n,)),
            dma((4,)),
            dma((9,)),
            dma((5,)),
            dma((9, 4)),
            dma((9, 4)),
            dma((6,)),
            dma((5,)),
            dma((2,)),
            pltpu.VMEM(near.shape, BF),
            pltpu.VMEM(keys.shape, BF),
            pltpu.VMEM(keys.shape, BF),
            dma((6,)),
        ],
        compiler_params=pltpu.CompilerParams(
            collective_id=1, has_side_effects=True, vmem_limit_bytes=60 << 20
        ),
        cost_estimate=lasting(85),
        name="attn_forward",
    )(tokens, small, near, *shards, feed)


def attn_backward_kernel(n, do_ref, lse_ref, bias_ref, feed_part, *rest):
    far = rest[:10]
    sides_far = far[4:]
    line_ref, *outs = rest[12:21]
    near = rest[21:31]
    kh, qh, ot_ref, vh = near[:4]
    given = dict(zip(MADE, zip(near[4::2], near[5::2], strict=True), strict=True))
    tall_pair, tall_one, flat_out, *feed_full, move_sem = rest[31:37]
    (
        doh, kt, stage, land, dk_acc, dv_acc, dq_acc, q_masked, do_masked, delta, tiles, dtiles,
        send, recv, gsend, grecv, ring_send, ring_recv,
    ) = rest[37:55]
    made = dict(zip(MADE, rest[55:58], strict=True))
    parts = dict(zip(EARLY, (rest[10], rest[11], *made.values()), strict=True))
    extra = rest[58:]
    moves = Moves(move_sem)
    loads = [moves.start(*pair) for pair in zip(far, near, strict=True)]
    fold_wa = Folding(EARLY, parts, (extra[0:4], extra[4:8], extra[8:13]))
    ring = Ring(FEED_LANES, ring_send, ring_recv, full=feed_full)
    for lane in range(2):
        feed_full[lane][ring.chunk(lane, 1)] = feed_part[lane]
    meet([*ctx_peers(n), {"wa": fold_wa.mate}, {"wa": fold_wa.across}])
    me = lax.axis_index("ctx")
    pairs = ((do_ref, doh),)
    spread(n, me, pairs, send, recv, 0)
    fold_wa.start("ck", "cv")
    bias_tiles(bias_ref, me, tiles)
    loads[0].wait()
    for j in range(n):
        part = slice(j * BLOCK, (j + 1) * BLOCK)
        kt[:, part] = (kh[part, :].astype(F32) * HD**-0.5).T.astype(BF)
    dtiles[...] = jnp.zeros_like(dtiles)
    for name in EARLY[:2]:
        fold_wa.send(name)
    ring.gather(jnp.int32(0), FEED_TURNS[0])
    ring.gather(jnp.int32(0), FEED_TURNS[1])
    wait_all(loads[1:])
    for name in MADE:
        product_into(made[name], *given[name])
        fold_wa.start(name)
    dq_acc[...] = jnp.zeros_like(dq_acc)
    for d in range(1, n):
        peer = lax.rem(me + n - d, n)
        to_ctx(
            do_ref.at[:, lanes_of(peer)], doh.at[rows_of(peer, BLOCK)], send.at[0, d], recv.at[0, d], peer
        ).wait_recv()
    for i in range(n):
        rows = slice(i * BLOCK, (i + 1) * BLOCK)
        q_now = qh[rows, :] * BF(HD**-0.5)
        do_now = doh[rows, :]
        products = do_now.astype(F32).T * ot_ref[:, rows]
        for h in range(2):
            mask = head_mask(h, BLOCK)
            q_masked[h, rows, :] = jnp.where(mask, q_now, BF(0))
            do_masked[h, rows, :] = jnp.where(mask, do_now, BF(0))
            delta[h : h + 1, rows] = jnp.sum(
                products[h * HD : (h + 1) * HD], axis=0, keepdims=True
            )

    def pair(t, now):
        i, j = now
        rows, there = rows_of(i, BLOCK), rows_of(j, BLOCK)

        @pl.when(t == 6)
        def _():
            for name in EARLY[2:]:
                fold_wa.send(name)

        for turn, lanes in enumerate(FEED_TURNS):

            @pl.when((lax.rem(t, 4) == 2 * turn + 1) & (t <= 4 * HOPS))
            def _():
                ring.gather(t // 4 + 1, lanes)

        first = i == j
        which = jnp.minimum(i - j, 2)
        keys, vals = kh[there, :], vh[there, :]
        dk_part, dv_part = None, None
        for h in range(2):
            query, dout = q_masked[h, rows, :], do_masked[h, rows, :]
            scores = nt_dot(keys, query)
            weights = jnp.exp(scores + tiles[h, which] - lse_ref[h : h + 1, rows])
            dweights = nt_dot(vals, dout)
            dscores = weights * (dweights - delta[h : h + 1, rows])
            dtiles[h, which] += dscores
            low = dscores.astype(BF)
            dv_now = nn_dot(weights.astype(BF), dout)
            dk_now = nn_dot(low, query)
            dv_part = dv_now if dv_part is None else dv_part + dv_now
            dk_part = dk_now if dk_part is None else dk_part + dk_now
            half = slice(h * HD, (h + 1) * HD)
            dq_acc[half, rows] += nn_dot(kt[half, there], low)

        @pl.when(first)
        def _():
            dk_acc[...] = dk_part
            dv_acc[...] = dv_part

        @pl.when(jnp.logical_not(first))
        def _():
            dk_acc[...] += dk_part
            dv_acc[...] += dv_part

        last = i == n - 1

        @pl.when(last)
        def _():
            stage[1, there, :] = dk_acc[...].astype(BF)
            stage[2, there, :] = dv_acc[...].astype(BF)
            deliver(j, (1, 2))

        after = lax.rem(j + 1, n)
        return jnp.where(last, after, i + 1), jnp.where(last, after, j)

    def deliver(i, arrays):
        rows = rows_of(i, BLOCK)

        @pl.when(i != me)
        def _():
            d = lax.rem(i - me + n, n)
            for t in arrays:
                to_ctx(
                    stage.at[t, rows], land.at[t, :, lanes_of(me)], gsend.at[t, d], grecv.at[t, d], i
                ).start()

        @pl.when(i == me)
        def _():
            for t in arrays:
                land[t, :, lanes_of(me)] = stage[t, rows, :]

    begin = lax.rem(me + 1, n)
    lax.fori_loop(0, n * (n + 1) // 2, pair, (begin, begin))

    def dq_block(step, unused):
        i = lax.rem(me + 1 + step, n)
        rows = rows_of(i, BLOCK)
        stage[0, rows, :] = dq_acc[:, rows].T.astype(BF)
        deliver(i, (0,))
        return unused

    lax.fori_loop(0, n, dq_block, 0)
    ring.finish(lambda lane: feed_full[FEED_LANES[lane][0]].at[0, FEED_LANES[lane][2]])
    stores = [moves.start(full, out) for full, out in zip(feed_full, outs[6:8], strict=True)]
    tall_pair[:224, :] = fold_wa.total("cq")
    tall_pair[224:, :] = fold_wa.total("ck")
    tall_one[...] = fold_wa.total("cv")
    for at, name in ((0, "co"), (32, "so")):
        flat_out[:, at : at + 32, :] = fold_wa.total(name).reshape(8, 32, 896)
    stores += [
        moves.start(tall_pair, outs[3]),
        moves.start(tall_one, outs[4]),
        moves.start(flat_out, outs[5]),
    ]
    fold_wa.finish()
    for h in range(2):
        line = jnp.concatenate(
            [dtiles[h, 0], dtiles[h, 1], jnp.zeros((BLOCK, LINE - 2 * BLOCK), F32)], axis=1
        )
        row = lax.broadcasted_iota(jnp.int32, (BLOCK, LINE), 0)
        for bit in range(8):
            moved = pltpu.roll(line, LINE - (1 << bit), 1)
            line = jnp.where((row >> bit) & 1 == 1, moved, line)
        line_ref[h : h + 1, :] = jnp.sum(line, axis=0, keepdims=True)
        line_ref[2 + h : 3 + h, :BLOCK] = jnp.sum(dtiles[h, 2], axis=0, keepdims=True)
    line_ref[2:4, BLOCK:] = jnp.zeros((2, LINE - BLOCK), F32)
    line_ref[4:8, :] = jnp.zeros((4, LINE), F32)
    for d in range(1, n):
        peer = lax.rem(me + d, n)
        to_ctx(
            do_ref.at[:, lanes_of(peer)], doh.at[rows_of(me, BLOCK)], send.at[0, d], recv.at[0, d], peer
        ).wait_send()
        for t in range(3):
            back = to_ctx(
                stage.at[t, rows_of(peer, BLOCK)], land.at[t, :, lanes_of(me)], gsend.at[t, d], grecv.at[t, d], peer
            )
            back.wait_send()
            back.wait_recv()
    wait_all(stores + [moves.start(land.at[t], outs[t]) for t in range(3)])


def attn_backward(n, dout, qh, kh, vh, ot, lse, bias_lines, parts, feed_part):
    rows, seq = dout.shape[0], n * dout.shape[0]
    grads = jax.ShapeDtypeStruct(dout.shape, BF)
    feed = jax.ShapeDtypeStruct(FEED, BF)
    low = functools.partial(jax.ShapeDtypeStruct, dtype=BF)
    any_spec = pl.BlockSpec(memory_space=pl.ANY)
    far = (kh, qh, ot, vh, *parts[2:])
    shares = (low((448, 1024)), low((224, 1024)), low((8, 64, 896)))
    line, *outs = pl.pallas_call(
        functools.partial(attn_backward_kernel, n),
        out_shape=(jax.ShapeDtypeStruct((8, LINE), F32), grads, grads, grads, *shares, feed, feed),
        in_specs=vmem(4) + [any_spec] * 12,
        out_specs=tuple(vmem(1) + [any_spec] * 8),
        scratch_shapes=[
            *(pltpu.VMEM(v.shape, v.dtype) for v in far),
            *(pltpu.VMEM(v.shape, v.dtype) for v in (*shares, feed, feed)),
            pltpu.SemaphoreType.DMA((18,)),
            pltpu.VMEM((seq, WIDE), BF),
            pltpu.VMEM((WIDE, seq), BF),
            pltpu.VMEM((3, seq, WIDE), BF),
            pltpu.VMEM((3, *dout.shape), BF),
            pltpu.VMEM((BLOCK, WIDE), F32),
            pltpu.VMEM((BLOCK, WIDE), F32),
            pltpu.VMEM((WIDE, seq), F32),
            pltpu.VMEM((2, seq, WIDE), BF),
            pltpu.VMEM((2, seq, WIDE), BF),
            pltpu.VMEM((8, seq), F32),
            pltpu.VMEM((2, 3, BLOCK, BLOCK), F32),
            pltpu.VMEM((2, 3, BLOCK, BLOCK), F32),
            pltpu.SemaphoreType.DMA((1, n)),
            pltpu.SemaphoreType.DMA((1, n)),
            pltpu.SemaphoreType.DMA((3, n)),
            pltpu.SemaphoreType.DMA((3, n)),
            pltpu.SemaphoreType.DMA((len(FEED_LANES), HOPS)),
            pltpu.SemaphoreType.DMA((len(FEED_LANES), HOPS)),
            pltpu.VMEM((896, 1024), BF),
            pltpu.VMEM((1024, 896), BF),
            pltpu.VMEM((1024, 896), BF),
            *Folding.scratch(EARLY),
        ],
        compiler_params=pltpu.CompilerParams(
            collective_id=2, has_side_effects=True, vmem_limit_bytes=60 << 20
        ),
        cost_estimate=lasting(100),
        name="attn_backward",
    )(dout, lse, bias_lines, feed_part, *far, *parts[:2])
    return *outs[:3], line, *outs[3:]


BUFFERS = {
    "cq": (1, (224, 1024)),
    "cv": (-1, (224, 1024)),
    "ck": (1, (224, 1024)),
    "co": (-1, (8, 32, 896)),
    "so0": (1, (8, 16, 896)),
    "so1": (-1, (8, 16, 896)),
}
NAMES = tuple(BUFFERS)


def chunk_shape(name):
    shape = BUFFERS[name][1]
    return (shape[0], WIDE) if len(shape) == 2 else shape[1:]


def chunk_of(ref, name, c):
    return ref.at[:, lanes_of(c)] if len(BUFFERS[name][1]) == 2 else ref.at[c]


class Grid:
    def __init__(self, u, share, half_in, half, quarters, whole, send, recv):
        self.u, self.share, self.half_in, self.half = u, share, half_in, half
        self.quarters, self.whole, self.sems = quarters, whole, (send, recv)
        me = lax.axis_index("ctx")
        self.y, self.z = lax.rem(me, 2), me // 2
        self.beside = me + 1 - 2 * self.y
        self.column = [lax.rem(self.z + d, 4) for d in range(1, 4)]

    def half_of(self, y):
        return pl.ds(pl.multiple_of(y * 4 * WIDE, WIDE), 4 * WIDE)

    def piece_of(self, z, y=None):
        start = z * WIDE if y is None else (4 * y + z) * WIDE
        return pl.ds(pl.multiple_of(start, WIDE), WIDE)

    def copy(self, number, src, dst, target):
        send, recv = self.sems
        return remote(src, dst, send.at[self.u, number], recv.at[self.u, number], ctx=target)

    def start(self, total):
        self.share[...] = total
        self.first = self.copy(
            0, self.share.at[:, self.half_of(1 - self.y)], self.half_in, self.beside
        )
        self.first.start()

    def spread(self):
        self.first.wait_recv()
        mine = self.share[:, self.half_of(self.y)]
        self.half[...] = (mine.astype(F32) + self.half_in[...].astype(F32)).astype(BF)
        self.out = []
        for d, z in enumerate(self.column):
            copy = self.copy(
                1 + d, self.half.at[:, self.piece_of(z)], self.quarters.at[self.z], 2 * z + self.y
            )
            copy.start()
            self.out.append(copy)
        self.quarters[self.z] = self.half[:, self.piece_of(self.z)]

    def total(self):
        for copy in self.out:
            copy.wait_recv()
        done = self.quarters[0].astype(F32)
        for z in range(1, 4):
            done = done + self.quarters[z].astype(F32)
        piece = self.whole.at[:, self.piece_of(self.z, self.y)]
        piece[...] = done.astype(BF)
        self.back = []
        for d, z in enumerate(self.column):
            copy = self.copy(4 + d, piece, piece, 2 * z + self.y)
            copy.start()
            self.back.append(copy)

    def join(self):
        for copy in self.back:
            copy.wait_recv()
        mine = self.whole.at[:, self.half_of(self.y)]
        self.last = self.copy(7, mine, mine, self.beside)
        self.last.start()

    def finish(self):
        self.last.wait_recv()
        for copy in (self.first, *self.out, *self.back, self.last):
            copy.wait_send()


def reduce_kernel(*refs):
    small_ref, ca_far, cb_far, out_far = refs[:4]
    sides_far, fin_ref = refs[4:8], refs[8]
    count = len(NAMES)
    small_out = refs[9]
    full_out = dict(zip((*NAMES, *LATE), refs[10 : 13 + count], strict=True))
    fin_out = refs[13 + count]
    refs = refs[14 + count :]
    low_ref, *sides = refs[:4]
    given = dict(zip(LATE, sides, strict=True))
    full = dict(zip((*NAMES, *LATE), refs[4 : 7 + count], strict=True))
    late_full = full
    move_sem = refs[7 + count]
    refs = refs[8 + count :]
    share = dict(zip(NAMES, refs[:count], strict=True))
    hold = dict(zip(NAMES, refs[count : 2 * count], strict=True))
    refs = refs[2 * count :]
    grid_share, half_in, half, quarters, small_in, small_mid, small_beside, small_column = refs[:8]
    small_send, small_recv, ring_send, ring_recv, grid_send, grid_recv, fin_send, fin_recv = refs[8:16]
    made, turned = refs[16:18]
    moves = Moves(move_sem)
    share_loads = [
        moves.start(*pair)
        for pair in (
            (ca_far.at[:224], share["cq"]),
            (cb_far, share["cv"]),
            (ca_far.at[224:], share["ck"]),
            (out_far.at[:, :32], share["co"]),
            (out_far.at[:, 32:48], share["so0"]),
            (out_far.at[:, 48:], share["so1"]),
        )
    ]
    side_loads = [moves.start(*pair) for pair in zip(sides_far, (low_ref, *sides), strict=True)]
    parts = {name: made.at[u] for u, name in enumerate(LATE)}
    extra = refs[18:]
    fold_wa = Folding(LATE, parts, (extra[0:4], None, extra[4:9]))
    place, after, before = ring_place(RING)
    grids = {
        name: Grid(
            u, grid_share.at[u], half_in.at[u], half.at[u], quarters.at[u], late_full[name], grid_send, grid_recv
        )
        for u, name in enumerate(LATE)
    }
    wa, both = fold_wa.wa, other_wa(fold_wa.across, 1)
    some = grids["q"]
    in_column = [2 * z + some.y for z in some.column]
    meet(
        [{"wa": peer} for peer in (fold_wa.mate, fold_wa.across, both)]
        + [{"ctx": peer} for peer in (after, before, some.beside, *in_column)]
    )
    near = remote(small_ref, small_in.at[0], small_send.at[0], small_recv.at[0], wa=fold_wa.mate)
    near.start()
    over = remote(small_mid.at[0], small_in.at[1], small_send.at[1], small_recv.at[1], wa=fold_wa.across)
    beside = remote(small_mid.at[1], small_beside, small_send.at[2], small_recv.at[2], ctx=some.beside)
    columns = [
        remote(small_mid.at[2], small_column.at[some.z], small_send.at[3 + d], small_recv.at[3 + d], ctx=peer)
        for d, peer in enumerate(in_column)
    ]
    own_fin = pltpu.make_async_copy(fin_ref.at[wa], fin_out.at[:, columns_of(wa)], fin_send.at[3])
    own_fin.start()
    fin_copies = [
        remote(fin_ref.at[peer], fin_out.at[:, columns_of(wa)], fin_send.at[d], fin_recv.at[d], wa=peer)
        for d, peer in enumerate((fold_wa.across, both, fold_wa.mate))
    ]
    wait_all(share_loads)
    copies = {}

    def ring_step(b, name, step):
        way = BUFFERS[name][0]
        here = place if way == 1 else RING - place
        target = after if way == 1 else before
        if step > 0:
            copies[name, step - 1].wait_recv()
        if step == 2 * HOPS:
            return
        now = lax.rem(here - step + 3 * RING, RING)
        mine = chunk_of(share[name], name, now)
        done = chunk_of(full[name], name, now)
        if 0 < step <= HOPS:
            total = mine[...].astype(F32) + hold[name][step - 1].astype(F32)
            (mine if step < HOPS else done)[...] = total.astype(BF)
        src, dst = (mine, hold[name].at[step]) if step < HOPS else (done, done)
        copy = remote(src, dst, ring_send.at[b, step], ring_recv.at[b, step], ctx=target)
        copy.start()
        copies[name, step] = copy

    def small_over():
        near.wait_recv()
        small_mid[0] = small_ref[...] + small_in[0]
        over.start()

    def small_next():
        over.wait_recv()
        small_mid[1] = small_mid[0] + small_in[1]
        beside.start()

    def small_last():
        beside.wait_recv()
        small_mid[2] = small_mid[1] + small_beside[...]
        small_column[some.z] = small_mid[2]
        for copy in columns:
            copy.start()

    def begin(name, following=None):
        total = fold_wa.total(name)
        if following:
            fold_wa.x_copies[following].start()
        grids[name].start(total)

    def make(name):
        parts[name][...] = nn_dot(turned[...], given[name][...]).astype(BF)
        fold_wa.start(name)

    def make_all():
        wait_all(side_loads)
        turned[...] = low_ref[...].astype(F32).T.astype(BF)
        make("q")
        make("k")
        fold_wa.send("q")
        make("v")
        fold_wa.prepare("k")
        fold_wa.prepare("v")

    events = {
        0: [make_all, small_over],
        4: [lambda: begin("q", "k"), small_next],
        6: [grids["q"].spread, lambda: begin("k", "v"), small_last],
        8: [grids["q"].total, grids["k"].spread],
        9: [lambda: begin("v"), grids["q"].join, *(copy.start for copy in fin_copies)],
        10: [grids["k"].total],
        11: [grids["v"].spread, grids["k"].join],
        12: [grids["v"].total],
        14: [grids["v"].join],
    }
    for tick in range(2 * HOPS + 1):
        for b, name in enumerate(NAMES):
            ring_step(b, name, tick)
        for event in events.get(tick, ()):
            event()
    stores = [moves.start(full[name], full_out[name]) for name in NAMES]
    for copy in columns:
        copy.wait_recv()
    total = small_column[0]
    for z in range(1, 4):
        total = total + small_column[z]
    small_out[...] = total
    for name in LATE:
        grids[name].finish()
        stores.append(moves.start(full[name], full_out[name]))
    fold_wa.finish()
    for copy in (near, over, beside, *columns, *copies.values()):
        copy.wait_send()
    own_fin.wait()
    for copy in fin_copies:
        copy.wait()
    wait_all(stores)


def columns_of(owner):
    return pl.ds(pl.multiple_of(owner * 896, WIDE), 896)


def reduce_grads(pair, one, flat, small, low, grads, fin):
    dma = pltpu.SemaphoreType.DMA
    any_spec = pl.BlockSpec(memory_space=pl.ANY)
    late = len(LATE)
    shapes = [*(BUFFERS[b][1] for b in NAMES), *[TALL] * late]
    small, *others = pl.pallas_call(
        reduce_kernel,
        out_shape=(
            jax.ShapeDtypeStruct(small.shape, F32),
            *(jax.ShapeDtypeStruct(shape, BF) for shape in shapes),
            jax.ShapeDtypeStruct((224, 3584), BF),
        ),
        in_specs=vmem(1) + [any_spec] * 8,
        out_specs=tuple(vmem(1) + [any_spec] * (len(shapes) + 1)),
        scratch_shapes=[
            pltpu.VMEM(low.shape, BF),
            *(pltpu.VMEM(grad.shape, BF) for grad in grads),
            *(pltpu.VMEM(shape, BF) for shape in shapes),
            dma((10 + len(shapes),)),
            *(pltpu.VMEM(BUFFERS[b][1], BF) for b in NAMES),
            *(pltpu.VMEM((HOPS, *chunk_shape(b)), BF) for b in NAMES),
            pltpu.VMEM((late, *TALL), BF),
            pltpu.VMEM((late, 224, 4 * WIDE), BF),
            pltpu.VMEM((late, 224, 4 * WIDE), BF),
            pltpu.VMEM((late, 4, 224, WIDE), BF),
            pltpu.VMEM((2, *small.shape), F32),
            pltpu.VMEM((3, *small.shape), F32),
            pltpu.VMEM(small.shape, F32),
            pltpu.VMEM((4, *small.shape), F32),
            dma((6,)),
            dma((6,)),
            dma((len(NAMES), 2 * HOPS)),
            dma((len(NAMES), 2 * HOPS)),
            dma((late, 8)),
            dma((late, 8)),
            dma((4,)),
            dma((3,)),
            pltpu.VMEM((late, 896, 1024), BF),
            pltpu.VMEM((896, 256), BF),
            *Folding.scratch(LATE),
        ],
        compiler_params=pltpu.CompilerParams(
            collective_id=3, has_side_effects=True, vmem_limit_bytes=56 << 20
        ),
        cost_estimate=lasting(90),
        name="reduce_grads",
    )(small, pair, one, flat, low, *grads, fin.reshape(4, 224, 896))
    return *others[:-1], small, others[-1]


WIDENED = ("cq", "ck", "cv", "q", "k", "v", "co", "fin", "fout")


def widen_kernel(*refs):
    count = len(WIDENED)
    so0, so1, near, last, back = refs[count : count + 5]
    outs = refs[count + 5 :]
    for src, dst in zip(refs[:count], outs[:count], strict=True):
        dst[...] = src[...].astype(F32)
    for c in range(so0.shape[0]):
        outs[count][c * 32 : c * 32 + 16, :] = so0[c].astype(F32)
        outs[count][c * 32 + 16 : c * 32 + 32, :] = so1[c].astype(F32)
    span = pl.program_id(0)

    @pl.when(span < 3)
    def _():
        outs[count + 1][...] = near[...]

    @pl.when(span == 3)
    def _():
        outs[count + 1][...] = (last[...] + back[...].astype(F32)).astype(BF)


def widen(full, near, last, back):
    values = [full[name] for name in WIDENED]
    blocks = {
        (224, 1024): ((224, 256), lambda i: (0, i)),
        (256, 896): ((64, 896), lambda i: (i, 0)),
        (224, 3584): ((224, 896), lambda i: (0, i)),
        (896, 896): ((224, 896), lambda i: (i, 0)),
    }
    specs = [pl.BlockSpec(*blocks[v.shape]) for v in values]
    halves = pl.BlockSpec((2, 16, 896), lambda i: (i, 0, 0))
    span = (256, 896)
    still = pl.BlockSpec(span, lambda i: (0, 0))
    moving = pl.BlockSpec(span, lambda i: (i, 0))
    *wide, neighbour = pl.pallas_call(
        widen_kernel,
        grid=(4,),
        out_shape=(
            *(jax.ShapeDtypeStruct(v.shape, F32) for v in values),
            jax.ShapeDtypeStruct(FLAT, F32),
            jax.ShapeDtypeStruct((1024, 896), BF),
        ),
        in_specs=[
            *specs,
            halves,
            halves,
            pl.BlockSpec(span, lambda i: (jnp.minimum(i, 2), 0)),
            still,
            still,
        ],
        out_specs=(*specs, pl.BlockSpec((64, 896), lambda i: (i, 0)), moving),
        compiler_params=pltpu.CompilerParams(vmem_limit_bytes=60 << 20),
        name="widen",
    )(*values, full["so0"], full["so1"], near, last, back)
    return dict(zip((*WIDENED, "so"), wide, strict=True)), neighbour


GELU = (2.0 / math.pi) ** 0.5


def ffn_kernel(
    late, f_ref, bias_ref, win_far, cot_far, wout_far, df_ref, dbias_ref, res_out, parts_out, dwin_out, dwout_out,
    win_ref, cot_ref, wout_ref, res_ref, parts_ref, dwin_ref, dwout_ref, move_sem, f_all, g_all, dul_all, ahead, own, kept, out_mate, out_cross, in_mate, in_cross, x_out, x_in,
    f_send, f_recv, p_send, p_recv,
):
    moves = Moves(move_sem)
    load_in, load_cot, load_out = (
        moves.start(*pair) for pair in ((win_far, win_ref), (cot_far, cot_ref), (wout_far, wout_ref))
    )
    me = lax.axis_index("wa")
    mate, across = other_wa(me, 1), other_wa(me, 2)
    both = other_wa(across, 1)
    barrier = pltpu.get_barrier_semaphore()
    for peer in (mate, across):
        pl.semaphore_signal(barrier, inc=1, device_id={"wa": peer}, device_id_type=MESH)
    pl.semaphore_wait(barrier, 2)
    to_across = remote(f_ref, f_all.at[me], f_send.at[1], f_recv.at[1], wa=across)
    to_across.start()
    to_mate = remote(f_ref, f_all.at[me], f_send.at[0], f_recv.at[0], wa=mate)
    to_mate.start()
    forward = remote(f_all.at[across], f_all.at[across], f_send.at[2], f_recv.at[2], wa=mate)
    f_all[me] = f_ref[...]
    order = (me, mate, across, both)
    dbias_ref[...] = jnp.zeros_like(dbias_ref)
    load_in.wait()
    for k, s in enumerate(order):
        if k == 1:
            to_mate.wait_recv()
        if k == 2:
            for d in range(2):
                ahead[d] = nt_dot(cot_ref[order[2 + d]], wout_ref[...])
            to_across.wait_recv()
            forward.start()
        if k == 3:
            forward.wait_recv()
        u = nn_dot(f_all[s], win_ref[...]) + bias_ref[...]
        square = u * u
        t = jnp.tanh(GELU * (u + 0.044715 * (square * u)))
        g_all[s] = (0.5 * u * (1.0 + t)).astype(BF)
        if k == 0:
            load_cot.wait()
            load_out.wait()
        slope = 0.5 * (1.0 + t) + 0.5 * u * (1.0 - t * t) * (GELU * (1.0 + 3 * 0.044715 * square))
        du = (nt_dot(cot_ref[s], wout_ref[...]) if k < 2 else ahead[k - 2]) * slope
        dbias_ref[...] += jnp.sum(du.reshape(32, 8, du.shape[1]), axis=0)
        dul_all[s] = du.astype(BF)

    def scatter(which, product):
        out_cross[which] = product(both).astype(BF)
        cross = remote(
            out_cross.at[which], in_cross.at[which], p_send.at[which, 0], p_recv.at[which, 0], wa=mate
        )
        cross.start()
        kept[...] = product(across)
        cross.wait_recv()
        x_out[which] = (kept[...] + in_cross[which].astype(F32)).astype(BF)
        over = remote(
            x_out.at[which], x_in.at[which], p_send.at[which, 1], p_recv.at[which, 1], wa=across
        )
        over.start()
        out_mate[which] = product(mate).astype(BF)
        near = remote(
            out_mate.at[which], in_mate.at[which], p_send.at[which, 2], p_recv.at[which, 2], wa=mate
        )
        near.start()
        own[which] = product(me)
        return cross, over, near

    def finish(which, copies, out_ref):
        cross, over, near = copies
        near.wait_recv()
        over.wait_recv()
        out_ref[...] = own[which] + in_mate[which].astype(F32) + x_in[which].astype(F32)
        for copy in copies:
            copy.wait_send()

    df_copies = scatter(0, lambda s: nt_dot(dul_all[s], win_ref[...]))
    if late:
        res_ref[...] = nn_dot(g_all[me], wout_ref[...])
        for d, s in enumerate(order[1:]):
            parts_ref[d] = nn_dot(g_all[s], wout_ref[...]).astype(BF)
    else:
        res_copies = scatter(1, lambda s: nn_dot(g_all[s], wout_ref[...]))
        parts_ref[...] = jnp.zeros_like(parts_ref)
    stores = []
    if late:
        stores += [moves.start(res_ref, res_out), moves.start(parts_ref, parts_out)]
    width = f_ref.shape[1]

    def outer(left_all, right, out_ref):
        for c in range(width // WIDE):
            lanes = slice(c * WIDE, (c + 1) * WIDE)
            total = None
            for s in range(4):
                left = left_all[s, :, lanes].astype(F32).T.astype(BF)
                now = nn_dot(left, right[s])
                total = now if total is None else total + now
            out_ref[lanes, :] = total.astype(BF)

    outer(f_all, dul_all, dwin_ref)
    stores.append(moves.start(dwin_ref, dwin_out))
    outer(g_all, cot_ref, dwout_ref)
    stores.append(moves.start(dwout_ref, dwout_out))
    finish(0, df_copies, df_ref)
    if not late:
        finish(1, res_copies, res_ref)
        stores += [moves.start(res_ref, res_out), moves.start(parts_ref, parts_out)]
    wait_all(stores)
    for copy in (to_mate, to_across, forward):
        copy.wait_send()


def ffn(late, f_low, cot_all, win, wout, bias):
    rows, width = f_low.shape
    hidden = win.shape[1]
    dma = pltpu.SemaphoreType.DMA
    block = (rows, width)
    any_spec = pl.BlockSpec(memory_space=pl.ANY)
    df, dbias, *others = pl.pallas_call(
        functools.partial(ffn_kernel, late),
        out_shape=(
            jax.ShapeDtypeStruct(block, F32),
            jax.ShapeDtypeStruct((8, hidden), F32),
            jax.ShapeDtypeStruct(block, F32),
            jax.ShapeDtypeStruct((3, *block), BF),
            jax.ShapeDtypeStruct(win.shape, BF),
            jax.ShapeDtypeStruct(wout.shape, BF),
        ),
        in_specs=vmem(2) + [any_spec] * 3,
        out_specs=tuple(vmem(2) + [any_spec] * 4),
        scratch_shapes=[
            pltpu.VMEM(win.shape, BF),
            pltpu.VMEM((4, *block), BF),
            pltpu.VMEM(wout.shape, BF),
            pltpu.VMEM(block, F32),
            pltpu.VMEM((3, *block), BF),
            pltpu.VMEM(win.shape, BF),
            pltpu.VMEM(wout.shape, BF),
            dma((7,)),
            pltpu.VMEM((4, *block), BF),
            pltpu.VMEM((4, rows, hidden), BF),
            pltpu.VMEM((4, rows, hidden), BF),
            pltpu.VMEM((2, rows, hidden), F32),
            pltpu.VMEM((2, *block), F32),
            pltpu.VMEM(block, F32),
            *[pltpu.VMEM((2, *block), BF)] * 6,
            dma((3,)),
            dma((3,)),
            dma((2, 3)),
            dma((2, 3)),
        ],
        compiler_params=pltpu.CompilerParams(
            collective_id=4, has_side_effects=True, vmem_limit_bytes=60 << 20
        ),
        cost_estimate=lasting(44),
        name="feed_forward",
    )(f_low, bias, win, cot_all, wout)
    res, parts, dwin, dwout = others
    return res, parts, df, dwin, dwout, dbias


def padded_rows(pad, values):
    rows = values.shape[0]
    pad[...] = jnp.zeros_like(pad)
    pad[1 : rows + 1, :] = values.astype(F32)


def both_heads(pad, g):
    here = pad[g * SPAN : (g + 1) * SPAN, :]
    left = head_mask(0, SPAN)
    return jnp.concatenate([jnp.where(left, here, 0.0), jnp.where(left, 0.0, here)], 0).astype(BF)


def join_heads(stacked):
    return jnp.where(head_mask(0, SPAN), stacked[:SPAN], stacked[SPAN:])


def cross_forward_kernel(groups, keep_ref, q_ref, k_ref, v_ref, x_ref, q_pad, x_pad):
    padded_rows(q_pad, q_ref[...])
    spans = range(groups)
    rows = [slice(g * 256, (g + 1) * 256) for g in spans]
    scores = [nt_dot(both_heads(q_pad, g) * BF(HD**-0.5), k_ref[rows[g], :]) for g in spans]
    weights = [jnp.exp(v - jnp.max(v, axis=1, keepdims=True)) for v in scores]
    weights = [v / jnp.sum(v, axis=1, keepdims=True) for v in weights]
    mixed = [join_heads(nn_dot(weights[g].astype(BF), v_ref[rows[g], :])) for g in spans]
    mixed[0] = mixed[0] * keep_ref[0:1, :]
    for g in spans:
        x_pad[g * SPAN : (g + 1) * SPAN, :] = mixed[g]
    x_ref[...] = x_pad[1 : x_ref.shape[0] + 1, :].astype(BF)


def pair_specs(*rows):
    return [pl.BlockSpec((r, WIDE), lambda p: (0, p)) for r in rows]


def cross_forward(keep, query, keys, values):
    rows, width = query.shape
    many = keys.shape[0]
    groups = many // 256
    return pl.pallas_call(
        functools.partial(cross_forward_kernel, groups),
        grid=(width // WIDE,),
        out_shape=jax.ShapeDtypeStruct(query.shape, BF),
        in_specs=[pl.BlockSpec((8, WIDE), lambda p: (0, 0)), *pair_specs(rows, many, many)],
        out_specs=pair_specs(rows)[0],
        scratch_shapes=[pltpu.VMEM((groups * SPAN, WIDE), F32)] * 2,
        compiler_params=pltpu.CompilerParams(vmem_limit_bytes=16 << 20),
        cost_estimate=lasting(9),
        name="cross_forward",
    )(keep, query, keys, values)


def cross_backward_kernel(
    groups, keep_ref, q_ref, dx_ref, k_ref, v_ref, dq_ref, dk_ref, dv_ref, q_pad, dx_pad, dq_pad
):
    padded_rows(q_pad, q_ref[...])
    padded_rows(dx_pad, dx_ref[...])
    dx_pad[:SPAN, :] = dx_pad[:SPAN, :] * keep_ref[0:1, :]
    for g in range(groups):
        rows = slice(g * 256, (g + 1) * 256)
        query = both_heads(q_pad, g) * BF(HD**-0.5)
        dmixed = both_heads(dx_pad, g)
        keys, values = k_ref[rows, :], v_ref[rows, :]
        scores = nt_dot(keys, query)
        weights = jnp.exp(scores - jnp.max(scores, axis=0, keepdims=True))
        weights = weights / jnp.sum(weights, axis=0, keepdims=True)
        dweights = nt_dot(values, dmixed)
        dscores = weights * (dweights - jnp.sum(weights * dweights, axis=0, keepdims=True))
        dk_ref[rows, :] = nn_dot(dscores.astype(BF), query).astype(BF)
        dv_ref[rows, :] = nn_dot(weights.astype(BF), dmixed).astype(BF)
        back = (dscores * HD**-0.5).T.astype(BF)
        dq_pad[g * SPAN : (g + 1) * SPAN, :] = join_heads(nn_dot(back, keys))
    dq_ref[...] = dq_pad[1 : dq_ref.shape[0] + 1, :].astype(BF)


def cross_backward(keep, query, dmixed, keys, values):
    rows, width = query.shape
    many = keys.shape[0]
    groups = many // 256
    return pl.pallas_call(
        functools.partial(cross_backward_kernel, groups),
        grid=(width // WIDE,),
        out_shape=(
            jax.ShapeDtypeStruct(query.shape, BF),
            jax.ShapeDtypeStruct(keys.shape, BF),
            jax.ShapeDtypeStruct(keys.shape, BF),
        ),
        in_specs=[
            pl.BlockSpec((8, WIDE), lambda p: (0, 0)),
            *pair_specs(rows, rows, many, many),
        ],
        out_specs=tuple(pair_specs(rows, many, many)),
        scratch_shapes=[pltpu.VMEM((groups * SPAN, WIDE), F32)] * 3,
        compiler_params=pltpu.CompilerParams(vmem_limit_bytes=16 << 20),
        cost_estimate=lasting(17),
        name="cross_backward",
    )(keep, query, dmixed, keys, values)


def line_selector():
    place = jnp.arange(LINE)
    offset = jnp.where(place < LINE // 2, -place, LINE - place)
    return (bucket_of(offset)[None, :] == jnp.arange(NB)[:, None]).astype(jnp.float32)


def ring_forward(query_low, key_low, value_low, bucket_table):
    row_count, attn_width = query_low.shape
    position = lax.axis_index("ctx")
    scale_factor = HD ** (-0.5)
    bias_set, onehots = make_bias(bucket_table.astype(jnp.float32), row_count)
    query_heads = query_low.reshape(row_count, H, HD)
    start_state = (
        jnp.full((H, row_count), negative, jnp.float32),
        jnp.zeros((H, row_count), jnp.float32),
        jnp.zeros((row_count, attn_width), jnp.float32),
    )
    running_max, running_sum, running_acc = forward_fold(
        query_heads,
        position,
        row_count,
        bias_set,
        scale_factor,
        start_state,
        (
            lax.all_gather(key_low, "ctx", axis=0, tiled=True),
            lax.all_gather(value_low, "ctx", axis=0, tiled=True),
        ),
    )
    attended = (running_acc.reshape(row_count, H, HD) / running_sum.T[:, :, None]).reshape(
        row_count, attn_width
    )
    log_total = running_max + jnp.log(running_sum)
    state = (query_heads, key_low, value_low, attended, log_total, bias_set, onehots)
    return attended.astype(jnp.bfloat16), state


def ring_backward(state, dout_low):
    query_heads, key_low, value_low, attended, log_total, bias_set, onehots = state
    row_count, attn_width = dout_low.shape
    cycle_size = lax.axis_size("ctx")
    position = lax.axis_index("ctx")
    scale_factor = HD ** (-0.5)
    dout_heads = dout_low.reshape(row_count, H, HD)
    row_delta = jnp.sum(
        (dout_low.astype(jnp.float32) * attended).reshape(row_count, H, HD), axis=-1
    ).T
    zero_rows = jnp.zeros((row_count, attn_width), jnp.float32)
    zero_tables = (
        jnp.zeros((H, row_count, row_count), jnp.float32),
        jnp.zeros((H, row_count, row_count), jnp.float32),
        jnp.zeros((H,), jnp.float32),
    )

    def visit(folded, key_now, value_now, relation):

        def visit_compute(current):
            dquery_acc, dkey_acc, dvalue_acc, relative_bias_tables = current
            key_heads = key_now.reshape(row_count, H, HD)
            weights_now, dscores, ds_low = pair_core(
                query_heads,
                dout_heads,
                log_total,
                row_delta,
                key_heads,
                value_now.reshape(row_count, H, HD),
                relation,
                bias_set,
                scale_factor,
            )
            dquery = jnp.einsum(
                "hqk,khd->qhd", ds_low, key_heads, preferred_element_type=jnp.float32
            ).reshape(row_count, attn_width)
            dkey = jnp.einsum(
                "hqk,qhd->khd", ds_low, query_heads, preferred_element_type=jnp.float32
            ).reshape(row_count, attn_width)
            dvalue = jnp.einsum(
                "hqk,qhd->khd",
                weights_now.astype(jnp.bfloat16),
                dout_heads,
                preferred_element_type=jnp.float32,
            ).reshape(row_count, attn_width)
            return (
                dquery_acc + dquery,
                dkey_acc + dkey,
                dvalue_acc + dvalue,
                add_tables(relative_bias_tables, dscores, relation),
            )

        return lax.cond(relation >= 0, visit_compute, lambda unchanged: unchanged, folded)

    first_state = visit(
        (zero_rows, zero_rows, zero_rows, zero_tables), key_low, value_low, jnp.array(0, jnp.int32)
    )

    def cycle_step(carried, cycle_index):
        key_now, value_now, (dquery_acc, dkey_acc, dvalue_acc, relative_bias_tables) = carried
        key_next, value_next = passed_along((key_now, value_now), "ctx", 1)
        dkey_next, dvalue_next = (
            from_behind(dkey_acc.astype(jnp.bfloat16), "ctx", 1).astype(dkey_acc.dtype),
            from_behind(dvalue_acc.astype(jnp.bfloat16), "ctx", 1).astype(dvalue_acc.dtype),
        )
        relation = jnp.where(position >= cycle_index, cycle_index, -1)
        updated = visit(
            (dquery_acc, dkey_next, dvalue_next, relative_bias_tables),
            key_next,
            value_next,
            relation,
        )
        return ((key_next, value_next, updated), None)

    (
        unused_key,
        unused_value,
        (dquery_total, dkey_part, dvalue_part, relative_bias_tables),
    ), unused = lax.scan(cycle_step, (key_low, value_low, first_state), jnp.arange(1, cycle_size))
    dkey_total, dvalue_total = (
        from_behind(dkey_part.astype(jnp.bfloat16), "ctx", 1).astype(dkey_part.dtype),
        from_behind(dvalue_part.astype(jnp.bfloat16), "ctx", 1).astype(dvalue_part.dtype),
    )
    dquery_low = dquery_total.astype(jnp.bfloat16)
    dkey_low = dkey_total.astype(jnp.bfloat16)
    dvalue_low = dvalue_total.astype(jnp.bfloat16)
    current_bucket_selector, previous_bucket_selector, onehot_far = onehots
    grad_biastable = (
        jnp.einsum(
            "afw,mfw->am",
            current_bucket_selector,
            relative_bias_tables[0],
            precision=strongest_precision,
        )
        + jnp.einsum(
            "afw,mfw->am",
            previous_bucket_selector,
            relative_bias_tables[1],
            precision=strongest_precision,
        )
        + onehot_far[:, None] * relative_bias_tables[2][None, :]
    )
    return dquery_low, dkey_low, dvalue_low, grad_biastable


def heads_forward(tokens, near, cotangent, given):
    wa, owners = lax.axis_index("wa"), lax.axis_size("wa")
    table = given["biastable"].astype(F32)
    selector = lax.dynamic_slice_in_dim(line_selector(), wa * table.shape[0], table.shape[0], 0)
    lines = jnp.dot(table.T, selector, precision=strongest_precision).astype(BF)
    gains = jnp.concatenate([given[name] for name in GAINS]).reshape(len(GAINS), -1)
    small = jnp.zeros((H, LINE), BF)
    small = lax.dynamic_update_slice(small, gains, (0, wa * gains.shape[1]))
    small = jnp.concatenate([lines, small], 0)
    shards = [given[LONG_NAMES[name]] for name in GATHERED]
    *wholes, upstream_all, feed_in, attended_low, low, ot, lse, small, before, qh, kh, vh, keys, values = attn_forward(
        lax.axis_size("ctx"), tokens, small, near, [*shards, cotangent], given["feedin"]
    )
    width = tokens.shape[1]
    gain_of = {name: small[H + g, :width] for g, name in enumerate(GAINS)}
    full = {LONG_NAMES[name]: whole for name, whole in zip(GATHERED, wholes, strict=True)}
    full["feedin"] = feed_in
    upstream_all = upstream_all.reshape(owners, *tokens.shape)
    saved = (qh, kh, vh, ot, lse, small[:H])
    return attended_low, low, full, gain_of, upstream_all, (before, keys, values), saved


def heads_backward(state, dout_low, parts, feed_part):
    peers = lax.axis_size("ctx")
    dquery_low, dkey_low, dvalue_low, sums, *shares = attn_backward(
        peers, dout_low, *state, parts, feed_part
    )
    selector = line_selector()
    table = jnp.dot(selector, sums[:2].T, precision=strongest_precision)
    far = jnp.sum(sums[2:4], axis=1)
    table = table + selector[:, WIDE : WIDE + 1] * far[None, :]
    whole = jnp.zeros((NB, H), jnp.float32)
    whole = lax.dynamic_update_slice(whole, table, (0, 2 * lax.axis_index("ctx")))
    return dquery_low, dkey_low, dvalue_low, whole, shares


def cross_pair(groups, keep_ref, q_ref, dx_ref, k_ref, v_ref, dq_ref, dk_ref, dv_ref, q_pad, dx_pad, dq_pad, p):
    lanes = lanes_of(p)
    padded_rows(q_pad, q_ref[:, lanes])
    padded_rows(dx_pad, dx_ref[:, lanes])
    dx_pad[:SPAN, :] = dx_pad[:SPAN, :] * keep_ref[0:1, :]
    for g in range(groups):
        rows = slice(g * 256, (g + 1) * 256)
        query = both_heads(q_pad, g) * BF(HD**-0.5)
        dmixed = both_heads(dx_pad, g)
        keys, values = k_ref[rows, lanes], v_ref[rows, lanes]
        scores = nt_dot(keys, query)
        weights = jnp.exp(scores - jnp.max(scores, axis=0, keepdims=True))
        weights = weights / jnp.sum(weights, axis=0, keepdims=True)
        dweights = nt_dot(values, dmixed)
        dscores = weights * (dweights - jnp.sum(weights * dweights, axis=0, keepdims=True))
        dk_ref[rows, lanes] = nn_dot(dscores.astype(BF), query).astype(BF)
        dv_ref[rows, lanes] = nn_dot(weights.astype(BF), dmixed).astype(BF)
        back = (dscores * HD**-0.5).T.astype(BF)
        dq_pad[g * SPAN : (g + 1) * SPAN, :] = join_heads(nn_dot(back, keys))
    dq_ref[:, lanes] = dq_pad[1 : dq_ref.shape[0] + 1, :].astype(BF)


def middle_kernel(
    keep_ref, fed_ref, fed_parts, q_far, dx_far, k_far, v_far, before_far, near_far, wk_far, wv_far, fin_ref,
    fout_ref, feed_out, fed_out, dq_out, dwk_out, dwv_out, first_out, near_out, last_out,
    q_ref, dx_ref, k_ref, v_ref, before_ref, near_ref, wk_ref, wv_ref, dq_ref, dwk_ref, dwv_ref, near_low, near_last,
    dk, dv, q_pad, dx_pad, dq_pad, share, hold, in_mate, in_cross, x_out, x_in, load_sem, ring_send, ring_recv,
    fed_send, fed_recv,
):
    ring = Ring(FEED_LANES, ring_send, ring_recv, share=share, hold=hold)
    moves = Moves(load_sem)
    loads = [moves.start(part, share.at[b]) for b, part in enumerate((fin_ref, fout_ref))]
    pair_loads = [
        moves.start(*pair) for pair in ((q_far, q_ref), (dx_far, dx_ref), (k_far, k_ref), (v_far, v_ref))
    ]
    later_loads = [
        moves.start(*pair)
        for pair in ((wk_far, wk_ref), (wv_far, wv_ref), (before_far, before_ref), (near_far, near_ref))
    ]
    wa = lax.axis_index("wa")
    mate, across = other_wa(wa, 1), other_wa(wa, 2)
    meet([{"ctx": ring.after}, {"ctx": ring.before}, {"wa": mate}, {"wa": across}])
    cross = remote(fed_parts.at[2], in_cross, fed_send.at[0], fed_recv.at[0], wa=mate)
    cross.start()
    near = remote(fed_parts.at[0], in_mate, fed_send.at[1], fed_recv.at[1], wa=mate)
    near.start()
    over = remote(x_out, x_in, fed_send.at[2], fed_recv.at[2], wa=across)
    wait_all(loads)
    for lanes in FEED_TURNS:
        ring.scatter(jnp.int32(0), lanes)
    cross.wait_recv()
    x_out[...] = (fed_parts[1].astype(F32) + in_cross[...].astype(F32)).astype(BF)
    over.start()
    groups = k_ref.shape[0] // 256
    wait_all(pair_loads)

    def two_pairs(m, unused):
        for turn, lanes in enumerate(FEED_TURNS):
            cross_pair(
                groups, keep_ref, q_ref, dx_ref, k_ref, v_ref, dq_ref, dk, dv, q_pad, dx_pad, dq_pad,
                2 * m + turn,
            )
            ring.scatter(m + 1, lanes)
        return unused

    pairs = q_ref.shape[1] // (2 * WIDE)
    lax.fori_loop(0, pairs, two_pairs, 0)
    stores = [moves.start(dq_ref, dq_out)]
    wait_all(later_loads)
    calls = [(step, lanes) for step in range(pairs + 1, HOPS + 1) for lanes in FEED_TURNS]

    def turn():
        if calls:
            step, lanes = calls.pop(0)
            ring.scatter(jnp.int32(step), lanes)

    for g in range(groups):
        rows = slice(g * 256, (g + 1) * 256)
        total = nt_dot(dk[rows, :], wk_ref[...]) + nt_dot(dv[rows, :], wv_ref[...])
        if g == groups - 1:
            near_last[...] = total
        else:
            near_low[rows, :] = total.astype(BF)
        if g % 2 == 1:
            turn()
    stores += [
        moves.start(near_low.at[:256], first_out),
        moves.start(near_low.at[256:], near_out),
        moves.start(near_last, last_out),
    ]
    for c in range(near_ref.shape[1] // WIDE):
        lanes = slice(c * WIDE, (c + 1) * WIDE)
        first = before_ref[:, lanes].astype(F32).T.astype(BF)
        left = near_ref[:, lanes].astype(F32).T.astype(BF)
        for grads, out_ref in ((dk, dwk_ref), (dv, dwv_ref)):
            total = nn_dot(first, grads[:256, :]) + nn_dot(left, grads[256:, :])
            out_ref[lanes, :] = total.astype(BF)
        if c % 2 == 1:
            turn()
    stores += [moves.start(dwk_ref, dwk_out), moves.start(dwv_ref, dwv_out)]
    while calls:
        turn()
    near.wait_recv()
    over.wait_recv()
    fed_out[...] = fed_ref[...] + in_mate[...].astype(F32) + x_in[...].astype(F32)
    for copy in (cross, near, over):
        copy.wait_send()
    for lane in range(2):
        feed_out[lane] = share[lane, ring.chunk(lane, 1)]
    ring.finish(lambda lane: share.at[FEED_LANES[lane][0], 0, FEED_LANES[lane][2]])
    wait_all(stores)


def middle(keep, query, dmixed, keys, values, before, near, wk, wv, fed, fed_parts, fin, fout):
    many, width = keys.shape
    wide = near.shape[1]
    rows = query.shape[0]
    low = functools.partial(jax.ShapeDtypeStruct, dtype=BF)
    dma = pltpu.SemaphoreType.DMA
    any_spec = pl.BlockSpec(memory_space=pl.ANY)
    pad = pltpu.VMEM((many // 256 * SPAN, WIDE), F32)
    feed_part, fed, *others = pl.pallas_call(
        middle_kernel,
        out_shape=(
            low((2, *FEED[1:])),
            jax.ShapeDtypeStruct(fed.shape, F32),
            low(query.shape),
            low(wk.shape),
            low(wv.shape),
            low((256, wide)),
            low((many - 512, wide)),
            jax.ShapeDtypeStruct((256, wide), F32),
        ),
        in_specs=vmem(3) + [any_spec] * 10,
        out_specs=tuple(vmem(2) + [any_spec] * 6),
        scratch_shapes=[
            *[pltpu.VMEM((rows, width), BF)] * 2,
            *[pltpu.VMEM((many, width), BF)] * 2,
            pltpu.VMEM((256, wide), BF),
            pltpu.VMEM((many - 256, wide), BF),
            *[pltpu.VMEM(wk.shape, BF)] * 2,
            pltpu.VMEM((rows, width), BF),
            *[pltpu.VMEM(wk.shape, BF)] * 2,
            pltpu.VMEM((many - 256, wide), BF),
            pltpu.VMEM((256, wide), F32),
            pltpu.VMEM((many, width), BF),
            pltpu.VMEM((many, width), BF),
            pad,
            pad,
            pad,
            pltpu.VMEM((2, *FEED), BF),
            pltpu.VMEM((2, HOPS, *FEED[1:]), BF),
            *[pltpu.VMEM(fed.shape, BF)] * 4,
            dma((16,)),
            dma((len(FEED_LANES), HOPS)),
            dma((len(FEED_LANES), HOPS)),
            dma((3,)),
            dma((3,)),
        ],
        compiler_params=pltpu.CompilerParams(
            collective_id=5, has_side_effects=True, vmem_limit_bytes=60 << 20
        ),
        cost_estimate=lasting(38),
        name="middle",
    )(
        keep, fed, fed_parts, query, dmixed, keys, values, before, near, wk, wv,
        fin.reshape(FEED), fout.reshape(FEED),
    )
    return *others, feed_part, fed


NAMES_OF_WEIGHTS = (
    "selfnorm", "selfquery", "selfkey", "selfvalue", "selfout", "biastable", "crossnorm", "crossquery",
    "crosskey", "crossvalue", "crossout", "feednorm", "feedin", "feedbias", "feedout", "outbias",
)
LONG_NAMES = {
    "q": "selfquery",
    "k": "selfkey",
    "v": "selfvalue",
    "so": "selfout",
    "ck": "crosskey",
    "cv": "crossvalue",
    "cq": "crossquery",
    "co": "crossout",
}


def whole_over_wa(shard):
    return lax.all_gather(shard, "wa", axis=0, tiled=True)


def reduce_plain(parts, smalls):
    shares = [
        lax.psum_scatter(part, "wa", scatter_dimension=0, tiled=True).astype(F32)
        for part in parts.values()
    ]
    totals = lax.psum(shares, "ctx")
    return dict(zip(parts, totals, strict=True)), lax.psum(smalls, ("ctx", "wa"))


def per_device(tokens, neighbours, cotangent, *shards):
    given = dict(zip(NAMES_OF_WEIGHTS, shards, strict=True))
    peers = lax.axis_size("ctx")
    position = lax.axis_index("ctx")
    row_count, model_width = tokens.shape[1:]
    split_heads = peers * 2 == H and row_count == BLOCK
    inputs = tokens[0].astype(F32)
    upstream_low = cotangent[0]
    upstream = upstream_low.astype(F32)
    spans = neighbours.shape[1]
    span_rows = neighbours.shape[2] * neighbours.shape[3]
    own_rows = neighbours[0].reshape(spans * span_rows, model_width)
    if split_heads and span_rows == BLOCK:
        attended_low, normed_low, full, small_of, upstream_all, projected, attention_state = (
            heads_forward(tokens[0], own_rows, upstream_low, given)
        )
        before, keys_cross, values_cross = projected
        feed_in = full["feedin"]
        normed_self, back_self = jax.vjp(root_norm, inputs, small_of["selfnorm"])
    else:
        small_of = {name: whole_over_wa(given[name]).astype(F32) for name in GAINS}
        full = {name: whole_over_wa(given[name]) for name in LONG_NAMES.values()}
        normed_self, back_self = jax.vjp(root_norm, inputs, small_of["selfnorm"])
        normed_low = normed_self.astype(BF)
        attended_low, attention_state = ring_forward(
            *(
                forward_product(normed_low, full[name]).astype(BF)
                for name in ("selfquery", "selfkey", "selfvalue")
            ),
            whole_over_wa(given["biastable"]),
        )
        upstream_all = lax.all_gather(upstream_low, "wa", axis=0)
        feed_in = lax.all_to_all(given["feedin"], "wa", 1, 0, tiled=True)
        before = passed_along(own_rows[-span_rows:], "ctx", 1)
        near_rows = jnp.concatenate([before, own_rows], 0)
        keys_cross = forward_product(near_rows, full["crosskey"]).astype(BF)
        values_cross = forward_product(near_rows, full["crossvalue"]).astype(BF)
    hidden = inputs + forward_product(attended_low, full["selfout"])

    normed_cross, back_cross = jax.vjp(root_norm, hidden, small_of["crossnorm"])
    cross_in = normed_cross.astype(BF)
    query_cross = forward_product(cross_in, full["crossquery"]).astype(BF)
    keep = jnp.full((8, WIDE), jnp.where(position > 0, 1.0, 0.0), F32)
    mixed_low = cross_forward(keep, query_cross, keys_cross, values_cross)
    hidden_two = hidden + forward_product(mixed_low, full["crossout"])

    normed_feed, back_feed = jax.vjp(root_norm, hidden_two, small_of["feednorm"])
    feed_low = normed_feed.astype(BF)
    bias_row = given["feedbias"].astype(F32)[None]
    fed, fed_parts, grad_feed, fin, fout, bias_sums = ffn(
        split_heads, feed_low, upstream_all, feed_in, given["feedout"], bias_row
    )
    grad_two_part, grad_feednorm = back_feed(grad_feed)
    grad_two = upstream + grad_two_part
    two_low = grad_two.astype(BF)

    grad_mixed = back_product(two_low, full["crossout"]).astype(BF)
    early = {}
    if split_heads:
        grad_query_cross, early["ck"], early["cv"], first, near_low, near_last, feed_part, fed = middle(
            keep,
            query_cross,
            grad_mixed,
            keys_cross,
            values_cross,
            before,
            own_rows,
            full["crosskey"],
            full["crossvalue"],
            fed,
            fed_parts,
            fin,
            fout,
        )
    else:
        grad_query_cross, dkeys, dvalues = cross_backward(
            keep, query_cross, grad_mixed, keys_cross, values_cross
        )
        near_grads = back_product(dkeys, full["crosskey"]) + back_product(
            dvalues, full["crossvalue"]
        )
        first, near_last = near_grads[:span_rows].astype(BF), near_grads[-span_rows:]
        near_low = near_grads[span_rows:-span_rows].astype(BF)
        early["ck"] = outer_product(near_rows, dkeys).astype(BF)
        early["cv"] = outer_product(near_rows, dvalues).astype(BF)
    result = (hidden_two + fed + small_of["outbias"]).astype(BF)
    back = passed_along(first, "ctx", -1)
    grad_hidden_part, grad_crossnorm = back_cross(
        back_product(grad_query_cross, full["crossquery"])
    )
    grad_hidden = grad_two + grad_hidden_part
    hidden_low = grad_hidden.astype(BF)
    dout_low = back_product(hidden_low, full["selfout"]).astype(BF)
    sides = {
        "cq": (cross_in, grad_query_cross),
        "co": (mixed_low, two_low),
        "so": (attended_low, hidden_low),
    }
    if split_heads:
        parts = [early["ck"], early["cv"], *(side for name in MADE for side in sides[name])]
        dquery_low, dkey_low, dvalue_low, grad_biastable, shares = heads_backward(
            attention_state, dout_low, parts, feed_part
        )
        *shares, fin, fout = shares
    else:
        dquery_low, dkey_low, dvalue_low, grad_biastable = ring_backward(attention_state, dout_low)
    grad_normed = (
        back_product(dquery_low, full["selfquery"])
        + back_product(dkey_low, full["selfkey"])
        + back_product(dvalue_low, full["selfvalue"])
    )
    grad_input_part, grad_selfnorm = back_self(grad_normed)
    grad_inputs = (grad_hidden + grad_input_part).astype(BF)

    late_grads = (dquery_low, dkey_low, dvalue_low)
    wa, owners = lax.axis_index("wa"), lax.axis_size("wa")
    bias_grad = jnp.sum(bias_sums, axis=0)
    placed = lax.dynamic_update_slice(
        jnp.zeros((owners, bias_grad.size), F32), bias_grad[None], (wa, 0)
    )
    sums = [grad_selfnorm, grad_crossnorm, grad_feednorm, jnp.sum(upstream, axis=0), grad_biastable]
    packed = jnp.concatenate([*(v.reshape(owners, -1) for v in sums), placed], axis=1)
    packed = jnp.pad(packed, ((0, 0), (0, LINE * 2 - packed.shape[1]))).reshape(-1, WIDE)
    if split_heads:
        *reduced, packed, fin = reduce_grads(
            *shares, packed, normed_low, late_grads, fin
        )
        reduced = dict(zip((*NAMES, *LATE), reduced, strict=True))
        reduced["co"] = reduced["co"].reshape(FLAT)
        reduced |= {"fin": fin, "fout": fout.reshape(given["feedout"].shape)}
        grads, grad_neigh = widen(reduced, near_low, near_last, back)
    else:
        for name, grad in zip(LATE, late_grads, strict=True):
            sides[name] = (normed_low, grad)
        for name, (left, right) in sides.items():
            early[name] = outer_product(left, right).astype(BF)
        grads, packed = reduce_plain(early, packed)
        fin, fout = lax.psum((fin, fout), "ctx")
        fin = lax.all_to_all(fin, "wa", 0, 1, tiled=True)
        grads["fin"], grads["fout"] = fin.astype(F32), fout.astype(F32)
        grad_neigh = jnp.concatenate([near_low, (near_last + back.astype(F32)).astype(BF)], 0)
    grad_neigh = grad_neigh.reshape(neighbours.shape)
    mine = lax.dynamic_index_in_dim(packed.reshape(owners, -1), wa, 0, keepdims=False)
    cuts, start = [], 0
    for v in (*sums, placed):
        cuts.append(mine[start : start + v.size // owners])
        start += v.size // owners
    own_selfnorm, own_crossnorm, own_feednorm, own_outbias, own_table, own_feedbias = cuts
    return (
        result[None],
        grad_inputs[None],
        grad_neigh,
        own_selfnorm,
        grads["q"],
        grads["k"],
        grads["v"],
        grads["so"],
        own_table.reshape(-1, H),
        own_crossnorm,
        grads["cq"],
        grads["ck"],
        grads["cv"],
        grads["co"],
        own_feednorm,
        grads["fin"],
        own_feedbias,
        grads["fout"],
        own_outbias,
    )


def solution(mesh):
    return jax.shard_map(
        per_device,
        mesh=mesh,
        in_specs=(
            P("wa", "ctx", None),
            P("wa", "ctx", None, None, None),
            P("wa", "ctx", None),
            P("wa"),
            P("wa", None),
            P("wa", None),
            P("wa", None),
            P("wa", None),
            P("wa", None),
            P("wa"),
            P("wa", None),
            P("wa", None),
            P("wa", None),
            P("wa", None),
            P("wa"),
            P("wa", None),
            P("wa"),
            P("wa", None),
            P("wa"),
        ),
        out_specs=(
            P("wa", "ctx", None),
            P("wa", "ctx", None),
            P("wa", "ctx", None, None, None),
            P("wa"),
            P("wa", None),
            P("wa", None),
            P("wa", None),
            P("wa", None),
            P("wa", None),
            P("wa"),
            P("wa", None),
            P("wa", None),
            P("wa", None),
            P("wa", None),
            P("wa"),
            P("wa", None),
            P("wa"),
            P("wa", None),
            P("wa"),
        ),
        check_vma=False,
    )
```

```python
import functools
import math

import jax
import jax.numpy as jnp
from jax import lax
from jax.experimental import pallas as pl
from jax.experimental.pallas import tpu as pltpu
from jax.sharding import PartitionSpec as P

H = 16
HD = 64
NB = 32
MAXD = 128
BLOCK = 256
SPAN = 64
MESH = pl.DeviceIdType.MESH
WIDE = 128
LINE = 1024
BF = jnp.bfloat16
F32 = jnp.float32


epsilon = 1e-06
negative = -1e30
strongest_precision = lax.Precision.HIGHEST


def passed_along(value, axis, by):
    peers = lax.axis_size(axis)
    pairs = [(i, i + by) for i in range(peers) if 0 <= i + by < peers]
    return lax.ppermute(value, axis, pairs)


def from_behind(block, axis, distance):
    devices = range(lax.axis_size(axis))
    route = [((i - distance) % len(devices), i) for i in devices]
    return lax.ppermute(block, axis, route)


def bucket_edges():
    half_count = NB // 2
    exact_part = half_count // 2
    edge_list = []
    for level_index in range(exact_part + 1, half_count):
        hits = [
            distance_now
            for distance_now in range(exact_part, MAXD + 1)
            if exact_part
            + int(
                math.log(distance_now / exact_part)
                / math.log(MAXD / exact_part)
                * (half_count - exact_part)
            )
            >= level_index
        ]
        edge_list.append(min(hits + [MAXD]))
    return (half_count, exact_part, edge_list)


def bucket_of(offset_value):
    half_count, exact_part, edge_list = bucket_edges()
    magnitude = jnp.abs(offset_value)
    far_part = exact_part + sum(
        [(magnitude >= edge_value).astype(magnitude.dtype) for edge_value in edge_list],
        jnp.zeros_like(magnitude),
    )
    return jnp.where(offset_value > 0, half_count, 0) + jnp.where(
        magnitude < exact_part, magnitude, far_part
    )


def root_norm(values, gain_vector):
    return (
        values
        * lax.rsqrt(jnp.mean(values * values, axis=-1, keepdims=True) + epsilon)
        * gain_vector
    )


def gelu_tanh(values):
    return jax.nn.gelu(values, approximate=True)


def forward_product(values, weight):
    return jnp.dot(values, weight, preferred_element_type=jnp.float32)


def outer_product(left_side, right_side):
    return lax.dot_general(
        left_side, right_side, (((0,), (0,)), ((), ())), preferred_element_type=jnp.float32
    )


def back_product(grad_low, weight):
    return lax.dot_general(
        grad_low, weight, (((1,), (1,)), ((), ())), preferred_element_type=jnp.float32
    )


def make_bias(bucket_bias_rows, row_count):
    query_place = jnp.arange(row_count)[:, None]
    key_place = jnp.arange(row_count)[None, :]
    levels = jnp.arange(NB)
    current_bucket_selector = (
        bucket_of(key_place - query_place)[None] == levels[:, None, None]
    ).astype(jnp.float32)
    previous_bucket_selector = (
        bucket_of(key_place - row_count - query_place)[None] == levels[:, None, None]
    ).astype(jnp.float32)
    onehot_far = (bucket_of(jnp.array(-MAXD, jnp.int32)) == levels).astype(jnp.float32)
    current_block_bias = jnp.einsum(
        "smz,sj->jmz", current_bucket_selector, bucket_bias_rows, precision=strongest_precision
    )
    previous_block_bias = jnp.einsum(
        "smz,sj->jmz", previous_bucket_selector, bucket_bias_rows, precision=strongest_precision
    )
    bias_far = jnp.dot(onehot_far, bucket_bias_rows, precision=strongest_precision)
    mask_same = key_place // BLOCK <= query_place // BLOCK
    return (
        (current_block_bias, previous_block_bias, bias_far, mask_same),
        (current_bucket_selector, previous_bucket_selector, onehot_far),
    )


def pair_scores(query_heads, key_heads, relation, bias_set, scale_factor):
    current_block_bias, previous_block_bias, bias_far, mask_same = bias_set
    raw_scores = jnp.einsum(
        "qhd,khd->hqk", query_heads, key_heads, preferred_element_type=jnp.float32
    )
    bias_rows = jnp.where(
        relation == 0,
        current_block_bias,
        jnp.where(relation == 1, previous_block_bias, bias_far[:, None, None]),
    )
    allowed = jnp.logical_or(relation > 0, mask_same)
    return jnp.where(allowed[None], raw_scores * scale_factor + bias_rows, negative)


def pair_core(
    query_heads,
    dout_heads,
    log_total,
    row_delta,
    key_heads,
    value_heads,
    relation,
    bias_set,
    scale_factor,
):
    scores = pair_scores(query_heads, key_heads, relation, bias_set, scale_factor)
    weights_now = jnp.exp(scores - log_total[:, :, None])
    grad_weights = jnp.einsum(
        "qhd,khd->hqk", dout_heads, value_heads, preferred_element_type=jnp.float32
    )
    dscores = weights_now * (grad_weights - row_delta[:, :, None])
    return (weights_now, dscores, (dscores * scale_factor).astype(jnp.bfloat16))


def add_tables(relative_bias_tables, dscores, relation):
    same_sum, prev_sum, far_sum = relative_bias_tables
    return (
        same_sum + jnp.where(relation == 0, dscores, 0.0),
        prev_sum + jnp.where(relation == 1, dscores, 0.0),
        far_sum + jnp.where(relation >= 2, jnp.sum(dscores, axis=(1, 2)), 0.0),
    )


def forward_fold(query_heads, position, row_count, bias_set, scale_factor, running, pieces):
    keys_all, values_all = pieces

    def one_shard(folded, shard_step):
        key_heads = lax.dynamic_slice_in_dim(
            keys_all, shard_step * row_count, row_count, 0
        ).reshape(row_count, H, HD)
        value_heads = lax.dynamic_slice_in_dim(
            values_all, shard_step * row_count, row_count, 0
        ).reshape(row_count, H, HD)
        relation = position - shard_step

        def one_compute(current):
            running_max, running_sum, running_acc = current
            scores = pair_scores(query_heads, key_heads, relation, bias_set, scale_factor)
            new_max = jnp.maximum(running_max, jnp.max(scores, axis=-1))
            factor = jnp.exp(running_max - new_max)
            weights_now = jnp.exp(scores - new_max[:, :, None])
            new_sum = running_sum * factor + jnp.sum(weights_now, axis=-1)
            update = jnp.einsum(
                "hqk,khd->qhd",
                weights_now.astype(jnp.bfloat16),
                value_heads,
                preferred_element_type=jnp.float32,
            )
            scaled = running_acc.reshape(row_count, H, HD) * factor.T[:, :, None]
            return (new_max, new_sum, (scaled + update).reshape(row_count, H * HD))

        return (lax.cond(relation >= 0, one_compute, lambda unchanged: unchanged, folded), None)

    running, unused = lax.scan(one_shard, running, jnp.arange(keys_all.shape[0] // row_count))
    return running


def nt_dot(left, right):
    return lax.dot_general(left, right, (((1,), (1,)), ((), ())), preferred_element_type=F32)


def nn_dot(left, right):
    return jnp.dot(left, right, preferred_element_type=F32)


def meet(neighbours):
    barrier = pltpu.get_barrier_semaphore()
    for who in neighbours:
        pl.semaphore_signal(barrier, inc=1, device_id=who, device_id_type=MESH)
    pl.semaphore_wait(barrier, len(neighbours))


def ctx_peers(n):
    me = lax.axis_index("ctx")
    return [{"ctx": lax.rem(me + d, n)} for d in range(1, n)]


def other_wa(me, bit):
    flipped = lax.rem(me // bit, 2)
    return me + bit - 2 * bit * flipped


def remote(src, dst, send_sem, recv_sem, **device):
    return pltpu.make_async_remote_copy(
        src_ref=src,
        dst_ref=dst,
        send_sem=send_sem,
        recv_sem=recv_sem,
        device_id=device,
        device_id_type=MESH,
    )


RING = 8
HOPS = RING - 1


def ring_place(n):
    me = lax.axis_index("ctx")
    half = n // 2

    def at(place):
        return jnp.where(place < half, 2 * place, 2 * (n - 1 - place) + 1)

    place = jnp.where(lax.rem(me, 2) == 0, me // 2, n - 1 - me // 2)
    return place, at(lax.rem(place + 1, n)), at(lax.rem(place + n - 1, n))


class Ring:
    def __init__(self, lanes, send, recv, share=None, hold=None, full=None):
        self.lanes, self.share, self.hold, self.full = lanes, share, hold, full
        self.sems = send, recv
        self.place, self.after, self.before = ring_place(RING)

    def copy(self, lane, src, dst, step):
        send, recv = self.sems
        way = self.lanes[lane][1]
        return remote(
            src, dst, send.at[lane, step], recv.at[lane, step], ctx=self.after if way == 1 else self.before
        )

    def chunk(self, lane, offset):
        here = self.place if self.lanes[lane][1] == 1 else RING - self.place
        return lax.rem(here + offset + 2 * RING, RING)

    def scatter(self, step, which):
        for lane in which:
            b, _, rows = self.lanes[lane]
            share = self.share.at[b, self.chunk(lane, -step), rows]

            @pl.when(step > 0)
            def _():
                there = self.hold.at[b, jnp.maximum(step - 1, 0), rows]
                self.copy(lane, share, there, jnp.maximum(step - 1, 0)).wait_recv()
                share[...] = (share[...].astype(F32) + there[...].astype(F32)).astype(BF)

            @pl.when(step < HOPS)
            def _():
                there = jnp.minimum(step, HOPS - 1)
                self.copy(lane, share, self.hold.at[b, there, rows], there).start()

    def gather(self, step, which):
        for lane in which:
            b, _, rows = self.lanes[lane]
            full = self.full[b].at[self.chunk(lane, 1 - step), rows]

            @pl.when(step > 0)
            def _():
                self.copy(lane, full, full, jnp.maximum(step - 1, 0)).wait_recv()

            @pl.when(step < HOPS)
            def _():
                self.copy(lane, full, full, jnp.minimum(step, HOPS - 1)).start()

    def finish(self, part):
        def one(step, unused):
            for lane in range(len(self.lanes)):
                self.copy(lane, part(lane), part(lane), step).wait_send()
            return unused

        lax.fori_loop(0, HOPS, one, 0)


TALL, FLAT = (224, 1024), (256, 896)
EARLY = ("ck", "cv", "cq", "co", "so")
MADE = ("cq", "co", "so")
LATE = ("q", "k", "v")
FEED = (8, 112, 896)
FEED_LANES = (
    (0, 1, slice(0, 64)),
    (1, -1, slice(0, 64)),
    (0, 1, slice(64, 112)),
    (1, -1, slice(64, 112)),
)
FEED_TURNS = ((0, 1), (2, 3))


def product_into(out_ref, left, right):
    for c in range(left.shape[1] // WIDE):
        lanes = slice(c * WIDE, (c + 1) * WIDE)
        turned = left[:, lanes].astype(F32).T.astype(BF)
        out_ref[lanes, :] = nn_dot(turned, right[...]).astype(BF)


class Folding:
    def __init__(self, names, parts, scratch):
        self.names = names
        self.parts = parts
        tall, flat, sems = scratch
        self.sets = {TALL: tall, FLAT: flat}
        self.own_sem, self.core_send, self.core_recv, self.x_send, self.x_recv = sems
        self.wa = lax.axis_index("wa")
        self.mate, self.across = other_wa(self.wa, 1), other_wa(self.wa, 2)
        self.core, self.half = lax.rem(self.wa, 2), self.wa // 2
        self.slots, count = {}, {TALL: 0, FLAT: 0}
        for name in names:
            shape = self.shape_of(name)
            self.slots[name] = (count[shape], self.sets[shape])
            count[shape] += 1
        self.own_copies, self.core_copies, self.x_copies = {}, {}, {}

    @staticmethod
    def shape_of(name):
        return FLAT if name in ("co", "so") else TALL

    @classmethod
    def scratch(cls, names):
        shapes = []
        for shape in (TALL, FLAT):
            many = sum(cls.shape_of(name) == shape for name in names)
            if many:
                shapes += [pltpu.VMEM((many, 2, *shape), BF)] * 2 + [pltpu.VMEM((many, *shape), BF)] * 2
        dma = pltpu.SemaphoreType.DMA
        many = len(names)
        return shapes + [dma((many, 2))] * 3 + [dma((many,))] * 2

    def start(self, *names):
        for name in names:
            u = self.names.index(name)
            slot, (own, inn, _, _) = self.slots[name]
            rows = self.shape_of(name)[0]
            for x in range(2):
                mine = pl.ds(pl.multiple_of((2 * x + self.core) * rows, 16), rows)
                theirs = pl.ds(pl.multiple_of((2 * x + 1 - self.core) * rows, 16), rows)
                copy = remote(
                    self.parts[name].at[theirs],
                    inn.at[slot, x],
                    self.core_send.at[u, x],
                    self.core_recv.at[u, x],
                    wa=self.mate,
                )
                copy.start()
                self.core_copies[name, x] = copy
                copy = pltpu.make_async_copy(
                    self.parts[name].at[mine], own.at[slot, x], self.own_sem.at[u, x]
                )
                copy.start()
                self.own_copies[name, x] = copy
            slot, (_, _, out, land) = self.slots[name]
            self.x_copies[name] = remote(
                out.at[slot], land.at[slot], self.x_send.at[u], self.x_recv.at[u], wa=self.across
            )

    def send(self, name):
        self.prepare(name)
        self.x_copies[name].start()

    def prepare(self, name):
        slot, (own, inn, out, _) = self.slots[name]
        for x in range(2):
            self.own_copies[name, x].wait()
            self.core_copies[name, x].wait_recv()
        away = 1 - self.half
        out[slot] = (own[slot, away].astype(F32) + inn[slot, away].astype(F32)).astype(BF)

    def total(self, name):
        slot, (own, inn, _, land) = self.slots[name]
        self.x_copies[name].wait_recv()
        here = self.half
        return (
            own[slot, here].astype(F32) + inn[slot, here].astype(F32) + land[slot].astype(F32)
        ).astype(BF)

    def finish(self):
        for name in self.names:
            for x in range(2):
                self.core_copies[name, x].wait_send()
            self.x_copies[name].wait_send()


class Moves:
    def __init__(self, sem):
        self.sem, self.count = sem, 0

    def start(self, src, dst):
        copy = pltpu.make_async_copy(src, dst, self.sem.at[self.count])
        copy.start()
        self.count += 1
        return copy


def wait_all(copies):
    for copy in copies:
        copy.wait()


def lasting(microseconds):
    return pl.CostEstimate(
        flops=0, bytes_accessed=int(microseconds * 3.0e6), transcendentals=0
    )


def lanes_of(index):
    return pl.ds(pl.multiple_of(index * WIDE, WIDE), WIDE)


def rows_of(index, rows):
    return pl.ds(pl.multiple_of(index * rows, rows), rows)


def to_ctx(src, dst, send_sem, recv_sem, target):
    return pltpu.make_async_remote_copy(
        src_ref=src,
        dst_ref=dst,
        send_sem=send_sem,
        recv_sem=recv_sem,
        device_id={"ctx": target},
        device_id_type=MESH,
    )


def head_mask(h, rows):
    lane = lax.broadcasted_iota(jnp.int32, (rows, WIDE), 1)
    return (lane < HD) if h == 0 else (lane >= HD)


def bias_tiles(bias_ref, me, tiles):
    for h in range(2):
        line = bias_ref[pl.ds(2 * me + h, 1), :]
        rolled = pltpu.roll(
            jnp.broadcast_to(line, (BLOCK, LINE)), 0, 1, stride=1, stride_axis=0
        )
        tiles[h, 0] = rolled[:, :BLOCK]
        tiles[h, 1] = rolled[:, BLOCK : 2 * BLOCK]
        tiles[h, 2] = jnp.broadcast_to(line[:, WIDE : WIDE + BLOCK], (BLOCK, BLOCK))


def spread(n, me, pairs, send, recv, t):
    src, dst = pairs[t]
    for d in range(1, n):
        peer = lax.rem(me + d, n)
        to_ctx(
            src.at[:, lanes_of(peer)], dst.at[rows_of(me, BLOCK)], send.at[t, d], recv.at[t, d], peer
        ).start()
    dst[rows_of(me, BLOCK), :] = src[:, lanes_of(me)]


GATHERED = ("q", "k", "v", "so", "ck", "cv", "cq", "co")
SINGLE = ("cot",)
GAINS = ("selfnorm", "crossnorm", "feednorm", "outbias")


class Gathering:
    def __init__(self, shards, whole, own_sem, send, recv):
        self.names, self.shards, self.whole = tuple(shards), shards, whole
        self.sems = own_sem, send, recv
        self.wa, me = lax.axis_index("wa"), lax.axis_index("ctx")
        self.mate, self.across = other_wa(self.wa, 1), other_wa(self.wa, 2)
        y, z = lax.rem(me, 2), lax.rem(me // 2, 2)
        self.pairs = ((y, me + 1 - 2 * y), (z, me + 2 - 4 * z))
        self.copies = {}

    def start(self):
        own_sem, send, recv = self.sems
        for u, name in enumerate(self.names):
            part, beside = self.pairs[(u + 1) % 2]
            shard, whole = self.shards[name], self.whole[name]
            rows = shard.shape[0]
            parts = 1 if name in SINGLE else 2
            some = rows // parts
            shift = 0 if parts == 1 else part * some

            def at(start, count, ref=whole):
                return ref.at[pl.ds(pl.multiple_of(start, 16), count)]

            mine = at(self.wa * rows, rows)
            theirs = at(self.across * rows, rows)
            theirs_some = at(self.across * rows + shift, some)
            self.copies[name] = {
                "over": remote(
                    at(shift, some, shard), at(self.wa * rows + shift, some), send.at[u, 0], recv.at[u, 0], wa=self.across
                ),
                "near": remote(shard, mine, send.at[u, 1], recv.at[u, 1], wa=self.mate),
                "pass": remote(theirs, theirs, send.at[u, 2], recv.at[u, 2], wa=self.mate),
                "side": remote(theirs_some, theirs_some, send.at[u, 3], recv.at[u, 3], ctx=beside),
                "own": pltpu.make_async_copy(shard, mine, own_sem.at[u]),
            }
            self.copies[name]["near"].start()
            self.copies[name]["own"].start()

    def cross(self, *names):
        for name in names:
            self.copies[name]["over"].start()

    def forward(self, *names):
        for name in names:
            self.copies[name]["over"].wait_recv()
            self.copies[name]["pass" if name in SINGLE else "side"].start()

    def land(self, *names):
        for name in names:
            self.copies[name]["side"].wait_recv()
            self.copies[name]["pass"].start()

    def arrive(self, *names):
        for name in names:
            self.copies[name]["near"].wait_recv()
            self.copies[name]["pass"].wait_recv()
            self.copies[name]["own"].wait()

    def finish(self):
        for name, copies in self.copies.items():
            for which in ("over", "near", "pass") + (() if name in SINGLE else ("side",)):
                copies[which].wait_send()


class Columns:
    def __init__(self, gathering, shard, whole, send, recv):
        wa, mate, across = gathering.wa, gathering.mate, gathering.across
        both = other_wa(across, 1)
        rows, width = shard.shape[0], whole.shape[1]
        some = rows // 2

        def block(owner, columns):
            return shard.at[owner, pl.ds(pl.multiple_of(columns * width, WIDE), width)]

        def at(start, count):
            return whole.at[pl.ds(pl.multiple_of(start, 16), count)]

        everything = slice(0, rows)
        self.own = pltpu.make_async_copy(block(everything, wa), at(wa * rows, rows), send.at[5])
        self.near = remote(block(everything, mate), at(wa * rows, rows), send.at[0], recv.at[0], wa=mate)
        self.over, self.side = [], []
        for d, peer in enumerate((across, both)):
            part, beside = gathering.pairs[d]
            mine = pl.ds(pl.multiple_of(part * some, 16), some)
            gone, got = at(wa * rows + part * some, some), at(peer * rows + part * some, some)
            self.over.append(remote(block(mine, peer), gone, send.at[1 + d], recv.at[1 + d], wa=peer))
            self.side.append(remote(got, got, send.at[3 + d], recv.at[3 + d], ctx=beside))

    def start(self):
        self.own.start()
        self.near.start()

    def cross(self):
        for copy in self.over:
            copy.start()

    def forward(self):
        for over, side in zip(self.over, self.side, strict=True):
            over.wait_recv()
            side.start()

    def finish(self):
        self.own.wait()
        self.near.wait()
        for over, side in zip(self.over, self.side, strict=True):
            side.wait()
            over.wait_send()


def attn_forward_kernel(n, tokens_ref, small_ref, near_far, *refs):
    shards = dict(zip((*GATHERED, "cot"), refs[:9], strict=True))
    feed_ref = refs[9]
    wholes = dict(zip((*GATHERED, "cot"), refs[10:19], strict=True))
    feed_whole = refs[19]
    o_ref, low_ref, ot_out, lse_out, small_out, before_ref, qh_out, kh_out, vh_out, keys_out, values_out = refs[20:31]
    (
        held_q, held_k, held_v, held_ck, held_cv, proj, small_in, small_mid, qh, kh, vh, vt, oh, land, tiles,
        acc, stat, send, recv, osend, orecv, small_sem, own_sem, out_sem, gather_send, gather_recv, feed_send,
        feed_recv, span_sem, near_ref, keys_ref, values_ref, move_sem,
    ) = refs[31:]
    moves = Moves(move_sem)
    load_near = moves.start(near_far, near_ref)
    held = {"q": held_q, "k": held_k, "v": held_v, "ck": held_ck, "cv": held_cv}
    gathering = Gathering(shards, wholes | held, own_sem, gather_send, gather_recv)
    columns = Columns(gathering, feed_ref, feed_whole, feed_send, feed_recv)
    both = other_wa(gathering.across, 1)
    meet([*ctx_peers(n), *({"wa": peer} for peer in (gathering.mate, gathering.across, both))])
    me = lax.axis_index("ctx")
    near = remote(small_ref, small_in.at[0], small_sem.at[0], small_sem.at[1], wa=gathering.mate)
    near.start()
    gathering.start()
    gathering.cross("q")
    columns.start()
    span_rows = before_ref.shape[0]
    span = remote(
        near_far.at[near_far.shape[0] - span_rows :],
        before_ref,
        span_sem.at[0],
        span_sem.at[1],
        ctx=lax.rem(me + 1, n),
    )
    over = remote(small_mid, small_in.at[1], small_sem.at[2], small_sem.at[3], wa=gathering.across)
    near.wait_recv()
    small_mid[...] = (small_ref[...].astype(F32) + small_in[0].astype(F32)).astype(BF)
    over.start()
    over.wait_recv()
    small_out[...] = small_mid[...].astype(F32) + small_in[1].astype(F32)
    bias_ref = small_out
    values = tokens_ref[...].astype(F32)
    width = values.shape[1]
    norm = lax.rsqrt(jnp.mean(values * values, axis=1, keepdims=True) + epsilon)
    low_ref[...] = (values * norm * small_out[H : H + 1, :width]).astype(BF)
    bias_tiles(bias_ref, me, tiles)
    pairs = tuple((proj.at[t], dst) for t, dst in enumerate((qh, kh, vh)))
    saving = []

    def save(name):
        copy = pltpu.make_async_copy(held[name], wholes[name], out_sem.at[len(saving)])
        copy.start()
        saving.append(copy)

    def project(t, name):
        gathering.land(name)
        gathering.arrive(name)
        proj[t] = nn_dot(low_ref[...], held[name][...]).astype(BF)
        spread(n, me, pairs, send, recv, t)
        save(name)

    gathering.forward("q")
    gathering.cross("k")
    gathering.forward("k")
    gathering.cross("v")
    project(0, "q")
    gathering.forward("v")
    gathering.cross("so", "ck")
    project(1, "k")
    project(2, "v")

    gathering.forward("so", "ck")
    gathering.cross("cv", "cq")

    for d in range(1, n):
        peer = lax.rem(me + n - d, n)
        for t, (src, dst) in enumerate(pairs):
            to_ctx(
                src.at[:, lanes_of(peer)], dst.at[rows_of(peer, BLOCK)], send.at[t, d], recv.at[t, d], peer
            ).wait_recv()
    stores = [moves.start(*pair) for pair in ((qh, qh_out), (kh, kh_out), (vh, vh_out))]
    for i in range(n):
        part = slice(i * BLOCK, (i + 1) * BLOCK)
        vt[:, part] = vh[part, :].astype(F32).T.astype(BF)

    def query_block(step, unused):
        @pl.when((step == 0) & (me < n - 1))
        def _():
            span.start()

        @pl.when(step == 1)
        def _():
            gathering.forward("cv", "cq")
            gathering.land("so", "ck")
            gathering.cross("co")
            columns.cross()

        @pl.when(step == 6)
        def _():
            gathering.land("cv", "cq")
            gathering.forward("co")
            columns.forward()
            gathering.cross("cot")

        i = lax.rem(me + 1 + step, n)
        rows = rows_of(i, BLOCK)
        q_now = qh[rows, :] * BF(HD**-0.5)
        masked = [jnp.where(head_mask(h, BLOCK), q_now, BF(0)) for h in range(2)]

        def fold(j, which, first):
            keys = kh[rows_of(j, BLOCK), :]
            for h in range(2):
                scores = nt_dot(keys, masked[h])
                if which is None:
                    scores = scores + bias_ref[pl.ds(2 * me + h, 1), WIDE : WIDE + BLOCK]
                else:
                    scores = scores + tiles[h, which]
                top = jnp.max(scores, axis=0, keepdims=True)
                if not first:
                    old = stat[h : h + 1, :]
                    top = jnp.maximum(old, top)
                weights = jnp.exp(scores - top)
                total = jnp.sum(weights, axis=0, keepdims=True)
                vals = vt[h * HD : (h + 1) * HD, rows_of(j, BLOCK)]
                mixed = nn_dot(vals, weights.astype(BF))
                if not first:
                    factor = jnp.exp(old - top)
                    total = total + stat[2 + h : 3 + h, :] * factor
                    mixed = mixed + acc[h * HD : (h + 1) * HD, :] * factor
                stat[h : h + 1, :] = top
                stat[2 + h : 3 + h, :] = total
                acc[h * HD : (h + 1) * HD, :] = mixed

        fold(i, 0, True)

        @pl.when(i >= 1)
        def _():
            fold(i - 1, 1, False)

        def far(j, unused):
            fold(j, None, False)
            return unused

        lax.fori_loop(0, i - 1, far, 0)
        for h in range(2):
            total = stat[2 + h : 3 + h, :]
            part = acc[h * HD : (h + 1) * HD, :] / total
            acc[h * HD : (h + 1) * HD, :] = part
            lse_out[h : h + 1, rows] = stat[h : h + 1, :] + jnp.log(total)
        done = acc[...]
        ot_out[:, rows] = done
        oh[rows, :] = done.T.astype(BF)

        @pl.when(i != me)
        def _():
            d = lax.rem(i - me + n, n)
            to_ctx(oh.at[rows], land.at[:, lanes_of(me)], osend.at[d], orecv.at[d], i).start()

        @pl.when(i == me)
        def _():
            land[:, lanes_of(me)] = oh[rows, :]

        return unused

    lax.fori_loop(0, n, query_block, 0)
    load_near.wait()

    @pl.when(me > 0)
    def _():
        span.wait_recv()

    @pl.when(me == 0)
    def _():
        before_ref[...] = jnp.zeros_like(before_ref)

    for name, out_ref, far_ref in (("ck", keys_ref, keys_out), ("cv", values_ref, values_out)):
        gathering.arrive(name)
        save(name)
        out_ref[:span_rows, :] = nn_dot(before_ref[...], held[name][...]).astype(BF)
        for g in range(near_ref.shape[0] // span_rows):
            rows = slice(g * span_rows, (g + 1) * span_rows)
            there = slice((g + 1) * span_rows, (g + 2) * span_rows)
            out_ref[there, :] = nn_dot(near_ref[rows, :], held[name][...]).astype(BF)
        stores.append(moves.start(out_ref, far_ref))
    gathering.land("co")
    gathering.forward("cot")
    for d in range(1, n):
        peer = lax.rem(me + d, n)
        for t, (src, dst) in enumerate(pairs):
            to_ctx(
                src.at[:, lanes_of(peer)], dst.at[rows_of(me, BLOCK)], send.at[t, d], recv.at[t, d], peer
            ).wait_send()
        back = to_ctx(
            oh.at[rows_of(peer, BLOCK)], land.at[:, lanes_of(me)], osend.at[d], orecv.at[d], peer
        )
        back.wait_send()
        back.wait_recv()
    o_ref[...] = land[...]
    gathering.arrive("so", "cq", "co", "cot")
    gathering.finish()
    columns.finish()

    @pl.when(me < n - 1)
    def _():
        span.wait_send()

    near.wait_send()
    over.wait_send()
    wait_all(saving + stores)


def vmem(count):
    return [pl.BlockSpec(memory_space=pltpu.VMEM)] * count


def attn_forward(n, tokens, small, near, shards, feed):
    rows, seq = tokens.shape[0], n * tokens.shape[0]
    owners = lax.axis_size("wa")
    low = functools.partial(jax.ShapeDtypeStruct, dtype=BF)
    heads = low((seq, WIDE))
    wholes = [low((owners * s.shape[0], s.shape[1])) for s in shards]
    width = wholes[0].shape[1]
    dma = pltpu.SemaphoreType.DMA
    span_rows = 256
    keys = low((span_rows + near.shape[0], width))
    any_spec = pl.BlockSpec(memory_space=pl.ANY)
    return pl.pallas_call(
        functools.partial(attn_forward_kernel, n),
        out_shape=(
            *wholes,
            low((owners * feed.shape[0], feed.shape[1] // owners)),
            low((rows, width)),
            low(tokens.shape),
            jax.ShapeDtypeStruct((WIDE, seq), F32),
            jax.ShapeDtypeStruct((8, seq), F32),
            jax.ShapeDtypeStruct(small.shape, F32),
            low((span_rows, near.shape[1])),
            heads,
            heads,
            heads,
            keys,
            keys,
        ),
        in_specs=vmem(2) + [any_spec] * 11,
        out_specs=tuple([any_spec] * 10 + vmem(6) + [any_spec] * 5),
        scratch_shapes=[
            *[pltpu.VMEM(wholes[0].shape, BF)] * 5,
            pltpu.VMEM((3, rows, width), BF),
            pltpu.VMEM((2, *small.shape), BF),
            pltpu.VMEM(small.shape, BF),
            pltpu.VMEM((seq, WIDE), BF),
            pltpu.VMEM((seq, WIDE), BF),
            pltpu.VMEM((seq, WIDE), BF),
            pltpu.VMEM((WIDE, seq), BF),
            pltpu.VMEM((seq, WIDE), BF),
            pltpu.VMEM((rows, width), BF),
            pltpu.VMEM((2, 3, BLOCK, BLOCK), F32),
            pltpu.VMEM((WIDE, BLOCK), F32),
            pltpu.VMEM((8, BLOCK), F32),
            dma((3, n)),
            dma((3, n)),
            dma((n,)),
            dma((n,)),
            dma((4,)),
            dma((9,)),
            dma((5,)),
            dma((9, 4)),
            dma((9, 4)),
            dma((6,)),
            dma((5,)),
            dma((2,)),
            pltpu.VMEM(near.shape, BF),
            pltpu.VMEM(keys.shape, BF),
            pltpu.VMEM(keys.shape, BF),
            dma((6,)),
        ],
        compiler_params=pltpu.CompilerParams(
            collective_id=1, has_side_effects=True, vmem_limit_bytes=60 << 20
        ),
        cost_estimate=lasting(85),
        name="attn_forward",
    )(tokens, small, near, *shards, feed)


def attn_backward_kernel(n, do_ref, lse_ref, bias_ref, feed_part, *rest):
    far = rest[:10]
    span_far = rest[12]
    line_ref, *outs = rest[13:23]
    rest = rest[2:]
    near = rest[21:31]
    kh, qh, ot_ref, vh = near[:4]
    given = dict(zip(MADE, zip(near[4::2], near[5::2], strict=True), strict=True))
    tall_pair, tall_one, flat_out, *feed_full, move_sem = rest[31:37]
    (
        doh, kt, stage, land, dk_acc, dv_acc, dq_acc, q_masked, do_masked, delta, tiles, dtiles,
        send, recv, gsend, grecv, ring_send, ring_recv,
    ) = rest[37:55]
    made = dict(zip(MADE, rest[55:58], strict=True))
    parts = dict(zip(EARLY, (rest[8], rest[9], *made.values()), strict=True))
    span_ref, span_sem = rest[58:60]
    extra = rest[60:]
    moves = Moves(move_sem)
    loads = [moves.start(*pair) for pair in zip(far, near, strict=True)]
    fold_wa = Folding(EARLY, parts, (extra[0:4], extra[4:8], extra[8:13]))
    ring = Ring(FEED_LANES, ring_send, ring_recv, full=feed_full)
    for lane in range(2):
        feed_full[lane][ring.chunk(lane, 1)] = feed_part[lane]
    meet([*ctx_peers(n), {"wa": fold_wa.mate}, {"wa": fold_wa.across}])
    me = lax.axis_index("ctx")
    pairs = ((do_ref, doh),)
    spread(n, me, pairs, send, recv, 0)
    fold_wa.start("ck", "cv")
    bias_tiles(bias_ref, me, tiles)
    loads[0].wait()
    for j in range(n):
        part = slice(j * BLOCK, (j + 1) * BLOCK)
        kt[:, part] = (kh[part, :].astype(F32) * HD**-0.5).T.astype(BF)
    dtiles[...] = jnp.zeros_like(dtiles)
    for name in EARLY[:2]:
        fold_wa.send(name)
    ring.gather(jnp.int32(0), FEED_TURNS[0])
    ring.gather(jnp.int32(0), FEED_TURNS[1])
    wait_all(loads[1:])
    for name in MADE:
        product_into(made[name], *given[name])
        fold_wa.start(name)
    dq_acc[...] = jnp.zeros_like(dq_acc)
    for d in range(1, n):
        peer = lax.rem(me + n - d, n)
        to_ctx(
            do_ref.at[:, lanes_of(peer)], doh.at[rows_of(peer, BLOCK)], send.at[0, d], recv.at[0, d], peer
        ).wait_recv()
    for i in range(n):
        rows = slice(i * BLOCK, (i + 1) * BLOCK)
        q_now = qh[rows, :] * BF(HD**-0.5)
        do_now = doh[rows, :]
        products = do_now.astype(F32).T * ot_ref[:, rows]
        for h in range(2):
            mask = head_mask(h, BLOCK)
            q_masked[h, rows, :] = jnp.where(mask, q_now, BF(0))
            do_masked[h, rows, :] = jnp.where(mask, do_now, BF(0))
            delta[h : h + 1, rows] = jnp.sum(
                products[h * HD : (h + 1) * HD], axis=0, keepdims=True
            )

    span = remote(
        span_far, span_ref, span_sem.at[0], span_sem.at[1], ctx=lax.rem(me + n - 1, n)
    )

    def pair(t, now):
        i, j = now

        @pl.when((t == 24) & (me > 0))
        def _():
            span.start()

        rows, there = rows_of(i, BLOCK), rows_of(j, BLOCK)

        @pl.when(t == 6)
        def _():
            for name in EARLY[2:]:
                fold_wa.send(name)

        for turn, lanes in enumerate(FEED_TURNS):

            @pl.when((lax.rem(t, 4) == 2 * turn + 1) & (t <= 4 * HOPS))
            def _():
                ring.gather(t // 4 + 1, lanes)

        first = i == j
        which = jnp.minimum(i - j, 2)
        keys, vals = kh[there, :], vh[there, :]
        dk_part, dv_part = None, None
        for h in range(2):
            query, dout = q_masked[h, rows, :], do_masked[h, rows, :]
            scores = nt_dot(keys, query)
            weights = jnp.exp(scores + tiles[h, which] - lse_ref[h : h + 1, rows])
            dweights = nt_dot(vals, dout)
            dscores = weights * (dweights - delta[h : h + 1, rows])
            dtiles[h, which] += dscores
            low = dscores.astype(BF)
            dv_now = nn_dot(weights.astype(BF), dout)
            dk_now = nn_dot(low, query)
            dv_part = dv_now if dv_part is None else dv_part + dv_now
            dk_part = dk_now if dk_part is None else dk_part + dk_now
            half = slice(h * HD, (h + 1) * HD)
            dq_acc[half, rows] += nn_dot(kt[half, there], low)

        @pl.when(first)
        def _():
            dk_acc[...] = dk_part
            dv_acc[...] = dv_part

        @pl.when(jnp.logical_not(first))
        def _():
            dk_acc[...] += dk_part
            dv_acc[...] += dv_part

        last = i == n - 1

        @pl.when(last)
        def _():
            stage[1, there, :] = dk_acc[...].astype(BF)
            stage[2, there, :] = dv_acc[...].astype(BF)
            deliver(j, (1, 2))

        after = lax.rem(j + 1, n)
        return jnp.where(last, after, i + 1), jnp.where(last, after, j)

    def deliver(i, arrays):
        rows = rows_of(i, BLOCK)

        @pl.when(i != me)
        def _():
            d = lax.rem(i - me + n, n)
            for t in arrays:
                to_ctx(
                    stage.at[t, rows], land.at[t, :, lanes_of(me)], gsend.at[t, d], grecv.at[t, d], i
                ).start()

        @pl.when(i == me)
        def _():
            for t in arrays:
                land[t, :, lanes_of(me)] = stage[t, rows, :]

    begin = lax.rem(me + 1, n)
    lax.fori_loop(0, n * (n + 1) // 2, pair, (begin, begin))

    def dq_block(step, unused):
        i = lax.rem(me + 1 + step, n)
        rows = rows_of(i, BLOCK)
        stage[0, rows, :] = dq_acc[:, rows].T.astype(BF)
        deliver(i, (0,))
        return unused

    lax.fori_loop(0, n, dq_block, 0)
    ring.finish(lambda lane: feed_full[FEED_LANES[lane][0]].at[0, FEED_LANES[lane][2]])
    stores = [moves.start(full, out) for full, out in zip(feed_full, outs[6:8], strict=True)]
    tall_pair[:224, :] = fold_wa.total("cq")
    tall_pair[224:, :] = fold_wa.total("ck")
    tall_one[...] = fold_wa.total("cv")
    for at, name in ((0, "co"), (32, "so")):
        flat_out[:, at : at + 32, :] = fold_wa.total(name).reshape(8, 32, 896)
    stores += [
        moves.start(tall_pair, outs[3]),
        moves.start(tall_one, outs[4]),
        moves.start(flat_out, outs[5]),
    ]
    fold_wa.finish()
    for h in range(2):
        line = jnp.concatenate(
            [dtiles[h, 0], dtiles[h, 1], jnp.zeros((BLOCK, LINE - 2 * BLOCK), F32)], axis=1
        )
        row = lax.broadcasted_iota(jnp.int32, (BLOCK, LINE), 0)
        for bit in range(8):
            moved = pltpu.roll(line, LINE - (1 << bit), 1)
            line = jnp.where((row >> bit) & 1 == 1, moved, line)
        line_ref[h : h + 1, :] = jnp.sum(line, axis=0, keepdims=True)
        line_ref[2 + h : 3 + h, :BLOCK] = jnp.sum(dtiles[h, 2], axis=0, keepdims=True)
    line_ref[2:4, BLOCK:] = jnp.zeros((2, LINE - BLOCK), F32)
    line_ref[4:8, :] = jnp.zeros((4, LINE), F32)
    for d in range(1, n):
        peer = lax.rem(me + d, n)
        to_ctx(
            do_ref.at[:, lanes_of(peer)], doh.at[rows_of(me, BLOCK)], send.at[0, d], recv.at[0, d], peer
        ).wait_send()
        for t in range(3):
            back = to_ctx(
                stage.at[t, rows_of(peer, BLOCK)], land.at[t, :, lanes_of(me)], gsend.at[t, d], grecv.at[t, d], peer
            )
            back.wait_send()
            back.wait_recv()
    stores += [moves.start(land.at[t], outs[t]) for t in range(3)]

    @pl.when(me < n - 1)
    def _():
        span.wait_recv()

    @pl.when(me == n - 1)
    def _():
        span_ref[...] = jnp.zeros_like(span_ref)

    stores.append(moves.start(span_ref, outs[8]))

    @pl.when(me > 0)
    def _():
        span.wait_send()

    wait_all(stores)


def attn_backward(n, dout, qh, kh, vh, ot, lse, bias_lines, parts, feed_part, span):
    rows, seq = dout.shape[0], n * dout.shape[0]
    grads = jax.ShapeDtypeStruct(dout.shape, BF)
    feed = jax.ShapeDtypeStruct(FEED, BF)
    low = functools.partial(jax.ShapeDtypeStruct, dtype=BF)
    any_spec = pl.BlockSpec(memory_space=pl.ANY)
    far = (kh, qh, ot, vh, *parts[2:])
    shares = (low((448, 1024)), low((224, 1024)), low((8, 64, 896)))
    line, *outs = pl.pallas_call(
        functools.partial(attn_backward_kernel, n),
        out_shape=(
            jax.ShapeDtypeStruct((8, LINE), F32),
            grads,
            grads,
            grads,
            *shares,
            feed,
            feed,
            low(span.shape),
        ),
        in_specs=vmem(4) + [any_spec] * 13,
        out_specs=tuple(vmem(1) + [any_spec] * 9),
        scratch_shapes=[
            *(pltpu.VMEM(v.shape, v.dtype) for v in far),
            *(pltpu.VMEM(v.shape, v.dtype) for v in (*shares, feed, feed)),
            pltpu.SemaphoreType.DMA((19,)),
            pltpu.VMEM((seq, WIDE), BF),
            pltpu.VMEM((WIDE, seq), BF),
            pltpu.VMEM((3, seq, WIDE), BF),
            pltpu.VMEM((3, *dout.shape), BF),
            pltpu.VMEM((BLOCK, WIDE), F32),
            pltpu.VMEM((BLOCK, WIDE), F32),
            pltpu.VMEM((WIDE, seq), F32),
            pltpu.VMEM((2, seq, WIDE), BF),
            pltpu.VMEM((2, seq, WIDE), BF),
            pltpu.VMEM((8, seq), F32),
            pltpu.VMEM((2, 3, BLOCK, BLOCK), F32),
            pltpu.VMEM((2, 3, BLOCK, BLOCK), F32),
            pltpu.SemaphoreType.DMA((1, n)),
            pltpu.SemaphoreType.DMA((1, n)),
            pltpu.SemaphoreType.DMA((3, n)),
            pltpu.SemaphoreType.DMA((3, n)),
            pltpu.SemaphoreType.DMA((len(FEED_LANES), HOPS)),
            pltpu.SemaphoreType.DMA((len(FEED_LANES), HOPS)),
            pltpu.VMEM((896, 1024), BF),
            pltpu.VMEM((1024, 896), BF),
            pltpu.VMEM((1024, 896), BF),
            pltpu.VMEM(span.shape, BF),
            pltpu.SemaphoreType.DMA((2,)),
            *Folding.scratch(EARLY),
        ],
        compiler_params=pltpu.CompilerParams(
            collective_id=2, has_side_effects=True, vmem_limit_bytes=60 << 20
        ),
        cost_estimate=lasting(100),
        name="attn_backward",
    )(dout, lse, bias_lines, feed_part, *far, *parts[:2], span)
    return *outs[:3], line, *outs[3:]


BUFFERS = {
    "cq": (1, (224, 1024)),
    "cv": (-1, (224, 1024)),
    "ck": (1, (224, 1024)),
    "co": (-1, (8, 32, 896)),
    "so0": (1, (8, 16, 896)),
    "so1": (-1, (8, 16, 896)),
}
NAMES = tuple(BUFFERS)


def chunk_shape(name):
    shape = BUFFERS[name][1]
    return (shape[0], WIDE) if len(shape) == 2 else shape[1:]


def chunk_of(ref, name, c):
    return ref.at[:, lanes_of(c)] if len(BUFFERS[name][1]) == 2 else ref.at[c]


class Grid:
    def __init__(self, u, share, half_in, half, quarters, whole, send, recv):
        self.u, self.share, self.half_in, self.half = u, share, half_in, half
        self.quarters, self.whole, self.sems = quarters, whole, (send, recv)
        me = lax.axis_index("ctx")
        self.y, self.z = lax.rem(me, 2), me // 2
        self.beside = me + 1 - 2 * self.y
        self.column = [lax.rem(self.z + d, 4) for d in range(1, 4)]

    def half_of(self, y):
        return pl.ds(pl.multiple_of(y * 4 * WIDE, WIDE), 4 * WIDE)

    def piece_of(self, z, y=None):
        start = z * WIDE if y is None else (4 * y + z) * WIDE
        return pl.ds(pl.multiple_of(start, WIDE), WIDE)

    def copy(self, number, src, dst, target):
        send, recv = self.sems
        return remote(src, dst, send.at[self.u, number], recv.at[self.u, number], ctx=target)

    def start(self, total):
        self.share[...] = total
        self.first = self.copy(
            0, self.share.at[:, self.half_of(1 - self.y)], self.half_in, self.beside
        )
        self.first.start()

    def spread(self):
        self.first.wait_recv()
        mine = self.share[:, self.half_of(self.y)]
        self.half[...] = (mine.astype(F32) + self.half_in[...].astype(F32)).astype(BF)
        self.out = []
        for d, z in enumerate(self.column):
            copy = self.copy(
                1 + d, self.half.at[:, self.piece_of(z)], self.quarters.at[self.z], 2 * z + self.y
            )
            copy.start()
            self.out.append(copy)
        self.quarters[self.z] = self.half[:, self.piece_of(self.z)]

    def total(self):
        for copy in self.out:
            copy.wait_recv()
        done = self.quarters[0].astype(F32)
        for z in range(1, 4):
            done = done + self.quarters[z].astype(F32)
        piece = self.whole.at[:, self.piece_of(self.z, self.y)]
        piece[...] = done.astype(BF)
        self.back = []
        for d, z in enumerate(self.column):
            copy = self.copy(4 + d, piece, piece, 2 * z + self.y)
            copy.start()
            self.back.append(copy)

    def join(self):
        for copy in self.back:
            copy.wait_recv()
        mine = self.whole.at[:, self.half_of(self.y)]
        self.last = self.copy(7, mine, mine, self.beside)
        self.last.start()

    def finish(self):
        self.last.wait_recv()
        for copy in (self.first, *self.out, *self.back, self.last):
            copy.wait_send()


def reduce_kernel(*refs):
    small_ref, ca_far, cb_far, out_far = refs[:4]
    sides_far, fin_ref = refs[4:8], refs[8]
    count = len(NAMES)
    small_out = refs[9]
    full_out = dict(zip((*NAMES, *LATE), refs[10 : 13 + count], strict=True))
    fin_out = refs[13 + count]
    refs = refs[14 + count :]
    low_ref, *sides = refs[:4]
    given = dict(zip(LATE, sides, strict=True))
    full = dict(zip((*NAMES, *LATE), refs[4 : 7 + count], strict=True))
    late_full = full
    move_sem = refs[7 + count]
    refs = refs[8 + count :]
    share = dict(zip(NAMES, refs[:count], strict=True))
    hold = dict(zip(NAMES, refs[count : 2 * count], strict=True))
    refs = refs[2 * count :]
    grid_share, half_in, half, quarters, small_in, small_mid, small_beside, small_column = refs[:8]
    small_send, small_recv, ring_send, ring_recv, grid_send, grid_recv, fin_send, fin_recv = refs[8:16]
    made, turned = refs[16:18]
    moves = Moves(move_sem)
    share_loads = [
        moves.start(*pair)
        for pair in (
            (ca_far.at[:224], share["cq"]),
            (cb_far, share["cv"]),
            (ca_far.at[224:], share["ck"]),
            (out_far.at[:, :32], share["co"]),
            (out_far.at[:, 32:48], share["so0"]),
            (out_far.at[:, 48:], share["so1"]),
        )
    ]
    side_loads = [moves.start(*pair) for pair in zip(sides_far, (low_ref, *sides), strict=True)]
    parts = {name: made.at[u] for u, name in enumerate(LATE)}
    extra = refs[18:]
    fold_wa = Folding(LATE, parts, (extra[0:4], None, extra[4:9]))
    place, after, before = ring_place(RING)
    grids = {
        name: Grid(
            u, grid_share.at[u], half_in.at[u], half.at[u], quarters.at[u], late_full[name], grid_send, grid_recv
        )
        for u, name in enumerate(LATE)
    }
    wa, both = fold_wa.wa, other_wa(fold_wa.across, 1)
    some = grids["q"]
    in_column = [2 * z + some.y for z in some.column]
    meet(
        [{"wa": peer} for peer in (fold_wa.mate, fold_wa.across, both)]
        + [{"ctx": peer} for peer in (after, before, some.beside, *in_column)]
    )
    near = remote(small_ref, small_in.at[0], small_send.at[0], small_recv.at[0], wa=fold_wa.mate)
    near.start()
    over = remote(small_mid.at[0], small_in.at[1], small_send.at[1], small_recv.at[1], wa=fold_wa.across)
    beside = remote(small_mid.at[1], small_beside, small_send.at[2], small_recv.at[2], ctx=some.beside)
    columns = [
        remote(small_mid.at[2], small_column.at[some.z], small_send.at[3 + d], small_recv.at[3 + d], ctx=peer)
        for d, peer in enumerate(in_column)
    ]
    own_fin = pltpu.make_async_copy(fin_ref.at[wa], fin_out.at[:, columns_of(wa)], fin_send.at[3])
    own_fin.start()
    fin_copies = [
        remote(fin_ref.at[peer], fin_out.at[:, columns_of(wa)], fin_send.at[d], fin_recv.at[d], wa=peer)
        for d, peer in enumerate((fold_wa.across, both, fold_wa.mate))
    ]
    wait_all(share_loads)
    copies = {}

    def ring_step(b, name, step):
        way = BUFFERS[name][0]
        here = place if way == 1 else RING - place
        target = after if way == 1 else before
        if step > 0:
            copies[name, step - 1].wait_recv()
        if step == 2 * HOPS:
            return
        now = lax.rem(here - step + 3 * RING, RING)
        mine = chunk_of(share[name], name, now)
        done = chunk_of(full[name], name, now)
        if 0 < step <= HOPS:
            total = mine[...].astype(F32) + hold[name][step - 1].astype(F32)
            (mine if step < HOPS else done)[...] = total.astype(BF)
        src, dst = (mine, hold[name].at[step]) if step < HOPS else (done, done)
        copy = remote(src, dst, ring_send.at[b, step], ring_recv.at[b, step], ctx=target)
        copy.start()
        copies[name, step] = copy

    def small_over():
        near.wait_recv()
        small_mid[0] = small_ref[...] + small_in[0]
        over.start()

    def small_next():
        over.wait_recv()
        small_mid[1] = small_mid[0] + small_in[1]
        beside.start()

    def small_last():
        beside.wait_recv()
        small_mid[2] = small_mid[1] + small_beside[...]
        small_column[some.z] = small_mid[2]
        for copy in columns:
            copy.start()

    def begin(name, following=None):
        total = fold_wa.total(name)
        if following:
            fold_wa.x_copies[following].start()
        grids[name].start(total)

    def make(name):
        parts[name][...] = nn_dot(turned[...], given[name][...]).astype(BF)
        fold_wa.start(name)

    def make_all():
        wait_all(side_loads)
        turned[...] = low_ref[...].astype(F32).T.astype(BF)
        make("q")
        make("k")
        fold_wa.send("q")
        make("v")
        fold_wa.prepare("k")
        fold_wa.prepare("v")

    events = {
        0: [make_all, small_over],
        4: [lambda: begin("q", "k"), small_next],
        6: [grids["q"].spread, lambda: begin("k", "v"), small_last],
        8: [grids["q"].total, grids["k"].spread],
        9: [lambda: begin("v"), grids["q"].join, *(copy.start for copy in fin_copies)],
        10: [grids["k"].total],
        11: [grids["v"].spread, grids["k"].join],
        12: [grids["v"].total],
        14: [grids["v"].join],
    }
    for tick in range(2 * HOPS + 1):
        for b, name in enumerate(NAMES):
            ring_step(b, name, tick)
        for event in events.get(tick, ()):
            event()
    stores = [moves.start(full[name], full_out[name]) for name in NAMES]
    for copy in columns:
        copy.wait_recv()
    total = small_column[0]
    for z in range(1, 4):
        total = total + small_column[z]
    small_out[...] = total
    for name in LATE:
        grids[name].finish()
        stores.append(moves.start(full[name], full_out[name]))
    fold_wa.finish()
    for copy in (near, over, beside, *columns, *copies.values()):
        copy.wait_send()
    own_fin.wait()
    for copy in fin_copies:
        copy.wait()
    wait_all(stores)


def columns_of(owner):
    return pl.ds(pl.multiple_of(owner * 896, WIDE), 896)


def reduce_grads(pair, one, flat, small, low, grads, fin):
    dma = pltpu.SemaphoreType.DMA
    any_spec = pl.BlockSpec(memory_space=pl.ANY)
    late = len(LATE)
    shapes = [*(BUFFERS[b][1] for b in NAMES), *[TALL] * late]
    small, *others = pl.pallas_call(
        reduce_kernel,
        out_shape=(
            jax.ShapeDtypeStruct(small.shape, F32),
            *(jax.ShapeDtypeStruct(shape, BF) for shape in shapes),
            jax.ShapeDtypeStruct((224, 3584), BF),
        ),
        in_specs=vmem(1) + [any_spec] * 8,
        out_specs=tuple(vmem(1) + [any_spec] * (len(shapes) + 1)),
        scratch_shapes=[
            pltpu.VMEM(low.shape, BF),
            *(pltpu.VMEM(grad.shape, BF) for grad in grads),
            *(pltpu.VMEM(shape, BF) for shape in shapes),
            dma((10 + len(shapes),)),
            *(pltpu.VMEM(BUFFERS[b][1], BF) for b in NAMES),
            *(pltpu.VMEM((HOPS, *chunk_shape(b)), BF) for b in NAMES),
            pltpu.VMEM((late, *TALL), BF),
            pltpu.VMEM((late, 224, 4 * WIDE), BF),
            pltpu.VMEM((late, 224, 4 * WIDE), BF),
            pltpu.VMEM((late, 4, 224, WIDE), BF),
            pltpu.VMEM((2, *small.shape), F32),
            pltpu.VMEM((3, *small.shape), F32),
            pltpu.VMEM(small.shape, F32),
            pltpu.VMEM((4, *small.shape), F32),
            dma((6,)),
            dma((6,)),
            dma((len(NAMES), 2 * HOPS)),
            dma((len(NAMES), 2 * HOPS)),
            dma((late, 8)),
            dma((late, 8)),
            dma((4,)),
            dma((3,)),
            pltpu.VMEM((late, 896, 1024), BF),
            pltpu.VMEM((896, 256), BF),
            *Folding.scratch(LATE),
        ],
        compiler_params=pltpu.CompilerParams(
            collective_id=3, has_side_effects=True, vmem_limit_bytes=56 << 20
        ),
        cost_estimate=lasting(90),
        name="reduce_grads",
    )(small, pair, one, flat, low, *grads, fin.reshape(4, 224, 896))
    return *others[:-1], small, others[-1]


WIDENED = ("cq", "ck", "cv", "q", "k", "v", "co", "fin", "fout")


def widen_kernel(*refs):
    count = len(WIDENED)
    so0, so1, near, last, back = refs[count : count + 5]
    outs = refs[count + 5 :]
    for src, dst in zip(refs[:count], outs[:count], strict=True):
        dst[...] = src[...].astype(F32)
    for c in range(so0.shape[0]):
        outs[count][c * 32 : c * 32 + 16, :] = so0[c].astype(F32)
        outs[count][c * 32 + 16 : c * 32 + 32, :] = so1[c].astype(F32)
    span = pl.program_id(0)

    @pl.when(span < 3)
    def _():
        outs[count + 1][...] = near[...]

    @pl.when(span == 3)
    def _():
        outs[count + 1][...] = (last[...] + back[...].astype(F32)).astype(BF)


def widen(full, near, last, back):
    values = [full[name] for name in WIDENED]
    blocks = {
        (224, 1024): ((224, 256), lambda i: (0, i)),
        (256, 896): ((64, 896), lambda i: (i, 0)),
        (224, 3584): ((224, 896), lambda i: (0, i)),
        (896, 896): ((224, 896), lambda i: (i, 0)),
    }
    specs = [pl.BlockSpec(*blocks[v.shape]) for v in values]
    halves = pl.BlockSpec((2, 16, 896), lambda i: (i, 0, 0))
    span = (256, 896)
    still = pl.BlockSpec(span, lambda i: (0, 0))
    moving = pl.BlockSpec(span, lambda i: (i, 0))
    *wide, neighbour = pl.pallas_call(
        widen_kernel,
        grid=(4,),
        out_shape=(
            *(jax.ShapeDtypeStruct(v.shape, F32) for v in values),
            jax.ShapeDtypeStruct(FLAT, F32),
            jax.ShapeDtypeStruct((1024, 896), BF),
        ),
        in_specs=[
            *specs,
            halves,
            halves,
            pl.BlockSpec(span, lambda i: (jnp.minimum(i, 2), 0)),
            still,
            still,
        ],
        out_specs=(*specs, pl.BlockSpec((64, 896), lambda i: (i, 0)), moving),
        compiler_params=pltpu.CompilerParams(vmem_limit_bytes=60 << 20),
        name="widen",
    )(*values, full["so0"], full["so1"], near, last, back)
    return dict(zip((*WIDENED, "so"), wide, strict=True)), neighbour


GELU = (2.0 / math.pi) ** 0.5


def ffn_kernel(
    late, f_ref, bias_ref, win_far, cot_far, wout_far, df_ref, dbias_ref, res_out, parts_out, dwin_out, dwout_out,
    win_ref, cot_ref, wout_ref, res_ref, parts_ref, dwin_ref, dwout_ref, move_sem, f_all, g_all, dul_all, ahead, own, kept, out_mate, out_cross, in_mate, in_cross, x_out, x_in,
    f_send, f_recv, p_send, p_recv,
):
    moves = Moves(move_sem)
    load_in, load_cot, load_out = (
        moves.start(*pair) for pair in ((win_far, win_ref), (cot_far, cot_ref), (wout_far, wout_ref))
    )
    me = lax.axis_index("wa")
    mate, across = other_wa(me, 1), other_wa(me, 2)
    both = other_wa(across, 1)
    barrier = pltpu.get_barrier_semaphore()
    for peer in (mate, across):
        pl.semaphore_signal(barrier, inc=1, device_id={"wa": peer}, device_id_type=MESH)
    pl.semaphore_wait(barrier, 2)
    to_across = remote(f_ref, f_all.at[me], f_send.at[1], f_recv.at[1], wa=across)
    to_across.start()
    to_mate = remote(f_ref, f_all.at[me], f_send.at[0], f_recv.at[0], wa=mate)
    to_mate.start()
    forward = remote(f_all.at[across], f_all.at[across], f_send.at[2], f_recv.at[2], wa=mate)
    f_all[me] = f_ref[...]
    order = (me, mate, across, both)
    dbias_ref[...] = jnp.zeros_like(dbias_ref)
    load_in.wait()
    for k, s in enumerate(order):
        if k == 1:
            to_mate.wait_recv()
        if k == 2:
            for d in range(2):
                ahead[d] = nt_dot(cot_ref[order[2 + d]], wout_ref[...])
            to_across.wait_recv()
            forward.start()
        if k == 3:
            forward.wait_recv()
        u = nn_dot(f_all[s], win_ref[...]) + bias_ref[...]
        square = u * u
        t = jnp.tanh(GELU * (u + 0.044715 * (square * u)))
        g_all[s] = (0.5 * u * (1.0 + t)).astype(BF)
        if k == 0:
            load_cot.wait()
            load_out.wait()
        slope = 0.5 * (1.0 + t) + 0.5 * u * (1.0 - t * t) * (GELU * (1.0 + 3 * 0.044715 * square))
        du = (nt_dot(cot_ref[s], wout_ref[...]) if k < 2 else ahead[k - 2]) * slope
        dbias_ref[...] += jnp.sum(du.reshape(32, 8, du.shape[1]), axis=0)
        dul_all[s] = du.astype(BF)

    def scatter(which, product):
        out_cross[which] = product(both).astype(BF)
        cross = remote(
            out_cross.at[which], in_cross.at[which], p_send.at[which, 0], p_recv.at[which, 0], wa=mate
        )
        cross.start()
        kept[...] = product(across)
        cross.wait_recv()
        x_out[which] = (kept[...] + in_cross[which].astype(F32)).astype(BF)
        over = remote(
            x_out.at[which], x_in.at[which], p_send.at[which, 1], p_recv.at[which, 1], wa=across
        )
        over.start()
        out_mate[which] = product(mate).astype(BF)
        near = remote(
            out_mate.at[which], in_mate.at[which], p_send.at[which, 2], p_recv.at[which, 2], wa=mate
        )
        near.start()
        own[which] = product(me)
        return cross, over, near

    def finish(which, copies, out_ref):
        cross, over, near = copies
        near.wait_recv()
        over.wait_recv()
        out_ref[...] = own[which] + in_mate[which].astype(F32) + x_in[which].astype(F32)
        for copy in copies:
            copy.wait_send()

    df_copies = scatter(0, lambda s: nt_dot(dul_all[s], win_ref[...]))
    if late:
        res_ref[...] = nn_dot(g_all[me], wout_ref[...])
        for d, s in enumerate(order[1:]):
            parts_ref[d] = nn_dot(g_all[s], wout_ref[...]).astype(BF)
    else:
        res_copies = scatter(1, lambda s: nn_dot(g_all[s], wout_ref[...]))
        parts_ref[...] = jnp.zeros_like(parts_ref)
    stores = []
    if late:
        stores += [moves.start(res_ref, res_out), moves.start(parts_ref, parts_out)]
    width = f_ref.shape[1]

    def outer(left_all, right, out_ref):
        for c in range(width // WIDE):
            lanes = slice(c * WIDE, (c + 1) * WIDE)
            total = None
            for s in range(4):
                left = left_all[s, :, lanes].astype(F32).T.astype(BF)
                now = nn_dot(left, right[s])
                total = now if total is None else total + now
            out_ref[lanes, :] = total.astype(BF)

    outer(f_all, dul_all, dwin_ref)
    stores.append(moves.start(dwin_ref, dwin_out))
    outer(g_all, cot_ref, dwout_ref)
    stores.append(moves.start(dwout_ref, dwout_out))
    finish(0, df_copies, df_ref)
    if not late:
        finish(1, res_copies, res_ref)
        stores += [moves.start(res_ref, res_out), moves.start(parts_ref, parts_out)]
    wait_all(stores)
    for copy in (to_mate, to_across, forward):
        copy.wait_send()


def ffn(late, f_low, cot_all, win, wout, bias):
    rows, width = f_low.shape
    hidden = win.shape[1]
    dma = pltpu.SemaphoreType.DMA
    block = (rows, width)
    any_spec = pl.BlockSpec(memory_space=pl.ANY)
    df, dbias, *others = pl.pallas_call(
        functools.partial(ffn_kernel, late),
        out_shape=(
            jax.ShapeDtypeStruct(block, F32),
            jax.ShapeDtypeStruct((8, hidden), F32),
            jax.ShapeDtypeStruct(block, F32),
            jax.ShapeDtypeStruct((3, *block), BF),
            jax.ShapeDtypeStruct(win.shape, BF),
            jax.ShapeDtypeStruct(wout.shape, BF),
        ),
        in_specs=vmem(2) + [any_spec] * 3,
        out_specs=tuple(vmem(2) + [any_spec] * 4),
        scratch_shapes=[
            pltpu.VMEM(win.shape, BF),
            pltpu.VMEM((4, *block), BF),
            pltpu.VMEM(wout.shape, BF),
            pltpu.VMEM(block, F32),
            pltpu.VMEM((3, *block), BF),
            pltpu.VMEM(win.shape, BF),
            pltpu.VMEM(wout.shape, BF),
            dma((7,)),
            pltpu.VMEM((4, *block), BF),
            pltpu.VMEM((4, rows, hidden), BF),
            pltpu.VMEM((4, rows, hidden), BF),
            pltpu.VMEM((2, rows, hidden), F32),
            pltpu.VMEM((2, *block), F32),
            pltpu.VMEM(block, F32),
            *[pltpu.VMEM((2, *block), BF)] * 6,
            dma((3,)),
            dma((3,)),
            dma((2, 3)),
            dma((2, 3)),
        ],
        compiler_params=pltpu.CompilerParams(
            collective_id=4, has_side_effects=True, vmem_limit_bytes=60 << 20
        ),
        cost_estimate=lasting(44),
        name="feed_forward",
    )(f_low, bias, win, cot_all, wout)
    res, parts, dwin, dwout = others
    return res, parts, df, dwin, dwout, dbias


def padded_rows(pad, values):
    rows = values.shape[0]
    pad[...] = jnp.zeros_like(pad)
    pad[1 : rows + 1, :] = values.astype(F32)


def both_heads(pad, g):
    here = pad[g * SPAN : (g + 1) * SPAN, :]
    left = head_mask(0, SPAN)
    return jnp.concatenate([jnp.where(left, here, 0.0), jnp.where(left, 0.0, here)], 0).astype(BF)


def join_heads(stacked):
    return jnp.where(head_mask(0, SPAN), stacked[:SPAN], stacked[SPAN:])


def cross_forward_kernel(groups, keep_ref, q_ref, k_ref, v_ref, x_ref, q_pad, x_pad):
    padded_rows(q_pad, q_ref[...])
    spans = range(groups)
    rows = [slice(g * 256, (g + 1) * 256) for g in spans]
    scores = [nt_dot(both_heads(q_pad, g) * BF(HD**-0.5), k_ref[rows[g], :]) for g in spans]
    weights = [jnp.exp(v - jnp.max(v, axis=1, keepdims=True)) for v in scores]
    weights = [v / jnp.sum(v, axis=1, keepdims=True) for v in weights]
    mixed = [join_heads(nn_dot(weights[g].astype(BF), v_ref[rows[g], :])) for g in spans]
    mixed[0] = mixed[0] * keep_ref[0:1, :]
    for g in spans:
        x_pad[g * SPAN : (g + 1) * SPAN, :] = mixed[g]
    x_ref[...] = x_pad[1 : x_ref.shape[0] + 1, :].astype(BF)


def pair_specs(*rows):
    return [pl.BlockSpec((r, WIDE), lambda p: (0, p)) for r in rows]


def cross_forward(keep, query, keys, values):
    rows, width = query.shape
    many = keys.shape[0]
    groups = many // 256
    return pl.pallas_call(
        functools.partial(cross_forward_kernel, groups),
        grid=(width // WIDE,),
        out_shape=jax.ShapeDtypeStruct(query.shape, BF),
        in_specs=[pl.BlockSpec((8, WIDE), lambda p: (0, 0)), *pair_specs(rows, many, many)],
        out_specs=pair_specs(rows)[0],
        scratch_shapes=[pltpu.VMEM((groups * SPAN, WIDE), F32)] * 2,
        compiler_params=pltpu.CompilerParams(vmem_limit_bytes=16 << 20),
        cost_estimate=lasting(9),
        name="cross_forward",
    )(keep, query, keys, values)


def cross_backward_kernel(
    groups, keep_ref, q_ref, dx_ref, k_ref, v_ref, dq_ref, dk_ref, dv_ref, q_pad, dx_pad, dq_pad
):
    padded_rows(q_pad, q_ref[...])
    padded_rows(dx_pad, dx_ref[...])
    dx_pad[:SPAN, :] = dx_pad[:SPAN, :] * keep_ref[0:1, :]
    for g in range(groups):
        rows = slice(g * 256, (g + 1) * 256)
        query = both_heads(q_pad, g) * BF(HD**-0.5)
        dmixed = both_heads(dx_pad, g)
        keys, values = k_ref[rows, :], v_ref[rows, :]
        scores = nt_dot(keys, query)
        weights = jnp.exp(scores - jnp.max(scores, axis=0, keepdims=True))
        weights = weights / jnp.sum(weights, axis=0, keepdims=True)
        dweights = nt_dot(values, dmixed)
        dscores = weights * (dweights - jnp.sum(weights * dweights, axis=0, keepdims=True))
        dk_ref[rows, :] = nn_dot(dscores.astype(BF), query).astype(BF)
        dv_ref[rows, :] = nn_dot(weights.astype(BF), dmixed).astype(BF)
        back = (dscores * HD**-0.5).T.astype(BF)
        dq_pad[g * SPAN : (g + 1) * SPAN, :] = join_heads(nn_dot(back, keys))
    dq_ref[...] = dq_pad[1 : dq_ref.shape[0] + 1, :].astype(BF)


def cross_backward(keep, query, dmixed, keys, values):
    rows, width = query.shape
    many = keys.shape[0]
    groups = many // 256
    return pl.pallas_call(
        functools.partial(cross_backward_kernel, groups),
        grid=(width // WIDE,),
        out_shape=(
            jax.ShapeDtypeStruct(query.shape, BF),
            jax.ShapeDtypeStruct(keys.shape, BF),
            jax.ShapeDtypeStruct(keys.shape, BF),
        ),
        in_specs=[
            pl.BlockSpec((8, WIDE), lambda p: (0, 0)),
            *pair_specs(rows, rows, many, many),
        ],
        out_specs=tuple(pair_specs(rows, many, many)),
        scratch_shapes=[pltpu.VMEM((groups * SPAN, WIDE), F32)] * 3,
        compiler_params=pltpu.CompilerParams(vmem_limit_bytes=16 << 20),
        cost_estimate=lasting(17),
        name="cross_backward",
    )(keep, query, dmixed, keys, values)


def line_selector():
    place = jnp.arange(LINE)
    offset = jnp.where(place < LINE // 2, -place, LINE - place)
    return (bucket_of(offset)[None, :] == jnp.arange(NB)[:, None]).astype(jnp.float32)


def ring_forward(query_low, key_low, value_low, bucket_table):
    row_count, attn_width = query_low.shape
    position = lax.axis_index("ctx")
    scale_factor = HD ** (-0.5)
    bias_set, onehots = make_bias(bucket_table.astype(jnp.float32), row_count)
    query_heads = query_low.reshape(row_count, H, HD)
    start_state = (
        jnp.full((H, row_count), negative, jnp.float32),
        jnp.zeros((H, row_count), jnp.float32),
        jnp.zeros((row_count, attn_width), jnp.float32),
    )
    running_max, running_sum, running_acc = forward_fold(
        query_heads,
        position,
        row_count,
        bias_set,
        scale_factor,
        start_state,
        (
            lax.all_gather(key_low, "ctx", axis=0, tiled=True),
            lax.all_gather(value_low, "ctx", axis=0, tiled=True),
        ),
    )
    attended = (running_acc.reshape(row_count, H, HD) / running_sum.T[:, :, None]).reshape(
        row_count, attn_width
    )
    log_total = running_max + jnp.log(running_sum)
    state = (query_heads, key_low, value_low, attended, log_total, bias_set, onehots)
    return attended.astype(jnp.bfloat16), state


def ring_backward(state, dout_low):
    query_heads, key_low, value_low, attended, log_total, bias_set, onehots = state
    row_count, attn_width = dout_low.shape
    cycle_size = lax.axis_size("ctx")
    position = lax.axis_index("ctx")
    scale_factor = HD ** (-0.5)
    dout_heads = dout_low.reshape(row_count, H, HD)
    row_delta = jnp.sum(
        (dout_low.astype(jnp.float32) * attended).reshape(row_count, H, HD), axis=-1
    ).T
    zero_rows = jnp.zeros((row_count, attn_width), jnp.float32)
    zero_tables = (
        jnp.zeros((H, row_count, row_count), jnp.float32),
        jnp.zeros((H, row_count, row_count), jnp.float32),
        jnp.zeros((H,), jnp.float32),
    )

    def visit(folded, key_now, value_now, relation):

        def visit_compute(current):
            dquery_acc, dkey_acc, dvalue_acc, relative_bias_tables = current
            key_heads = key_now.reshape(row_count, H, HD)
            weights_now, dscores, ds_low = pair_core(
                query_heads,
                dout_heads,
                log_total,
                row_delta,
                key_heads,
                value_now.reshape(row_count, H, HD),
                relation,
                bias_set,
                scale_factor,
            )
            dquery = jnp.einsum(
                "hqk,khd->qhd", ds_low, key_heads, preferred_element_type=jnp.float32
            ).reshape(row_count, attn_width)
            dkey = jnp.einsum(
                "hqk,qhd->khd", ds_low, query_heads, preferred_element_type=jnp.float32
            ).reshape(row_count, attn_width)
            dvalue = jnp.einsum(
                "hqk,qhd->khd",
                weights_now.astype(jnp.bfloat16),
                dout_heads,
                preferred_element_type=jnp.float32,
            ).reshape(row_count, attn_width)
            return (
                dquery_acc + dquery,
                dkey_acc + dkey,
                dvalue_acc + dvalue,
                add_tables(relative_bias_tables, dscores, relation),
            )

        return lax.cond(relation >= 0, visit_compute, lambda unchanged: unchanged, folded)

    first_state = visit(
        (zero_rows, zero_rows, zero_rows, zero_tables), key_low, value_low, jnp.array(0, jnp.int32)
    )

    def cycle_step(carried, cycle_index):
        key_now, value_now, (dquery_acc, dkey_acc, dvalue_acc, relative_bias_tables) = carried
        key_next, value_next = passed_along((key_now, value_now), "ctx", 1)
        dkey_next, dvalue_next = (
            from_behind(dkey_acc.astype(jnp.bfloat16), "ctx", 1).astype(dkey_acc.dtype),
            from_behind(dvalue_acc.astype(jnp.bfloat16), "ctx", 1).astype(dvalue_acc.dtype),
        )
        relation = jnp.where(position >= cycle_index, cycle_index, -1)
        updated = visit(
            (dquery_acc, dkey_next, dvalue_next, relative_bias_tables),
            key_next,
            value_next,
            relation,
        )
        return ((key_next, value_next, updated), None)

    (
        unused_key,
        unused_value,
        (dquery_total, dkey_part, dvalue_part, relative_bias_tables),
    ), unused = lax.scan(cycle_step, (key_low, value_low, first_state), jnp.arange(1, cycle_size))
    dkey_total, dvalue_total = (
        from_behind(dkey_part.astype(jnp.bfloat16), "ctx", 1).astype(dkey_part.dtype),
        from_behind(dvalue_part.astype(jnp.bfloat16), "ctx", 1).astype(dvalue_part.dtype),
    )
    dquery_low = dquery_total.astype(jnp.bfloat16)
    dkey_low = dkey_total.astype(jnp.bfloat16)
    dvalue_low = dvalue_total.astype(jnp.bfloat16)
    current_bucket_selector, previous_bucket_selector, onehot_far = onehots
    grad_biastable = (
        jnp.einsum(
            "afw,mfw->am",
            current_bucket_selector,
            relative_bias_tables[0],
            precision=strongest_precision,
        )
        + jnp.einsum(
            "afw,mfw->am",
            previous_bucket_selector,
            relative_bias_tables[1],
            precision=strongest_precision,
        )
        + onehot_far[:, None] * relative_bias_tables[2][None, :]
    )
    return dquery_low, dkey_low, dvalue_low, grad_biastable


def heads_forward(tokens, near, cotangent, given):
    wa, owners = lax.axis_index("wa"), lax.axis_size("wa")
    table = given["biastable"].astype(F32)
    selector = lax.dynamic_slice_in_dim(line_selector(), wa * table.shape[0], table.shape[0], 0)
    lines = jnp.dot(table.T, selector, precision=strongest_precision).astype(BF)
    gains = jnp.concatenate([given[name] for name in GAINS]).reshape(len(GAINS), -1)
    small = jnp.zeros((H, LINE), BF)
    small = lax.dynamic_update_slice(small, gains, (0, wa * gains.shape[1]))
    small = jnp.concatenate([lines, small], 0)
    shards = [given[LONG_NAMES[name]] for name in GATHERED]
    *wholes, upstream_all, feed_in, attended_low, low, ot, lse, small, before, qh, kh, vh, keys, values = attn_forward(
        lax.axis_size("ctx"), tokens, small, near, [*shards, cotangent], given["feedin"]
    )
    width = tokens.shape[1]
    gain_of = {name: small[H + g, :width] for g, name in enumerate(GAINS)}
    full = {LONG_NAMES[name]: whole for name, whole in zip(GATHERED, wholes, strict=True)}
    full["feedin"] = feed_in
    upstream_all = upstream_all.reshape(owners, *tokens.shape)
    saved = (qh, kh, vh, ot, lse, small[:H])
    return attended_low, low, full, gain_of, upstream_all, (before, keys, values), saved


def heads_backward(state, dout_low, parts, feed_part, span):
    peers = lax.axis_size("ctx")
    dquery_low, dkey_low, dvalue_low, sums, *shares = attn_backward(
        peers, dout_low, *state, parts, feed_part, span
    )
    selector = line_selector()
    table = jnp.dot(selector, sums[:2].T, precision=strongest_precision)
    far = jnp.sum(sums[2:4], axis=1)
    table = table + selector[:, WIDE : WIDE + 1] * far[None, :]
    whole = jnp.zeros((NB, H), jnp.float32)
    whole = lax.dynamic_update_slice(whole, table, (0, 2 * lax.axis_index("ctx")))
    return dquery_low, dkey_low, dvalue_low, whole, shares


def cross_pair(groups, keep_ref, q_ref, dx_ref, k_ref, v_ref, dq_ref, dk_ref, dv_ref, q_pad, dx_pad, dq_pad, p):
    lanes = lanes_of(p)
    padded_rows(q_pad, q_ref[:, lanes])
    padded_rows(dx_pad, dx_ref[:, lanes])
    dx_pad[:SPAN, :] = dx_pad[:SPAN, :] * keep_ref[0:1, :]
    for g in range(groups):
        rows = slice(g * 256, (g + 1) * 256)
        query = both_heads(q_pad, g) * BF(HD**-0.5)
        dmixed = both_heads(dx_pad, g)
        keys, values = k_ref[rows, lanes], v_ref[rows, lanes]
        scores = nt_dot(keys, query)
        weights = jnp.exp(scores - jnp.max(scores, axis=0, keepdims=True))
        weights = weights / jnp.sum(weights, axis=0, keepdims=True)
        dweights = nt_dot(values, dmixed)
        dscores = weights * (dweights - jnp.sum(weights * dweights, axis=0, keepdims=True))
        dk_ref[rows, lanes] = nn_dot(dscores.astype(BF), query).astype(BF)
        dv_ref[rows, lanes] = nn_dot(weights.astype(BF), dmixed).astype(BF)
        back = (dscores * HD**-0.5).T.astype(BF)
        dq_pad[g * SPAN : (g + 1) * SPAN, :] = join_heads(nn_dot(back, keys))
    dq_ref[:, lanes] = dq_pad[1 : dq_ref.shape[0] + 1, :].astype(BF)


def middle_kernel(
    keep_ref, fed_ref, fed_parts, q_far, dx_far, k_far, v_far, before_far, near_far, wk_far, wv_far, fin_ref,
    fout_ref, feed_out, fed_out, dq_out, dwk_out, dwv_out, first_out, near_out, last_out,
    q_ref, dx_ref, k_ref, v_ref, before_ref, near_ref, wk_ref, wv_ref, dq_ref, dwk_ref, dwv_ref, near_low, near_last,
    dk, dv, q_pad, dx_pad, dq_pad, share, hold, in_mate, in_cross, x_out, x_in, load_sem, ring_send, ring_recv,
    fed_send, fed_recv,
):
    ring = Ring(FEED_LANES, ring_send, ring_recv, share=share, hold=hold)
    moves = Moves(load_sem)
    loads = [moves.start(part, share.at[b]) for b, part in enumerate((fin_ref, fout_ref))]
    pair_loads = [
        moves.start(*pair) for pair in ((q_far, q_ref), (dx_far, dx_ref), (k_far, k_ref), (v_far, v_ref))
    ]
    later_loads = [
        moves.start(*pair)
        for pair in ((wk_far, wk_ref), (wv_far, wv_ref), (before_far, before_ref), (near_far, near_ref))
    ]
    wa = lax.axis_index("wa")
    mate, across = other_wa(wa, 1), other_wa(wa, 2)
    meet([{"ctx": ring.after}, {"ctx": ring.before}, {"wa": mate}, {"wa": across}])
    cross = remote(fed_parts.at[2], in_cross, fed_send.at[0], fed_recv.at[0], wa=mate)
    cross.start()
    near = remote(fed_parts.at[0], in_mate, fed_send.at[1], fed_recv.at[1], wa=mate)
    near.start()
    over = remote(x_out, x_in, fed_send.at[2], fed_recv.at[2], wa=across)
    wait_all(loads)
    for lanes in FEED_TURNS:
        ring.scatter(jnp.int32(0), lanes)
    cross.wait_recv()
    x_out[...] = (fed_parts[1].astype(F32) + in_cross[...].astype(F32)).astype(BF)
    over.start()
    groups = k_ref.shape[0] // 256
    wait_all(pair_loads)

    def two_pairs(m, unused):
        for turn, lanes in enumerate(FEED_TURNS):
            cross_pair(
                groups, keep_ref, q_ref, dx_ref, k_ref, v_ref, dq_ref, dk, dv, q_pad, dx_pad, dq_pad,
                2 * m + turn,
            )
            ring.scatter(m + 1, lanes)
        return unused

    pairs = q_ref.shape[1] // (2 * WIDE)
    lax.fori_loop(0, pairs, two_pairs, 0)
    stores = [moves.start(dq_ref, dq_out)]
    wait_all(later_loads)
    calls = [(step, lanes) for step in range(pairs + 1, HOPS + 1) for lanes in FEED_TURNS]

    def turn():
        if calls:
            step, lanes = calls.pop(0)
            ring.scatter(jnp.int32(step), lanes)

    for g in range(groups):
        rows = slice(g * 256, (g + 1) * 256)
        total = nt_dot(dk[rows, :], wk_ref[...]) + nt_dot(dv[rows, :], wv_ref[...])
        if g == groups - 1:
            near_last[...] = total
        else:
            near_low[rows, :] = total.astype(BF)
        if g % 2 == 1:
            turn()
    stores += [
        moves.start(near_low.at[:256], first_out),
        moves.start(near_low.at[256:], near_out),
        moves.start(near_last, last_out),
    ]
    for c in range(near_ref.shape[1] // WIDE):
        lanes = slice(c * WIDE, (c + 1) * WIDE)
        first = before_ref[:, lanes].astype(F32).T.astype(BF)
        left = near_ref[:, lanes].astype(F32).T.astype(BF)
        for grads, out_ref in ((dk, dwk_ref), (dv, dwv_ref)):
            total = nn_dot(first, grads[:256, :]) + nn_dot(left, grads[256:, :])
            out_ref[lanes, :] = total.astype(BF)
        if c % 2 == 1:
            turn()
    stores += [moves.start(dwk_ref, dwk_out), moves.start(dwv_ref, dwv_out)]
    while calls:
        turn()
    near.wait_recv()
    over.wait_recv()
    fed_out[...] = fed_ref[...] + in_mate[...].astype(F32) + x_in[...].astype(F32)
    for copy in (cross, near, over):
        copy.wait_send()
    for lane in range(2):
        feed_out[lane] = share[lane, ring.chunk(lane, 1)]
    ring.finish(lambda lane: share.at[FEED_LANES[lane][0], 0, FEED_LANES[lane][2]])
    wait_all(stores)


def middle(keep, query, dmixed, keys, values, before, near, wk, wv, fed, fed_parts, fin, fout):
    many, width = keys.shape
    wide = near.shape[1]
    rows = query.shape[0]
    low = functools.partial(jax.ShapeDtypeStruct, dtype=BF)
    dma = pltpu.SemaphoreType.DMA
    any_spec = pl.BlockSpec(memory_space=pl.ANY)
    pad = pltpu.VMEM((many // 256 * SPAN, WIDE), F32)
    feed_part, fed, *others = pl.pallas_call(
        middle_kernel,
        out_shape=(
            low((2, *FEED[1:])),
            jax.ShapeDtypeStruct(fed.shape, F32),
            low(query.shape),
            low(wk.shape),
            low(wv.shape),
            low((256, wide)),
            low((many - 512, wide)),
            jax.ShapeDtypeStruct((256, wide), F32),
        ),
        in_specs=vmem(3) + [any_spec] * 10,
        out_specs=tuple(vmem(2) + [any_spec] * 6),
        scratch_shapes=[
            *[pltpu.VMEM((rows, width), BF)] * 2,
            *[pltpu.VMEM((many, width), BF)] * 2,
            pltpu.VMEM((256, wide), BF),
            pltpu.VMEM((many - 256, wide), BF),
            *[pltpu.VMEM(wk.shape, BF)] * 2,
            pltpu.VMEM((rows, width), BF),
            *[pltpu.VMEM(wk.shape, BF)] * 2,
            pltpu.VMEM((many - 256, wide), BF),
            pltpu.VMEM((256, wide), F32),
            pltpu.VMEM((many, width), BF),
            pltpu.VMEM((many, width), BF),
            pad,
            pad,
            pad,
            pltpu.VMEM((2, *FEED), BF),
            pltpu.VMEM((2, HOPS, *FEED[1:]), BF),
            *[pltpu.VMEM(fed.shape, BF)] * 4,
            dma((16,)),
            dma((len(FEED_LANES), HOPS)),
            dma((len(FEED_LANES), HOPS)),
            dma((3,)),
            dma((3,)),
        ],
        compiler_params=pltpu.CompilerParams(
            collective_id=5, has_side_effects=True, vmem_limit_bytes=60 << 20
        ),
        cost_estimate=lasting(38),
        name="middle",
    )(
        keep, fed, fed_parts, query, dmixed, keys, values, before, near, wk, wv,
        fin.reshape(FEED), fout.reshape(FEED),
    )
    return *others, feed_part, fed


NAMES_OF_WEIGHTS = (
    "selfnorm", "selfquery", "selfkey", "selfvalue", "selfout", "biastable", "crossnorm", "crossquery",
    "crosskey", "crossvalue", "crossout", "feednorm", "feedin", "feedbias", "feedout", "outbias",
)
LONG_NAMES = {
    "q": "selfquery",
    "k": "selfkey",
    "v": "selfvalue",
    "so": "selfout",
    "ck": "crosskey",
    "cv": "crossvalue",
    "cq": "crossquery",
    "co": "crossout",
}


def whole_over_wa(shard):
    return lax.all_gather(shard, "wa", axis=0, tiled=True)


def reduce_plain(parts, smalls):
    shares = [
        lax.psum_scatter(part, "wa", scatter_dimension=0, tiled=True).astype(F32)
        for part in parts.values()
    ]
    totals = lax.psum(shares, "ctx")
    return dict(zip(parts, totals, strict=True)), lax.psum(smalls, ("ctx", "wa"))


def per_device(tokens, neighbours, cotangent, *shards):
    given = dict(zip(NAMES_OF_WEIGHTS, shards, strict=True))
    peers = lax.axis_size("ctx")
    position = lax.axis_index("ctx")
    row_count, model_width = tokens.shape[1:]
    split_heads = peers * 2 == H and row_count == BLOCK
    inputs = tokens[0].astype(F32)
    upstream_low = cotangent[0]
    upstream = upstream_low.astype(F32)
    spans = neighbours.shape[1]
    span_rows = neighbours.shape[2] * neighbours.shape[3]
    own_rows = neighbours[0].reshape(spans * span_rows, model_width)
    if split_heads and span_rows == BLOCK:
        attended_low, normed_low, full, small_of, upstream_all, projected, attention_state = (
            heads_forward(tokens[0], own_rows, upstream_low, given)
        )
        before, keys_cross, values_cross = projected
        feed_in = full["feedin"]
        normed_self, back_self = jax.vjp(root_norm, inputs, small_of["selfnorm"])
    else:
        small_of = {name: whole_over_wa(given[name]).astype(F32) for name in GAINS}
        full = {name: whole_over_wa(given[name]) for name in LONG_NAMES.values()}
        normed_self, back_self = jax.vjp(root_norm, inputs, small_of["selfnorm"])
        normed_low = normed_self.astype(BF)
        attended_low, attention_state = ring_forward(
            *(
                forward_product(normed_low, full[name]).astype(BF)
                for name in ("selfquery", "selfkey", "selfvalue")
            ),
            whole_over_wa(given["biastable"]),
        )
        upstream_all = lax.all_gather(upstream_low, "wa", axis=0)
        feed_in = lax.all_to_all(given["feedin"], "wa", 1, 0, tiled=True)
        before = passed_along(own_rows[-span_rows:], "ctx", 1)
        near_rows = jnp.concatenate([before, own_rows], 0)
        keys_cross = forward_product(near_rows, full["crosskey"]).astype(BF)
        values_cross = forward_product(near_rows, full["crossvalue"]).astype(BF)
    hidden = inputs + forward_product(attended_low, full["selfout"])

    normed_cross, back_cross = jax.vjp(root_norm, hidden, small_of["crossnorm"])
    cross_in = normed_cross.astype(BF)
    query_cross = forward_product(cross_in, full["crossquery"]).astype(BF)
    keep = jnp.full((8, WIDE), jnp.where(position > 0, 1.0, 0.0), F32)
    mixed_low = cross_forward(keep, query_cross, keys_cross, values_cross)
    hidden_two = hidden + forward_product(mixed_low, full["crossout"])

    normed_feed, back_feed = jax.vjp(root_norm, hidden_two, small_of["feednorm"])
    feed_low = normed_feed.astype(BF)
    bias_row = given["feedbias"].astype(F32)[None]
    fed, fed_parts, grad_feed, fin, fout, bias_sums = ffn(
        split_heads, feed_low, upstream_all, feed_in, given["feedout"], bias_row
    )
    grad_two_part, grad_feednorm = back_feed(grad_feed)
    grad_two = upstream + grad_two_part
    two_low = grad_two.astype(BF)

    grad_mixed = back_product(two_low, full["crossout"]).astype(BF)
    early = {}
    if split_heads:
        grad_query_cross, early["ck"], early["cv"], first, near_low, near_last, feed_part, fed = middle(
            keep,
            query_cross,
            grad_mixed,
            keys_cross,
            values_cross,
            before,
            own_rows,
            full["crosskey"],
            full["crossvalue"],
            fed,
            fed_parts,
            fin,
            fout,
        )
    else:
        grad_query_cross, dkeys, dvalues = cross_backward(
            keep, query_cross, grad_mixed, keys_cross, values_cross
        )
        near_grads = back_product(dkeys, full["crosskey"]) + back_product(
            dvalues, full["crossvalue"]
        )
        first, near_last = near_grads[:span_rows].astype(BF), near_grads[-span_rows:]
        near_low = near_grads[span_rows:-span_rows].astype(BF)
        early["ck"] = outer_product(near_rows, dkeys).astype(BF)
        early["cv"] = outer_product(near_rows, dvalues).astype(BF)
    result = (hidden_two + fed + small_of["outbias"]).astype(BF)
    grad_hidden_part, grad_crossnorm = back_cross(
        back_product(grad_query_cross, full["crossquery"])
    )
    grad_hidden = grad_two + grad_hidden_part
    hidden_low = grad_hidden.astype(BF)
    dout_low = back_product(hidden_low, full["selfout"]).astype(BF)
    sides = {
        "cq": (cross_in, grad_query_cross),
        "co": (mixed_low, two_low),
        "so": (attended_low, hidden_low),
    }
    if split_heads:
        parts = [early["ck"], early["cv"], *(side for name in MADE for side in sides[name])]
        dquery_low, dkey_low, dvalue_low, grad_biastable, shares = heads_backward(
            attention_state, dout_low, parts, feed_part, first
        )
        *shares, fin, fout, back = shares
    else:
        dquery_low, dkey_low, dvalue_low, grad_biastable = ring_backward(attention_state, dout_low)
        back = passed_along(first, "ctx", -1)
    grad_normed = (
        back_product(dquery_low, full["selfquery"])
        + back_product(dkey_low, full["selfkey"])
        + back_product(dvalue_low, full["selfvalue"])
    )
    grad_input_part, grad_selfnorm = back_self(grad_normed)
    grad_inputs = (grad_hidden + grad_input_part).astype(BF)

    late_grads = (dquery_low, dkey_low, dvalue_low)
    wa, owners = lax.axis_index("wa"), lax.axis_size("wa")
    bias_grad = jnp.sum(bias_sums, axis=0)
    placed = lax.dynamic_update_slice(
        jnp.zeros((owners, bias_grad.size), F32), bias_grad[None], (wa, 0)
    )
    sums = [grad_selfnorm, grad_crossnorm, grad_feednorm, jnp.sum(upstream, axis=0), grad_biastable]
    packed = jnp.concatenate([*(v.reshape(owners, -1) for v in sums), placed], axis=1)
    packed = jnp.pad(packed, ((0, 0), (0, LINE * 2 - packed.shape[1]))).reshape(-1, WIDE)
    if split_heads:
        *reduced, packed, fin = reduce_grads(
            *shares, packed, normed_low, late_grads, fin
        )
        reduced = dict(zip((*NAMES, *LATE), reduced, strict=True))
        reduced["co"] = reduced["co"].reshape(FLAT)
        reduced |= {"fin": fin, "fout": fout.reshape(given["feedout"].shape)}
        grads, grad_neigh = widen(reduced, near_low, near_last, back)
    else:
        for name, grad in zip(LATE, late_grads, strict=True):
            sides[name] = (normed_low, grad)
        for name, (left, right) in sides.items():
            early[name] = outer_product(left, right).astype(BF)
        grads, packed = reduce_plain(early, packed)
        fin, fout = lax.psum((fin, fout), "ctx")
        fin = lax.all_to_all(fin, "wa", 0, 1, tiled=True)
        grads["fin"], grads["fout"] = fin.astype(F32), fout.astype(F32)
        grad_neigh = jnp.concatenate([near_low, (near_last + back.astype(F32)).astype(BF)], 0)
    grad_neigh = grad_neigh.reshape(neighbours.shape)
    mine = lax.dynamic_index_in_dim(packed.reshape(owners, -1), wa, 0, keepdims=False)
    cuts, start = [], 0
    for v in (*sums, placed):
        cuts.append(mine[start : start + v.size // owners])
        start += v.size // owners
    own_selfnorm, own_crossnorm, own_feednorm, own_outbias, own_table, own_feedbias = cuts
    return (
        result[None],
        grad_inputs[None],
        grad_neigh,
        own_selfnorm,
        grads["q"],
        grads["k"],
        grads["v"],
        grads["so"],
        own_table.reshape(-1, H),
        own_crossnorm,
        grads["cq"],
        grads["ck"],
        grads["cv"],
        grads["co"],
        own_feednorm,
        grads["fin"],
        own_feedbias,
        grads["fout"],
        own_outbias,
    )


def solution(mesh):
    return jax.shard_map(
        per_device,
        mesh=mesh,
        in_specs=(
            P("wa", "ctx", None),
            P("wa", "ctx", None, None, None),
            P("wa", "ctx", None),
            P("wa"),
            P("wa", None),
            P("wa", None),
            P("wa", None),
            P("wa", None),
            P("wa", None),
            P("wa"),
            P("wa", None),
            P("wa", None),
            P("wa", None),
            P("wa", None),
            P("wa"),
            P("wa", None),
            P("wa"),
            P("wa", None),
            P("wa"),
        ),
        out_specs=(
            P("wa", "ctx", None),
            P("wa", "ctx", None),
            P("wa", "ctx", None, None, None),
            P("wa"),
            P("wa", None),
            P("wa", None),
            P("wa", None),
            P("wa", None),
            P("wa", None),
            P("wa"),
            P("wa", None),
            P("wa", None),
            P("wa", None),
            P("wa", None),
            P("wa"),
            P("wa", None),
            P("wa"),
            P("wa", None),
            P("wa"),
        ),
        check_vma=False,
    )
```

```python
import functools
import math

import jax
import jax.numpy as jnp
from jax import lax
from jax.experimental import pallas as pl
from jax.experimental.pallas import tpu as pltpu
from jax.sharding import PartitionSpec as P

H = 16
HD = 64
NB = 32
MAXD = 128
BLOCK = 256
SPAN = 64
MESH = pl.DeviceIdType.MESH
WIDE = 128
LINE = 1024
BF = jnp.bfloat16
F32 = jnp.float32


epsilon = 1e-06
negative = -1e30
strongest_precision = lax.Precision.HIGHEST


def passed_along(value, axis, by):
    peers = lax.axis_size(axis)
    pairs = [(i, i + by) for i in range(peers) if 0 <= i + by < peers]
    return lax.ppermute(value, axis, pairs)


def from_behind(block, axis, distance):
    devices = range(lax.axis_size(axis))
    route = [((i - distance) % len(devices), i) for i in devices]
    return lax.ppermute(block, axis, route)


def bucket_edges():
    half_count = NB // 2
    exact_part = half_count // 2
    edge_list = []
    for level_index in range(exact_part + 1, half_count):
        hits = [
            distance_now
            for distance_now in range(exact_part, MAXD + 1)
            if exact_part
            + int(
                math.log(distance_now / exact_part)
                / math.log(MAXD / exact_part)
                * (half_count - exact_part)
            )
            >= level_index
        ]
        edge_list.append(min(hits + [MAXD]))
    return (half_count, exact_part, edge_list)


def bucket_of(offset_value):
    half_count, exact_part, edge_list = bucket_edges()
    magnitude = jnp.abs(offset_value)
    far_part = exact_part + sum(
        [(magnitude >= edge_value).astype(magnitude.dtype) for edge_value in edge_list],
        jnp.zeros_like(magnitude),
    )
    return jnp.where(offset_value > 0, half_count, 0) + jnp.where(
        magnitude < exact_part, magnitude, far_part
    )


def root_norm(values, gain_vector):
    return (
        values
        * lax.rsqrt(jnp.mean(values * values, axis=-1, keepdims=True) + epsilon)
        * gain_vector
    )


def gelu_tanh(values):
    return jax.nn.gelu(values, approximate=True)


def forward_product(values, weight):
    return jnp.dot(values, weight, preferred_element_type=jnp.float32)


def outer_product(left_side, right_side):
    return lax.dot_general(
        left_side, right_side, (((0,), (0,)), ((), ())), preferred_element_type=jnp.float32
    )


def back_product(grad_low, weight):
    return lax.dot_general(
        grad_low, weight, (((1,), (1,)), ((), ())), preferred_element_type=jnp.float32
    )


def make_bias(bucket_bias_rows, row_count):
    query_place = jnp.arange(row_count)[:, None]
    key_place = jnp.arange(row_count)[None, :]
    levels = jnp.arange(NB)
    current_bucket_selector = (
        bucket_of(key_place - query_place)[None] == levels[:, None, None]
    ).astype(jnp.float32)
    previous_bucket_selector = (
        bucket_of(key_place - row_count - query_place)[None] == levels[:, None, None]
    ).astype(jnp.float32)
    onehot_far = (bucket_of(jnp.array(-MAXD, jnp.int32)) == levels).astype(jnp.float32)
    current_block_bias = jnp.einsum(
        "smz,sj->jmz", current_bucket_selector, bucket_bias_rows, precision=strongest_precision
    )
    previous_block_bias = jnp.einsum(
        "smz,sj->jmz", previous_bucket_selector, bucket_bias_rows, precision=strongest_precision
    )
    bias_far = jnp.dot(onehot_far, bucket_bias_rows, precision=strongest_precision)
    mask_same = key_place // BLOCK <= query_place // BLOCK
    return (
        (current_block_bias, previous_block_bias, bias_far, mask_same),
        (current_bucket_selector, previous_bucket_selector, onehot_far),
    )


def pair_scores(query_heads, key_heads, relation, bias_set, scale_factor):
    current_block_bias, previous_block_bias, bias_far, mask_same = bias_set
    raw_scores = jnp.einsum(
        "qhd,khd->hqk", query_heads, key_heads, preferred_element_type=jnp.float32
    )
    bias_rows = jnp.where(
        relation == 0,
        current_block_bias,
        jnp.where(relation == 1, previous_block_bias, bias_far[:, None, None]),
    )
    allowed = jnp.logical_or(relation > 0, mask_same)
    return jnp.where(allowed[None], raw_scores * scale_factor + bias_rows, negative)


def pair_core(
    query_heads,
    dout_heads,
    log_total,
    row_delta,
    key_heads,
    value_heads,
    relation,
    bias_set,
    scale_factor,
):
    scores = pair_scores(query_heads, key_heads, relation, bias_set, scale_factor)
    weights_now = jnp.exp(scores - log_total[:, :, None])
    grad_weights = jnp.einsum(
        "qhd,khd->hqk", dout_heads, value_heads, preferred_element_type=jnp.float32
    )
    dscores = weights_now * (grad_weights - row_delta[:, :, None])
    return (weights_now, dscores, (dscores * scale_factor).astype(jnp.bfloat16))


def add_tables(relative_bias_tables, dscores, relation):
    same_sum, prev_sum, far_sum = relative_bias_tables
    return (
        same_sum + jnp.where(relation == 0, dscores, 0.0),
        prev_sum + jnp.where(relation == 1, dscores, 0.0),
        far_sum + jnp.where(relation >= 2, jnp.sum(dscores, axis=(1, 2)), 0.0),
    )


def forward_fold(query_heads, position, row_count, bias_set, scale_factor, running, pieces):
    keys_all, values_all = pieces

    def one_shard(folded, shard_step):
        key_heads = lax.dynamic_slice_in_dim(
            keys_all, shard_step * row_count, row_count, 0
        ).reshape(row_count, H, HD)
        value_heads = lax.dynamic_slice_in_dim(
            values_all, shard_step * row_count, row_count, 0
        ).reshape(row_count, H, HD)
        relation = position - shard_step

        def one_compute(current):
            running_max, running_sum, running_acc = current
            scores = pair_scores(query_heads, key_heads, relation, bias_set, scale_factor)
            new_max = jnp.maximum(running_max, jnp.max(scores, axis=-1))
            factor = jnp.exp(running_max - new_max)
            weights_now = jnp.exp(scores - new_max[:, :, None])
            new_sum = running_sum * factor + jnp.sum(weights_now, axis=-1)
            update = jnp.einsum(
                "hqk,khd->qhd",
                weights_now.astype(jnp.bfloat16),
                value_heads,
                preferred_element_type=jnp.float32,
            )
            scaled = running_acc.reshape(row_count, H, HD) * factor.T[:, :, None]
            return (new_max, new_sum, (scaled + update).reshape(row_count, H * HD))

        return (lax.cond(relation >= 0, one_compute, lambda unchanged: unchanged, folded), None)

    running, unused = lax.scan(one_shard, running, jnp.arange(keys_all.shape[0] // row_count))
    return running


def nt_dot(left, right):
    return lax.dot_general(left, right, (((1,), (1,)), ((), ())), preferred_element_type=F32)


def nn_dot(left, right):
    return jnp.dot(left, right, preferred_element_type=F32)


def meet(neighbours):
    barrier = pltpu.get_barrier_semaphore()
    for who in neighbours:
        pl.semaphore_signal(barrier, inc=1, device_id=who, device_id_type=MESH)
    pl.semaphore_wait(barrier, len(neighbours))


def ctx_peers(n):
    me = lax.axis_index("ctx")
    return [{"ctx": lax.rem(me + d, n)} for d in range(1, n)]


def other_wa(me, bit):
    flipped = lax.rem(me // bit, 2)
    return me + bit - 2 * bit * flipped


def remote(src, dst, send_sem, recv_sem, **device):
    return pltpu.make_async_remote_copy(
        src_ref=src,
        dst_ref=dst,
        send_sem=send_sem,
        recv_sem=recv_sem,
        device_id=device,
        device_id_type=MESH,
    )


RING = 8
HOPS = RING - 1


def ring_place(n):
    me = lax.axis_index("ctx")
    half = n // 2

    def at(place):
        return jnp.where(place < half, 2 * place, 2 * (n - 1 - place) + 1)

    place = jnp.where(lax.rem(me, 2) == 0, me // 2, n - 1 - me // 2)
    return place, at(lax.rem(place + 1, n)), at(lax.rem(place + n - 1, n))


class Ring:
    def __init__(self, lanes, send, recv, share=None, hold=None, full=None):
        self.lanes, self.share, self.hold, self.full = lanes, share, hold, full
        self.sems = send, recv
        self.place, self.after, self.before = ring_place(RING)

    def copy(self, lane, src, dst, step):
        send, recv = self.sems
        way = self.lanes[lane][1]
        return remote(
            src, dst, send.at[lane, step], recv.at[lane, step], ctx=self.after if way == 1 else self.before
        )

    def chunk(self, lane, offset):
        here = self.place if self.lanes[lane][1] == 1 else RING - self.place
        return lax.rem(here + offset + 2 * RING, RING)

    def scatter(self, step, which):
        for lane in which:
            b, _, rows = self.lanes[lane]
            share = self.share.at[b, self.chunk(lane, -step), rows]

            @pl.when(step > 0)
            def _():
                there = self.hold.at[b, jnp.maximum(step - 1, 0), rows]
                self.copy(lane, share, there, jnp.maximum(step - 1, 0)).wait_recv()
                share[...] = (share[...].astype(F32) + there[...].astype(F32)).astype(BF)

            @pl.when(step < HOPS)
            def _():
                there = jnp.minimum(step, HOPS - 1)
                self.copy(lane, share, self.hold.at[b, there, rows], there).start()

    def gather(self, step, which):
        for lane in which:
            b, _, rows = self.lanes[lane]
            full = self.full[b].at[self.chunk(lane, 1 - step), rows]

            @pl.when(step > 0)
            def _():
                self.copy(lane, full, full, jnp.maximum(step - 1, 0)).wait_recv()

            @pl.when(step < HOPS)
            def _():
                self.copy(lane, full, full, jnp.minimum(step, HOPS - 1)).start()

    def finish(self, part):
        def one(step, unused):
            for lane in range(len(self.lanes)):
                self.copy(lane, part(lane), part(lane), step).wait_send()
            return unused

        lax.fori_loop(0, HOPS, one, 0)


TALL, FLAT = (224, 1024), (256, 896)
EARLY = ("ck", "cv", "cq", "co", "so")
MADE = ("cq", "co", "so")
LATE = ("q", "k", "v")
FEED = (8, 112, 896)
FEED_LANES = (
    (0, 1, slice(0, 64)),
    (1, -1, slice(0, 64)),
    (0, 1, slice(64, 112)),
    (1, -1, slice(64, 112)),
)
FEED_TURNS = ((0, 1), (2, 3))


def product_into(out_ref, left, right):
    for c in range(left.shape[1] // WIDE):
        lanes = slice(c * WIDE, (c + 1) * WIDE)
        turned = left[:, lanes].astype(F32).T.astype(BF)
        out_ref[lanes, :] = nn_dot(turned, right[...]).astype(BF)


class Folding:
    def __init__(self, names, parts, scratch):
        self.names = names
        self.parts = parts
        tall, flat, sems = scratch
        self.sets = {TALL: tall, FLAT: flat}
        self.own_sem, self.core_send, self.core_recv, self.x_send, self.x_recv = sems
        self.wa = lax.axis_index("wa")
        self.mate, self.across = other_wa(self.wa, 1), other_wa(self.wa, 2)
        self.core, self.half = lax.rem(self.wa, 2), self.wa // 2
        self.slots, count = {}, {TALL: 0, FLAT: 0}
        for name in names:
            shape = self.shape_of(name)
            self.slots[name] = (count[shape], self.sets[shape])
            count[shape] += 1
        self.own_copies, self.core_copies, self.x_copies = {}, {}, {}

    @staticmethod
    def shape_of(name):
        return FLAT if name in ("co", "so") else TALL

    @classmethod
    def scratch(cls, names):
        shapes = []
        for shape in (TALL, FLAT):
            many = sum(cls.shape_of(name) == shape for name in names)
            if many:
                shapes += [pltpu.VMEM((many, 2, *shape), BF)] * 2 + [pltpu.VMEM((many, *shape), BF)] * 2
        dma = pltpu.SemaphoreType.DMA
        many = len(names)
        return shapes + [dma((many, 2))] * 3 + [dma((many,))] * 2

    def start(self, *names):
        for name in names:
            u = self.names.index(name)
            slot, (own, inn, _, _) = self.slots[name]
            rows = self.shape_of(name)[0]
            for x in range(2):
                mine = pl.ds(pl.multiple_of((2 * x + self.core) * rows, 16), rows)
                theirs = pl.ds(pl.multiple_of((2 * x + 1 - self.core) * rows, 16), rows)
                copy = remote(
                    self.parts[name].at[theirs],
                    inn.at[slot, x],
                    self.core_send.at[u, x],
                    self.core_recv.at[u, x],
                    wa=self.mate,
                )
                copy.start()
                self.core_copies[name, x] = copy
                copy = pltpu.make_async_copy(
                    self.parts[name].at[mine], own.at[slot, x], self.own_sem.at[u, x]
                )
                copy.start()
                self.own_copies[name, x] = copy
            slot, (_, _, out, land) = self.slots[name]
            self.x_copies[name] = remote(
                out.at[slot], land.at[slot], self.x_send.at[u], self.x_recv.at[u], wa=self.across
            )

    def send(self, name):
        self.prepare(name)
        self.x_copies[name].start()

    def prepare(self, name):
        slot, (own, inn, out, _) = self.slots[name]
        for x in range(2):
            self.own_copies[name, x].wait()
            self.core_copies[name, x].wait_recv()
        away = 1 - self.half
        out[slot] = (own[slot, away].astype(F32) + inn[slot, away].astype(F32)).astype(BF)

    def total(self, name):
        slot, (own, inn, _, land) = self.slots[name]
        self.x_copies[name].wait_recv()
        here = self.half
        return (
            own[slot, here].astype(F32) + inn[slot, here].astype(F32) + land[slot].astype(F32)
        ).astype(BF)

    def finish(self):
        for name in self.names:
            for x in range(2):
                self.core_copies[name, x].wait_send()
            self.x_copies[name].wait_send()


class Moves:
    def __init__(self, sem):
        self.sem, self.count = sem, 0

    def start(self, src, dst):
        copy = pltpu.make_async_copy(src, dst, self.sem.at[self.count])
        copy.start()
        self.count += 1
        return copy


def wait_all(copies):
    for copy in copies:
        copy.wait()


def lasting(microseconds):
    return pl.CostEstimate(
        flops=0, bytes_accessed=int(microseconds * 3.0e6), transcendentals=0
    )


def lanes_of(index):
    return pl.ds(pl.multiple_of(index * WIDE, WIDE), WIDE)


def rows_of(index, rows):
    return pl.ds(pl.multiple_of(index * rows, rows), rows)


def to_ctx(src, dst, send_sem, recv_sem, target):
    return pltpu.make_async_remote_copy(
        src_ref=src,
        dst_ref=dst,
        send_sem=send_sem,
        recv_sem=recv_sem,
        device_id={"ctx": target},
        device_id_type=MESH,
    )


def head_mask(h, rows):
    lane = lax.broadcasted_iota(jnp.int32, (rows, WIDE), 1)
    return (lane < HD) if h == 0 else (lane >= HD)


def bias_tiles(bias_ref, me, tiles):
    for h in range(2):
        line = bias_ref[pl.ds(2 * me + h, 1), :]
        rolled = pltpu.roll(
            jnp.broadcast_to(line, (BLOCK, LINE)), 0, 1, stride=1, stride_axis=0
        )
        tiles[h, 0] = rolled[:, :BLOCK]
        tiles[h, 1] = rolled[:, BLOCK : 2 * BLOCK]
        tiles[h, 2] = jnp.broadcast_to(line[:, WIDE : WIDE + BLOCK], (BLOCK, BLOCK))


def spread(n, me, pairs, send, recv, t):
    src, dst = pairs[t]
    for d in range(1, n):
        peer = lax.rem(me + d, n)
        to_ctx(
            src.at[:, lanes_of(peer)], dst.at[rows_of(me, BLOCK)], send.at[t, d], recv.at[t, d], peer
        ).start()
    dst[rows_of(me, BLOCK), :] = src[:, lanes_of(me)]


GATHERED = ("q", "k", "v", "so", "ck", "cv", "cq", "co")
SINGLE = ("cot",)
GAINS = ("selfnorm", "crossnorm", "feednorm", "outbias")


class Gathering:
    def __init__(self, shards, whole, own_sem, send, recv):
        self.names, self.shards, self.whole = tuple(shards), shards, whole
        self.sems = own_sem, send, recv
        self.wa, me = lax.axis_index("wa"), lax.axis_index("ctx")
        self.mate, self.across = other_wa(self.wa, 1), other_wa(self.wa, 2)
        y, z = lax.rem(me, 2), lax.rem(me // 2, 2)
        self.pairs = ((y, me + 1 - 2 * y), (z, me + 2 - 4 * z))
        self.copies = {}

    def start(self):
        own_sem, send, recv = self.sems
        for u, name in enumerate(self.names):
            part, beside = self.pairs[(u + 1) % 2]
            shard, whole = self.shards[name], self.whole[name]
            rows = shard.shape[0]
            parts = 1 if name in SINGLE else 2
            some = rows // parts
            shift = 0 if parts == 1 else part * some

            def at(start, count, ref=whole):
                return ref.at[pl.ds(pl.multiple_of(start, 16), count)]

            mine = at(self.wa * rows, rows)
            theirs = at(self.across * rows, rows)
            theirs_some = at(self.across * rows + shift, some)
            self.copies[name] = {
                "over": remote(
                    at(shift, some, shard), at(self.wa * rows + shift, some), send.at[u, 0], recv.at[u, 0], wa=self.across
                ),
                "near": remote(shard, mine, send.at[u, 1], recv.at[u, 1], wa=self.mate),
                "pass": remote(theirs, theirs, send.at[u, 2], recv.at[u, 2], wa=self.mate),
                "side": remote(theirs_some, theirs_some, send.at[u, 3], recv.at[u, 3], ctx=beside),
                "own": pltpu.make_async_copy(shard, mine, own_sem.at[u]),
            }
            self.copies[name]["near"].start()
            self.copies[name]["own"].start()

    def cross(self, *names):
        for name in names:
            self.copies[name]["over"].start()

    def forward(self, *names):
        for name in names:
            self.copies[name]["over"].wait_recv()
            self.copies[name]["pass" if name in SINGLE else "side"].start()

    def land(self, *names):
        for name in names:
            self.copies[name]["side"].wait_recv()
            self.copies[name]["pass"].start()

    def arrive(self, *names):
        for name in names:
            self.copies[name]["near"].wait_recv()
            self.copies[name]["pass"].wait_recv()
            self.copies[name]["own"].wait()

    def finish(self):
        for name, copies in self.copies.items():
            for which in ("over", "near", "pass") + (() if name in SINGLE else ("side",)):
                copies[which].wait_send()


class Columns:
    def __init__(self, gathering, shard, whole, send, recv):
        wa, mate, across = gathering.wa, gathering.mate, gathering.across
        both = other_wa(across, 1)
        rows, width = shard.shape[0], whole.shape[1]
        some = rows // 2

        def block(owner, columns):
            return shard.at[owner, pl.ds(pl.multiple_of(columns * width, WIDE), width)]

        def at(start, count):
            return whole.at[pl.ds(pl.multiple_of(start, 16), count)]

        everything = slice(0, rows)
        self.own = pltpu.make_async_copy(block(everything, wa), at(wa * rows, rows), send.at[5])
        self.near = remote(block(everything, mate), at(wa * rows, rows), send.at[0], recv.at[0], wa=mate)
        self.over, self.side = [], []
        for d, peer in enumerate((across, both)):
            part, beside = gathering.pairs[d]
            mine = pl.ds(pl.multiple_of(part * some, 16), some)
            gone, got = at(wa * rows + part * some, some), at(peer * rows + part * some, some)
            self.over.append(remote(block(mine, peer), gone, send.at[1 + d], recv.at[1 + d], wa=peer))
            self.side.append(remote(got, got, send.at[3 + d], recv.at[3 + d], ctx=beside))

    def start(self):
        self.own.start()
        self.near.start()

    def cross(self):
        for copy in self.over:
            copy.start()

    def forward(self):
        for over, side in zip(self.over, self.side, strict=True):
            over.wait_recv()
            side.start()

    def finish(self):
        self.own.wait()
        self.near.wait()
        for over, side in zip(self.over, self.side, strict=True):
            side.wait()
            over.wait_send()


def attn_forward_kernel(n, tokens_ref, small_ref, near_far, *refs):
    shards = dict(zip((*GATHERED, "cot"), refs[:9], strict=True))
    feed_ref = refs[9]
    wholes = dict(zip((*GATHERED, "cot"), refs[10:19], strict=True))
    feed_whole = refs[19]
    o_ref, low_ref, ot_out, lse_out, small_out, before_ref, qh_out, kh_out, vh_out, keys_out, values_out = refs[20:31]
    (
        held_q, held_k, held_v, held_ck, held_cv, proj, small_in, small_mid, qh, kh, vh, vt, oh, land, tiles,
        acc, stat, send, recv, osend, orecv, small_sem, own_sem, out_sem, gather_send, gather_recv, feed_send,
        feed_recv, span_sem, near_ref, keys_ref, values_ref, move_sem,
    ) = refs[31:]
    moves = Moves(move_sem)
    load_near = moves.start(near_far, near_ref)
    held = {"q": held_q, "k": held_k, "v": held_v, "ck": held_ck, "cv": held_cv}
    gathering = Gathering(shards, wholes | held, own_sem, gather_send, gather_recv)
    columns = Columns(gathering, feed_ref, feed_whole, feed_send, feed_recv)
    both = other_wa(gathering.across, 1)
    meet([*ctx_peers(n), *({"wa": peer} for peer in (gathering.mate, gathering.across, both))])
    me = lax.axis_index("ctx")
    near = remote(small_ref, small_in.at[0], small_sem.at[0], small_sem.at[1], wa=gathering.mate)
    near.start()
    gathering.start()
    gathering.cross("q")
    columns.start()
    span_rows = before_ref.shape[0]
    span = remote(
        near_far.at[near_far.shape[0] - span_rows :],
        before_ref,
        span_sem.at[0],
        span_sem.at[1],
        ctx=lax.rem(me + 1, n),
    )
    over = remote(small_mid, small_in.at[1], small_sem.at[2], small_sem.at[3], wa=gathering.across)
    near.wait_recv()
    small_mid[...] = (small_ref[...].astype(F32) + small_in[0].astype(F32)).astype(BF)
    over.start()
    over.wait_recv()
    small_out[...] = small_mid[...].astype(F32) + small_in[1].astype(F32)
    bias_ref = small_out
    values = tokens_ref[...].astype(F32)
    width = values.shape[1]
    norm = lax.rsqrt(jnp.mean(values * values, axis=1, keepdims=True) + epsilon)
    low_ref[...] = (values * norm * small_out[H : H + 1, :width]).astype(BF)
    bias_tiles(bias_ref, me, tiles)
    pairs = tuple((proj.at[t], dst) for t, dst in enumerate((qh, kh, vh)))
    saving = []

    def save(name):
        copy = pltpu.make_async_copy(held[name], wholes[name], out_sem.at[len(saving)])
        copy.start()
        saving.append(copy)

    def project(t, name):
        gathering.land(name)
        gathering.arrive(name)
        proj[t] = nn_dot(low_ref[...], held[name][...]).astype(BF)
        spread(n, me, pairs, send, recv, t)
        save(name)

    gathering.forward("q")
    gathering.cross("k")
    gathering.forward("k")
    gathering.cross("v")
    project(0, "q")
    gathering.forward("v")
    gathering.cross("so", "ck")
    project(1, "k")
    project(2, "v")

    gathering.forward("so", "ck")
    gathering.cross("cv", "cq")

    for d in range(1, n):
        peer = lax.rem(me + n - d, n)
        for t, (src, dst) in enumerate(pairs):
            to_ctx(
                src.at[:, lanes_of(peer)], dst.at[rows_of(peer, BLOCK)], send.at[t, d], recv.at[t, d], peer
            ).wait_recv()
    stores = [moves.start(*pair) for pair in ((qh, qh_out), (kh, kh_out), (vh, vh_out))]
    for i in range(n):
        part = slice(i * BLOCK, (i + 1) * BLOCK)
        vt[:, part] = vh[part, :].astype(F32).T.astype(BF)

    def query_block(step, unused):
        @pl.when((step == 0) & (me < n - 1))
        def _():
            span.start()

        @pl.when(step == 1)
        def _():
            gathering.forward("cv", "cq")
            gathering.land("so", "ck")
            gathering.cross("co")
            columns.cross()

        @pl.when(step == 6)
        def _():
            gathering.land("cv", "cq")
            gathering.forward("co")
            columns.forward()
            gathering.cross("cot")

        i = lax.rem(me + 1 + step, n)
        rows = rows_of(i, BLOCK)
        q_now = qh[rows, :] * BF(HD**-0.5)
        masked = [jnp.where(head_mask(h, BLOCK), q_now, BF(0)) for h in range(2)]

        def fold(j, which, first):
            keys = kh[rows_of(j, BLOCK), :]
            for h in range(2):
                scores = nt_dot(keys, masked[h])
                if which is None:
                    scores = scores + bias_ref[pl.ds(2 * me + h, 1), WIDE : WIDE + BLOCK]
                else:
                    scores = scores + tiles[h, which]
                top = jnp.max(scores, axis=0, keepdims=True)
                if not first:
                    old = stat[h : h + 1, :]
                    top = jnp.maximum(old, top)
                weights = jnp.exp(scores - top)
                total = jnp.sum(weights, axis=0, keepdims=True)
                vals = vt[h * HD : (h + 1) * HD, rows_of(j, BLOCK)]
                mixed = nn_dot(vals, weights.astype(BF))
                if not first:
                    factor = jnp.exp(old - top)
                    total = total + stat[2 + h : 3 + h, :] * factor
                    mixed = mixed + acc[h * HD : (h + 1) * HD, :] * factor
                stat[h : h + 1, :] = top
                stat[2 + h : 3 + h, :] = total
                acc[h * HD : (h + 1) * HD, :] = mixed

        fold(i, 0, True)

        @pl.when(i >= 1)
        def _():
            fold(i - 1, 1, False)

        def far(j, unused):
            fold(j, None, False)
            return unused

        lax.fori_loop(0, i - 1, far, 0)
        for h in range(2):
            total = stat[2 + h : 3 + h, :]
            part = acc[h * HD : (h + 1) * HD, :] / total
            acc[h * HD : (h + 1) * HD, :] = part
            lse_out[h : h + 1, rows] = stat[h : h + 1, :] + jnp.log(total)
        done = acc[...]
        ot_out[:, rows] = done
        oh[rows, :] = done.T.astype(BF)

        @pl.when(i != me)
        def _():
            d = lax.rem(i - me + n, n)
            to_ctx(oh.at[rows], land.at[:, lanes_of(me)], osend.at[d], orecv.at[d], i).start()

        @pl.when(i == me)
        def _():
            land[:, lanes_of(me)] = oh[rows, :]

        return unused

    lax.fori_loop(0, n, query_block, 0)
    load_near.wait()

    @pl.when(me > 0)
    def _():
        span.wait_recv()

    @pl.when(me == 0)
    def _():
        before_ref[...] = jnp.zeros_like(before_ref)

    for name, out_ref, far_ref in (("ck", keys_ref, keys_out), ("cv", values_ref, values_out)):
        gathering.arrive(name)
        save(name)
        out_ref[:span_rows, :] = nn_dot(before_ref[...], held[name][...]).astype(BF)
        for g in range(near_ref.shape[0] // span_rows):
            rows = slice(g * span_rows, (g + 1) * span_rows)
            there = slice((g + 1) * span_rows, (g + 2) * span_rows)
            out_ref[there, :] = nn_dot(near_ref[rows, :], held[name][...]).astype(BF)
        stores.append(moves.start(out_ref, far_ref))
    gathering.land("co")
    gathering.forward("cot")
    for d in range(1, n):
        peer = lax.rem(me + d, n)
        for t, (src, dst) in enumerate(pairs):
            to_ctx(
                src.at[:, lanes_of(peer)], dst.at[rows_of(me, BLOCK)], send.at[t, d], recv.at[t, d], peer
            ).wait_send()
        back = to_ctx(
            oh.at[rows_of(peer, BLOCK)], land.at[:, lanes_of(me)], osend.at[d], orecv.at[d], peer
        )
        back.wait_send()
        back.wait_recv()
    o_ref[...] = land[...]
    gathering.arrive("so", "cq", "co", "cot")
    gathering.finish()
    columns.finish()

    @pl.when(me < n - 1)
    def _():
        span.wait_send()

    near.wait_send()
    over.wait_send()
    wait_all(saving + stores)


def vmem(count):
    return [pl.BlockSpec(memory_space=pltpu.VMEM)] * count


def attn_forward(n, tokens, small, near, shards, feed):
    rows, seq = tokens.shape[0], n * tokens.shape[0]
    owners = lax.axis_size("wa")
    low = functools.partial(jax.ShapeDtypeStruct, dtype=BF)
    heads = low((seq, WIDE))
    wholes = [low((owners * s.shape[0], s.shape[1])) for s in shards]
    width = wholes[0].shape[1]
    dma = pltpu.SemaphoreType.DMA
    span_rows = 256
    keys = low((span_rows + near.shape[0], width))
    any_spec = pl.BlockSpec(memory_space=pl.ANY)
    return pl.pallas_call(
        functools.partial(attn_forward_kernel, n),
        out_shape=(
            *wholes,
            low((owners * feed.shape[0], feed.shape[1] // owners)),
            low((rows, width)),
            low(tokens.shape),
            jax.ShapeDtypeStruct((WIDE, seq), F32),
            jax.ShapeDtypeStruct((8, seq), F32),
            jax.ShapeDtypeStruct(small.shape, F32),
            low((span_rows, near.shape[1])),
            heads,
            heads,
            heads,
            keys,
            keys,
        ),
        in_specs=vmem(2) + [any_spec] * 11,
        out_specs=tuple([any_spec] * 10 + vmem(6) + [any_spec] * 5),
        scratch_shapes=[
            *[pltpu.VMEM(wholes[0].shape, BF)] * 5,
            pltpu.VMEM((3, rows, width), BF),
            pltpu.VMEM((2, *small.shape), BF),
            pltpu.VMEM(small.shape, BF),
            pltpu.VMEM((seq, WIDE), BF),
            pltpu.VMEM((seq, WIDE), BF),
            pltpu.VMEM((seq, WIDE), BF),
            pltpu.VMEM((WIDE, seq), BF),
            pltpu.VMEM((seq, WIDE), BF),
            pltpu.VMEM((rows, width), BF),
            pltpu.VMEM((2, 3, BLOCK, BLOCK), F32),
            pltpu.VMEM((WIDE, BLOCK), F32),
            pltpu.VMEM((8, BLOCK), F32),
            dma((3, n)),
            dma((3, n)),
            dma((n,)),
            dma((n,)),
            dma((4,)),
            dma((9,)),
            dma((5,)),
            dma((9, 4)),
            dma((9, 4)),
            dma((6,)),
            dma((5,)),
            dma((2,)),
            pltpu.VMEM(near.shape, BF),
            pltpu.VMEM(keys.shape, BF),
            pltpu.VMEM(keys.shape, BF),
            dma((6,)),
        ],
        compiler_params=pltpu.CompilerParams(
            collective_id=1, has_side_effects=True, vmem_limit_bytes=60 << 20
        ),
        cost_estimate=lasting(85),
        name="attn_forward",
    )(tokens, small, near, *shards, feed)


def attn_backward_kernel(n, do_ref, lse_ref, bias_ref, feed_part, *rest):
    far = rest[:10]
    span_far = rest[12]
    line_ref, *outs = rest[13:23]
    rest = rest[2:]
    near = rest[21:31]
    kh, qh, ot_ref, vh = near[:4]
    given = dict(zip(MADE, zip(near[4::2], near[5::2], strict=True), strict=True))
    tall_pair, tall_one, flat_out, *feed_full, move_sem = rest[31:37]
    (
        doh, kt, stage, land, dk_acc, dv_acc, dq_acc, q_masked, do_masked, delta, tiles, dtiles,
        send, recv, gsend, grecv, ring_send, ring_recv,
    ) = rest[37:55]
    made = dict(zip(MADE, rest[55:58], strict=True))
    parts = dict(zip(EARLY, (rest[8], rest[9], *made.values()), strict=True))
    span_ref, span_sem = rest[58:60]
    extra = rest[60:]
    moves = Moves(move_sem)
    loads = [moves.start(*pair) for pair in zip(far, near, strict=True)]
    fold_wa = Folding(EARLY, parts, (extra[0:4], extra[4:8], extra[8:13]))
    ring = Ring(FEED_LANES, ring_send, ring_recv, full=feed_full)
    for lane in range(2):
        feed_full[lane][ring.chunk(lane, 1)] = feed_part[lane]
    meet([*ctx_peers(n), {"wa": fold_wa.mate}, {"wa": fold_wa.across}])
    me = lax.axis_index("ctx")
    pairs = ((do_ref, doh),)
    spread(n, me, pairs, send, recv, 0)
    fold_wa.start("ck", "cv")
    bias_tiles(bias_ref, me, tiles)
    loads[0].wait()
    for j in range(n):
        part = slice(j * BLOCK, (j + 1) * BLOCK)
        kt[:, part] = (kh[part, :].astype(F32) * HD**-0.5).T.astype(BF)
    dtiles[...] = jnp.zeros_like(dtiles)
    for name in EARLY[:2]:
        fold_wa.send(name)
    ring.gather(jnp.int32(0), FEED_TURNS[0])
    ring.gather(jnp.int32(0), FEED_TURNS[1])
    wait_all(loads[1:])
    for name in MADE:
        product_into(made[name], *given[name])
        fold_wa.start(name)
    dq_acc[...] = jnp.zeros_like(dq_acc)
    for d in range(1, n):
        peer = lax.rem(me + n - d, n)
        to_ctx(
            do_ref.at[:, lanes_of(peer)], doh.at[rows_of(peer, BLOCK)], send.at[0, d], recv.at[0, d], peer
        ).wait_recv()
    for i in range(n):
        rows = slice(i * BLOCK, (i + 1) * BLOCK)
        q_now = qh[rows, :] * BF(HD**-0.5)
        do_now = doh[rows, :]
        products = do_now.astype(F32).T * ot_ref[:, rows]
        for h in range(2):
            mask = head_mask(h, BLOCK)
            q_masked[h, rows, :] = jnp.where(mask, q_now, BF(0))
            do_masked[h, rows, :] = jnp.where(mask, do_now, BF(0))
            delta[h : h + 1, rows] = jnp.sum(
                products[h * HD : (h + 1) * HD], axis=0, keepdims=True
            )

    span = remote(
        span_far, span_ref, span_sem.at[0], span_sem.at[1], ctx=lax.rem(me + n - 1, n)
    )

    def pair(t, now):
        i, j = now

        @pl.when((t == 24) & (me > 0))
        def _():
            span.start()

        rows, there = rows_of(i, BLOCK), rows_of(j, BLOCK)

        @pl.when(t == 6)
        def _():
            for name in EARLY[2:]:
                fold_wa.send(name)

        for turn, lanes in enumerate(FEED_TURNS):

            @pl.when((lax.rem(t, 4) == 2 * turn + 1) & (t <= 4 * HOPS))
            def _():
                ring.gather(t // 4 + 1, lanes)

        first = i == j
        which = jnp.minimum(i - j, 2)
        keys, vals = kh[there, :], vh[there, :]
        dk_part, dv_part = None, None
        for h in range(2):
            query, dout = q_masked[h, rows, :], do_masked[h, rows, :]
            scores = nt_dot(keys, query)
            weights = jnp.exp(scores + tiles[h, which] - lse_ref[h : h + 1, rows])
            dweights = nt_dot(vals, dout)
            dscores = weights * (dweights - delta[h : h + 1, rows])
            dtiles[h, which] += dscores
            low = dscores.astype(BF)
            dv_now = nn_dot(weights.astype(BF), dout)
            dk_now = nn_dot(low, query)
            dv_part = dv_now if dv_part is None else dv_part + dv_now
            dk_part = dk_now if dk_part is None else dk_part + dk_now
            half = slice(h * HD, (h + 1) * HD)
            dq_acc[half, rows] += nn_dot(kt[half, there], low)

        @pl.when(first)
        def _():
            dk_acc[...] = dk_part
            dv_acc[...] = dv_part

        @pl.when(jnp.logical_not(first))
        def _():
            dk_acc[...] += dk_part
            dv_acc[...] += dv_part

        last = i == n - 1

        @pl.when(last)
        def _():
            stage[1, there, :] = dk_acc[...].astype(BF)
            stage[2, there, :] = dv_acc[...].astype(BF)
            deliver(j, (1, 2))

        after = lax.rem(j + 1, n)
        return jnp.where(last, after, i + 1), jnp.where(last, after, j)

    def deliver(i, arrays):
        rows = rows_of(i, BLOCK)

        @pl.when(i != me)
        def _():
            d = lax.rem(i - me + n, n)
            for t in arrays:
                to_ctx(
                    stage.at[t, rows], land.at[t, :, lanes_of(me)], gsend.at[t, d], grecv.at[t, d], i
                ).start()

        @pl.when(i == me)
        def _():
            for t in arrays:
                land[t, :, lanes_of(me)] = stage[t, rows, :]

    begin = lax.rem(me + 1, n)
    lax.fori_loop(0, n * (n + 1) // 2, pair, (begin, begin))

    def dq_block(step, unused):
        i = lax.rem(me + 1 + step, n)
        rows = rows_of(i, BLOCK)
        stage[0, rows, :] = dq_acc[:, rows].T.astype(BF)
        deliver(i, (0,))
        return unused

    lax.fori_loop(0, n, dq_block, 0)
    ring.finish(lambda lane: feed_full[FEED_LANES[lane][0]].at[0, FEED_LANES[lane][2]])
    stores = [moves.start(full, out) for full, out in zip(feed_full, outs[6:8], strict=True)]
    tall_pair[:224, :] = fold_wa.total("cq")
    tall_pair[224:, :] = fold_wa.total("ck")
    tall_one[...] = fold_wa.total("cv")
    for at, name in ((0, "co"), (32, "so")):
        flat_out[:, at : at + 32, :] = fold_wa.total(name).reshape(8, 32, 896)
    stores += [
        moves.start(tall_pair, outs[3]),
        moves.start(tall_one, outs[4]),
        moves.start(flat_out, outs[5]),
    ]
    fold_wa.finish()
    for h in range(2):
        line = jnp.concatenate(
            [dtiles[h, 0], dtiles[h, 1], jnp.zeros((BLOCK, LINE - 2 * BLOCK), F32)], axis=1
        )
        row = lax.broadcasted_iota(jnp.int32, (BLOCK, LINE), 0)
        for bit in range(8):
            moved = pltpu.roll(line, LINE - (1 << bit), 1)
            line = jnp.where((row >> bit) & 1 == 1, moved, line)
        line_ref[h : h + 1, :] = jnp.sum(line, axis=0, keepdims=True)
        line_ref[2 + h : 3 + h, :BLOCK] = jnp.sum(dtiles[h, 2], axis=0, keepdims=True)
    line_ref[2:4, BLOCK:] = jnp.zeros((2, LINE - BLOCK), F32)
    line_ref[4:8, :] = jnp.zeros((4, LINE), F32)
    for d in range(1, n):
        peer = lax.rem(me + d, n)
        to_ctx(
            do_ref.at[:, lanes_of(peer)], doh.at[rows_of(me, BLOCK)], send.at[0, d], recv.at[0, d], peer
        ).wait_send()
        for t in range(3):
            back = to_ctx(
                stage.at[t, rows_of(peer, BLOCK)], land.at[t, :, lanes_of(me)], gsend.at[t, d], grecv.at[t, d], peer
            )
            back.wait_send()
            back.wait_recv()
    stores += [moves.start(land.at[t], outs[t]) for t in range(3)]

    @pl.when(me < n - 1)
    def _():
        span.wait_recv()

    @pl.when(me == n - 1)
    def _():
        span_ref[...] = jnp.zeros_like(span_ref)

    stores.append(moves.start(span_ref, outs[8]))

    @pl.when(me > 0)
    def _():
        span.wait_send()

    wait_all(stores)


def attn_backward(n, dout, qh, kh, vh, ot, lse, bias_lines, parts, feed_part, span):
    rows, seq = dout.shape[0], n * dout.shape[0]
    grads = jax.ShapeDtypeStruct(dout.shape, BF)
    feed = jax.ShapeDtypeStruct(FEED, BF)
    low = functools.partial(jax.ShapeDtypeStruct, dtype=BF)
    any_spec = pl.BlockSpec(memory_space=pl.ANY)
    far = (kh, qh, ot, vh, *parts[2:])
    shares = (low((448, 1024)), low((224, 1024)), low((8, 64, 896)))
    line, *outs = pl.pallas_call(
        functools.partial(attn_backward_kernel, n),
        out_shape=(
            jax.ShapeDtypeStruct((8, LINE), F32),
            grads,
            grads,
            grads,
            *shares,
            feed,
            feed,
            low(span.shape),
        ),
        in_specs=vmem(4) + [any_spec] * 13,
        out_specs=tuple(vmem(1) + [any_spec] * 9),
        scratch_shapes=[
            *(pltpu.VMEM(v.shape, v.dtype) for v in far),
            *(pltpu.VMEM(v.shape, v.dtype) for v in (*shares, feed, feed)),
            pltpu.SemaphoreType.DMA((19,)),
            pltpu.VMEM((seq, WIDE), BF),
            pltpu.VMEM((WIDE, seq), BF),
            pltpu.VMEM((3, seq, WIDE), BF),
            pltpu.VMEM((3, *dout.shape), BF),
            pltpu.VMEM((BLOCK, WIDE), F32),
            pltpu.VMEM((BLOCK, WIDE), F32),
            pltpu.VMEM((WIDE, seq), F32),
            pltpu.VMEM((2, seq, WIDE), BF),
            pltpu.VMEM((2, seq, WIDE), BF),
            pltpu.VMEM((8, seq), F32),
            pltpu.VMEM((2, 3, BLOCK, BLOCK), F32),
            pltpu.VMEM((2, 3, BLOCK, BLOCK), F32),
            pltpu.SemaphoreType.DMA((1, n)),
            pltpu.SemaphoreType.DMA((1, n)),
            pltpu.SemaphoreType.DMA((3, n)),
            pltpu.SemaphoreType.DMA((3, n)),
            pltpu.SemaphoreType.DMA((len(FEED_LANES), HOPS)),
            pltpu.SemaphoreType.DMA((len(FEED_LANES), HOPS)),
            pltpu.VMEM((896, 1024), BF),
            pltpu.VMEM((1024, 896), BF),
            pltpu.VMEM((1024, 896), BF),
            pltpu.VMEM(span.shape, BF),
            pltpu.SemaphoreType.DMA((2,)),
            *Folding.scratch(EARLY),
        ],
        compiler_params=pltpu.CompilerParams(
            collective_id=2, has_side_effects=True, vmem_limit_bytes=60 << 20
        ),
        cost_estimate=lasting(100),
        name="attn_backward",
    )(dout, lse, bias_lines, feed_part, *far, *parts[:2], span)
    return *outs[:3], line, *outs[3:]


BUFFERS = {
    "cq": (1, (224, 1024)),
    "cv": (-1, (224, 1024)),
    "ck": (1, (224, 1024)),
    "co": (-1, (8, 32, 896)),
    "so0": (1, (8, 16, 896)),
    "so1": (-1, (8, 16, 896)),
}
NAMES = tuple(BUFFERS)


def chunk_shape(name):
    shape = BUFFERS[name][1]
    return (shape[0], WIDE) if len(shape) == 2 else shape[1:]


def chunk_of(ref, name, c):
    return ref.at[:, lanes_of(c)] if len(BUFFERS[name][1]) == 2 else ref.at[c]


class Grid:
    def __init__(self, u, share, half_in, half, quarters, whole, send, recv):
        self.u, self.share, self.half_in, self.half = u, share, half_in, half
        self.quarters, self.whole, self.sems = quarters, whole, (send, recv)
        me = lax.axis_index("ctx")
        self.y, self.z = lax.rem(me, 2), me // 2
        self.beside = me + 1 - 2 * self.y
        self.column = [lax.rem(self.z + d, 4) for d in range(1, 4)]

    def half_of(self, y):
        return pl.ds(pl.multiple_of(y * 4 * WIDE, WIDE), 4 * WIDE)

    def piece_of(self, z, y=None):
        start = z * WIDE if y is None else (4 * y + z) * WIDE
        return pl.ds(pl.multiple_of(start, WIDE), WIDE)

    def copy(self, number, src, dst, target):
        send, recv = self.sems
        return remote(src, dst, send.at[self.u, number], recv.at[self.u, number], ctx=target)

    def start(self, total):
        self.share[...] = total
        self.first = self.copy(
            0, self.share.at[:, self.half_of(1 - self.y)], self.half_in, self.beside
        )
        self.first.start()

    def spread(self):
        self.first.wait_recv()
        mine = self.share[:, self.half_of(self.y)]
        self.half[...] = (mine.astype(F32) + self.half_in[...].astype(F32)).astype(BF)
        self.out = []
        for d, z in enumerate(self.column):
            copy = self.copy(
                1 + d, self.half.at[:, self.piece_of(z)], self.quarters.at[self.z], 2 * z + self.y
            )
            copy.start()
            self.out.append(copy)
        self.quarters[self.z] = self.half[:, self.piece_of(self.z)]

    def total(self):
        for copy in self.out:
            copy.wait_recv()
        done = self.quarters[0].astype(F32)
        for z in range(1, 4):
            done = done + self.quarters[z].astype(F32)
        piece = self.whole.at[:, self.piece_of(self.z, self.y)]
        piece[...] = done.astype(BF)
        self.back = []
        for d, z in enumerate(self.column):
            copy = self.copy(4 + d, piece, piece, 2 * z + self.y)
            copy.start()
            self.back.append(copy)

    def join(self):
        for copy in self.back:
            copy.wait_recv()
        mine = self.whole.at[:, self.half_of(self.y)]
        self.last = self.copy(7, mine, mine, self.beside)
        self.last.start()

    def finish(self):
        self.last.wait_recv()
        for copy in (self.first, *self.out, *self.back, self.last):
            copy.wait_send()


def reduce_kernel(*refs):
    small_ref, ca_far, cb_far, out_far = refs[:4]
    sides_far, fin_ref = refs[4:8], refs[8]
    count = len(NAMES)
    small_out = refs[9]
    full_out = dict(zip((*NAMES, *LATE), refs[10 : 13 + count], strict=True))
    fin_out = refs[13 + count]
    refs = refs[14 + count :]
    low_ref, *sides = refs[:4]
    given = dict(zip(LATE, sides, strict=True))
    full = dict(zip((*NAMES, *LATE), refs[4 : 7 + count], strict=True))
    late_full = full
    move_sem = refs[7 + count]
    refs = refs[8 + count :]
    share = dict(zip(NAMES, refs[:count], strict=True))
    hold = dict(zip(NAMES, refs[count : 2 * count], strict=True))
    refs = refs[2 * count :]
    grid_share, half_in, half, quarters, small_in, small_mid, small_beside, small_column = refs[:8]
    small_send, small_recv, ring_send, ring_recv, grid_send, grid_recv, fin_send, fin_recv = refs[8:16]
    made, turned = refs[16:18]
    moves = Moves(move_sem)
    share_loads = [
        moves.start(*pair)
        for pair in (
            (ca_far.at[:224], share["cq"]),
            (cb_far, share["cv"]),
            (ca_far.at[224:], share["ck"]),
            (out_far.at[:, :32], share["co"]),
            (out_far.at[:, 32:48], share["so0"]),
            (out_far.at[:, 48:], share["so1"]),
        )
    ]
    side_loads = [moves.start(*pair) for pair in zip(sides_far, (low_ref, *sides), strict=True)]
    parts = {name: made.at[u] for u, name in enumerate(LATE)}
    extra = refs[18:]
    fold_wa = Folding(LATE, parts, (extra[0:4], None, extra[4:9]))
    place, after, before = ring_place(RING)
    grids = {
        name: Grid(
            u, grid_share.at[u], half_in.at[u], half.at[u], quarters.at[u], late_full[name], grid_send, grid_recv
        )
        for u, name in enumerate(LATE)
    }
    wa, both = fold_wa.wa, other_wa(fold_wa.across, 1)
    some = grids["q"]
    in_column = [2 * z + some.y for z in some.column]
    meet(
        [{"wa": peer} for peer in (fold_wa.mate, fold_wa.across, both)]
        + [{"ctx": peer} for peer in (after, before, some.beside, *in_column)]
    )
    near = remote(small_ref, small_in.at[0], small_send.at[0], small_recv.at[0], wa=fold_wa.mate)
    near.start()
    over = remote(small_mid.at[0], small_in.at[1], small_send.at[1], small_recv.at[1], wa=fold_wa.across)
    beside = remote(small_mid.at[1], small_beside, small_send.at[2], small_recv.at[2], ctx=some.beside)
    columns = [
        remote(small_mid.at[2], small_column.at[some.z], small_send.at[3 + d], small_recv.at[3 + d], ctx=peer)
        for d, peer in enumerate(in_column)
    ]
    own_fin = pltpu.make_async_copy(fin_ref.at[wa], fin_out.at[:, columns_of(wa)], fin_send.at[3])
    own_fin.start()
    fin_copies = [
        remote(fin_ref.at[peer], fin_out.at[:, columns_of(wa)], fin_send.at[d], fin_recv.at[d], wa=peer)
        for d, peer in enumerate((fold_wa.across, both, fold_wa.mate))
    ]
    wait_all(share_loads)
    copies = {}

    def ring_step(b, name, step):
        way = BUFFERS[name][0]
        here = place if way == 1 else RING - place
        target = after if way == 1 else before
        if step > 0:
            copies[name, step - 1].wait_recv()
        if step == 2 * HOPS:
            return
        now = lax.rem(here - step + 3 * RING, RING)
        mine = chunk_of(share[name], name, now)
        done = chunk_of(full[name], name, now)
        if 0 < step <= HOPS:
            total = mine[...].astype(F32) + hold[name][step - 1].astype(F32)
            (mine if step < HOPS else done)[...] = total.astype(BF)
        src, dst = (mine, hold[name].at[step]) if step < HOPS else (done, done)
        copy = remote(src, dst, ring_send.at[b, step], ring_recv.at[b, step], ctx=target)
        copy.start()
        copies[name, step] = copy

    def small_over():
        near.wait_recv()
        small_mid[0] = small_ref[...] + small_in[0]
        over.start()

    def small_next():
        over.wait_recv()
        small_mid[1] = small_mid[0] + small_in[1]
        beside.start()

    def small_last():
        beside.wait_recv()
        small_mid[2] = small_mid[1] + small_beside[...]
        small_column[some.z] = small_mid[2]
        for copy in columns:
            copy.start()

    def begin(name, following=None):
        total = fold_wa.total(name)
        if following:
            fold_wa.x_copies[following].start()
        grids[name].start(total)

    def make(name):
        parts[name][...] = nn_dot(turned[...], given[name][...]).astype(BF)
        fold_wa.start(name)

    def make_all():
        wait_all(side_loads)
        turned[...] = low_ref[...].astype(F32).T.astype(BF)
        make("q")
        make("k")
        fold_wa.send("q")
        make("v")
        fold_wa.prepare("k")
        fold_wa.prepare("v")

    events = {
        0: [make_all, small_over],
        3: [lambda: begin("q", "k"), small_next],
        5: [grids["q"].spread, lambda: begin("k", "v"), small_last],
        7: [grids["q"].total, grids["k"].spread],
        8: [lambda: begin("v"), grids["q"].join, *(copy.start for copy in fin_copies)],
        9: [grids["k"].total],
        10: [grids["v"].spread, grids["k"].join],
        11: [grids["v"].total],
        12: [grids["v"].join],
    }
    for tick in range(2 * HOPS + 1):
        for b, name in enumerate(NAMES):
            ring_step(b, name, tick)
        for event in events.get(tick, ()):
            event()
    stores = [moves.start(full[name], full_out[name]) for name in NAMES]
    for copy in columns:
        copy.wait_recv()
    total = small_column[0]
    for z in range(1, 4):
        total = total + small_column[z]
    small_out[...] = total
    for name in LATE:
        grids[name].finish()
        stores.append(moves.start(full[name], full_out[name]))
    fold_wa.finish()
    for copy in (near, over, beside, *columns, *copies.values()):
        copy.wait_send()
    own_fin.wait()
    for copy in fin_copies:
        copy.wait()
    wait_all(stores)


def columns_of(owner):
    return pl.ds(pl.multiple_of(owner * 896, WIDE), 896)


def reduce_grads(pair, one, flat, small, low, grads, fin):
    dma = pltpu.SemaphoreType.DMA
    any_spec = pl.BlockSpec(memory_space=pl.ANY)
    late = len(LATE)
    shapes = [*(BUFFERS[b][1] for b in NAMES), *[TALL] * late]
    small, *others = pl.pallas_call(
        reduce_kernel,
        out_shape=(
            jax.ShapeDtypeStruct(small.shape, F32),
            *(jax.ShapeDtypeStruct(shape, BF) for shape in shapes),
            jax.ShapeDtypeStruct((224, 3584), BF),
        ),
        in_specs=vmem(1) + [any_spec] * 8,
        out_specs=tuple(vmem(1) + [any_spec] * (len(shapes) + 1)),
        scratch_shapes=[
            pltpu.VMEM(low.shape, BF),
            *(pltpu.VMEM(grad.shape, BF) for grad in grads),
            *(pltpu.VMEM(shape, BF) for shape in shapes),
            dma((10 + len(shapes),)),
            *(pltpu.VMEM(BUFFERS[b][1], BF) for b in NAMES),
            *(pltpu.VMEM((HOPS, *chunk_shape(b)), BF) for b in NAMES),
            pltpu.VMEM((late, *TALL), BF),
            pltpu.VMEM((late, 224, 4 * WIDE), BF),
            pltpu.VMEM((late, 224, 4 * WIDE), BF),
            pltpu.VMEM((late, 4, 224, WIDE), BF),
            pltpu.VMEM((2, *small.shape), F32),
            pltpu.VMEM((3, *small.shape), F32),
            pltpu.VMEM(small.shape, F32),
            pltpu.VMEM((4, *small.shape), F32),
            dma((6,)),
            dma((6,)),
            dma((len(NAMES), 2 * HOPS)),
            dma((len(NAMES), 2 * HOPS)),
            dma((late, 8)),
            dma((late, 8)),
            dma((4,)),
            dma((3,)),
            pltpu.VMEM((late, 896, 1024), BF),
            pltpu.VMEM((896, 256), BF),
            *Folding.scratch(LATE),
        ],
        compiler_params=pltpu.CompilerParams(
            collective_id=3, has_side_effects=True, vmem_limit_bytes=56 << 20
        ),
        cost_estimate=lasting(90),
        name="reduce_grads",
    )(small, pair, one, flat, low, *grads, fin.reshape(4, 224, 896))
    return *others[:-1], small, others[-1]


WIDENED = ("cq", "ck", "cv", "q", "k", "v", "co", "fin", "fout")


def widen_kernel(*refs):
    count = len(WIDENED)
    so0, so1, near, last, back = refs[count : count + 5]
    outs = refs[count + 5 :]
    for src, dst in zip(refs[:count], outs[:count], strict=True):
        dst[...] = src[...].astype(F32)
    for c in range(so0.shape[0]):
        outs[count][c * 32 : c * 32 + 16, :] = so0[c].astype(F32)
        outs[count][c * 32 + 16 : c * 32 + 32, :] = so1[c].astype(F32)
    span = pl.program_id(0)

    @pl.when(span < 3)
    def _():
        outs[count + 1][...] = near[...]

    @pl.when(span == 3)
    def _():
        outs[count + 1][...] = (last[...] + back[...].astype(F32)).astype(BF)


def widen(full, near, last, back):
    values = [full[name] for name in WIDENED]
    blocks = {
        (224, 1024): ((224, 256), lambda i: (0, i)),
        (256, 896): ((64, 896), lambda i: (i, 0)),
        (224, 3584): ((224, 896), lambda i: (0, i)),
        (896, 896): ((224, 896), lambda i: (i, 0)),
    }
    specs = [pl.BlockSpec(*blocks[v.shape]) for v in values]
    halves = pl.BlockSpec((2, 16, 896), lambda i: (i, 0, 0))
    span = (256, 896)
    still = pl.BlockSpec(span, lambda i: (0, 0))
    moving = pl.BlockSpec(span, lambda i: (i, 0))
    *wide, neighbour = pl.pallas_call(
        widen_kernel,
        grid=(4,),
        out_shape=(
            *(jax.ShapeDtypeStruct(v.shape, F32) for v in values),
            jax.ShapeDtypeStruct(FLAT, F32),
            jax.ShapeDtypeStruct((1024, 896), BF),
        ),
        in_specs=[
            *specs,
            halves,
            halves,
            pl.BlockSpec(span, lambda i: (jnp.minimum(i, 2), 0)),
            still,
            still,
        ],
        out_specs=(*specs, pl.BlockSpec((64, 896), lambda i: (i, 0)), moving),
        compiler_params=pltpu.CompilerParams(vmem_limit_bytes=60 << 20),
        name="widen",
    )(*values, full["so0"], full["so1"], near, last, back)
    return dict(zip((*WIDENED, "so"), wide, strict=True)), neighbour


GELU = (2.0 / math.pi) ** 0.5


def ffn_kernel(
    late, f_ref, bias_ref, win_far, cot_far, wout_far, df_ref, dbias_ref, res_out, parts_out, dwin_out, dwout_out,
    win_ref, cot_ref, wout_ref, res_ref, parts_ref, dwin_ref, dwout_ref, move_sem, f_all, g_all, dul_all, ahead, own, kept, out_mate, out_cross, in_mate, in_cross, x_out, x_in,
    f_send, f_recv, p_send, p_recv,
):
    moves = Moves(move_sem)
    load_in, load_cot, load_out = (
        moves.start(*pair) for pair in ((win_far, win_ref), (cot_far, cot_ref), (wout_far, wout_ref))
    )
    me = lax.axis_index("wa")
    mate, across = other_wa(me, 1), other_wa(me, 2)
    both = other_wa(across, 1)
    barrier = pltpu.get_barrier_semaphore()
    for peer in (mate, across):
        pl.semaphore_signal(barrier, inc=1, device_id={"wa": peer}, device_id_type=MESH)
    pl.semaphore_wait(barrier, 2)
    to_across = remote(f_ref, f_all.at[me], f_send.at[1], f_recv.at[1], wa=across)
    to_across.start()
    to_mate = remote(f_ref, f_all.at[me], f_send.at[0], f_recv.at[0], wa=mate)
    to_mate.start()
    forward = remote(f_all.at[across], f_all.at[across], f_send.at[2], f_recv.at[2], wa=mate)
    f_all[me] = f_ref[...]
    order = (me, mate, across, both)
    dbias_ref[...] = jnp.zeros_like(dbias_ref)
    load_in.wait()
    for k, s in enumerate(order):
        if k == 1:
            to_mate.wait_recv()
        if k == 2:
            for d in range(2):
                ahead[d] = nt_dot(cot_ref[order[2 + d]], wout_ref[...])
            to_across.wait_recv()
            forward.start()
        if k == 3:
            forward.wait_recv()
        u = nn_dot(f_all[s], win_ref[...]) + bias_ref[...]
        square = u * u
        t = jnp.tanh(GELU * (u + 0.044715 * (square * u)))
        g_all[s] = (0.5 * u * (1.0 + t)).astype(BF)
        if k == 0:
            load_cot.wait()
            load_out.wait()
        slope = 0.5 * (1.0 + t) + 0.5 * u * (1.0 - t * t) * (GELU * (1.0 + 3 * 0.044715 * square))
        du = (nt_dot(cot_ref[s], wout_ref[...]) if k < 2 else ahead[k - 2]) * slope
        dbias_ref[...] += jnp.sum(du.reshape(32, 8, du.shape[1]), axis=0)
        dul_all[s] = du.astype(BF)

    def scatter(which, product):
        out_cross[which] = product(both).astype(BF)
        cross = remote(
            out_cross.at[which], in_cross.at[which], p_send.at[which, 0], p_recv.at[which, 0], wa=mate
        )
        cross.start()
        kept[...] = product(across)
        cross.wait_recv()
        x_out[which] = (kept[...] + in_cross[which].astype(F32)).astype(BF)
        over = remote(
            x_out.at[which], x_in.at[which], p_send.at[which, 1], p_recv.at[which, 1], wa=across
        )
        over.start()
        out_mate[which] = product(mate).astype(BF)
        near = remote(
            out_mate.at[which], in_mate.at[which], p_send.at[which, 2], p_recv.at[which, 2], wa=mate
        )
        near.start()
        own[which] = product(me)
        return cross, over, near

    def finish(which, copies, out_ref):
        cross, over, near = copies
        near.wait_recv()
        over.wait_recv()
        out_ref[...] = own[which] + in_mate[which].astype(F32) + x_in[which].astype(F32)
        for copy in copies:
            copy.wait_send()

    df_copies = scatter(0, lambda s: nt_dot(dul_all[s], win_ref[...]))
    if late:
        res_ref[...] = nn_dot(g_all[me], wout_ref[...])
        for d, s in enumerate(order[1:]):
            parts_ref[d] = nn_dot(g_all[s], wout_ref[...]).astype(BF)
    else:
        res_copies = scatter(1, lambda s: nn_dot(g_all[s], wout_ref[...]))
        parts_ref[...] = jnp.zeros_like(parts_ref)
    stores = []
    if late:
        stores += [moves.start(res_ref, res_out), moves.start(parts_ref, parts_out)]
    width = f_ref.shape[1]

    def outer(left_all, right, out_ref):
        for c in range(width // WIDE):
            lanes = slice(c * WIDE, (c + 1) * WIDE)
            total = None
            for s in range(4):
                left = left_all[s, :, lanes].astype(F32).T.astype(BF)
                now = nn_dot(left, right[s])
                total = now if total is None else total + now
            out_ref[lanes, :] = total.astype(BF)

    outer(f_all, dul_all, dwin_ref)
    stores.append(moves.start(dwin_ref, dwin_out))
    outer(g_all, cot_ref, dwout_ref)
    stores.append(moves.start(dwout_ref, dwout_out))
    finish(0, df_copies, df_ref)
    if not late:
        finish(1, res_copies, res_ref)
        stores += [moves.start(res_ref, res_out), moves.start(parts_ref, parts_out)]
    wait_all(stores)
    for copy in (to_mate, to_across, forward):
        copy.wait_send()


def ffn(late, f_low, cot_all, win, wout, bias):
    rows, width = f_low.shape
    hidden = win.shape[1]
    dma = pltpu.SemaphoreType.DMA
    block = (rows, width)
    any_spec = pl.BlockSpec(memory_space=pl.ANY)
    df, dbias, *others = pl.pallas_call(
        functools.partial(ffn_kernel, late),
        out_shape=(
            jax.ShapeDtypeStruct(block, F32),
            jax.ShapeDtypeStruct((8, hidden), F32),
            jax.ShapeDtypeStruct(block, F32),
            jax.ShapeDtypeStruct((3, *block), BF),
            jax.ShapeDtypeStruct(win.shape, BF),
            jax.ShapeDtypeStruct(wout.shape, BF),
        ),
        in_specs=vmem(2) + [any_spec] * 3,
        out_specs=tuple(vmem(2) + [any_spec] * 4),
        scratch_shapes=[
            pltpu.VMEM(win.shape, BF),
            pltpu.VMEM((4, *block), BF),
            pltpu.VMEM(wout.shape, BF),
            pltpu.VMEM(block, F32),
            pltpu.VMEM((3, *block), BF),
            pltpu.VMEM(win.shape, BF),
            pltpu.VMEM(wout.shape, BF),
            dma((7,)),
            pltpu.VMEM((4, *block), BF),
            pltpu.VMEM((4, rows, hidden), BF),
            pltpu.VMEM((4, rows, hidden), BF),
            pltpu.VMEM((2, rows, hidden), F32),
            pltpu.VMEM((2, *block), F32),
            pltpu.VMEM(block, F32),
            *[pltpu.VMEM((2, *block), BF)] * 6,
            dma((3,)),
            dma((3,)),
            dma((2, 3)),
            dma((2, 3)),
        ],
        compiler_params=pltpu.CompilerParams(
            collective_id=4, has_side_effects=True, vmem_limit_bytes=60 << 20
        ),
        cost_estimate=lasting(44),
        name="feed_forward",
    )(f_low, bias, win, cot_all, wout)
    res, parts, dwin, dwout = others
    return res, parts, df, dwin, dwout, dbias


def padded_rows(pad, values):
    rows = values.shape[0]
    pad[...] = jnp.zeros_like(pad)
    pad[1 : rows + 1, :] = values.astype(F32)


def both_heads(pad, g):
    here = pad[g * SPAN : (g + 1) * SPAN, :]
    left = head_mask(0, SPAN)
    return jnp.concatenate([jnp.where(left, here, 0.0), jnp.where(left, 0.0, here)], 0).astype(BF)


def join_heads(stacked):
    return jnp.where(head_mask(0, SPAN), stacked[:SPAN], stacked[SPAN:])


def cross_forward_kernel(groups, keep_ref, q_ref, k_ref, v_ref, x_ref, q_pad, x_pad):
    padded_rows(q_pad, q_ref[...])
    spans = range(groups)
    rows = [slice(g * 256, (g + 1) * 256) for g in spans]
    scores = [nt_dot(both_heads(q_pad, g) * BF(HD**-0.5), k_ref[rows[g], :]) for g in spans]
    weights = [jnp.exp(v - jnp.max(v, axis=1, keepdims=True)) for v in scores]
    weights = [v / jnp.sum(v, axis=1, keepdims=True) for v in weights]
    mixed = [join_heads(nn_dot(weights[g].astype(BF), v_ref[rows[g], :])) for g in spans]
    mixed[0] = mixed[0] * keep_ref[0:1, :]
    for g in spans:
        x_pad[g * SPAN : (g + 1) * SPAN, :] = mixed[g]
    x_ref[...] = x_pad[1 : x_ref.shape[0] + 1, :].astype(BF)


def pair_specs(*rows):
    return [pl.BlockSpec((r, WIDE), lambda p: (0, p)) for r in rows]


def cross_forward(keep, query, keys, values):
    rows, width = query.shape
    many = keys.shape[0]
    groups = many // 256
    return pl.pallas_call(
        functools.partial(cross_forward_kernel, groups),
        grid=(width // WIDE,),
        out_shape=jax.ShapeDtypeStruct(query.shape, BF),
        in_specs=[pl.BlockSpec((8, WIDE), lambda p: (0, 0)), *pair_specs(rows, many, many)],
        out_specs=pair_specs(rows)[0],
        scratch_shapes=[pltpu.VMEM((groups * SPAN, WIDE), F32)] * 2,
        compiler_params=pltpu.CompilerParams(vmem_limit_bytes=16 << 20),
        cost_estimate=lasting(9),
        name="cross_forward",
    )(keep, query, keys, values)


def cross_backward_kernel(
    groups, keep_ref, q_ref, dx_ref, k_ref, v_ref, dq_ref, dk_ref, dv_ref, q_pad, dx_pad, dq_pad
):
    padded_rows(q_pad, q_ref[...])
    padded_rows(dx_pad, dx_ref[...])
    dx_pad[:SPAN, :] = dx_pad[:SPAN, :] * keep_ref[0:1, :]
    for g in range(groups):
        rows = slice(g * 256, (g + 1) * 256)
        query = both_heads(q_pad, g) * BF(HD**-0.5)
        dmixed = both_heads(dx_pad, g)
        keys, values = k_ref[rows, :], v_ref[rows, :]
        scores = nt_dot(keys, query)
        weights = jnp.exp(scores - jnp.max(scores, axis=0, keepdims=True))
        weights = weights / jnp.sum(weights, axis=0, keepdims=True)
        dweights = nt_dot(values, dmixed)
        dscores = weights * (dweights - jnp.sum(weights * dweights, axis=0, keepdims=True))
        dk_ref[rows, :] = nn_dot(dscores.astype(BF), query).astype(BF)
        dv_ref[rows, :] = nn_dot(weights.astype(BF), dmixed).astype(BF)
        back = (dscores * HD**-0.5).T.astype(BF)
        dq_pad[g * SPAN : (g + 1) * SPAN, :] = join_heads(nn_dot(back, keys))
    dq_ref[...] = dq_pad[1 : dq_ref.shape[0] + 1, :].astype(BF)


def cross_backward(keep, query, dmixed, keys, values):
    rows, width = query.shape
    many = keys.shape[0]
    groups = many // 256
    return pl.pallas_call(
        functools.partial(cross_backward_kernel, groups),
        grid=(width // WIDE,),
        out_shape=(
            jax.ShapeDtypeStruct(query.shape, BF),
            jax.ShapeDtypeStruct(keys.shape, BF),
            jax.ShapeDtypeStruct(keys.shape, BF),
        ),
        in_specs=[
            pl.BlockSpec((8, WIDE), lambda p: (0, 0)),
            *pair_specs(rows, rows, many, many),
        ],
        out_specs=tuple(pair_specs(rows, many, many)),
        scratch_shapes=[pltpu.VMEM((groups * SPAN, WIDE), F32)] * 3,
        compiler_params=pltpu.CompilerParams(vmem_limit_bytes=16 << 20),
        cost_estimate=lasting(17),
        name="cross_backward",
    )(keep, query, dmixed, keys, values)


def line_selector():
    place = jnp.arange(LINE)
    offset = jnp.where(place < LINE // 2, -place, LINE - place)
    return (bucket_of(offset)[None, :] == jnp.arange(NB)[:, None]).astype(jnp.float32)


def ring_forward(query_low, key_low, value_low, bucket_table):
    row_count, attn_width = query_low.shape
    position = lax.axis_index("ctx")
    scale_factor = HD ** (-0.5)
    bias_set, onehots = make_bias(bucket_table.astype(jnp.float32), row_count)
    query_heads = query_low.reshape(row_count, H, HD)
    start_state = (
        jnp.full((H, row_count), negative, jnp.float32),
        jnp.zeros((H, row_count), jnp.float32),
        jnp.zeros((row_count, attn_width), jnp.float32),
    )
    running_max, running_sum, running_acc = forward_fold(
        query_heads,
        position,
        row_count,
        bias_set,
        scale_factor,
        start_state,
        (
            lax.all_gather(key_low, "ctx", axis=0, tiled=True),
            lax.all_gather(value_low, "ctx", axis=0, tiled=True),
        ),
    )
    attended = (running_acc.reshape(row_count, H, HD) / running_sum.T[:, :, None]).reshape(
        row_count, attn_width
    )
    log_total = running_max + jnp.log(running_sum)
    state = (query_heads, key_low, value_low, attended, log_total, bias_set, onehots)
    return attended.astype(jnp.bfloat16), state


def ring_backward(state, dout_low):
    query_heads, key_low, value_low, attended, log_total, bias_set, onehots = state
    row_count, attn_width = dout_low.shape
    cycle_size = lax.axis_size("ctx")
    position = lax.axis_index("ctx")
    scale_factor = HD ** (-0.5)
    dout_heads = dout_low.reshape(row_count, H, HD)
    row_delta = jnp.sum(
        (dout_low.astype(jnp.float32) * attended).reshape(row_count, H, HD), axis=-1
    ).T
    zero_rows = jnp.zeros((row_count, attn_width), jnp.float32)
    zero_tables = (
        jnp.zeros((H, row_count, row_count), jnp.float32),
        jnp.zeros((H, row_count, row_count), jnp.float32),
        jnp.zeros((H,), jnp.float32),
    )

    def visit(folded, key_now, value_now, relation):

        def visit_compute(current):
            dquery_acc, dkey_acc, dvalue_acc, relative_bias_tables = current
            key_heads = key_now.reshape(row_count, H, HD)
            weights_now, dscores, ds_low = pair_core(
                query_heads,
                dout_heads,
                log_total,
                row_delta,
                key_heads,
                value_now.reshape(row_count, H, HD),
                relation,
                bias_set,
                scale_factor,
            )
            dquery = jnp.einsum(
                "hqk,khd->qhd", ds_low, key_heads, preferred_element_type=jnp.float32
            ).reshape(row_count, attn_width)
            dkey = jnp.einsum(
                "hqk,qhd->khd", ds_low, query_heads, preferred_element_type=jnp.float32
            ).reshape(row_count, attn_width)
            dvalue = jnp.einsum(
                "hqk,qhd->khd",
                weights_now.astype(jnp.bfloat16),
                dout_heads,
                preferred_element_type=jnp.float32,
            ).reshape(row_count, attn_width)
            return (
                dquery_acc + dquery,
                dkey_acc + dkey,
                dvalue_acc + dvalue,
                add_tables(relative_bias_tables, dscores, relation),
            )

        return lax.cond(relation >= 0, visit_compute, lambda unchanged: unchanged, folded)

    first_state = visit(
        (zero_rows, zero_rows, zero_rows, zero_tables), key_low, value_low, jnp.array(0, jnp.int32)
    )

    def cycle_step(carried, cycle_index):
        key_now, value_now, (dquery_acc, dkey_acc, dvalue_acc, relative_bias_tables) = carried
        key_next, value_next = passed_along((key_now, value_now), "ctx", 1)
        dkey_next, dvalue_next = (
            from_behind(dkey_acc.astype(jnp.bfloat16), "ctx", 1).astype(dkey_acc.dtype),
            from_behind(dvalue_acc.astype(jnp.bfloat16), "ctx", 1).astype(dvalue_acc.dtype),
        )
        relation = jnp.where(position >= cycle_index, cycle_index, -1)
        updated = visit(
            (dquery_acc, dkey_next, dvalue_next, relative_bias_tables),
            key_next,
            value_next,
            relation,
        )
        return ((key_next, value_next, updated), None)

    (
        unused_key,
        unused_value,
        (dquery_total, dkey_part, dvalue_part, relative_bias_tables),
    ), unused = lax.scan(cycle_step, (key_low, value_low, first_state), jnp.arange(1, cycle_size))
    dkey_total, dvalue_total = (
        from_behind(dkey_part.astype(jnp.bfloat16), "ctx", 1).astype(dkey_part.dtype),
        from_behind(dvalue_part.astype(jnp.bfloat16), "ctx", 1).astype(dvalue_part.dtype),
    )
    dquery_low = dquery_total.astype(jnp.bfloat16)
    dkey_low = dkey_total.astype(jnp.bfloat16)
    dvalue_low = dvalue_total.astype(jnp.bfloat16)
    current_bucket_selector, previous_bucket_selector, onehot_far = onehots
    grad_biastable = (
        jnp.einsum(
            "afw,mfw->am",
            current_bucket_selector,
            relative_bias_tables[0],
            precision=strongest_precision,
        )
        + jnp.einsum(
            "afw,mfw->am",
            previous_bucket_selector,
            relative_bias_tables[1],
            precision=strongest_precision,
        )
        + onehot_far[:, None] * relative_bias_tables[2][None, :]
    )
    return dquery_low, dkey_low, dvalue_low, grad_biastable


def heads_forward(tokens, near, cotangent, given):
    wa, owners = lax.axis_index("wa"), lax.axis_size("wa")
    table = given["biastable"].astype(F32)
    selector = lax.dynamic_slice_in_dim(line_selector(), wa * table.shape[0], table.shape[0], 0)
    lines = jnp.dot(table.T, selector, precision=strongest_precision).astype(BF)
    gains = jnp.concatenate([given[name] for name in GAINS]).reshape(len(GAINS), -1)
    small = jnp.zeros((H, LINE), BF)
    small = lax.dynamic_update_slice(small, gains, (0, wa * gains.shape[1]))
    small = jnp.concatenate([lines, small], 0)
    shards = [given[LONG_NAMES[name]] for name in GATHERED]
    *wholes, upstream_all, feed_in, attended_low, low, ot, lse, small, before, qh, kh, vh, keys, values = attn_forward(
        lax.axis_size("ctx"), tokens, small, near, [*shards, cotangent], given["feedin"]
    )
    width = tokens.shape[1]
    gain_of = {name: small[H + g, :width] for g, name in enumerate(GAINS)}
    full = {LONG_NAMES[name]: whole for name, whole in zip(GATHERED, wholes, strict=True)}
    full["feedin"] = feed_in
    upstream_all = upstream_all.reshape(owners, *tokens.shape)
    saved = (qh, kh, vh, ot, lse, small[:H])
    return attended_low, low, full, gain_of, upstream_all, (before, keys, values), saved


def heads_backward(state, dout_low, parts, feed_part, span):
    peers = lax.axis_size("ctx")
    dquery_low, dkey_low, dvalue_low, sums, *shares = attn_backward(
        peers, dout_low, *state, parts, feed_part, span
    )
    selector = line_selector()
    table = jnp.dot(selector, sums[:2].T, precision=strongest_precision)
    far = jnp.sum(sums[2:4], axis=1)
    table = table + selector[:, WIDE : WIDE + 1] * far[None, :]
    whole = jnp.zeros((NB, H), jnp.float32)
    whole = lax.dynamic_update_slice(whole, table, (0, 2 * lax.axis_index("ctx")))
    return dquery_low, dkey_low, dvalue_low, whole, shares


def cross_pair(groups, keep_ref, q_ref, dx_ref, k_ref, v_ref, dq_ref, dk_ref, dv_ref, q_pad, dx_pad, dq_pad, p):
    lanes = lanes_of(p)
    padded_rows(q_pad, q_ref[:, lanes])
    padded_rows(dx_pad, dx_ref[:, lanes])
    dx_pad[:SPAN, :] = dx_pad[:SPAN, :] * keep_ref[0:1, :]
    for g in range(groups):
        rows = slice(g * 256, (g + 1) * 256)
        query = both_heads(q_pad, g) * BF(HD**-0.5)
        dmixed = both_heads(dx_pad, g)
        keys, values = k_ref[rows, lanes], v_ref[rows, lanes]
        scores = nt_dot(keys, query)
        weights = jnp.exp(scores - jnp.max(scores, axis=0, keepdims=True))
        weights = weights / jnp.sum(weights, axis=0, keepdims=True)
        dweights = nt_dot(values, dmixed)
        dscores = weights * (dweights - jnp.sum(weights * dweights, axis=0, keepdims=True))
        dk_ref[rows, lanes] = nn_dot(dscores.astype(BF), query).astype(BF)
        dv_ref[rows, lanes] = nn_dot(weights.astype(BF), dmixed).astype(BF)
        back = (dscores * HD**-0.5).T.astype(BF)
        dq_pad[g * SPAN : (g + 1) * SPAN, :] = join_heads(nn_dot(back, keys))
    dq_ref[:, lanes] = dq_pad[1 : dq_ref.shape[0] + 1, :].astype(BF)


def middle_kernel(
    keep_ref, fed_ref, fed_parts, q_far, dx_far, k_far, v_far, before_far, near_far, wk_far, wv_far, fin_ref,
    fout_ref, feed_out, fed_out, dq_out, dwk_out, dwv_out, first_out, near_out, last_out,
    q_ref, dx_ref, k_ref, v_ref, before_ref, near_ref, wk_ref, wv_ref, dq_ref, dwk_ref, dwv_ref, near_low, near_last,
    dk, dv, q_pad, dx_pad, dq_pad, share, hold, in_mate, in_cross, x_out, x_in, load_sem, ring_send, ring_recv,
    fed_send, fed_recv,
):
    ring = Ring(FEED_LANES, ring_send, ring_recv, share=share, hold=hold)
    moves = Moves(load_sem)
    loads = [moves.start(part, share.at[b]) for b, part in enumerate((fin_ref, fout_ref))]
    pair_loads = [
        moves.start(*pair) for pair in ((q_far, q_ref), (dx_far, dx_ref), (k_far, k_ref), (v_far, v_ref))
    ]
    later_loads = [
        moves.start(*pair)
        for pair in ((wk_far, wk_ref), (wv_far, wv_ref), (before_far, before_ref), (near_far, near_ref))
    ]
    wa = lax.axis_index("wa")
    mate, across = other_wa(wa, 1), other_wa(wa, 2)
    meet([{"ctx": ring.after}, {"ctx": ring.before}, {"wa": mate}, {"wa": across}])
    cross = remote(fed_parts.at[2], in_cross, fed_send.at[0], fed_recv.at[0], wa=mate)
    cross.start()
    near = remote(fed_parts.at[0], in_mate, fed_send.at[1], fed_recv.at[1], wa=mate)
    near.start()
    over = remote(x_out, x_in, fed_send.at[2], fed_recv.at[2], wa=across)
    wait_all(loads)
    for lanes in FEED_TURNS:
        ring.scatter(jnp.int32(0), lanes)
    cross.wait_recv()
    x_out[...] = (fed_parts[1].astype(F32) + in_cross[...].astype(F32)).astype(BF)
    over.start()
    groups = k_ref.shape[0] // 256
    wait_all(pair_loads)

    def two_pairs(m, unused):
        for turn, lanes in enumerate(FEED_TURNS):
            cross_pair(
                groups, keep_ref, q_ref, dx_ref, k_ref, v_ref, dq_ref, dk, dv, q_pad, dx_pad, dq_pad,
                2 * m + turn,
            )
            ring.scatter(m + 1, lanes)
        return unused

    pairs = q_ref.shape[1] // (2 * WIDE)
    lax.fori_loop(0, pairs, two_pairs, 0)
    stores = [moves.start(dq_ref, dq_out)]
    wait_all(later_loads)
    calls = [(step, lanes) for step in range(pairs + 1, HOPS + 1) for lanes in FEED_TURNS]

    def turn():
        if calls:
            step, lanes = calls.pop(0)
            ring.scatter(jnp.int32(step), lanes)

    for g in range(groups):
        rows = slice(g * 256, (g + 1) * 256)
        total = nt_dot(dk[rows, :], wk_ref[...]) + nt_dot(dv[rows, :], wv_ref[...])
        if g == groups - 1:
            near_last[...] = total
        else:
            near_low[rows, :] = total.astype(BF)
        if g % 2 == 1:
            turn()
    stores += [
        moves.start(near_low.at[:256], first_out),
        moves.start(near_low.at[256:], near_out),
        moves.start(near_last, last_out),
    ]
    for c in range(near_ref.shape[1] // WIDE):
        lanes = slice(c * WIDE, (c + 1) * WIDE)
        first = before_ref[:, lanes].astype(F32).T.astype(BF)
        left = near_ref[:, lanes].astype(F32).T.astype(BF)
        for grads, out_ref in ((dk, dwk_ref), (dv, dwv_ref)):
            total = nn_dot(first, grads[:256, :]) + nn_dot(left, grads[256:, :])
            out_ref[lanes, :] = total.astype(BF)
        if c % 2 == 1:
            turn()
    stores += [moves.start(dwk_ref, dwk_out), moves.start(dwv_ref, dwv_out)]
    while calls:
        turn()
    near.wait_recv()
    over.wait_recv()
    fed_out[...] = fed_ref[...] + in_mate[...].astype(F32) + x_in[...].astype(F32)
    for copy in (cross, near, over):
        copy.wait_send()
    for lane in range(2):
        feed_out[lane] = share[lane, ring.chunk(lane, 1)]
    ring.finish(lambda lane: share.at[FEED_LANES[lane][0], 0, FEED_LANES[lane][2]])
    wait_all(stores)


def middle(keep, query, dmixed, keys, values, before, near, wk, wv, fed, fed_parts, fin, fout):
    many, width = keys.shape
    wide = near.shape[1]
    rows = query.shape[0]
    low = functools.partial(jax.ShapeDtypeStruct, dtype=BF)
    dma = pltpu.SemaphoreType.DMA
    any_spec = pl.BlockSpec(memory_space=pl.ANY)
    pad = pltpu.VMEM((many // 256 * SPAN, WIDE), F32)
    feed_part, fed, *others = pl.pallas_call(
        middle_kernel,
        out_shape=(
            low((2, *FEED[1:])),
            jax.ShapeDtypeStruct(fed.shape, F32),
            low(query.shape),
            low(wk.shape),
            low(wv.shape),
            low((256, wide)),
            low((many - 512, wide)),
            jax.ShapeDtypeStruct((256, wide), F32),
        ),
        in_specs=vmem(3) + [any_spec] * 10,
        out_specs=tuple(vmem(2) + [any_spec] * 6),
        scratch_shapes=[
            *[pltpu.VMEM((rows, width), BF)] * 2,
            *[pltpu.VMEM((many, width), BF)] * 2,
            pltpu.VMEM((256, wide), BF),
            pltpu.VMEM((many - 256, wide), BF),
            *[pltpu.VMEM(wk.shape, BF)] * 2,
            pltpu.VMEM((rows, width), BF),
            *[pltpu.VMEM(wk.shape, BF)] * 2,
            pltpu.VMEM((many - 256, wide), BF),
            pltpu.VMEM((256, wide), F32),
            pltpu.VMEM((many, width), BF),
            pltpu.VMEM((many, width), BF),
            pad,
            pad,
            pad,
            pltpu.VMEM((2, *FEED), BF),
            pltpu.VMEM((2, HOPS, *FEED[1:]), BF),
            *[pltpu.VMEM(fed.shape, BF)] * 4,
            dma((16,)),
            dma((len(FEED_LANES), HOPS)),
            dma((len(FEED_LANES), HOPS)),
            dma((3,)),
            dma((3,)),
        ],
        compiler_params=pltpu.CompilerParams(
            collective_id=5, has_side_effects=True, vmem_limit_bytes=60 << 20
        ),
        cost_estimate=lasting(38),
        name="middle",
    )(
        keep, fed, fed_parts, query, dmixed, keys, values, before, near, wk, wv,
        fin.reshape(FEED), fout.reshape(FEED),
    )
    return *others, feed_part, fed


NAMES_OF_WEIGHTS = (
    "selfnorm", "selfquery", "selfkey", "selfvalue", "selfout", "biastable", "crossnorm", "crossquery",
    "crosskey", "crossvalue", "crossout", "feednorm", "feedin", "feedbias", "feedout", "outbias",
)
LONG_NAMES = {
    "q": "selfquery",
    "k": "selfkey",
    "v": "selfvalue",
    "so": "selfout",
    "ck": "crosskey",
    "cv": "crossvalue",
    "cq": "crossquery",
    "co": "crossout",
}


def whole_over_wa(shard):
    return lax.all_gather(shard, "wa", axis=0, tiled=True)


def reduce_plain(parts, smalls):
    shares = [
        lax.psum_scatter(part, "wa", scatter_dimension=0, tiled=True).astype(F32)
        for part in parts.values()
    ]
    totals = lax.psum(shares, "ctx")
    return dict(zip(parts, totals, strict=True)), lax.psum(smalls, ("ctx", "wa"))


def per_device(tokens, neighbours, cotangent, *shards):
    given = dict(zip(NAMES_OF_WEIGHTS, shards, strict=True))
    peers = lax.axis_size("ctx")
    position = lax.axis_index("ctx")
    row_count, model_width = tokens.shape[1:]
    split_heads = peers * 2 == H and row_count == BLOCK
    inputs = tokens[0].astype(F32)
    upstream_low = cotangent[0]
    upstream = upstream_low.astype(F32)
    spans = neighbours.shape[1]
    span_rows = neighbours.shape[2] * neighbours.shape[3]
    own_rows = neighbours[0].reshape(spans * span_rows, model_width)
    if split_heads and span_rows == BLOCK:
        attended_low, normed_low, full, small_of, upstream_all, projected, attention_state = (
            heads_forward(tokens[0], own_rows, upstream_low, given)
        )
        before, keys_cross, values_cross = projected
        feed_in = full["feedin"]
        normed_self, back_self = jax.vjp(root_norm, inputs, small_of["selfnorm"])
    else:
        small_of = {name: whole_over_wa(given[name]).astype(F32) for name in GAINS}
        full = {name: whole_over_wa(given[name]) for name in LONG_NAMES.values()}
        normed_self, back_self = jax.vjp(root_norm, inputs, small_of["selfnorm"])
        normed_low = normed_self.astype(BF)
        attended_low, attention_state = ring_forward(
            *(
                forward_product(normed_low, full[name]).astype(BF)
                for name in ("selfquery", "selfkey", "selfvalue")
            ),
            whole_over_wa(given["biastable"]),
        )
        upstream_all = lax.all_gather(upstream_low, "wa", axis=0)
        feed_in = lax.all_to_all(given["feedin"], "wa", 1, 0, tiled=True)
        before = passed_along(own_rows[-span_rows:], "ctx", 1)
        near_rows = jnp.concatenate([before, own_rows], 0)
        keys_cross = forward_product(near_rows, full["crosskey"]).astype(BF)
        values_cross = forward_product(near_rows, full["crossvalue"]).astype(BF)
    hidden = inputs + forward_product(attended_low, full["selfout"])

    normed_cross, back_cross = jax.vjp(root_norm, hidden, small_of["crossnorm"])
    cross_in = normed_cross.astype(BF)
    query_cross = forward_product(cross_in, full["crossquery"]).astype(BF)
    keep = jnp.full((8, WIDE), jnp.where(position > 0, 1.0, 0.0), F32)
    mixed_low = cross_forward(keep, query_cross, keys_cross, values_cross)
    hidden_two = hidden + forward_product(mixed_low, full["crossout"])

    normed_feed, back_feed = jax.vjp(root_norm, hidden_two, small_of["feednorm"])
    feed_low = normed_feed.astype(BF)
    bias_row = given["feedbias"].astype(F32)[None]
    fed, fed_parts, grad_feed, fin, fout, bias_sums = ffn(
        split_heads, feed_low, upstream_all, feed_in, given["feedout"], bias_row
    )
    grad_two_part, grad_feednorm = back_feed(grad_feed)
    grad_two = upstream + grad_two_part
    two_low = grad_two.astype(BF)

    grad_mixed = back_product(two_low, full["crossout"]).astype(BF)
    early = {}
    if split_heads:
        grad_query_cross, early["ck"], early["cv"], first, near_low, near_last, feed_part, fed = middle(
            keep,
            query_cross,
            grad_mixed,
            keys_cross,
            values_cross,
            before,
            own_rows,
            full["crosskey"],
            full["crossvalue"],
            fed,
            fed_parts,
            fin,
            fout,
        )
    else:
        grad_query_cross, dkeys, dvalues = cross_backward(
            keep, query_cross, grad_mixed, keys_cross, values_cross
        )
        near_grads = back_product(dkeys, full["crosskey"]) + back_product(
            dvalues, full["crossvalue"]
        )
        first, near_last = near_grads[:span_rows].astype(BF), near_grads[-span_rows:]
        near_low = near_grads[span_rows:-span_rows].astype(BF)
        early["ck"] = outer_product(near_rows, dkeys).astype(BF)
        early["cv"] = outer_product(near_rows, dvalues).astype(BF)
    result = (hidden_two + fed + small_of["outbias"]).astype(BF)
    grad_hidden_part, grad_crossnorm = back_cross(
        back_product(grad_query_cross, full["crossquery"])
    )
    grad_hidden = grad_two + grad_hidden_part
    hidden_low = grad_hidden.astype(BF)
    dout_low = back_product(hidden_low, full["selfout"]).astype(BF)
    sides = {
        "cq": (cross_in, grad_query_cross),
        "co": (mixed_low, two_low),
        "so": (attended_low, hidden_low),
    }
    if split_heads:
        parts = [early["ck"], early["cv"], *(side for name in MADE for side in sides[name])]
        dquery_low, dkey_low, dvalue_low, grad_biastable, shares = heads_backward(
            attention_state, dout_low, parts, feed_part, first
        )
        *shares, fin, fout, back = shares
    else:
        dquery_low, dkey_low, dvalue_low, grad_biastable = ring_backward(attention_state, dout_low)
        back = passed_along(first, "ctx", -1)
    grad_normed = (
        back_product(dquery_low, full["selfquery"])
        + back_product(dkey_low, full["selfkey"])
        + back_product(dvalue_low, full["selfvalue"])
    )
    grad_input_part, grad_selfnorm = back_self(grad_normed)
    grad_inputs = (grad_hidden + grad_input_part).astype(BF)

    late_grads = (dquery_low, dkey_low, dvalue_low)
    wa, owners = lax.axis_index("wa"), lax.axis_size("wa")
    bias_grad = jnp.sum(bias_sums, axis=0)
    placed = lax.dynamic_update_slice(
        jnp.zeros((owners, bias_grad.size), F32), bias_grad[None], (wa, 0)
    )
    sums = [grad_selfnorm, grad_crossnorm, grad_feednorm, jnp.sum(upstream, axis=0), grad_biastable]
    packed = jnp.concatenate([*(v.reshape(owners, -1) for v in sums), placed], axis=1)
    packed = jnp.pad(packed, ((0, 0), (0, LINE * 2 - packed.shape[1]))).reshape(-1, WIDE)
    if split_heads:
        *reduced, packed, fin = reduce_grads(
            *shares, packed, normed_low, late_grads, fin
        )
        reduced = dict(zip((*NAMES, *LATE), reduced, strict=True))
        reduced["co"] = reduced["co"].reshape(FLAT)
        reduced |= {"fin": fin, "fout": fout.reshape(given["feedout"].shape)}
        grads, grad_neigh = widen(reduced, near_low, near_last, back)
    else:
        for name, grad in zip(LATE, late_grads, strict=True):
            sides[name] = (normed_low, grad)
        for name, (left, right) in sides.items():
            early[name] = outer_product(left, right).astype(BF)
        grads, packed = reduce_plain(early, packed)
        fin, fout = lax.psum((fin, fout), "ctx")
        fin = lax.all_to_all(fin, "wa", 0, 1, tiled=True)
        grads["fin"], grads["fout"] = fin.astype(F32), fout.astype(F32)
        grad_neigh = jnp.concatenate([near_low, (near_last + back.astype(F32)).astype(BF)], 0)
    grad_neigh = grad_neigh.reshape(neighbours.shape)
    mine = lax.dynamic_index_in_dim(packed.reshape(owners, -1), wa, 0, keepdims=False)
    cuts, start = [], 0
    for v in (*sums, placed):
        cuts.append(mine[start : start + v.size // owners])
        start += v.size // owners
    own_selfnorm, own_crossnorm, own_feednorm, own_outbias, own_table, own_feedbias = cuts
    return (
        result[None],
        grad_inputs[None],
        grad_neigh,
        own_selfnorm,
        grads["q"],
        grads["k"],
        grads["v"],
        grads["so"],
        own_table.reshape(-1, H),
        own_crossnorm,
        grads["cq"],
        grads["ck"],
        grads["cv"],
        grads["co"],
        own_feednorm,
        grads["fin"],
        own_feedbias,
        grads["fout"],
        own_outbias,
    )


def solution(mesh):
    return jax.shard_map(
        per_device,
        mesh=mesh,
        in_specs=(
            P("wa", "ctx", None),
            P("wa", "ctx", None, None, None),
            P("wa", "ctx", None),
            P("wa"),
            P("wa", None),
            P("wa", None),
            P("wa", None),
            P("wa", None),
            P("wa", None),
            P("wa"),
            P("wa", None),
            P("wa", None),
            P("wa", None),
            P("wa", None),
            P("wa"),
            P("wa", None),
            P("wa"),
            P("wa", None),
            P("wa"),
        ),
        out_specs=(
            P("wa", "ctx", None),
            P("wa", "ctx", None),
            P("wa", "ctx", None, None, None),
            P("wa"),
            P("wa", None),
            P("wa", None),
            P("wa", None),
            P("wa", None),
            P("wa", None),
            P("wa"),
            P("wa", None),
            P("wa", None),
            P("wa", None),
            P("wa", None),
            P("wa"),
            P("wa", None),
            P("wa"),
            P("wa", None),
            P("wa"),
        ),
        check_vma=False,
    )
```
